32 devices in a mesh: fsdp: 16 (over z, y, core), tp: 2 (over x).
Axes of the slice: x: 2, y: 2, z: 4, core: 2. Of those that a mesh axis runs over, the one named last changes fastest.
Arguments:
- points: bfloat16 [192, 512], P('fsdp'), may hold values from -6 to 6
- missing: int32 [192, 512], P('fsdp'), may hold values 0 or 1
- tok_hidden_w: bfloat16 [2, 640, 64], P('tp', 'fsdp'), may hold values from -0.75 to 0.75
- tok_hidden_b: bfloat16 [2, 640], P('tp', 'fsdp'), may hold values from -3 to 3
- tok_out_w: bfloat16 [1280, 1280], P('fsdp', 'tp'), may hold values from -0.15625 to 0.15625
- tok_res_w: bfloat16 [1280, 64], P('fsdp', 'tp'), may hold values from -0.75 to 0.75
- tok_out_b: bfloat16 [1280], P('fsdp'), may hold values from -3 to 3
- attn_gain: bfloat16 [1280], P('fsdp'), may hold values from 0.25 to 1.75
- qkv_w: bfloat16 [1280, 3, 1280], P('fsdp', None, 'tp'), may hold values from -0.15625 to 0.15625
- attn_out_w: bfloat16 [1280, 1280], P('fsdp', 'tp'), may hold values from -0.3125 to 0.3125
- mlp_gain: bfloat16 [1280], P('fsdp'), may hold values from 0.25 to 1.75
- mlp_in_w: bfloat16 [1280, 5120], P('fsdp', 'tp'), may hold values from -0.15625 to 0.15625
- mlp_in_b: bfloat16 [2, 2560], P('tp', 'fsdp'), may hold values from -3 to 3
- mlp_out_w: bfloat16 [1280, 5120], P('fsdp', 'tp'), may hold values from -0.078125 to 0.078125
- mlp_out_b: bfloat16 [1280], P('fsdp'), may hold values from -3 to 3
- cotangent: bfloat16 [3072, 1280], P('fsdp'), may hold values from -6 to 6
Outputs:
- output: bfloat16 [3072, 1280], P('fsdp')
- points_grad: float32 [192, 512], P('fsdp')
- grad_tok_hidden_w: float32 [2, 640, 64], P('tp', 'fsdp')
- grad_tok_hidden_b: float32 [2, 640], P('tp', 'fsdp')
- grad_tok_out_w: float32 [1280, 1280], P('fsdp', 'tp')
- grad_tok_res_w: float32 [1280, 64], P('fsdp', 'tp')
- grad_tok_out_b: float32 [1280], P('fsdp')
- grad_attn_gain: float32 [1280], P('fsdp')
- grad_qkv_w: float32 [1280, 3, 1280], P('fsdp', None, 'tp')
- grad_attn_out_w: float32 [1280, 1280], P('fsdp', 'tp')
- grad_mlp_gain: float32 [1280], P('fsdp')
- grad_mlp_in_w: float32 [1280, 5120], P('fsdp', 'tp')
- grad_mlp_in_b: float32 [2, 2560], P('tp', 'fsdp')
- grad_mlp_out_w: float32 [1280, 5120], P('fsdp', 'tp')
- grad_mlp_out_b: float32 [1280], P('fsdp')
The draws below stay inside these ranges and needn't reach their ends.
Inputs may be any that keep to these rules, and one draw needn't show every extreme that they name: 1 marks a missing point, 0 an observed one.
All inputs are finite; a program needn't handle non-finite values. No bound on the sum of `missing` on one device may be relied on, other than what follows from the above.
Results may differ from the reference program's by a relative error of at most 0.02.
Values may be sent and summed in bfloat16 or wider, within the bound.
A program may use at most 192 MiB of HBM per device.

```python
import math
import jax
import jax.numpy as jnp
from jax import lax

D = 1280
HEADS = 16
HEAD_DIM = 80
FF = 5120
PL = 32
CTXLEN = 16
CONTEXTS = 192
TOKENS = 3072
N_TP = 2


def touch_ends(values, key, low, top_value):
    dims = values.shape
    index_at = [jax.random.randint(jax.random.fold_in(key, axis), (), 0, dims[axis]) for axis in range(len(dims))]
    values = values.at[tuple(index_at)].set(low)
    longest = dims.index(max(dims))
    index_at[longest] = (index_at[longest] + 1) % dims[longest]
    return values.at[tuple(index_at)].set(top_value)


def strengthened(values, key, source, target, blocks, factor):
    owner, partner = [(jnp.arange(values.shape[dim]) // (values.shape[dim] // blocks)).reshape([-1 if axis == dim else 1 for axis in range(values.ndim)]) for dim in (source, target)]
    chosen = jax.random.permutation(key, blocks)[partner]
    strong = (owner == chosen) | (owner == (partner + blocks // 2) % blocks)
    return jnp.where(strong, factor * values, values)


def levels(key, dims, shards, low, largest):
    factor_of, own = 1.0, jax.random.fold_in(key, 6)
    for dim, shards_of in shards:
        heights = jnp.exp(jax.random.uniform(jax.random.fold_in(own, dim), (shards_of,), jnp.float32, low / len(shards), largest / len(shards)))
        factor_of = factor_of * jnp.repeat(heights, dims[dim] // shards_of).reshape([-1 if axis == dim else 1 for axis in range(len(dims))])
    return factor_of


def normal_values(rng, dims, width, limit, shards=(), kind=jnp.bfloat16):
    drawn = width * jax.random.normal(rng, dims, jnp.float32)
    if shards:
        drawn = drawn * levels(rng, dims, shards, -0.22, 0.18)
    return jnp.clip(drawn, -limit, limit).astype(kind)


def heavy_noise(stream_key, shape, deviation, bound, cuts, heavy, held_as=jnp.bfloat16):
    values = deviation * jax.random.normal(stream_key, shape, jnp.float32)
    if cuts:
        values = values * levels(stream_key, shape, cuts, -0.22, 0.18)
    return jnp.clip(strengthened(values, jax.random.fold_in(stream_key, 3), *heavy), -bound, bound).astype(held_as)


def setup_inputs(seed: int = 0) -> dict:
    keys = jax.random.split(jax.random.key(seed), 17)
    return {
        "points": normal_values(keys[0], (CONTEXTS, CTXLEN * PL), 1.0, 6.0, ((0, 16),)),
        "missing": touch_ends((jax.random.randint(keys[1], (CONTEXTS, CTXLEN * PL), 0, 5) < 1).astype(jnp.int32), jax.random.fold_in(keys[1], 1), 0, 1),
        "tok_hidden_w": normal_values(keys[2], (N_TP, D // N_TP, 2 * PL), (2 * PL) ** -0.5, 0.75, ((0, 2), (1, 16))),
        "tok_hidden_b": normal_values(keys[3], (N_TP, D // N_TP), 0.5, 3.0, ((0, 2), (1, 16))),
        "tok_out_w": normal_values(keys[4], (D, D), D ** -0.5, 0.15625, ((0, 16), (1, 2))),
        "tok_res_w": normal_values(keys[5], (D, 2 * PL), (2 * PL) ** -0.5, 0.75, ((0, 16), (1, 2))),
        "tok_out_b": normal_values(keys[6], (D,), 0.5, 3.0, ((0, 16),)),
        "attn_gain": jnp.clip(1.0 + 0.15 * jax.random.normal(keys[7], (D,), jnp.float32), 0.25, 1.75).astype(jnp.bfloat16),
        "qkv_w": normal_values(keys[8], (D, 3, D), D ** -0.5, 0.15625, ((0, 16), (2, 2))),
        "attn_out_w": normal_values(keys[9], (D, D), (D // 4) ** -0.5, 0.3125, ((0, 16), (1, 2))),
        "mlp_gain": jnp.clip(1.0 + 0.15 * jax.random.normal(keys[10], (D,), jnp.float32), 0.25, 1.75).astype(jnp.bfloat16),
        "mlp_in_w": normal_values(keys[11], (D, FF), D ** -0.5, 0.15625, ((0, 16), (1, 2))),
        "mlp_in_b": normal_values(keys[12], (N_TP, FF // N_TP), 0.5, 3.0, ((0, 2), (1, 16))),
        "mlp_out_w": normal_values(keys[13], (D, FF), FF ** -0.5, 0.078125, ((0, 16), (1, 2))),
        "mlp_out_b": normal_values(keys[14], (D,), 0.5, 3.0, ((0, 16),)),
        "cotangent": heavy_noise(keys[15], (TOKENS, D), 1.0, 6.0, ((0, 16),), (0, 1, 16, 2.0)),
    }


@jax.custom_vjp
def low(v):
    return lax.optimization_barrier(v.astype(jnp.bfloat16)).astype(jnp.float32)

@jax.custom_vjp
def low_back(v):
    return v

def low_keep(v):
    return (low(v), None)

def low_pass(kept, grad):
    return (grad,)

def back_keep(v):
    return (v, None)

def back_low(kept, grad):
    return (low(grad),)
low.defvjp(low_keep, low_pass)
low_back.defvjp(back_keep, back_low)

def matmul(left, right):
    return jnp.dot(left, right, precision=lax.Precision.HIGHEST, preferred_element_type=jnp.float32)

def rms_norm(values, gain):
    return values * lax.rsqrt(lax.optimization_barrier(jnp.mean(values * values, axis=-1, keepdims=True)) + 1e-06) * gain

def rotary_tables():
    positions = jnp.arange(CTXLEN, dtype=jnp.float32)
    freqs = 10000.0 ** (-2.0 * jnp.arange(HEAD_DIM // 2, dtype=jnp.float32) / HEAD_DIM)
    angles = positions[:, None] * freqs[None, :]
    return (jnp.cos(angles)[None, :, None, :], jnp.sin(angles)[None, :, None, :])

def rotate(vector, cosine, sine):
    half = vector.shape[-1] // 2
    first = vector[..., :half]
    second = vector[..., half:]
    return jnp.concatenate([first * cosine - second * sine, second * cosine + first * sine], axis=-1)

def layer(points, missing, weights):
    tok_hidden_w, tok_hidden_b, tok_out_w, tok_res_w, tok_out_b, attn_gain, qkv_w, attn_out_w, mlp_gain, mlp_in_w, mlp_in_b, mlp_out_w, mlp_out_b = weights
    count = points.shape[0]
    rows = count * CTXLEN
    kept = (1 - missing).astype(jnp.float32).reshape(rows, PL)
    absent = missing.astype(jnp.float32).reshape(rows, PL)
    features = jnp.concatenate([points.reshape(rows, PL) * kept, absent], axis=1)
    pre_tok = low_back(matmul(features, tok_hidden_w.reshape(D, 2 * PL).T) + tok_hidden_b.reshape(D))
    hidden_tok = low(jax.nn.silu(pre_tok))
    embedded = low_back(matmul(hidden_tok, tok_out_w.T) + matmul(features, tok_res_w.T))
    state_zero = embedded + tok_out_b
    normed1 = low(rms_norm(state_zero, attn_gain))
    proj = matmul(normed1, qkv_w.reshape(D, 3 * D)).reshape(count, CTXLEN, 3, HEADS, HEAD_DIM)
    cosine, sine = rotary_tables()
    queries = low(rotate(low_back(proj[:, :, 0]), cosine, sine))
    keys_rot = low(rotate(low_back(proj[:, :, 1]), cosine, sine))
    values_b = low_back(low(proj[:, :, 2]))
    scores = low_back(jnp.einsum('cihd,cjhd->chij', queries, keys_rot, precision=lax.Precision.HIGHEST) / math.sqrt(HEAD_DIM))
    causal = jnp.arange(CTXLEN)[:, None] >= jnp.arange(CTXLEN)[None, :]
    probs = low(jax.nn.softmax(jnp.where(causal, scores, -1e+30), axis=-1))
    attended = jnp.einsum('chij,cjhd->cihd', probs, values_b, precision=lax.Precision.HIGHEST)
    attended = low_back(low(attended.reshape(rows, D)))
    state_one = state_zero + low_back(matmul(attended, attn_out_w.T))
    normed2 = low(rms_norm(state_one, mlp_gain))
    pre_mlp = low_back(matmul(normed2, mlp_in_w) + mlp_in_b.reshape(FF))
    act = low(jax.nn.silu(pre_mlp))
    return state_one + matmul(act, mlp_out_w.T) + mlp_out_b

def reference(points, missing, tok_hidden_w, tok_hidden_b, tok_out_w, tok_res_w, tok_out_b, attn_gain, qkv_w, attn_out_w, mlp_gain, mlp_in_w, mlp_in_b, mlp_out_w, mlp_out_b, cotangent):
    weights = tuple((item.astype(jnp.float32) for item in (tok_hidden_w, tok_hidden_b, tok_out_w, tok_res_w, tok_out_b, attn_gain, qkv_w, attn_out_w, mlp_gain, mlp_in_w, mlp_in_b, mlp_out_w, mlp_out_b)))
    contexts = points.shape[0]
    group = math.gcd(contexts, 256)
    blocks = contexts // group
    point_blocks = points.astype(jnp.float32).reshape(blocks, group, CTXLEN * PL)
    miss_blocks = missing.reshape(blocks, group, CTXLEN * PL)
    cot_blocks = cotangent.astype(jnp.float32).reshape(blocks, group * CTXLEN, D)

    def one_block(totals, pieces):
        block_points, block_missing, block_cot = pieces

        def forward(point_values, *params):
            return layer(point_values, block_missing, params)
        result, pullback = jax.vjp(forward, block_points, *weights)
        grads = pullback(block_cot)
        totals = tuple((total + grad for total, grad in zip(totals, grads[1:])))
        return (totals, (result.astype(jnp.bfloat16), grads[0]))
    start = tuple((jnp.zeros_like(item) for item in weights))
    totals, (results, point_grads) = lax.scan(one_block, start, (point_blocks, miss_blocks, cot_blocks))
    output = results.reshape(contexts * CTXLEN, D)
    points_grad = point_grads.reshape(contexts, CTXLEN * PL)
    return (output, points_grad, totals[0], totals[1], totals[2], totals[3], totals[4], totals[5], totals[6], totals[7], totals[8], totals[9], totals[10], totals[11], totals[12])
```

```python
import math

import jax
import jax.numpy as jnp
import numpy as np
from jax import lax
from jax.experimental import pallas as pl
from jax.experimental.pallas import tpu as pltpu
from jax.sharding import PartitionSpec as P

D = 1280
HEAD_DIM = 80
PL = 32
CTXLEN = 16


def dot_plain(left, right):
    return jnp.dot(left, right, preferred_element_type=jnp.float32)


def dot_last(left, right):
    return lax.dot_general(
        left, right, (((1,), (1,)), ((), ())), preferred_element_type=jnp.float32
    )


def dot_rows(left, right):
    return lax.dot_general(
        left, right, (((0,), (0,)), ((), ())), preferred_element_type=jnp.float32
    )


def silu_slope(values):
    sigma = jax.nn.sigmoid(values)
    return sigma * (1.0 + values * (1.0 - sigma))


def rotary_tables():
    positions = jnp.arange(CTXLEN, dtype=jnp.float32)
    freqs = 10000.0 ** (-2.0 * jnp.arange(HEAD_DIM // 2, dtype=jnp.float32) / HEAD_DIM)
    angles = positions[:, None] * freqs[None, :]
    return (jnp.cos(angles)[None, :, None, :], jnp.sin(angles)[None, :, None, :])


def rotate(vector, cosine, sine):
    half = vector.shape[-1] // 2
    first = vector[..., :half]
    second = vector[..., half:]
    return jnp.concatenate(
        [first * cosine - second * sine, second * cosine + first * sine], axis=-1
    )


def rotate_back(vector, cosine, sine):
    half = vector.shape[-1] // 2
    first = vector[..., :half]
    second = vector[..., half:]
    return jnp.concatenate(
        [first * cosine + second * sine, second * cosine - first * sine], axis=-1
    )


def norm_stats(values):
    factor = lax.rsqrt(jnp.mean(values * values, axis=-1, keepdims=True) + 1e-06)
    return (factor, values * factor)


def norm_back(grad, normal, factor, gain):
    scaled = grad * gain
    inner = jnp.mean(scaled * normal, axis=-1, keepdims=True)
    return (factor * (scaled - normal * inner), jnp.sum(grad * normal, axis=0))


def body(
    points,
    missing,
    tok_hidden_w,
    tok_hidden_b,
    tok_out_w,
    tok_res_w,
    tok_out_b,
    attn_gain,
    qkv_w,
    attn_out_w,
    mlp_gain,
    mlp_in_w,
    mlp_in_b,
    mlp_out_w,
    mlp_out_b,
    cotangent,
):
    gathered = (
        lax.all_gather(tok_hidden_w, "fsdp", axis=1, tiled=True),
        lax.all_gather(tok_hidden_b, "fsdp", axis=1, tiled=True),
        lax.all_gather(tok_out_w, "fsdp", axis=0, tiled=True),
        lax.all_gather(tok_res_w, "fsdp", axis=0, tiled=True),
        lax.all_gather(tok_out_b, "fsdp", axis=0, tiled=True),
        lax.all_gather(attn_gain, "fsdp", axis=0, tiled=True),
        lax.all_gather(qkv_w, "fsdp", axis=0, tiled=True),
        lax.all_gather(attn_out_w, "fsdp", axis=0, tiled=True),
        lax.all_gather(mlp_gain, "fsdp", axis=0, tiled=True),
        lax.all_gather(mlp_in_w, "fsdp", axis=0, tiled=True),
        lax.all_gather(mlp_in_b, "fsdp", axis=1, tiled=True),
        lax.all_gather(mlp_out_w, "fsdp", axis=0, tiled=True),
        lax.all_gather(mlp_out_b, "fsdp", axis=0, tiled=True),
    )
    (
        hidden_full,
        hidden_bias,
        token_full,
        residual_full,
        token_bias,
        first_gain,
        project_full,
        attend_full,
        second_gain,
        inner_full,
        inner_bias,
        outer_full,
        outer_bias,
    ) = gathered
    contexts = points.shape[0]
    rows = contexts * CTXLEN
    tensor_rank = lax.axis_index("tp")
    kept_mask = (1 - missing).astype(jnp.float32).reshape(rows, PL)
    absent = missing.astype(jnp.float32).reshape(rows, PL)
    observed = points.astype(jnp.float32).reshape(rows, PL) * kept_mask
    features = jnp.concatenate([observed, absent], axis=1).astype(jnp.bfloat16)
    half_features = jnp.where(tensor_rank == 0, observed, absent).astype(jnp.bfloat16)
    hidden_matrix = hidden_full.reshape(-1, 2 * PL)
    pre_tok = dot_last(features, hidden_matrix) + hidden_bias.reshape(-1).astype(jnp.float32)
    hidden_tok = jax.nn.silu(pre_tok).astype(jnp.bfloat16)
    partial_tok = dot_last(hidden_tok, token_full) + dot_last(half_features, residual_full)
    embedded = lax.psum(partial_tok.astype(jnp.bfloat16), "tp").astype(jnp.float32)
    state_zero = embedded + token_bias.astype(jnp.float32)
    factor_one, normal_one = norm_stats(state_zero)
    normed_one = (normal_one * first_gain.astype(jnp.float32)).astype(jnp.bfloat16)
    local_width = project_full.shape[2]
    local_heads = local_width // HEAD_DIM
    project_matrix = project_full.reshape(D, 3 * local_width)
    projected = dot_plain(normed_one, project_matrix).reshape(
        contexts, CTXLEN, 3, local_heads, HEAD_DIM
    )
    cosine, sine = rotary_tables()
    queries = rotate(projected[:, :, 0], cosine, sine).astype(jnp.bfloat16)
    keys_rot = rotate(projected[:, :, 1], cosine, sine).astype(jnp.bfloat16)
    values_b = projected[:, :, 2].astype(jnp.bfloat16)
    scale = 1.0 / math.sqrt(HEAD_DIM)
    causal = jnp.arange(CTXLEN)[:, None] >= jnp.arange(CTXLEN)[None, :]

    def scores_of(left, right):
        raw = jnp.einsum("cihd,cjhd->chij", left, right, preferred_element_type=jnp.float32) * scale
        return jnp.where(causal, raw, -1e30)

    scores = scores_of(queries, keys_rot)
    row_top = jnp.max(scores, axis=-1, keepdims=True)
    log_total = row_top + jnp.log(jnp.sum(jnp.exp(scores - row_top), axis=-1, keepdims=True))
    probs_b = jnp.exp(scores - log_total).astype(jnp.bfloat16)
    attended = jnp.einsum("chij,cjhd->cihd", probs_b, values_b, preferred_element_type=jnp.float32)
    attended = attended.astype(jnp.bfloat16).reshape(rows, local_width)
    branch_attn = lax.psum(dot_last(attended, attend_full).astype(jnp.bfloat16), "tp").astype(
        jnp.float32
    )
    state_one = state_zero + branch_attn
    factor_two, normal_two = norm_stats(state_one)
    normed_two = (normal_two * second_gain.astype(jnp.float32)).astype(jnp.bfloat16)
    pre_mlp = dot_plain(normed_two, inner_full) + inner_bias.reshape(-1).astype(jnp.float32)
    activation = jax.nn.silu(pre_mlp).astype(jnp.bfloat16)
    branch_mlp = lax.psum(dot_last(activation, outer_full).astype(jnp.bfloat16), "tp").astype(
        jnp.float32
    )
    output = (state_one + branch_mlp + outer_bias.astype(jnp.float32)).astype(jnp.bfloat16)
    again = (
        lax.all_gather(tok_hidden_w, "fsdp", axis=1, tiled=True),
        lax.all_gather(tok_hidden_b, "fsdp", axis=1, tiled=True),
        lax.all_gather(tok_out_w, "fsdp", axis=0, tiled=True),
        lax.all_gather(tok_res_w, "fsdp", axis=0, tiled=True),
        lax.all_gather(tok_out_b, "fsdp", axis=0, tiled=True),
        lax.all_gather(attn_gain, "fsdp", axis=0, tiled=True),
        lax.all_gather(qkv_w, "fsdp", axis=0, tiled=True),
        lax.all_gather(attn_out_w, "fsdp", axis=0, tiled=True),
        lax.all_gather(mlp_gain, "fsdp", axis=0, tiled=True),
        lax.all_gather(mlp_in_w, "fsdp", axis=0, tiled=True),
        lax.all_gather(mlp_in_b, "fsdp", axis=1, tiled=True),
        lax.all_gather(mlp_out_w, "fsdp", axis=0, tiled=True),
        lax.all_gather(mlp_out_b, "fsdp", axis=0, tiled=True),
    )
    (
        hidden_full,
        hidden_bias,
        token_full,
        residual_full,
        token_bias,
        first_gain,
        project_full,
        attend_full,
        second_gain,
        inner_full,
        inner_bias,
        outer_full,
        outer_bias,
    ) = again
    hidden_matrix = hidden_full.reshape(-1, 2 * PL)
    project_matrix = project_full.reshape(D, 3 * local_width)
    grad_outer_bias = jnp.sum(cotangent, axis=0, dtype=jnp.float32)
    grad_outer = dot_rows(cotangent, activation)
    d_pre = (dot_plain(cotangent, outer_full) * silu_slope(pre_mlp)).astype(jnp.bfloat16)
    grad_inner_bias = jnp.sum(d_pre, axis=0, dtype=jnp.float32).reshape(1, -1)
    grad_inner = dot_rows(normed_two, d_pre)
    d_normed_two = lax.psum(dot_last(d_pre, inner_full).astype(jnp.bfloat16), "tp").astype(
        jnp.float32
    )
    through_two, grad_second_gain = norm_back(
        d_normed_two, normal_two, factor_two, second_gain.astype(jnp.float32)
    )
    d_state_one = cotangent.astype(jnp.float32) + through_two
    d_branch = d_state_one.astype(jnp.bfloat16)
    grad_attend = dot_rows(d_branch, attended)
    d_attended = (
        dot_plain(d_branch, attend_full)
        .astype(jnp.bfloat16)
        .reshape(contexts, CTXLEN, local_heads, HEAD_DIM)
    )
    probs = jnp.exp(scores_of(queries, keys_rot) - log_total)
    probs_b = probs.astype(jnp.bfloat16)
    d_probs = jnp.einsum(
        "cihd,cjhd->chij", d_attended, values_b, preferred_element_type=jnp.float32
    )
    d_values = jnp.einsum(
        "chij,cihd->cjhd", probs_b, d_attended, preferred_element_type=jnp.float32
    ).astype(jnp.bfloat16)
    row_inner = jnp.sum(probs * d_probs, axis=-1, keepdims=True)
    d_scores = (probs * (d_probs - row_inner)).astype(jnp.bfloat16)
    d_queries = (
        jnp.einsum("chij,cjhd->cihd", d_scores, keys_rot, preferred_element_type=jnp.float32)
        * scale
    )
    d_keys = (
        jnp.einsum("chij,cihd->cjhd", d_scores, queries, preferred_element_type=jnp.float32) * scale
    )
    d_queries = rotate_back(d_queries, cosine, sine).astype(jnp.bfloat16)
    d_keys = rotate_back(d_keys, cosine, sine).astype(jnp.bfloat16)
    d_projected = jnp.stack([d_queries, d_keys, d_values], axis=2).reshape(rows, 3 * local_width)
    grad_project = dot_rows(normed_one, d_projected).reshape(D, 3, local_width)
    d_normed_one = lax.psum(
        dot_last(d_projected, project_matrix).astype(jnp.bfloat16), "tp"
    ).astype(jnp.float32)
    through_one, grad_first_gain = norm_back(
        d_normed_one, normal_one, factor_one, first_gain.astype(jnp.float32)
    )
    d_state_zero = d_state_one + through_one
    grad_token_bias = jnp.sum(d_state_zero, axis=0)
    d_embedded = d_state_zero.astype(jnp.bfloat16)
    grad_token = dot_rows(d_embedded, hidden_tok)
    grad_residual = dot_rows(d_embedded, half_features)
    d_pre_tok = (dot_plain(d_embedded, token_full) * silu_slope(pre_tok)).astype(jnp.bfloat16)
    grad_hidden_bias = jnp.sum(d_pre_tok, axis=0, dtype=jnp.float32).reshape(1, -1)
    grad_hidden = dot_rows(d_pre_tok, features).reshape(1, -1, 2 * PL)
    through_hidden = dot_plain(d_pre_tok, hidden_matrix)[:, :PL]
    through_residual = dot_plain(d_embedded, residual_full)
    point_terms = through_hidden + jnp.where(tensor_rank == 0, through_residual, 0.0)
    point_sums = lax.psum(point_terms, "tp")
    points_grad = (point_sums * kept_mask).reshape(contexts, CTXLEN * PL)
    owned = (
        lax.psum_scatter(grad_hidden, "fsdp", scatter_dimension=1, tiled=True),
        lax.psum_scatter(grad_hidden_bias, "fsdp", scatter_dimension=1, tiled=True),
        lax.psum_scatter(grad_token, "fsdp", scatter_dimension=0, tiled=True),
        lax.psum_scatter(grad_residual, "fsdp", scatter_dimension=0, tiled=True),
        lax.psum_scatter(grad_token_bias, "fsdp", scatter_dimension=0, tiled=True),
        lax.psum_scatter(grad_first_gain, "fsdp", scatter_dimension=0, tiled=True),
        lax.psum_scatter(grad_project, "fsdp", scatter_dimension=0, tiled=True),
        lax.psum_scatter(grad_attend, "fsdp", scatter_dimension=0, tiled=True),
        lax.psum_scatter(grad_second_gain, "fsdp", scatter_dimension=0, tiled=True),
        lax.psum_scatter(grad_inner, "fsdp", scatter_dimension=0, tiled=True),
        lax.psum_scatter(grad_inner_bias, "fsdp", scatter_dimension=1, tiled=True),
        lax.psum_scatter(grad_outer, "fsdp", scatter_dimension=0, tiled=True),
        lax.psum_scatter(grad_outer_bias, "fsdp", scatter_dimension=0, tiled=True),
    )
    return (
        output,
        points_grad,
        owned[0],
        owned[1],
        owned[2],
        owned[3],
        owned[4],
        owned[5],
        owned[6],
        owned[7],
        owned[8],
        owned[9],
        owned[10],
        owned[11],
        owned[12],
    )


MESH = pl.DeviceIdType.MESH
RING = 8
TOK = 384
OWN = 192
BLOCK = 160
HALF = 80
C_TO, C_QKV, C_AT, C_IN, C_OUT, C_ALL = 128, 512, 1536, 1920, 3200, 4480
CHUNKS = ((0, 512), (512, 512), (1024, 512), (1536, 384), (1920, 640), (2560, 640), (3200, 640), (3840, 640))
RB_ROW = (0, 80, 240, 400)
RB_LEN = (80, 160, 160, 160)
TILE = 256
TILES = D // TILE
SCALE = 1.0 / math.sqrt(HEAD_DIM)


def iota(shape, dim):
    return lax.broadcasted_iota(jnp.int32, shape, dim)


def layer_kernel(
    fe_in, cot_in, sp_in, pt_in, win_in, wout_in, rot_c, rot_a, rot_b,
    out_o, pts_o, go_o, gin_o, gout_o, gsp_o,
    w, g, rb, fe, cot, spx, part, pre, act, dpre, n1, n2, db, x0, x1,
    hc, dpe, pret, q_s, k_s, v_s, att, datt, dpj, ps, fs, gspf, gbs, ghs, hidf, hid, vec, bin_s, sums, ptx, ptr,
    cs, cr, xs, xr,
    ag_s, ag_r, rs_s, rs_r, ar_s, ar_r, nx_s, nx_r, in_s, in_r, lo_s, fin_s, fin_r, pt_s, pt_r,
):
    f32, bf16 = jnp.float32, jnp.bfloat16
    f = lax.axis_index("fsdp")
    x = lax.axis_index("tp")
    chip = lax.div(f, 2)
    c = f - 2 * chip
    zz = lax.div(chip, 2)
    yy = chip - 2 * zz
    pos = zz + yy * (7 - 2 * zz)

    def chip_at(p):
        p = lax.rem(p + 2 * RING, RING)
        h = lax.div(p, 4)
        return 2 * (p + h * (7 - 2 * p)) + h

    nxt = {"fsdp": 2 * chip_at(pos + 1) + c}
    prv = {"fsdp": 2 * chip_at(pos - 1) + c}
    mate = {"fsdp": f + 1 - 2 * c}
    across = {"tp": 1 - x}
    other = 1 - c
    own0 = pl.multiple_of(OWN * c, OWN)
    oth0 = pl.multiple_of(OWN * other, OWN)

    def m16(v):
        return pl.multiple_of(v, 16)

    def remote(src, dst, s_sem, r_sem, to):
        return pltpu.make_async_remote_copy(
            src_ref=src, dst_ref=dst, send_sem=s_sem, recv_sem=r_sem, device_id=to, device_id_type=MESH
        )

    sent = []

    def go(copy):
        copy.start()
        sent.append(copy)

    barrier = pltpu.get_barrier_semaphore()
    for to in (nxt, prv, mate, across):
        pl.semaphore_signal(barrier, inc=1, device_id=to, device_id_type=MESH)
    pl.semaphore_wait(barrier, 4)

    def piece(k, half):
        if k == 0:
            return pt_in.at[half, :, 0:384], 128, 384
        lo, width = CHUNKS[k]
        if lo < C_IN:
            return pt_in.at[half, :, lo - C_TO : lo - C_TO + width], lo, width
        src, base = (win_in, C_IN) if lo < C_OUT else (wout_in, C_OUT)
        start = pl.multiple_of(1280 * half + (lo - base), 128)
        return src.at[:, pl.ds(start, width)], lo, width

    myrow = m16(BLOCK * chip)
    locals_in = {}
    for k in range(len(CHUNKS)):
        if k == 0:
            r = remote(sp_in, spx, in_s.at[8], in_r.at[8], mate)
            go(r)
            sp_copy = pltpu.make_async_copy(sp_in, w.at[pl.ds(myrow, BLOCK), 0:128], lo_s.at[8])
            sp_copy.start()
            fe_copy = pltpu.make_async_copy(fe_in, fe.at[pl.ds(own0, OWN)], lo_s.at[9])
            fe_copy.start()
            fe_send = remote(fe_in, fe.at[pl.ds(own0, OWN)], in_s.at[9], in_r.at[9], mate)
            go(fe_send)
        src, lo, width = piece(k, other)
        dst = w.at[pl.ds(m16(myrow + HALF * c), HALF), lo : lo + width]
        go(remote(src, dst, in_s.at[k], in_r.at[k], mate))
        src, lo, width = piece(k, c)
        cp = pltpu.make_async_copy(src, dst, lo_s.at[k])
        cp.start()
        locals_in[k] = cp
    cot_copy = pltpu.make_async_copy(cot_in, cot.at[pl.ds(own0, OWN)], lo_s.at[10])
    cot_copy.start()
    cot_send = remote(cot_in, cot.at[pl.ds(own0, OWN)], in_s.at[10], in_r.at[10], mate)
    go(cot_send)

    def own_block_ready(k):
        locals_in[k].wait()
        _, lo, width = piece(k, c)
        arrived = w.at[pl.ds(m16(myrow + HALF * other), HALF), lo : lo + width]
        remote(arrived, arrived, in_s.at[k], in_r.at[k], mate).wait_recv()
        if k == 0:
            sp_copy.wait()
            remote(spx, spx, in_s.at[8], in_r.at[8], mate).wait_recv()
            mine = w[pl.ds(myrow, BLOCK), 0:128]
            theirs = jnp.where(iota((BLOCK, 128), 1) >= 65, spx[...].astype(f32), 0.0)
            w[pl.ds(myrow, BLOCK), 0:128] = (mine.astype(f32) + theirs).astype(bf16)

    def ag_ref(k, p, s, d):
        lo, width = CHUNKS[k]
        row = BLOCK * chip_at(p)
        if s == 3:
            return w.at[pl.ds(m16(row + HALF * d), HALF), lo : lo + width]
        return w.at[pl.ds(m16(row), BLOCK), lo : lo + width]

    def ag_recv(k, s, d):
        ref = ag_ref(k, pos - 1 - s if d == 0 else pos + 1 + s, s, d)
        remote(ref, ref, ag_s.at[k, s, d], ag_r.at[k, s, d], nxt if d == 0 else prv).wait_recv()

    def ag_send(k, s):
        if s == 0:
            own_block_ready(k)
        for d in (0, 1):
            if s > 0:
                ag_recv(k, s - 1, d)
            ref = ag_ref(k, pos - s if d == 0 else pos + s, s, d)
            go(remote(ref, ref, ag_s.at[k, s, d], ag_r.at[k, s, d], nxt if d == 0 else prv))

    def ag_slot(t):
        for s in (3, 2, 1, 0):
            if 0 <= t - s < len(CHUNKS):
                ag_send(t - s, s)

    def ag_done(k):
        for d in (0, 1):
            ag_recv(k, 3, d)

    def rs_send(k, s):
        lo, width = CHUNKS[k]
        cols = slice(lo, lo + width)
        for d in (0, 1):
            block = m16(BLOCK * chip_at(pos + 4 - s if d == 0 else pos - 4 + s))
            if s == 0:
                src = g.at[pl.ds(m16(block + HALF * d), HALF), cols]
            else:
                rs_recv(k, s - 1, d)
                first = m16(block + HALF * d) if s == 1 else block
                rs_add(first, d, RB_ROW[s - 1], RB_LEN[s - 1], cols)
                src = g.at[pl.ds(block, BLOCK), cols]
            dst = rb.at[d, RB_ROW[s] : RB_ROW[s] + RB_LEN[s], cols]
            go(remote(src, dst, rs_s.at[k, s, d], rs_r.at[k, s, d], nxt if d == 0 else prv))

    def rs_recv(k, s, d):
        lo, width = CHUNKS[k]
        ref = rb.at[d, RB_ROW[s] : RB_ROW[s] + RB_LEN[s], lo : lo + width]
        remote(ref, ref, rs_s.at[k, s, d], rs_r.at[k, s, d], nxt if d == 0 else prv).wait_recv()

    def rs_add(row, d, rb_row, length, cols):
        def step(i, carry):
            here = pl.ds(m16(row + 16 * i), 16)
            g[here, cols] = g[here, cols] + rb[d, pl.ds(m16(rb_row + 16 * i), 16), cols]
            return carry

        lax.fori_loop(0, length // 16, step, 0)

    def grad_ref(k, half):
        lo, width = CHUNKS[k]
        if k == 0:
            return go_o.at[half, :, 0:384]
        if lo < C_IN:
            return go_o.at[half, :, lo - C_TO : lo - C_TO + width]
        dst, base = (gin_o, C_IN) if lo < C_OUT else (gout_o, C_OUT)
        return dst.at[:, pl.ds(pl.multiple_of(1280 * half + (lo - base), 128), width)]

    def rs_last(k):
        lo, width = CHUNKS[k]
        for d in (0, 1):
            rs_recv(k, 3, d)
        if k == 0:
            total = g[pl.ds(myrow, BLOCK), 0:128].astype(f32)
            total = total + rb[0, 400:560, 0:128].astype(f32) + rb[1, 400:560, 0:128].astype(f32)
            gsp_o[c, :, :] = total
            go(remote(gsp_o.at[c], gsp_o.at[c], fin_s.at[8], fin_r.at[8], mate))
            lo, width = 128, 384
        cols = slice(lo, lo + width)

        def total_at(start):
            rows = pl.ds(m16(myrow + start), 16)
            there = pl.ds(m16(400 + start), 16)
            return g[rows, cols].astype(f32) + (rb[0, there, cols].astype(f32) + rb[1, there, cols].astype(f32))

        def theirs(i, carry):
            fs[pl.ds(m16(16 * i), 16), cols] = total_at(HALF * other + 16 * i)
            return carry

        lax.fori_loop(0, HALF // 16, theirs, 0)
        go(remote(fs.at[:, cols], grad_ref(k, c), fin_s.at[k], fin_r.at[k], mate))
        mine_ref = grad_ref(k, c)

        def mine(i, carry):
            mine_ref[pl.ds(m16(16 * i), 16), :] = total_at(HALF * c + 16 * i)
            return carry

        lax.fori_loop(0, HALF // 16, mine, 0)

    rs_at = {}

    def rs_start(k):
        rs_send(k, 0)
        rs_at[k] = 1

    def rs_tick(only=None):
        for k in list(rs_at):
            if only is not None and k not in only:
                continue
            s = rs_at[k]
            if s < 4:
                rs_send(k, s)
                rs_at[k] = s + 1
            else:
                rs_last(k)
                del rs_at[k]

    def ar_tile(i):
        return slice(TILE * i, TILE * i + TILE)

    def ar_begin(a, left, lo, width):
        b = a % 2
        if a >= 2:
            for i in range(TILES):
                done = cs.at[b, :, ar_tile(i)]
                remote(done, done, ar_s.at[a - 2, 0, i], ar_r.at[a - 2, 0, i], mate).wait_send()
        for i in range(TILES):
            part[:, ar_tile(i)] = dot_last(left[...], w[ar_tile(i), lo : lo + width])
            cs[b, :, ar_tile(i)] = part[pl.ds(oth0, OWN), ar_tile(i)].astype(bf16)
            copy = remote(cs.at[b, :, ar_tile(i)], cr.at[b, :, ar_tile(i)], ar_s.at[a, 0, i], ar_r.at[a, 0, i], mate)
            copy.start()
            if a >= 3:
                sent.append(copy)

    def ar_mid(a):
        b = a % 2
        if a >= 2:
            for i in range(TILES):
                done = xs.at[b, :, ar_tile(i)]
                remote(done, done, ar_s.at[a - 2, 1, i], ar_r.at[a - 2, 1, i], across).wait_send()
        for i in range(TILES):
            here = cr.at[b, :, ar_tile(i)]
            remote(here, here, ar_s.at[a, 0, i], ar_r.at[a, 0, i], mate).wait_recv()
            xs[b, :, ar_tile(i)] = (
                part[pl.ds(own0, OWN), ar_tile(i)] + cr[b, :, ar_tile(i)].astype(f32)
            ).astype(bf16)
            copy = remote(
                xs.at[b, :, ar_tile(i)], xr.at[a % 3, :, ar_tile(i)], ar_s.at[a, 1, i], ar_r.at[a, 1, i], across
            )
            copy.start()
            if a >= 3:
                sent.append(copy)

    def ar_end(a):
        for i in range(TILES):
            here = xr.at[a % 3, :, ar_tile(i)]
            remote(here, here, ar_s.at[a, 1, i], ar_r.at[a, 1, i], across).wait_recv()

    def summed(a, rows):
        return xs[a % 2, rows, :].astype(f32) + xr[a % 3, rows, :].astype(f32)

    def own_rows(body, block=32):
        def step(j, carry):
            start = pl.multiple_of(block * j, block)
            body(pl.ds(start, block), pl.ds(m16(own0 + start), block))
            return carry

        lax.fori_loop(0, OWN // block, step, 0)

    def share(j, ref):
        rows = ref.at[pl.ds(own0, OWN)]
        go(remote(rows, rows, nx_s.at[j], nx_r.at[j], mate))

    def shared(j, ref):
        rows = ref.at[pl.ds(oth0, OWN)]
        remote(rows, rows, nx_s.at[j], nx_r.at[j], mate).wait_recv()

    def rms(v):
        return lax.rsqrt(jnp.mean(v * v, axis=-1, keepdims=True) + 1e-06)

    def fold(v):
        return jnp.sum(v.reshape(v.shape[0] // 8, 8, v.shape[1]), axis=0)

    def tiles_loop(count, body):
        def step(i, carry):
            body(pl.ds(pl.multiple_of(TILE * i, TILE), TILE), i)
            return carry

        lax.fori_loop(0, count, step, 0)

    def grad_block(left, right, lo, width, dst):
        def body(rows, i):
            g[rows, dst : dst + width] = dot_rows(left[:, rows], right[:, lo : lo + width]).astype(bf16)

        tiles_loop(TILES, body)

    for t in range(5):
        ag_slot(t) if t < 4 else None
    sums[...] = jnp.zeros(sums.shape, f32)
    ag_done(0)
    ag_slot(4)

    lane = iota((64, 128), 1)
    row = iota((64, 128), 0)
    hidf[320:384, :] = jnp.where((row < PL) & (lane == PL * x + row), 1.0, 0.0)
    for p in range(RING):
        hidf[40 * p : 40 * p + 40, :] = w[BLOCK * p : BLOCK * p + 48, 0:128].astype(f32)[:40]
    hid[...] = hidf[...].astype(bf16)
    fe_copy.wait()
    arrived = fe.at[pl.ds(oth0, OWN)]
    remote(arrived, arrived, in_s.at[9], in_r.at[9], mate).wait_recv()
    pret[...] = dot_last(fe[...], hid[...])
    lane = iota((TOK, 384), 1)
    v = pret[...]
    hc[...] = jnp.where(
        lane < 320, v * jax.nn.sigmoid(v), jnp.where(lane < 352, v, jnp.where(lane == 352, 1.0, 0.0))
    ).astype(bf16)
    ar_begin(0, hc, C_TO, 384)
    sel = jnp.where(iota((16, 128), 1) == 97 + iota((16, 128), 0), 1.0, 0.0)
    sel = jnp.where(iota((16, 128), 0) < 4, sel, 0.0).astype(bf16)
    vec[...] = dot_last(sel, w[:, 384:512])
    sel = jnp.where(iota((16, 128), 1) == 65 + iota((16, 128), 0), 1.0, 0.0)
    sel = jnp.where(iota((16, 128), 0) < 2, sel, 0.0).astype(bf16)
    for q in range(4):
        both = dot_last(sel, w[pl.ds(m16(640 * c + 160 * q), 160), 0:128])
        bin_s[0:1, 320 * q : 320 * q + 160] = both[0:1]
        bin_s[0:1, 320 * q + 160 : 320 * q + 320] = both[1:2]
    ar_mid(0)
    ag_slot(5)
    ar_end(0)

    def first_norm(rows, mine):
        v = summed(0, rows) + vec[3:4, :]
        x0[rows, :] = v
        n1[mine, :] = (v * rms(v) * vec[0:1, :]).astype(bf16)

    own_rows(first_norm)
    share(0, n1)
    ag_done(1)
    ag_slot(6)
    ag_done(2)
    shared(0, n1)

    def project(cols, i):
        part[:, cols] = dot_plain(n1[...], w[:, pl.ds(pl.multiple_of(C_QKV + TILE * i, TILE), TILE)])

    tiles_loop(4, project)

    def turn(j, carry):
        rows = pl.ds(m16(16 * j), 16)
        v = part[rows, 0:1024]
        v = v * rot_c[...] + pltpu.roll(v, 984, 1) * rot_a[...] + pltpu.roll(v, 40, 1) * rot_b[...]
        q_s[rows, :] = v[:, 0:384].astype(bf16)
        k_s[rows, :] = pltpu.roll(v, 704, 1)[:, 0:384].astype(bf16)
        v_s[rows, :] = v[:, 640:1024].astype(bf16)
        return carry

    lax.fori_loop(0, TOK // 16, turn, 0)

    def stacked(v):
        head = iota((128, 384), 1)
        return jnp.concatenate(
            [
                jnp.where((head >= HEAD_DIM * h) & (head < HEAD_DIM * h + HEAD_DIM), v, jnp.zeros_like(v))
                for h in range(4)
            ],
            axis=0,
        )

    def side(v):
        return jnp.concatenate([v[128 * h : 128 * h + 128] for h in range(4)], axis=1)

    def attend(b, carry):
        rows = pl.ds(pl.multiple_of(128 * b, 128), 128)
        scores = dot_last(stacked(q_s[rows, :]), k_s[rows, :]) * SCALE
        qi = iota((512, 128), 0) & 127
        kj = iota((512, 128), 1)
        allowed = ((qi >> 4) == (kj >> 4)) & (kj <= qi)
        scores = jnp.where(allowed, scores, -1e30)
        e = jnp.exp(scores - jnp.max(scores, axis=-1, keepdims=True))
        probs = e * (1.0 / jnp.sum(e, axis=-1, keepdims=True))
        ps[pl.ds(pl.multiple_of(512 * b, 512), 512), :] = probs
        att[rows, :] = dot_plain(side(probs.astype(bf16)), stacked(v_s[rows, :])).astype(bf16)
        return carry

    lax.fori_loop(0, 3, attend, 0)
    ag_slot(7)
    ag_done(3)
    ar_begin(1, att, C_AT, 384)
    ag_slot(8)
    ar_mid(1)
    ag_done(4)
    ag_slot(9)
    ar_end(1)

    def second_norm(rows, mine):
        v = x0[rows, :] + summed(1, rows)
        x1[rows, :] = v
        n2[mine, :] = (v * rms(v) * vec[1:2, :]).astype(bf16)

    own_rows(second_norm)
    share(1, n2)
    ag_done(5)
    ag_slot(10)
    shared(1, n2)

    def inner(cols, i):
        v = dot_plain(n2[...], w[:, pl.ds(pl.multiple_of(C_IN + TILE * i, 128), TILE)]) + bin_s[0:1, cols]
        pre[:, cols] = v
        act[:, cols] = (v * jax.nn.sigmoid(v)).astype(bf16)

    tiles_loop(TILES, inner)

    cot_copy.wait()
    arrived = cot.at[pl.ds(oth0, OWN)]
    remote(arrived, arrived, in_s.at[10], in_r.at[10], mate).wait_recv()
    grad_block(cot, act, 0, 640, 3200)
    rs_start(6)
    grad_block(cot, act, 640, 640, 3840)
    rs_start(7)
    ag_done(6)
    ag_done(7)

    def outer_back(cols, i):
        v = pre[:, cols]
        s = jax.nn.sigmoid(v)
        d = dot_plain(cot[...], w[:, pl.ds(pl.multiple_of(C_OUT + TILE * i, 128), TILE)])
        dpre[:, cols] = (d * (s * (1.0 + v * (1.0 - s)))).astype(bf16)

    tiles_loop(TILES, outer_back)
    ar_begin(2, dpre, C_IN, 1280)
    rs_tick()
    ar_mid(2)
    grad_block(n2, dpre, 0, 640, 1920)
    rs_start(4)
    rs_tick()
    grad_block(n2, dpre, 640, 640, 2560)
    rs_start(5)
    ar_end(2)

    def second_back(rows, mine):
        dn = summed(2, rows)
        v = x1[rows, :]
        r = rms(v)
        xh = v * r
        scaled = dn * vec[1:2, :]
        inside = jnp.mean(scaled * xh, axis=-1, keepdims=True)
        ct = cot[mine, :].astype(f32)
        d = ct + r * (scaled - xh * inside)
        pre[rows, :] = d
        db[mine, :] = d.astype(bf16)
        sums[8:16, :] += fold(dn * xh)
        sums[16:24, :] += fold(ct)

    own_rows(second_back)
    share(2, db)
    ar_begin(3, act, C_OUT, 1280)
    ar_mid(3)
    shared(2, db)

    def attend_back(cols, i):
        datt[:, cols] = dot_plain(db[...], w[:, pl.ds(pl.multiple_of(C_AT + 128 * i, 128), 128)]).astype(bf16)

    for i in range(3):
        attend_back(slice(128 * i, 128 * i + 128), i)

    def attention_back(b, carry):
        rows = pl.ds(pl.multiple_of(128 * b, 128), 128)
        probs = ps[pl.ds(pl.multiple_of(512 * b, 512), 512), :]
        heads_d = stacked(datt[rows, :])
        dp = dot_last(heads_d, v_s[rows, :])
        ds = (probs * (dp - jnp.sum(probs * dp, axis=-1, keepdims=True))).astype(bf16)
        part[rows, 0:384] = dot_plain(side(ds), stacked(k_s[rows, :])) * SCALE
        part[rows, 320:704] = dot_rows(ds, stacked(q_s[rows, :])) * SCALE
        part[rows, 640:1024] = dot_rows(probs.astype(bf16), heads_d)
        return carry

    lax.fori_loop(0, 3, attention_back, 0)

    def turn_back(j, carry):
        rows = pl.ds(m16(16 * j), 16)
        v = part[rows, 0:1024]
        v = v * rot_c[...] - pltpu.roll(v, 984, 1) * rot_a[...] - pltpu.roll(v, 40, 1) * rot_b[...]
        dpj[rows, :] = v.astype(bf16)
        return carry

    lax.fori_loop(0, TOK // 16, turn_back, 0)
    rs_tick()
    ar_begin(4, dpj, C_QKV, 1024)
    ar_end(3)

    def finish(rows, mine):
        out_o[rows, :] = (x1[rows, :] + summed(3, rows) + vec[2:3, :]).astype(bf16)

    own_rows(finish)
    ar_mid(4)
    grad_block(db, att, 0, 384, C_AT)
    rs_start(3)
    rs_tick()
    grad_block(n1, dpj, 0, 512, 512)
    rs_start(1)
    rs_tick()
    grad_block(n1, dpj, 512, 512, 1024)
    rs_start(2)
    ar_end(4)

    de = act

    def first_back(rows, mine):
        dn = summed(4, rows)
        v = x0[rows, :]
        r = rms(v)
        xh = v * r
        scaled = dn * vec[0:1, :]
        inside = jnp.mean(scaled * xh, axis=-1, keepdims=True)
        d = pre[rows, :] + r * (scaled - xh * inside)
        de[mine, :] = d.astype(bf16)
        sums[0:8, :] += fold(dn * xh)

    own_rows(first_back)
    share(3, de)
    rs_tick()
    shared(3, de)

    v = pret[...]
    s = jax.nn.sigmoid(v)
    lane = iota((TOK, 384), 1)
    d = dot_plain(de[...], w[:, C_TO : C_TO + 384])
    dpe[...] = jnp.where(lane < 320, d * (s * (1.0 + v * (1.0 - s))), jnp.where(lane < 352, d, 0.0)).astype(bf16)
    ptx[...] = dot_plain(dpe[...], hid[...])
    go(remote(ptx.at[pl.ds(oth0, OWN)], ptr.at[0], pt_s.at[0], pt_r.at[0], mate))

    pick = jnp.where(iota((32, 128), 1) == 97 + (iota((32, 128), 0) >> 3), 1.0, 0.0)
    pick = jnp.where(iota((32, 128), 0) < 24, pick, 0.0).astype(bf16)

    def grad_tok(rows, i):
        val = dot_rows(de[:, rows], hc[...])
        g[rows, 128:384] = val[:, 0:256].astype(bf16)
        g[rows, 384:512] = (val[:, 256:384] + dot_rows(sums[:, rows].astype(bf16), pick)).astype(bf16)

    tiles_loop(TILES, grad_tok)
    ghs[...] = dot_rows(dpe[...], fe[...])
    ones = jnp.where((iota((TOK, 128), 1) >= 65) & (iota((TOK, 128), 1) <= 66), 1.0, 0.0).astype(bf16)

    def bias_cols(rows, i):
        gbs[rows, :] = dot_rows(dpre[:, rows], ones)

    tiles_loop(TILES, bias_cols)
    gspf[...] = jnp.zeros(gspf.shape, f32)
    for p in range(RING):
        gspf[BLOCK * p : BLOCK * p + 40, :] = ghs[40 * p : 40 * p + 40, :]
    lane = iota((BLOCK, 128), 1)
    for q in range(4):
        rows = pl.ds(m16(640 * c + 160 * q), 160)
        first = jnp.where(lane == 65, gbs[320 * q : 320 * q + 160, :], 0.0)
        second = jnp.where(lane == 66, gbs[320 * q + 160 : 320 * q + 320, :], 0.0)
        gspf[rows, :] = gspf[rows, :] + first + second

    def small_cols(rows, i):
        g[rows, 0:128] = gspf[rows, :].astype(bf16)

    tiles_loop(TILES, small_cols)
    rs_start(0)
    remote(ptr.at[0], ptr.at[0], pt_s.at[0], pt_r.at[0], mate).wait_recv()
    ptr[1] = ptx[pl.ds(own0, OWN), :] + ptr[0]
    go(remote(ptr.at[1], ptr.at[2], pt_s.at[1], pt_r.at[1], across))
    while rs_at:
        rs_tick()
    remote(ptr.at[2], ptr.at[2], pt_s.at[1], pt_r.at[1], across).wait_recv()
    pts_o[...] = ptr[1] + ptr[2]
    for k in range(len(CHUNKS)):
        there = grad_ref(k, other)
        remote(there, there, fin_s.at[k], fin_r.at[k], mate).wait_recv()
    there = gsp_o.at[other]
    remote(there, there, fin_s.at[8], fin_r.at[8], mate).wait_recv()
    for copy in sent:
        copy.wait_send()


def rotary_lanes():
    lanes = np.arange(1024)
    inside = lanes % HEAD_DIM
    turned = lanes < 640
    freqs = 10000.0 ** (-2.0 * (inside % 40) / HEAD_DIM)
    angles = np.arange(CTXLEN)[:, None] * freqs[None, :]
    cosine = np.where(turned, np.cos(angles), 1.0)
    sine = np.where(turned, np.sin(angles), 0.0)
    lower = np.where(inside < 40, -sine, 0.0)
    upper = np.where(inside >= 40, sine, 0.0)
    return [np.asarray(t, np.float32) for t in (cosine, lower, upper)]


def fast_body(
    points, missing, tok_hidden_w, tok_hidden_b, tok_out_w, tok_res_w, tok_out_b, attn_gain, qkv_w, attn_out_w,
    mlp_gain, mlp_in_w, mlp_in_b, mlp_out_w, mlp_out_b, cotangent,
):
    f32, bf16 = jnp.float32, jnp.bfloat16
    f = lax.axis_index("fsdp")
    core = lax.rem(f, 2)
    contexts = points.shape[0]
    rows = contexts * CTXLEN
    kept = (1 - missing).astype(bf16)
    feats = jnp.concatenate(
        [
            (points * kept).reshape(rows, PL),
            missing.astype(bf16).reshape(rows, PL),
            jnp.ones((rows, 1), bf16),
            jnp.zeros((rows, 63), bf16),
        ],
        axis=1,
    )
    hidden = jnp.concatenate([tok_hidden_w[0], tok_hidden_b[0][:, None]], axis=1)
    small = jnp.pad(hidden, ((0, 120), (0, 63)))
    lane = lax.broadcasted_iota(jnp.int32, (BLOCK, 128), 1)
    small = jnp.where(lane == 65 + core, mlp_in_b[0][:, None], small)
    vectors = jnp.stack([attn_gain, mlp_gain, mlp_out_b, tok_out_b], axis=1)
    tok = tok_out_w.reshape(HALF, 8, 2, 40)
    qkv = qkv_w.reshape(HALF, 3, 2, 320)

    def zeros(n):
        return jnp.zeros((HALF, n), bf16)

    packed = jnp.stack(
        [
            jnp.concatenate(
                [
                    tok[:, :, h].reshape(HALF, 320),
                    zeros(16 * h), tok_res_w[:, 16 * h : 16 * h + 16], zeros(16 - 16 * h + 1),
                    vectors, zeros(27),
                    qkv[:, :, h].reshape(HALF, 960), zeros(64),
                    attn_out_w[:, 320 * h : 320 * h + 320], zeros(64),
                ],
                axis=1,
            )
            for h in (0, 1)
        ]
    )
    any_space = pl.BlockSpec(memory_space=pl.ANY)
    vmem = pl.BlockSpec(memory_space=pltpu.VMEM)

    def sems(*shape):
        return pltpu.SemaphoreType.DMA(shape)

    out, pts, go, gin, gout, gsp = pl.pallas_call(
        layer_kernel,
        out_shape=(
            jax.ShapeDtypeStruct((OWN, D), bf16),
            jax.ShapeDtypeStruct((OWN, 128), f32),
            jax.ShapeDtypeStruct((2, HALF, 1792), f32),
            jax.ShapeDtypeStruct((HALF, 2560), f32),
            jax.ShapeDtypeStruct((HALF, 2560), f32),
            jax.ShapeDtypeStruct((2, BLOCK, 128), f32),
        ),
        in_specs=[any_space] * 6 + [vmem] * 3,
        out_specs=[vmem] * 6,
        scratch_shapes=[
            pltpu.VMEM((D, C_ALL), bf16),
            pltpu.VMEM((D, C_ALL), bf16),
            pltpu.VMEM((2, 560, C_ALL), bf16),
            pltpu.VMEM((TOK, 128), bf16),
            pltpu.VMEM((TOK, D), bf16),
            pltpu.VMEM((BLOCK, 128), bf16),
            pltpu.VMEM((TOK, D), f32),
            pltpu.VMEM((TOK, D), f32),
            pltpu.VMEM((TOK, D), bf16),
            pltpu.VMEM((TOK, D), bf16),
            pltpu.VMEM((TOK, D), bf16),
            pltpu.VMEM((TOK, D), bf16),
            pltpu.VMEM((TOK, D), bf16),
            pltpu.VMEM((OWN, D), f32),
            pltpu.VMEM((OWN, D), f32),
            pltpu.VMEM((TOK, 384), bf16),
            pltpu.VMEM((TOK, 384), bf16),
            pltpu.VMEM((TOK, 384), f32),
            pltpu.VMEM((TOK, 384), bf16),
            pltpu.VMEM((TOK, 384), bf16),
            pltpu.VMEM((TOK, 384), bf16),
            pltpu.VMEM((TOK, 384), bf16),
            pltpu.VMEM((TOK, 384), bf16),
            pltpu.VMEM((TOK, 1024), bf16),
            pltpu.VMEM((1536, 128), f32),
            pltpu.VMEM((HALF, C_ALL), f32),
            pltpu.VMEM((D, 128), f32),
            pltpu.VMEM((D, 128), f32),
            pltpu.VMEM((TOK, 128), f32),
            pltpu.VMEM((TOK, 128), f32),
            pltpu.VMEM((TOK, 128), bf16),
            pltpu.VMEM((16, D), f32),
            pltpu.VMEM((8, D), f32),
            pltpu.VMEM((32, D), f32),
            pltpu.VMEM((TOK, 128), f32),
            pltpu.VMEM((3, OWN, 128), f32),
            pltpu.VMEM((2, OWN, D), bf16),
            pltpu.VMEM((2, OWN, D), bf16),
            pltpu.VMEM((2, OWN, D), bf16),
            pltpu.VMEM((3, OWN, D), bf16),
            sems(8, 4, 2), sems(8, 4, 2), sems(8, 4, 2), sems(8, 4, 2),
            sems(5, 2, TILES), sems(5, 2, TILES),
            sems(4), sems(4), sems(11), sems(11), sems(11), sems(9), sems(9), sems(2), sems(2),
        ],
        compiler_params=pltpu.CompilerParams(
            collective_id=0, has_side_effects=True, vmem_limit_bytes=64 * 1024 * 1024 - 512 * 1024
        ),
        cost_estimate=pl.CostEstimate(flops=13 * 10**9, bytes_accessed=10**7, transcendentals=10**6),
    )(feats, cotangent, small, packed, mlp_in_w, mlp_out_w, *[jnp.asarray(t) for t in rotary_lanes()])

    chip = lax.div(f, 2)
    points_grad = (pts[:, :PL] * (1 - missing).astype(f32).reshape(rows, PL)).reshape(contexts, CTXLEN * PL)
    small_own = lax.dynamic_index_in_dim(gsp, core, 0, keepdims=False)
    small_bias = lax.dynamic_index_in_dim(gsp, lax.div(chip, 4), 0, keepdims=False)
    bias_col = jnp.where(core == 0, small_bias[:, 65], small_bias[:, 66])
    grad_tok_out = go[:, :, 0:320].reshape(2, HALF, 8, 40).transpose(1, 2, 0, 3).reshape(HALF, 640)
    grad_qkv = go[:, :, 384:1344].reshape(2, HALF, 3, 320).transpose(1, 2, 0, 3).reshape(HALF, 3, 640)
    grad_attn = jnp.concatenate([go[0, :, 1408:1728], go[1, :, 1408:1728]], axis=1)
    both = go[0, :, 352:356] + go[1, :, 352:356]
    return (
        out,
        points_grad,
        small_own[None, 0:40, 0:64],
        small_own[None, 0:40, 64],
        grad_tok_out,
        go[0, :, 320:352],
        go[0, :, 352],
        both[:, 1],
        grad_qkv,
        grad_attn,
        both[:, 2],
        gin,
        bias_col[None, :],
        gout,
        both[:, 3],
    )


def solution(mesh):
    placed = (
        P("fsdp", None),
        P("fsdp", None),
        P("tp", "fsdp", None),
        P("tp", "fsdp"),
        P("fsdp", "tp"),
        P("fsdp", "tp"),
        P("fsdp"),
        P("fsdp"),
        P("fsdp", None, "tp"),
        P("fsdp", "tp"),
        P("fsdp"),
        P("fsdp", "tp"),
        P("tp", "fsdp"),
        P("fsdp", "tp"),
        P("fsdp"),
        P("fsdp", None),
    )
    small_slice = mesh.shape["fsdp"] == 2 * RING and mesh.shape["tp"] == 2
    return jax.shard_map(
        fast_body if small_slice else body,
        mesh=mesh,
        in_specs=placed,
        out_specs=(
            P("fsdp", None),
            P("fsdp", None),
            P("tp", "fsdp", None),
            P("tp", "fsdp"),
            P("fsdp", "tp"),
            P("fsdp", "tp"),
            P("fsdp"),
            P("fsdp"),
            P("fsdp", None, "tp"),
            P("fsdp", "tp"),
            P("fsdp"),
            P("fsdp", "tp"),
            P("tp", "fsdp"),
            P("fsdp", "tp"),
            P("fsdp"),
        ),
        check_vma=False,
    )
```

```python
import math

import jax
import jax.numpy as jnp
import numpy as np
from jax import lax
from jax.experimental import pallas as pl
from jax.experimental.pallas import tpu as pltpu
from jax.sharding import PartitionSpec as P

D = 1280
HEAD_DIM = 80
PL = 32
CTXLEN = 16


def dot_plain(left, right):
    return jnp.dot(left, right, preferred_element_type=jnp.float32)


def dot_last(left, right):
    return lax.dot_general(
        left, right, (((1,), (1,)), ((), ())), preferred_element_type=jnp.float32
    )


def dot_rows(left, right):
    return lax.dot_general(
        left, right, (((0,), (0,)), ((), ())), preferred_element_type=jnp.float32
    )


def silu_slope(values):
    sigma = jax.nn.sigmoid(values)
    return sigma * (1.0 + values * (1.0 - sigma))


def rotary_tables():
    positions = jnp.arange(CTXLEN, dtype=jnp.float32)
    freqs = 10000.0 ** (-2.0 * jnp.arange(HEAD_DIM // 2, dtype=jnp.float32) / HEAD_DIM)
    angles = positions[:, None] * freqs[None, :]
    return (jnp.cos(angles)[None, :, None, :], jnp.sin(angles)[None, :, None, :])


def rotate(vector, cosine, sine):
    half = vector.shape[-1] // 2
    first = vector[..., :half]
    second = vector[..., half:]
    return jnp.concatenate(
        [first * cosine - second * sine, second * cosine + first * sine], axis=-1
    )


def rotate_back(vector, cosine, sine):
    half = vector.shape[-1] // 2
    first = vector[..., :half]
    second = vector[..., half:]
    return jnp.concatenate(
        [first * cosine + second * sine, second * cosine - first * sine], axis=-1
    )


def norm_stats(values):
    factor = lax.rsqrt(jnp.mean(values * values, axis=-1, keepdims=True) + 1e-06)
    return (factor, values * factor)


def norm_back(grad, normal, factor, gain):
    scaled = grad * gain
    inner = jnp.mean(scaled * normal, axis=-1, keepdims=True)
    return (factor * (scaled - normal * inner), jnp.sum(grad * normal, axis=0))


def body(
    points,
    missing,
    tok_hidden_w,
    tok_hidden_b,
    tok_out_w,
    tok_res_w,
    tok_out_b,
    attn_gain,
    qkv_w,
    attn_out_w,
    mlp_gain,
    mlp_in_w,
    mlp_in_b,
    mlp_out_w,
    mlp_out_b,
    cotangent,
):
    gathered = (
        lax.all_gather(tok_hidden_w, "fsdp", axis=1, tiled=True),
        lax.all_gather(tok_hidden_b, "fsdp", axis=1, tiled=True),
        lax.all_gather(tok_out_w, "fsdp", axis=0, tiled=True),
        lax.all_gather(tok_res_w, "fsdp", axis=0, tiled=True),
        lax.all_gather(tok_out_b, "fsdp", axis=0, tiled=True),
        lax.all_gather(attn_gain, "fsdp", axis=0, tiled=True),
        lax.all_gather(qkv_w, "fsdp", axis=0, tiled=True),
        lax.all_gather(attn_out_w, "fsdp", axis=0, tiled=True),
        lax.all_gather(mlp_gain, "fsdp", axis=0, tiled=True),
        lax.all_gather(mlp_in_w, "fsdp", axis=0, tiled=True),
        lax.all_gather(mlp_in_b, "fsdp", axis=1, tiled=True),
        lax.all_gather(mlp_out_w, "fsdp", axis=0, tiled=True),
        lax.all_gather(mlp_out_b, "fsdp", axis=0, tiled=True),
    )
    (
        hidden_full,
        hidden_bias,
        token_full,
        residual_full,
        token_bias,
        first_gain,
        project_full,
        attend_full,
        second_gain,
        inner_full,
        inner_bias,
        outer_full,
        outer_bias,
    ) = gathered
    contexts = points.shape[0]
    rows = contexts * CTXLEN
    tensor_rank = lax.axis_index("tp")
    kept_mask = (1 - missing).astype(jnp.float32).reshape(rows, PL)
    absent = missing.astype(jnp.float32).reshape(rows, PL)
    observed = points.astype(jnp.float32).reshape(rows, PL) * kept_mask
    features = jnp.concatenate([observed, absent], axis=1).astype(jnp.bfloat16)
    half_features = jnp.where(tensor_rank == 0, observed, absent).astype(jnp.bfloat16)
    hidden_matrix = hidden_full.reshape(-1, 2 * PL)
    pre_tok = dot_last(features, hidden_matrix) + hidden_bias.reshape(-1).astype(jnp.float32)
    hidden_tok = jax.nn.silu(pre_tok).astype(jnp.bfloat16)
    partial_tok = dot_last(hidden_tok, token_full) + dot_last(half_features, residual_full)
    embedded = lax.psum(partial_tok.astype(jnp.bfloat16), "tp").astype(jnp.float32)
    state_zero = embedded + token_bias.astype(jnp.float32)
    factor_one, normal_one = norm_stats(state_zero)
    normed_one = (normal_one * first_gain.astype(jnp.float32)).astype(jnp.bfloat16)
    local_width = project_full.shape[2]
    local_heads = local_width // HEAD_DIM
    project_matrix = project_full.reshape(D, 3 * local_width)
    projected = dot_plain(normed_one, project_matrix).reshape(
        contexts, CTXLEN, 3, local_heads, HEAD_DIM
    )
    cosine, sine = rotary_tables()
    queries = rotate(projected[:, :, 0], cosine, sine).astype(jnp.bfloat16)
    keys_rot = rotate(projected[:, :, 1], cosine, sine).astype(jnp.bfloat16)
    values_b = projected[:, :, 2].astype(jnp.bfloat16)
    scale = 1.0 / math.sqrt(HEAD_DIM)
    causal = jnp.arange(CTXLEN)[:, None] >= jnp.arange(CTXLEN)[None, :]

    def scores_of(left, right):
        raw = jnp.einsum("cihd,cjhd->chij", left, right, preferred_element_type=jnp.float32) * scale
        return jnp.where(causal, raw, -1e30)

    scores = scores_of(queries, keys_rot)
    row_top = jnp.max(scores, axis=-1, keepdims=True)
    log_total = row_top + jnp.log(jnp.sum(jnp.exp(scores - row_top), axis=-1, keepdims=True))
    probs_b = jnp.exp(scores - log_total).astype(jnp.bfloat16)
    attended = jnp.einsum("chij,cjhd->cihd", probs_b, values_b, preferred_element_type=jnp.float32)
    attended = attended.astype(jnp.bfloat16).reshape(rows, local_width)
    branch_attn = lax.psum(dot_last(attended, attend_full).astype(jnp.bfloat16), "tp").astype(
        jnp.float32
    )
    state_one = state_zero + branch_attn
    factor_two, normal_two = norm_stats(state_one)
    normed_two = (normal_two * second_gain.astype(jnp.float32)).astype(jnp.bfloat16)
    pre_mlp = dot_plain(normed_two, inner_full) + inner_bias.reshape(-1).astype(jnp.float32)
    activation = jax.nn.silu(pre_mlp).astype(jnp.bfloat16)
    branch_mlp = lax.psum(dot_last(activation, outer_full).astype(jnp.bfloat16), "tp").astype(
        jnp.float32
    )
    output = (state_one + branch_mlp + outer_bias.astype(jnp.float32)).astype(jnp.bfloat16)
    again = (
        lax.all_gather(tok_hidden_w, "fsdp", axis=1, tiled=True),
        lax.all_gather(tok_hidden_b, "fsdp", axis=1, tiled=True),
        lax.all_gather(tok_out_w, "fsdp", axis=0, tiled=True),
        lax.all_gather(tok_res_w, "fsdp", axis=0, tiled=True),
        lax.all_gather(tok_out_b, "fsdp", axis=0, tiled=True),
        lax.all_gather(attn_gain, "fsdp", axis=0, tiled=True),
        lax.all_gather(qkv_w, "fsdp", axis=0, tiled=True),
        lax.all_gather(attn_out_w, "fsdp", axis=0, tiled=True),
        lax.all_gather(mlp_gain, "fsdp", axis=0, tiled=True),
        lax.all_gather(mlp_in_w, "fsdp", axis=0, tiled=True),
        lax.all_gather(mlp_in_b, "fsdp", axis=1, tiled=True),
        lax.all_gather(mlp_out_w, "fsdp", axis=0, tiled=True),
        lax.all_gather(mlp_out_b, "fsdp", axis=0, tiled=True),
    )
    (
        hidden_full,
        hidden_bias,
        token_full,
        residual_full,
        token_bias,
        first_gain,
        project_full,
        attend_full,
        second_gain,
        inner_full,
        inner_bias,
        outer_full,
        outer_bias,
    ) = again
    hidden_matrix = hidden_full.reshape(-1, 2 * PL)
    project_matrix = project_full.reshape(D, 3 * local_width)
    grad_outer_bias = jnp.sum(cotangent, axis=0, dtype=jnp.float32)
    grad_outer = dot_rows(cotangent, activation)
    d_pre = (dot_plain(cotangent, outer_full) * silu_slope(pre_mlp)).astype(jnp.bfloat16)
    grad_inner_bias = jnp.sum(d_pre, axis=0, dtype=jnp.float32).reshape(1, -1)
    grad_inner = dot_rows(normed_two, d_pre)
    d_normed_two = lax.psum(dot_last(d_pre, inner_full).astype(jnp.bfloat16), "tp").astype(
        jnp.float32
    )
    through_two, grad_second_gain = norm_back(
        d_normed_two, normal_two, factor_two, second_gain.astype(jnp.float32)
    )
    d_state_one = cotangent.astype(jnp.float32) + through_two
    d_branch = d_state_one.astype(jnp.bfloat16)
    grad_attend = dot_rows(d_branch, attended)
    d_attended = (
        dot_plain(d_branch, attend_full)
        .astype(jnp.bfloat16)
        .reshape(contexts, CTXLEN, local_heads, HEAD_DIM)
    )
    probs = jnp.exp(scores_of(queries, keys_rot) - log_total)
    probs_b = probs.astype(jnp.bfloat16)
    d_probs = jnp.einsum(
        "cihd,cjhd->chij", d_attended, values_b, preferred_element_type=jnp.float32
    )
    d_values = jnp.einsum(
        "chij,cihd->cjhd", probs_b, d_attended, preferred_element_type=jnp.float32
    ).astype(jnp.bfloat16)
    row_inner = jnp.sum(probs * d_probs, axis=-1, keepdims=True)
    d_scores = (probs * (d_probs - row_inner)).astype(jnp.bfloat16)
    d_queries = (
        jnp.einsum("chij,cjhd->cihd", d_scores, keys_rot, preferred_element_type=jnp.float32)
        * scale
    )
    d_keys = (
        jnp.einsum("chij,cihd->cjhd", d_scores, queries, preferred_element_type=jnp.float32) * scale
    )
    d_queries = rotate_back(d_queries, cosine, sine).astype(jnp.bfloat16)
    d_keys = rotate_back(d_keys, cosine, sine).astype(jnp.bfloat16)
    d_projected = jnp.stack([d_queries, d_keys, d_values], axis=2).reshape(rows, 3 * local_width)
    grad_project = dot_rows(normed_one, d_projected).reshape(D, 3, local_width)
    d_normed_one = lax.psum(
        dot_last(d_projected, project_matrix).astype(jnp.bfloat16), "tp"
    ).astype(jnp.float32)
    through_one, grad_first_gain = norm_back(
        d_normed_one, normal_one, factor_one, first_gain.astype(jnp.float32)
    )
    d_state_zero = d_state_one + through_one
    grad_token_bias = jnp.sum(d_state_zero, axis=0)
    d_embedded = d_state_zero.astype(jnp.bfloat16)
    grad_token = dot_rows(d_embedded, hidden_tok)
    grad_residual = dot_rows(d_embedded, half_features)
    d_pre_tok = (dot_plain(d_embedded, token_full) * silu_slope(pre_tok)).astype(jnp.bfloat16)
    grad_hidden_bias = jnp.sum(d_pre_tok, axis=0, dtype=jnp.float32).reshape(1, -1)
    grad_hidden = dot_rows(d_pre_tok, features).reshape(1, -1, 2 * PL)
    through_hidden = dot_plain(d_pre_tok, hidden_matrix)[:, :PL]
    through_residual = dot_plain(d_embedded, residual_full)
    point_terms = through_hidden + jnp.where(tensor_rank == 0, through_residual, 0.0)
    point_sums = lax.psum(point_terms, "tp")
    points_grad = (point_sums * kept_mask).reshape(contexts, CTXLEN * PL)
    owned = (
        lax.psum_scatter(grad_hidden, "fsdp", scatter_dimension=1, tiled=True),
        lax.psum_scatter(grad_hidden_bias, "fsdp", scatter_dimension=1, tiled=True),
        lax.psum_scatter(grad_token, "fsdp", scatter_dimension=0, tiled=True),
        lax.psum_scatter(grad_residual, "fsdp", scatter_dimension=0, tiled=True),
        lax.psum_scatter(grad_token_bias, "fsdp", scatter_dimension=0, tiled=True),
        lax.psum_scatter(grad_first_gain, "fsdp", scatter_dimension=0, tiled=True),
        lax.psum_scatter(grad_project, "fsdp", scatter_dimension=0, tiled=True),
        lax.psum_scatter(grad_attend, "fsdp", scatter_dimension=0, tiled=True),
        lax.psum_scatter(grad_second_gain, "fsdp", scatter_dimension=0, tiled=True),
        lax.psum_scatter(grad_inner, "fsdp", scatter_dimension=0, tiled=True),
        lax.psum_scatter(grad_inner_bias, "fsdp", scatter_dimension=1, tiled=True),
        lax.psum_scatter(grad_outer, "fsdp", scatter_dimension=0, tiled=True),
        lax.psum_scatter(grad_outer_bias, "fsdp", scatter_dimension=0, tiled=True),
    )
    return (
        output,
        points_grad,
        owned[0],
        owned[1],
        owned[2],
        owned[3],
        owned[4],
        owned[5],
        owned[6],
        owned[7],
        owned[8],
        owned[9],
        owned[10],
        owned[11],
        owned[12],
    )


MESH = pl.DeviceIdType.MESH
TOK = 384
OWN = 192
PART = 96
HALF = 80
C_SL, C_QKV, C_IN, C_OUT, C_ALL, C_ONE = 0, 768, 1792, 3072, 4352, 2176
CHUNKS = (
    (0, 384, 128, 0),
    (128, 384, 128, 128),
    (256, 384, 128, 256),
    (768, 512, 256, 384),
    (1024, 512, 256, 640),
    (1792, 640, 256, 896),
    (2048, 640, 384, 1152),
    (3072, 640, 256, 1536),
    (3328, 640, 256, 1792),
    (3584, 640, 128, 2048),
)
GATHER_ORDER = ("zxy", "zyx", "zxy", "zyx", "zxy", "zyx", "zxy", "zyx", "zxy", "zyx")
SUM_ORDER = ("yxz", "xyz", "yxz", "xyz", "yxz", "xyz", "yxz", "xyz", "yxz", "xyz")
(
    FIRST, OWNED, SECOND, THIRD, HERE, SUM, FEATS, COT, COT_HERE, TOKENS, VECTORS, NORM_1, PROJECT, TURN, ATTEND,
    NORM_2, INNER, GRAD_OUT, OUTER, GRAD_IN, BACK_2, D_ATT, ATTEND_B, TURN_B, FINISH, GRAD_QKV, GRAD_ATT,
    GRAD_BIAS, BACK_1, D_HID, GRAD_TOK, GRAD_HID, POINTS, SEND, PASS,
) = range(35)
PLAN = (
    (FIRST, 2), (FIRST, 5), (FIRST, 1), (OWNED, 2), (FIRST, 0), (OWNED, 5), (OWNED, 1), (FIRST, 3), (OWNED, 0),
    (FIRST, 4), (OWNED, 3), (FIRST, 6), (OWNED, 4), (SECOND, 2), (SECOND, 1), (FIRST, 8), (THIRD, 2), (SECOND, 0),
    (THIRD, 1), (FIRST, 7), (THIRD, 0), (OWNED, 6), (FEATS,), (HERE, 0), (HERE, 2), (SECOND, 5), (HERE, 1), (TOKENS,),
    (FIRST, 9), (SECOND, 3), (SEND, 0), (PASS, 0), (SECOND, 4), (OWNED, 7), (THIRD, 3), (OWNED, 8), (THIRD, 4),
    (VECTORS,), (SECOND, 6), (COT,), (NORM_1,), (HERE, 4), (OWNED, 9), (THIRD, 5), (HERE, 3), (PROJECT,), (SECOND, 7),
    (TURN,), (THIRD, 6), (SECOND, 8), (ATTEND, 0), (ATTEND, 1), (ATTEND, 2), (SEND, 1), (PASS, 1), (THIRD, 7),
    (HERE, 5), (SECOND, 9), (NORM_2,), (THIRD, 8), (THIRD, 9), (HERE, 6), (INNER,), (COT_HERE,), (GRAD_OUT, 9),
    (GRAD_OUT, 8), (HERE, 9), (GRAD_OUT, 7), (HERE, 7), (HERE, 8), (OUTER,), (SEND, 2), (PASS, 2), (SUM, 9),
    (SEND, 3), (GRAD_IN, 6), (SUM, 8), (SUM, 9), (PASS, 3), (BACK_2,), (GRAD_IN, 5), (D_ATT,), (ATTEND_B, 1),
    (ATTEND_B, 2), (ATTEND_B, 0), (SUM, 8), (SUM, 9), (TURN_B,), (SEND, 4), (SUM, 7), (PASS, 4), (SUM, 6),
    (GRAD_BIAS,), (GRAD_ATT,), (SUM, 5), (SUM, 7), (SUM, 8), (GRAD_QKV, 3), (GRAD_QKV, 4), (BACK_1,), (SUM, 7),
    (SUM, 9), (SUM, 6), (SUM, 8), (SUM, 3), (SUM, 4), (SUM, 5), (D_HID,), (SUM, 5), (SUM, 7), (GRAD_TOK,),
    (POINTS, 0), (SUM, 4), (SUM, 6), (SUM, 3), (SUM, 4), (POINTS, 1), (SUM, 3), (GRAD_HID,), (SUM, 0), (SUM, 5),
    (SUM, 0), (SUM, 6), (SUM, 1), (SUM, 2), (SUM, 2), (SUM, 3), (POINTS, 2), (SUM, 1), (SUM, 0), (FINISH,), (SUM, 0),
    (SUM, 2), (SUM, 2), (SUM, 4), (SUM, 1), (SUM, 1), (POINTS, 3),
)
L_RES, L_ONE, L_VEC, L_BIN, L_HID = 64, 72, 73, 77, 79
TILE = 256
TILES = D // TILE
SCALE = 1.0 / math.sqrt(HEAD_DIM)


def iota(shape, dim):
    return lax.broadcasted_iota(jnp.int32, shape, dim)


def one_hot(cond):
    return jnp.where(cond, 1.0, 0.0).astype(jnp.bfloat16)


def layer_kernel(
    points, missing, hid_w, hid_b, tok_in, res_t, tok_b, gain1, qkv_in, att_in, gain2, win_in, b_in, wout_in,
    out_b, cot_in, rot_c, rot_a, rot_b,
    out_o, pts_o, fb,
    w, g, rb, fe, cot, part, pre, act, dpre, n1, n2, db, x0, x1,
    hc, dpe, pret, q_s, kv_s, att, datt, dpj, ps, gbs, ghs, hidf, hid, vec, bin_s, sums, ptx, ptr,
    pk, pkf, srcf, tmp,
    cs, cr, xs, xr,
    ag_s, ag_r, rs_s, rs_r, ar_s, ar_r, nx_s, nx_r, in_s, in_r, lo_s, tk_s, tk_r, fin_s, fin_r, pt_s, pt_r,
):
    f32, bf16 = jnp.float32, jnp.bfloat16
    f = lax.axis_index("fsdp")
    x = lax.axis_index("tp")
    z = lax.div(f, 4)
    zh = lax.div(z, 2)
    l = z - 2 * zh
    y = lax.div(f, 2) - 2 * z
    c = f - 4 * z - 2 * y
    m = 2 * l + c
    mate = {"fsdp": f + 1 - 2 * c}
    beside = {"fsdp": f + 4 - 8 * l}
    corner = {"fsdp": f + 4 - 8 * l + 1 - 2 * c}
    along = {"z": {"fsdp": f + 8 - 16 * zh}, "y": {"fsdp": f + 2 - 4 * y}, "x": {"tp": 1 - x}}
    own0 = pl.multiple_of(OWN * c, OWN)
    oth0 = pl.multiple_of(OWN * (1 - c), OWN)

    def m16(v):
        return pl.multiple_of(v, 16)

    def remote(src, dst, s_sem, r_sem, to):
        return pltpu.make_async_remote_copy(
            src_ref=src, dst_ref=dst, send_sem=s_sem, recv_sem=r_sem, device_id=to, device_id_type=MESH
        )

    sent = []

    def go(copy):
        copy.start()
        sent.append(copy)

    barrier = pltpu.get_barrier_semaphore()
    peers = (mate, beside, corner, along["z"], along["y"], along["x"])
    for to in peers:
        pl.semaphore_signal(barrier, inc=1, device_id=to, device_id_type=MESH)

    part[0:80, 0:640] = tok_in[...].astype(f32)
    part[80:160, 0:640] = att_in[...].astype(f32)
    part[160:240, 0:640] = qkv_in[0].astype(f32)
    part[240:320, 0:640] = qkv_in[1].astype(f32)
    part[0:80, 640:1280] = qkv_in[2].astype(f32)
    srcf[...] = jnp.zeros(srcf.shape, f32)
    srcf[0:32, 0:80] = res_t[...].astype(f32)
    for i, v in enumerate((gain1, gain2, out_b, tok_b)):
        srcf[32 + i : 33 + i, 0:80] = v[...].astype(f32)
    tmp[0:1, 0:160] = b_in[...].astype(f32)
    srcf[36:37, 0:80] = tmp[0:1, 0:80]
    srcf[37:38, 0:80] = tmp[0:1, 80:160]
    srcf[40:80, 0:64] = hid_w[...].astype(f32)
    src = srcf[...].astype(bf16)
    row = iota((80, 128), 0)
    lane = iota((80, 128), 1)
    for q in range(4):
        col = 160 * q
        pkf[:, 0:160] = part[0:80, col : col + 160]
        pkf[:, 160:320] = part[80:160, col : col + 160]
        pkf[:, 320:384] = jnp.zeros((80, 64), f32)
        place = (row < 32) & (row >= 8 * q) & (row < 8 * q + 8) & (lane == L_RES + row - 8 * q)
        place = place | ((row >= 32) & (row < 38) & (lane == L_VEC + row - 32))
        place = place | ((row >= 40) & (lane == L_HID + row - 40))
        pkf[:, 256:384] = pkf[:, 256:384] + dot_rows(src, one_hot(place))[0:80]
        pkf[64:65, 256 + L_HID : 256 + L_HID + 40] = hid_b[...].astype(f32)
        pkf[:, 384:544] = part[160:240, col : col + 160]
        pkf[:, 544:704] = part[240:320, col : col + 160]
        pkf[:, 704:864] = part[0:80, 640 + col : 800 + col]
        pkf[:, 864:896] = jnp.zeros((80, 32), f32)
        pk[q] = pkf[...].astype(bf16)

    pl.semaphore_wait(barrier, len(peers))

    def cols(k, h):
        first, apart, width, _ = CHUNKS[k]
        return pl.ds(pl.multiple_of(first + apart * h, 128), width)

    def piece(k, member):
        first, _, width, at = CHUNKS[k]
        if at < 896:
            return pk.at[member, :, at : at + width]
        src, base = (win_in, 896) if at < 1536 else (wout_in, 1536)
        return src.at[:, pl.ds(pl.multiple_of(640 * member + at - base, 128), width)]

    group = ((mate, 2 * l + 1 - c), (beside, 2 - 2 * l + c), (corner, 3 - 2 * l - c))
    home = w.at[pl.ds(m16(HALF * f), HALF)]
    locals_in = {}

    def rows_of(to):
        return pl.ds(m16(HALF * to["fsdp"]), HALF)

    def g_first(k):
        dst = w.at[pl.ds(m16(HALF * f), HALF), cols(k, x)]
        for i, (to, member) in enumerate(group):
            go(remote(piece(k, member), dst, in_s.at[k, i], in_r.at[k, i], to))
        locals_in[k] = pltpu.make_async_copy(piece(k, m), dst, lo_s.at[k])
        locals_in[k].start()

    w4 = w.reshape(4, 2, 160, C_ALL)
    g4 = g.reshape(4, 2, 160, C_ALL)

    def block(ref, k, flips):
        zz = 1 - zh if "z" in flips else zh
        yy = 1 - y if "y" in flips else y
        h = 1 - x if "x" in flips else x
        return ref.at[pl.ds(2 * zz, 2), yy, :, cols(k, h)]

    def g_send(k, i, flips, axis):
        ref = block(w4, k, flips)
        go(remote(ref, ref, ag_s.at[k, i], ag_r.at[k, i], along[axis]))

    def g_recv(k, i, flips):
        ref = block(w4, k, flips)
        remote(ref, ref, ag_s.at[k, i], ag_r.at[k, i], along[flips[-1]]).wait_recv()

    def g_own(k):
        a, b, d = GATHER_ORDER[k]
        locals_in[k].wait()
        for i, (to, member) in enumerate(group):
            ref = w.at[rows_of(to), cols(k, x)]
            remote(ref, ref, in_s.at[k, i], in_r.at[k, i], to).wait_recv()
        g_send(k, 0, "", a)
        g_send(k, 1, "", b)
        g_send(k, 3, "", d)

    def g_second(k):
        a, b, d = GATHER_ORDER[k]
        g_recv(k, 0, a)
        g_send(k, 2, a, b)
        g_send(k, 4, a, d)

    def g_third(k):
        a, b, d = GATHER_ORDER[k]
        g_recv(k, 1, b)
        g_send(k, 5, b, d)
        g_recv(k, 2, a + b)
        g_send(k, 6, a + b, d)

    def g_done(k):
        a, b, d = GATHER_ORDER[k]
        g_recv(k, 3, d)
        g_recv(k, 4, a + d)
        g_recv(k, 5, b + d)
        g_recv(k, 6, a + b + d)

    def s_buf(k, i):
        _, _, width, at = CHUNKS[k]
        return rb.at[i, :, :, at : at + width]

    def s_send(k, i, flips, axis):
        go(remote(block(g4, k, flips), s_buf(k, i), rs_s.at[k, i], rs_r.at[k, i], along[axis]))

    def s_add(k, i, flips, axis):
        ref = s_buf(k, i)
        remote(ref, ref, rs_s.at[k, i], rs_r.at[k, i], along[axis]).wait_recv()
        _, _, width, at = CHUNKS[k]
        zz = 1 - zh if "z" in flips else zh
        yy = 1 - y if "y" in flips else y
        there = cols(k, 1 - x if "x" in flips else x)

        def step(j, carry):
            half = lax.div(j, 2)
            inside = 80 * (j - 2 * half)
            here = pl.ds(m16(640 * zz + 320 * half + 160 * yy + inside), 80)
            g[here, there] = g[here, there] + rb[i, half, pl.ds(m16(inside), 80), at : at + width]
            return carry

        lax.fori_loop(0, 4, step, 0)

    def s_start(k):
        a, b, d = SUM_ORDER[k]
        s_send(k, 0, a + b + d, a)
        s_send(k, 1, a + b, a)
        s_send(k, 2, a + d, a)
        s_send(k, 3, a, a)
        s_at[k] = 0

    def s_step(k):
        a, b, d = SUM_ORDER[k]
        stage = s_at[k]
        if stage == 0:
            s_add(k, 0, b + d, a)
            s_send(k, 4, b + d, b)
            s_add(k, 1, b, a)
            s_send(k, 5, b, b)
        elif stage == 1:
            s_add(k, 2, d, a)
            s_add(k, 4, d, b)
            s_send(k, 6, d, d)
        elif stage == 2:
            s_add(k, 3, "", a)
            s_add(k, 5, "", b)
        else:
            s_add(k, 6, "", d)
            _, _, width, at = CHUNKS[k]
            for i, (to, member) in enumerate(group):
                src = g.at[rows_of(to), cols(k, x)]
                go(remote(src, fb.at[m, :, at : at + width], fin_s.at[k, i], fin_r.at[k, i], to))
            fb[m, :, at : at + width] = g[pl.ds(m16(HALF * f), HALF), cols(k, x)]
            del s_at[k]
            return
        s_at[k] = stage + 1

    s_at = {}

    def ar_tile(i):
        return slice(TILE * i, TILE * i + TILE)

    def ar_begin(a):
        left, lo, width = operands[a]
        b = a % 2
        if a >= 2:
            for i in range(TILES):
                done = cs.at[b, :, ar_tile(i)]
                remote(done, done, ar_s.at[a - 2, 0, i], ar_r.at[a - 2, 0, i], mate).wait_send()
        for i in range(TILES):
            part[:, ar_tile(i)] = dot_last(left[...], w[ar_tile(i), lo : lo + width])
            cs[b, :, ar_tile(i)] = part[pl.ds(oth0, OWN), ar_tile(i)].astype(bf16)
            copy = remote(cs.at[b, :, ar_tile(i)], cr.at[b, :, ar_tile(i)], ar_s.at[a, 0, i], ar_r.at[a, 0, i], mate)
            copy.start()
            if a >= 3:
                sent.append(copy)

    def ar_mid(a):
        b = a % 2
        if a >= 2:
            for i in range(TILES):
                done = xs.at[b, :, ar_tile(i)]
                remote(done, done, ar_s.at[a - 2, 1, i], ar_r.at[a - 2, 1, i], beside).wait_send()
        for i in range(TILES):
            here = cr.at[b, :, ar_tile(i)]
            remote(here, here, ar_s.at[a, 0, i], ar_r.at[a, 0, i], mate).wait_recv()
            xs[b, :, ar_tile(i)] = (
                part[pl.ds(own0, OWN), ar_tile(i)] + cr[b, :, ar_tile(i)].astype(f32)
            ).astype(bf16)
            copy = remote(
                xs.at[b, :, ar_tile(i)], xr.at[a % 3, :, ar_tile(i)], ar_s.at[a, 1, i], ar_r.at[a, 1, i], beside
            )
            copy.start()
            if a >= 3:
                sent.append(copy)

    def ar_end(a):
        for i in range(TILES):
            here = xr.at[a % 3, :, ar_tile(i)]
            remote(here, here, ar_s.at[a, 1, i], ar_r.at[a, 1, i], beside).wait_recv()

    def summed(a, rows):
        return xs[a % 2, rows, :].astype(f32) + xr[a % 3, rows, :].astype(f32)

    def own_rows(body, first=0, count=OWN, size=32):
        def step(j, carry):
            start = m16(first + size * j)
            body(pl.ds(start, size), pl.ds(m16(own0 + start), size))
            return carry

        lax.fori_loop(0, count // size, step, 0)

    def share(j, ref):
        rows = ref.at[pl.ds(own0, OWN)]
        go(remote(rows, rows, nx_s.at[j], nx_r.at[j], mate))

    def shared(j, ref):
        rows = ref.at[pl.ds(oth0, OWN)]
        remote(rows, rows, nx_s.at[j], nx_r.at[j], mate).wait_recv()

    def rms(v):
        return lax.rsqrt(jnp.mean(v * v, axis=-1, keepdims=True) + 1e-06)

    def fold(v):
        return jnp.sum(v.reshape(v.shape[0] // 8, 8, v.shape[1]), axis=0)

    def tiles_loop(count, body):
        def step(i, carry):
            body(pl.ds(pl.multiple_of(TILE * i, TILE), TILE), i)
            return carry

        lax.fori_loop(0, count, step, 0)

    def grad_block(k, left, right, base):
        first, apart, width, _ = CHUNKS[k]

        def body(rows, i):
            for h in (0, 1):
                lo = first - base + apart * h
                g[rows, first + apart * h : first + apart * h + width] = dot_rows(
                    left[:, rows], right[:, lo : lo + width]
                ).astype(bf16)

        tiles_loop(TILES, body)

    def slab(h):
        return slice(256 + 384 * h, 384 + 384 * h)

    spread = one_hot(lax.div(iota((OWN, 12), 0), CTXLEN) == iota((OWN, 12), 1))
    right_patch = lax.div(iota((OWN, 512), 1), PL) == (iota((OWN, 512), 0) & (CTXLEN - 1))
    lane_of = iota((512, 128), 1)
    place_of = iota((512, 128), 0) & (PL - 1)
    mine0 = m16(own0 + PART * l)
    cot_part = cot_in.at[pl.ds(m16(PART * x), PART)]
    cot_copy = pltpu.make_async_copy(cot_part, cot.at[pl.ds(mine0, PART)], lo_s.at[len(CHUNKS)])
    lane768 = iota((TOK, 768), 1)
    lane384 = jnp.where(lane768 >= 384, lane768 - 384, lane768)
    units = lane384 < 160
    resids = (lane384 >= 256 + L_RES) & (lane384 < 256 + L_RES + 8)
    de = act

    def tokens_here(j, ref):
        for i, (to, member) in enumerate(group):
            cc = 1 - c if i != 1 else c
            ll = l if i == 0 else 1 - l
            rows = ref.at[pl.ds(m16(OWN * cc + PART * ll), PART)]
            remote(rows, rows, tk_s.at[j, i], tk_r.at[j, i], to).wait_recv()

    def features():
        keep = 1.0 - missing[...].astype(f32)
        seen = dot_plain(spread, (points[...].astype(f32) * keep).astype(bf16))
        gone = dot_plain(spread, missing[...].astype(f32).astype(bf16))
        feats = dot_plain(jnp.where(right_patch, seen, 0.0).astype(bf16), one_hot(lane_of == place_of))
        feats = feats + dot_plain(jnp.where(right_patch, gone, 0.0).astype(bf16), one_hot(lane_of == place_of + PL))
        ptx[0:OWN, :] = jnp.where(iota((OWN, 128), 1) == 2 * PL, 1.0, feats)
        fe[pl.ds(mine0, PART), :] = ptx[pl.ds(m16(PART * x), PART), :].astype(bf16)
        for i, (to, member) in enumerate(group):
            rows = fe.at[pl.ds(mine0, PART)]
            go(remote(rows, rows, tk_s.at[0, i], tk_r.at[0, i], to))
        sums[...] = jnp.zeros(sums.shape, f32)
        hidf[...] = jnp.zeros(hidf.shape, f32)

    def cot_out():
        cot_copy.start()
        for i, (to, member) in enumerate(group):
            go(remote(cot_part, cot.at[pl.ds(mine0, PART)], tk_s.at[1, i], tk_r.at[1, i], to))

    def cot_here():
        cot_copy.wait()
        tokens_here(1, cot)

    def tokenize():
        for h in (0, 1):
            for j in range(4):
                rows = pl.ds(m16(320 * m + 80 * j), 80)
                tmp[:, 0:128] = w[rows, slab(h)].astype(f32)
                hidf[0:72, 384 * h + 40 * j : 384 * h + 40 * j + 40] = tmp[0:72, L_HID : L_HID + 40]
            row = iota((128, 128), 0)
            lane = iota((128, 128), 1)
            chosen = (lane >= L_RES) & (lane < L_RES + 8) & (row == PL * h + 8 * m + lane - L_RES)
            hidf[:, slab(h)] = jnp.where(chosen, 1.0, 0.0)
        hid[...] = hidf[...].astype(bf16)
        tokens_here(0, fe)
        pret[...] = dot_plain(fe[...], hid[...])
        v = pret[...]
        hc[...] = jnp.where(
            units, v * jax.nn.sigmoid(v), jnp.where(resids, v, jnp.where(lane384 == 256 + L_ONE, 1.0, 0.0))
        ).astype(bf16)

    def vectors():
        row16 = iota((16, 128), 0)
        lane16 = iota((16, 128), 1)
        vec[...] = dot_last(one_hot((row16 < 4) & (lane16 == L_VEC + row16)), w[:, slab(0)])
        for h in (0, 1):
            pair = dot_last(one_hot((row16 < 2) & (lane16 == L_BIN + row16)), w[pl.ds(m16(320 * m), 320), slab(h)])
            tmp[0:16, 0:320] = pair
            for j in range(4):
                at = 640 * h + 160 * j
                bin_s[0:1, at : at + 80] = tmp[0:1, 80 * j : 80 * j + 80]
                bin_s[0:1, at + 80 : at + 160] = tmp[1:2, 80 * j : 80 * j + 80]

    def first_norm():
        ar_end(0)

        def body(rows, mine):
            v = summed(0, rows) + vec[3:4, :]
            x0[rows, :] = v
            n1[mine, :] = (v * rms(v) * vec[0:1, :]).astype(bf16)

        own_rows(body)
        share(0, n1)

    def project():
        shared(0, n1)

        def body(cols, i):
            part[:, cols] = dot_plain(n1[...], w[:, pl.ds(pl.multiple_of(C_QKV + TILE * i, TILE), TILE)])

        tiles_loop(4, body)

    def turn():
        def body(j, carry):
            rows = pl.ds(m16(16 * j), 16)
            v = part[rows, 0:1024]
            v = v * rot_c[...] + pltpu.roll(v, 984, 1) * rot_a[...] + pltpu.roll(v, 40, 1) * rot_b[...]
            for h in (0, 1):
                one = v[:, 512 * h : 512 * h + 512]
                q_s[h, rows, :] = one[:, 0:256].astype(bf16)
                kv_s[h, rows, :] = pltpu.roll(one, 352, 1)[:, 0:384].astype(bf16)
            return carry

        lax.fori_loop(0, TOK // 16, body, 0)

    def stacked(v, first):
        head = iota(v.shape, 1)
        return jnp.concatenate(
            [
                jnp.where((head >= first + HEAD_DIM * h) & (head < first + HEAD_DIM * h + HEAD_DIM), v, jnp.zeros_like(v))
                for h in (0, 1)
            ],
            axis=0,
        )

    def side(v):
        return jnp.concatenate([v[0:128], v[128:256]], axis=1)

    def attend(b):
        rows = slice(128 * b, 128 * b + 128)
        qi = iota((256, 128), 0) & 127
        kj = iota((256, 128), 1)
        allowed = ((qi >> 4) == (kj >> 4)) & (kj <= qi)
        for h in (0, 1):
            kv = kv_s[h, rows, :]
            scores = dot_last(stacked(q_s[h, rows, :], 0), kv[:, 0:256]) * SCALE
            scores = jnp.where(allowed, scores, -1e30)
            e = jnp.exp(scores - jnp.max(scores, axis=-1, keepdims=True))
            probs = e * (1.0 / jnp.sum(e, axis=-1, keepdims=True))
            ps[512 * b + 256 * h : 512 * b + 256 * h + 256, :] = probs
            att[rows, 384 * h : 384 * h + 384] = dot_plain(side(probs.astype(bf16)), stacked(kv, 160)).astype(bf16)

    def second_norm():
        ar_end(1)

        def body(rows, mine):
            v = x0[rows, :] + summed(1, rows)
            x1[rows, :] = v
            n2[mine, :] = (v * rms(v) * vec[1:2, :]).astype(bf16)

        own_rows(body)
        share(1, n2)

    def inner():
        shared(1, n2)

        def body(cols, i):
            v = dot_plain(n2[...], w[:, pl.ds(pl.multiple_of(C_IN + TILE * i, 128), TILE)]) + bin_s[0:1, cols]
            pre[:, cols] = v
            act[:, cols] = (v * jax.nn.sigmoid(v)).astype(bf16)

        tiles_loop(TILES, body)

    def outer_back():
        def body(cols, i):
            v = pre[:, cols]
            s = jax.nn.sigmoid(v)
            d = dot_plain(cot[...], w[:, pl.ds(pl.multiple_of(C_OUT + TILE * i, 128), TILE)])
            dpre[:, cols] = (d * (s * (1.0 + v * (1.0 - s)))).astype(bf16)

        tiles_loop(TILES, body)

    def second_back():
        ar_end(2)

        def body(rows, mine):
            dn = summed(2, rows)
            v = x1[rows, :]
            r = rms(v)
            xh = v * r
            scaled = dn * vec[1:2, :]
            inside = jnp.mean(scaled * xh, axis=-1, keepdims=True)
            ct = cot[mine, :].astype(f32)
            d = ct + r * (scaled - xh * inside)
            pre[rows, :] = d
            db[mine, :] = d.astype(bf16)
            sums[8:16, :] += fold(dn * xh)
            sums[16:24, :] += fold(ct)

        own_rows(body)
        share(2, db)

    def attended_back():
        shared(2, db)

        def body(cols, i):
            datt[:, cols] = dot_plain(db[...], w[:, cols]).astype(bf16)

        tiles_loop(3, body)

    def attend_back(b):
        rows = slice(128 * b, 128 * b + 128)
        for h in (0, 1):
            probs = ps[512 * b + 256 * h : 512 * b + 256 * h + 256, :]
            kv = kv_s[h, rows, :]
            heads_d = stacked(datt[rows, 384 * h : 384 * h + 384], 160)
            dp = dot_last(heads_d, kv)
            ds = (probs * (dp - jnp.sum(probs * dp, axis=-1, keepdims=True))).astype(bf16)
            part[rows, 512 * h : 512 * h + 256] = dot_plain(side(ds), stacked(kv[:, 0:256], 0)) * SCALE
            dv = dot_rows(probs.astype(bf16), heads_d)
            dk = dot_rows(ds, stacked(q_s[h, rows, :], 0)) * SCALE
            dkv = jnp.concatenate([dv[:, 0:256] + dk, dv[:, 256:384]], axis=1)
            part[rows, 512 * h + 160 : 512 * h + 512] = dkv[:, 0:352]

    def turn_back():
        def body(j, carry):
            rows = pl.ds(m16(16 * j), 16)
            v = part[rows, 0:1024]
            v = v * rot_c[...] - pltpu.roll(v, 984, 1) * rot_a[...] - pltpu.roll(v, 40, 1) * rot_b[...]
            dpj[rows, :] = v.astype(bf16)
            return carry

        lax.fori_loop(0, TOK // 16, body, 0)

    def finish():
        ar_end(3)

        def body(rows, mine):
            start = rows.start - PART * l + PART * x
            out_o[pl.ds(m16(start), 32), :] = (x1[rows, :] + summed(3, rows) + vec[2:3, :]).astype(bf16)

        own_rows(body, PART * l, PART)
        ref = out_o.at[pl.ds(m16(PART * x), PART)]
        go(remote(ref, ref, pt_s.at[3], pt_r.at[3], along["x"]))

    def grad_out(k):
        grad_block(k, cot, act, C_OUT)
        s_start(k)

    def grad_in(k):
        grad_block(k, n2, dpre, C_IN)
        s_start(k)

    def grad_qkv(k):
        grad_block(k, n1, dpj, C_QKV)
        s_start(k)

    def grad_att():
        def body(rows, i):
            g[rows, 0:768] = dot_rows(db[:, rows], att[...]).astype(bf16)

        tiles_loop(TILES, body)

    def grad_bias():
        ones = one_hot((iota((TOK, 128), 1) >= L_BIN) & (iota((TOK, 128), 1) < L_BIN + 2))

        def body(rows, i):
            gbs[rows, :] = dot_rows(dpre[:, rows], ones)

        tiles_loop(TILES, body)

    def first_back():
        ar_end(4)

        def body(rows, mine):
            dn = summed(4, rows)
            v = x0[rows, :]
            r = rms(v)
            xh = v * r
            scaled = dn * vec[0:1, :]
            inside = jnp.mean(scaled * xh, axis=-1, keepdims=True)
            d = pre[rows, :] + r * (scaled - xh * inside)
            de[mine, :] = d.astype(bf16)
            sums[0:8, :] += fold(dn * xh)

        own_rows(body)
        share(3, de)

    def hidden_back():
        shared(3, de)
        v = pret[...]
        s = jax.nn.sigmoid(v)
        d = dot_plain(de[...], w[:, 0:768])
        dpe[...] = jnp.where(units, d * (s * (1.0 + v * (1.0 - s))), jnp.where(resids, d, 0.0)).astype(bf16)

    def grad_tok():
        row32 = iota((32, 128), 0)
        pick = one_hot((row32 < 24) & (iota((32, 128), 1) == L_VEC + (row32 >> 3)))

        def body(rows, i):
            both = g[rows, 0:768].astype(f32) + dot_rows(de[:, rows], hc[...])
            columns = dot_rows(sums[:, rows].astype(bf16), pick)
            for h in (0, 1):
                g[rows, 384 * h : 384 * h + 256] = both[:, 384 * h : 384 * h + 256].astype(bf16)
                g[rows, slab(h)] = (both[:, slab(h)] + columns).astype(bf16)

        tiles_loop(TILES, body)
        s_start(0)
        s_start(1)

    def grad_hidden():
        ghs[...] = dot_rows(fe[...], dpe[...])
        lane = iota((80, 128), 1)
        for h in (0, 1):
            for j in range(4):
                at = 640 * h + 160 * j
                tmp[:, 0:128] = jnp.where(lane == L_BIN, gbs[at : at + 80, :], 0.0) + jnp.where(
                    lane == L_BIN + 1, gbs[at + 80 : at + 160, :], 0.0
                )
                tmp[:, L_HID : L_HID + 40] = ghs[0:80, 384 * h + 40 * j : 384 * h + 40 * j + 40]
                rows = pl.ds(m16(320 * m + 80 * j), 80)
                g[rows, slab(h)] = (g[rows, slab(h)].astype(f32) + tmp[:, 0:128]).astype(bf16)
        s_start(2)

    def points_back(stage):
        theirs = m16(PART * (1 - l))
        mine = m16(PART * l)
        half = pl.ds(m16(PART * x), PART)
        if stage == 0:
            ptx[...] = dot_last(dpe[...], hid[...])
            go(remote(ptx.at[pl.ds(oth0, OWN)], ptr.at[0], pt_s.at[0], pt_r.at[0], mate))
        elif stage == 1:
            remote(ptr.at[0], ptr.at[0], pt_s.at[0], pt_r.at[0], mate).wait_recv()
            ptr[1] = ptx[pl.ds(own0, OWN), :] + ptr[0]
            go(remote(ptr.at[1, pl.ds(theirs, PART)], ptr.at[2, pl.ds(theirs, PART)], pt_s.at[1], pt_r.at[1], beside))
        elif stage == 2:
            there = ptr.at[2, pl.ds(mine, PART)]
            remote(there, there, pt_s.at[1], pt_r.at[1], beside).wait_recv()
            ptr[3, half, :] = ptr[1, pl.ds(mine, PART), :] + ptr[2, pl.ds(mine, PART), :]
            go(remote(ptr.at[3, half], ptr.at[3, half], pt_s.at[2], pt_r.at[2], along["x"]))
        else:
            there = ptr.at[3, pl.ds(m16(PART * (1 - x)), PART)]
            remote(there, there, pt_s.at[2], pt_r.at[2], along["x"]).wait_recv()
            wide = dot_last(ptr[3].astype(bf16), one_hot(lane_of == place_of))
            wide = jnp.where(right_patch, wide, 0.0).astype(bf16)
            pts_o[...] = dot_rows(spread, wide) * (1.0 - missing[...].astype(f32))

    operands = ((hc, 0, 768), (att, 0, 768), (dpre, C_IN, 1280), (act, C_OUT, 1280), (dpj, C_QKV, 1024))
    steps = (
        g_first, g_own, g_second, g_third, g_done, s_step, features, cot_out, cot_here, tokenize, vectors,
        first_norm, project, turn, attend, second_norm, inner, grad_out, outer_back, grad_in, second_back,
        attended_back, attend_back, turn_back, finish, grad_qkv, grad_att, grad_bias, first_back, hidden_back,
        grad_tok, grad_hidden, points_back, ar_begin, ar_mid,
    )
    for name, *which in PLAN:
        steps[name](*which)

    there = out_o.at[pl.ds(m16(PART * (1 - x)), PART)]
    remote(there, there, pt_s.at[3], pt_r.at[3], along["x"]).wait_recv()
    for k, (_, _, width, at) in enumerate(CHUNKS):
        for i, (to, member) in enumerate(group):
            there = fb.at[member, :, at : at + width]
            remote(there, there, fin_s.at[k, i], fin_r.at[k, i], to).wait_recv()
    for copy in sent:
        copy.wait_send()


def unpack_kernel(
    out_i, pts_i, fb,
    out_o, pts_o, hw_o, hb_o, tok_o, res_o, tokb_o, gain1_o, qkv_o, att_o, gain2_o, in_o, inb_o, outw_o, outb_o,
):
    f32 = jnp.float32
    out_o[...] = out_i[...]
    pts_o[...] = pts_i[...]
    turned = []
    hidden = jnp.zeros((8, 128), f32)
    for q in range(4):
        at = slice(160 * q, 160 * q + 160)
        lead = fb[q, :, 0:384].astype(f32)
        tok_o[:, at] = lead[:, 0:160]
        att_o[:, at] = lead[:, 160:320]
        tile = lead[:, 256:384]
        hidden = hidden + tile[64:72]
        t = jnp.transpose(jnp.concatenate([tile, jnp.zeros((48, 128), f32)], axis=0))
        turned.append(t)
        res_o[8 * q : 8 * q + 8, :] = t[L_RES : L_RES + 8, 0:80]
        qkv = fb[q, :, 384:896].astype(f32)
        for j in range(3):
            qkv_o[j, :, at] = qkv[:, 160 * j : 160 * j + 160]
        in_o[:, 640 * q : 640 * q + 640] = fb[q, :, 896:1536].astype(f32)
        outw_o[:, 640 * q : 640 * q + 640] = fb[q, :, 1536:2176].astype(f32)
    both = turned[0] + turned[1]
    every = both + turned[2] + turned[3]
    tokb_o[...] = turned[0][L_ONE : L_ONE + 1, 0:80]
    gain1_o[...] = both[L_VEC : L_VEC + 1, 0:80]
    gain2_o[...] = both[L_VEC + 1 : L_VEC + 2, 0:80]
    outb_o[...] = both[L_VEC + 2 : L_VEC + 3, 0:80]
    inb_o[:, 0:80] = every[L_BIN : L_BIN + 1, 0:80]
    inb_o[:, 80:160] = every[L_BIN + 1 : L_BIN + 2, 0:80]
    hw_o[...] = every[L_HID : L_HID + 40, 0:64]
    hb_o[...] = hidden[0:1, L_HID : L_HID + 40]


def rotary_lanes():
    lanes = np.arange(1024) % 512
    inside = lanes % HEAD_DIM
    turned = lanes < 320
    freqs = 10000.0 ** (-2.0 * (inside % 40) / HEAD_DIM)
    angles = np.arange(CTXLEN)[:, None] * freqs[None, :]
    cosine = np.where(turned, np.cos(angles), 1.0)
    sine = np.where(turned, np.sin(angles), 0.0)
    lower = np.where(inside < 40, -sine, 0.0)
    upper = np.where(inside >= 40, sine, 0.0)
    return [np.asarray(t, np.float32) for t in (cosine, lower, upper)]


def fast_body(
    points, missing, tok_hidden_w, tok_hidden_b, tok_out_w, tok_res_w, tok_out_b, attn_gain, qkv_w, attn_out_w,
    mlp_gain, mlp_in_w, mlp_in_b, mlp_out_w, mlp_out_b, cotangent,
):
    f32, bf16 = jnp.float32, jnp.bfloat16
    any_space = pl.BlockSpec(memory_space=pl.ANY)
    vmem = pl.BlockSpec(memory_space=pltpu.VMEM)

    def sems(*shape):
        return pltpu.SemaphoreType.DMA(shape)

    def like(*shape):
        return jax.ShapeDtypeStruct(shape, f32)

    chunks = len(CHUNKS)
    specs = [vmem] * 19
    specs[11] = specs[13] = specs[15] = any_space
    out, pts, packed = pl.pallas_call(
        layer_kernel,
        out_shape=(
            jax.ShapeDtypeStruct((OWN, D), bf16),
            like(12, 512),
            jax.ShapeDtypeStruct((4, HALF, C_ONE), bf16),
        ),
        in_specs=specs,
        out_specs=[vmem] * 3,
        scratch_shapes=[
            pltpu.VMEM((D, C_ALL), bf16),
            pltpu.VMEM((D, C_ALL), bf16),
            pltpu.VMEM((7, 2, 160, C_ONE), bf16),
            pltpu.VMEM((TOK, 128), bf16),
            pltpu.VMEM((TOK, D), bf16),
            pltpu.VMEM((TOK, D), f32),
            pltpu.VMEM((TOK, D), f32),
            pltpu.VMEM((TOK, D), bf16),
            pltpu.VMEM((TOK, D), bf16),
            pltpu.VMEM((TOK, D), bf16),
            pltpu.VMEM((TOK, D), bf16),
            pltpu.VMEM((TOK, D), bf16),
            pltpu.VMEM((OWN, D), f32),
            pltpu.VMEM((OWN, D), f32),
            pltpu.VMEM((TOK, 768), bf16),
            pltpu.VMEM((TOK, 768), bf16),
            pltpu.VMEM((TOK, 768), f32),
            pltpu.VMEM((2, TOK, 256), bf16),
            pltpu.VMEM((2, TOK, 384), bf16),
            pltpu.VMEM((TOK, 768), bf16),
            pltpu.VMEM((TOK, 768), bf16),
            pltpu.VMEM((TOK, 1024), bf16),
            pltpu.VMEM((1536, 128), f32),
            pltpu.VMEM((D, 128), f32),
            pltpu.VMEM((128, 768), f32),
            pltpu.VMEM((128, 768), f32),
            pltpu.VMEM((128, 768), bf16),
            pltpu.VMEM((16, D), f32),
            pltpu.VMEM((8, D), f32),
            pltpu.VMEM((32, D), f32),
            pltpu.VMEM((TOK, 128), f32),
            pltpu.VMEM((4, OWN, 128), f32),
            pltpu.VMEM((4, HALF, 896), bf16),
            pltpu.VMEM((HALF, 896), f32),
            pltpu.VMEM((HALF, 128), f32),
            pltpu.VMEM((HALF, 384), f32),
            pltpu.VMEM((2, OWN, D), bf16),
            pltpu.VMEM((2, OWN, D), bf16),
            pltpu.VMEM((2, OWN, D), bf16),
            pltpu.VMEM((3, OWN, D), bf16),
            sems(chunks, 7), sems(chunks, 7), sems(chunks, 7), sems(chunks, 7),
            sems(5, 2, TILES), sems(5, 2, TILES),
            sems(4), sems(4), sems(chunks, 3), sems(chunks, 3), sems(chunks + 1), sems(2, 3), sems(2, 3),
            sems(chunks, 3), sems(chunks, 3), sems(4), sems(4),
        ],
        compiler_params=pltpu.CompilerParams(
            collective_id=0, has_side_effects=True, vmem_limit_bytes=64 * 1024 * 1024 - 512 * 1024
        ),
        cost_estimate=pl.CostEstimate(flops=13 * 10**9, bytes_accessed=10**7, transcendentals=10**6),
    )(
        points, missing, tok_hidden_w[0], tok_hidden_b, tok_out_w, tok_res_w.T, tok_out_b[None], attn_gain[None],
        qkv_w.transpose(1, 0, 2), attn_out_w, mlp_gain[None], mlp_in_w, mlp_in_b, mlp_out_w, mlp_out_b[None],
        cotangent, *[jnp.asarray(t) for t in rotary_lanes()],
    )
    (
        output, points_grad, hidden_w, hidden_b, tok, res_t, tok_b, gain1, qkv, att, gain2, inner, inner_b, outer,
        outer_b,
    ) = pl.pallas_call(
        unpack_kernel,
        out_shape=(
            jax.ShapeDtypeStruct((OWN, D), bf16),
            like(12, 512), like(40, 64), like(1, 40), like(HALF, 640), like(32, HALF), like(1, HALF), like(1, HALF),
            like(3, HALF, 640), like(HALF, 640), like(1, HALF), like(HALF, 2560), like(1, 160), like(HALF, 2560),
            like(1, HALF),
        ),
        in_specs=[vmem] * 3,
        out_specs=[vmem] * 15,
        compiler_params=pltpu.CompilerParams(vmem_limit_bytes=32 * 1024 * 1024),
    )(out, pts, packed)
    return (
        output, points_grad, hidden_w[None], hidden_b, tok, res_t.T, tok_b[0], gain1[0], qkv.transpose(1, 0, 2), att,
        gain2[0], inner, inner_b, outer, outer_b[0],
    )


def solution(mesh):
    placed = (
        P("fsdp", None),
        P("fsdp", None),
        P("tp", "fsdp", None),
        P("tp", "fsdp"),
        P("fsdp", "tp"),
        P("fsdp", "tp"),
        P("fsdp"),
        P("fsdp"),
        P("fsdp", None, "tp"),
        P("fsdp", "tp"),
        P("fsdp"),
        P("fsdp", "tp"),
        P("tp", "fsdp"),
        P("fsdp", "tp"),
        P("fsdp"),
        P("fsdp", None),
    )
    small_slice = mesh.shape["fsdp"] == 16 and mesh.shape["tp"] == 2
    return jax.shard_map(
        fast_body if small_slice else body,
        mesh=mesh,
        in_specs=placed,
        out_specs=(
            P("fsdp", None),
            P("fsdp", None),
            P("tp", "fsdp", None),
            P("tp", "fsdp"),
            P("fsdp", "tp"),
            P("fsdp", "tp"),
            P("fsdp"),
            P("fsdp"),
            P("fsdp", None, "tp"),
            P("fsdp", "tp"),
            P("fsdp"),
            P("fsdp", "tp"),
            P("tp", "fsdp"),
            P("fsdp", "tp"),
            P("fsdp"),
        ),
        check_vma=False,
    )
```

```python
import math

import jax
import jax.numpy as jnp
import numpy as np
from jax import lax
from jax.experimental import pallas as pl
from jax.experimental.pallas import tpu as pltpu
from jax.sharding import PartitionSpec as P

D = 1280
HEAD_DIM = 80
PL = 32
CTXLEN = 16


def dot_plain(left, right):
    return jnp.dot(left, right, preferred_element_type=jnp.float32)


def dot_last(left, right):
    return lax.dot_general(
        left, right, (((1,), (1,)), ((), ())), preferred_element_type=jnp.float32
    )


def dot_rows(left, right):
    return lax.dot_general(
        left, right, (((0,), (0,)), ((), ())), preferred_element_type=jnp.float32
    )


def silu_slope(values):
    sigma = jax.nn.sigmoid(values)
    return sigma * (1.0 + values * (1.0 - sigma))


def rotary_tables():
    positions = jnp.arange(CTXLEN, dtype=jnp.float32)
    freqs = 10000.0 ** (-2.0 * jnp.arange(HEAD_DIM // 2, dtype=jnp.float32) / HEAD_DIM)
    angles = positions[:, None] * freqs[None, :]
    return (jnp.cos(angles)[None, :, None, :], jnp.sin(angles)[None, :, None, :])


def rotate(vector, cosine, sine):
    half = vector.shape[-1] // 2
    first = vector[..., :half]
    second = vector[..., half:]
    return jnp.concatenate(
        [first * cosine - second * sine, second * cosine + first * sine], axis=-1
    )


def rotate_back(vector, cosine, sine):
    half = vector.shape[-1] // 2
    first = vector[..., :half]
    second = vector[..., half:]
    return jnp.concatenate(
        [first * cosine + second * sine, second * cosine - first * sine], axis=-1
    )


def norm_stats(values):
    factor = lax.rsqrt(jnp.mean(values * values, axis=-1, keepdims=True) + 1e-06)
    return (factor, values * factor)


def norm_back(grad, normal, factor, gain):
    scaled = grad * gain
    inner = jnp.mean(scaled * normal, axis=-1, keepdims=True)
    return (factor * (scaled - normal * inner), jnp.sum(grad * normal, axis=0))


def body(
    points,
    missing,
    tok_hidden_w,
    tok_hidden_b,
    tok_out_w,
    tok_res_w,
    tok_out_b,
    attn_gain,
    qkv_w,
    attn_out_w,
    mlp_gain,
    mlp_in_w,
    mlp_in_b,
    mlp_out_w,
    mlp_out_b,
    cotangent,
):
    gathered = (
        lax.all_gather(tok_hidden_w, "fsdp", axis=1, tiled=True),
        lax.all_gather(tok_hidden_b, "fsdp", axis=1, tiled=True),
        lax.all_gather(tok_out_w, "fsdp", axis=0, tiled=True),
        lax.all_gather(tok_res_w, "fsdp", axis=0, tiled=True),
        lax.all_gather(tok_out_b, "fsdp", axis=0, tiled=True),
        lax.all_gather(attn_gain, "fsdp", axis=0, tiled=True),
        lax.all_gather(qkv_w, "fsdp", axis=0, tiled=True),
        lax.all_gather(attn_out_w, "fsdp", axis=0, tiled=True),
        lax.all_gather(mlp_gain, "fsdp", axis=0, tiled=True),
        lax.all_gather(mlp_in_w, "fsdp", axis=0, tiled=True),
        lax.all_gather(mlp_in_b, "fsdp", axis=1, tiled=True),
        lax.all_gather(mlp_out_w, "fsdp", axis=0, tiled=True),
        lax.all_gather(mlp_out_b, "fsdp", axis=0, tiled=True),
    )
    (
        hidden_full,
        hidden_bias,
        token_full,
        residual_full,
        token_bias,
        first_gain,
        project_full,
        attend_full,
        second_gain,
        inner_full,
        inner_bias,
        outer_full,
        outer_bias,
    ) = gathered
    contexts = points.shape[0]
    rows = contexts * CTXLEN
    tensor_rank = lax.axis_index("tp")
    kept_mask = (1 - missing).astype(jnp.float32).reshape(rows, PL)
    absent = missing.astype(jnp.float32).reshape(rows, PL)
    observed = points.astype(jnp.float32).reshape(rows, PL) * kept_mask
    features = jnp.concatenate([observed, absent], axis=1).astype(jnp.bfloat16)
    half_features = jnp.where(tensor_rank == 0, observed, absent).astype(jnp.bfloat16)
    hidden_matrix = hidden_full.reshape(-1, 2 * PL)
    pre_tok = dot_last(features, hidden_matrix) + hidden_bias.reshape(-1).astype(jnp.float32)
    hidden_tok = jax.nn.silu(pre_tok).astype(jnp.bfloat16)
    partial_tok = dot_last(hidden_tok, token_full) + dot_last(half_features, residual_full)
    embedded = lax.psum(partial_tok.astype(jnp.bfloat16), "tp").astype(jnp.float32)
    state_zero = embedded + token_bias.astype(jnp.float32)
    factor_one, normal_one = norm_stats(state_zero)
    normed_one = (normal_one * first_gain.astype(jnp.float32)).astype(jnp.bfloat16)
    local_width = project_full.shape[2]
    local_heads = local_width // HEAD_DIM
    project_matrix = project_full.reshape(D, 3 * local_width)
    projected = dot_plain(normed_one, project_matrix).reshape(
        contexts, CTXLEN, 3, local_heads, HEAD_DIM
    )
    cosine, sine = rotary_tables()
    queries = rotate(projected[:, :, 0], cosine, sine).astype(jnp.bfloat16)
    keys_rot = rotate(projected[:, :, 1], cosine, sine).astype(jnp.bfloat16)
    values_b = projected[:, :, 2].astype(jnp.bfloat16)
    scale = 1.0 / math.sqrt(HEAD_DIM)
    causal = jnp.arange(CTXLEN)[:, None] >= jnp.arange(CTXLEN)[None, :]

    def scores_of(left, right):
        raw = jnp.einsum("cihd,cjhd->chij", left, right, preferred_element_type=jnp.float32) * scale
        return jnp.where(causal, raw, -1e30)

    scores = scores_of(queries, keys_rot)
    row_top = jnp.max(scores, axis=-1, keepdims=True)
    log_total = row_top + jnp.log(jnp.sum(jnp.exp(scores - row_top), axis=-1, keepdims=True))
    probs_b = jnp.exp(scores - log_total).astype(jnp.bfloat16)
    attended = jnp.einsum("chij,cjhd->cihd", probs_b, values_b, preferred_element_type=jnp.float32)
    attended = attended.astype(jnp.bfloat16).reshape(rows, local_width)
    branch_attn = lax.psum(dot_last(attended, attend_full).astype(jnp.bfloat16), "tp").astype(
        jnp.float32
    )
    state_one = state_zero + branch_attn
    factor_two, normal_two = norm_stats(state_one)
    normed_two = (normal_two * second_gain.astype(jnp.float32)).astype(jnp.bfloat16)
    pre_mlp = dot_plain(normed_two, inner_full) + inner_bias.reshape(-1).astype(jnp.float32)
    activation = jax.nn.silu(pre_mlp).astype(jnp.bfloat16)
    branch_mlp = lax.psum(dot_last(activation, outer_full).astype(jnp.bfloat16), "tp").astype(
        jnp.float32
    )
    output = (state_one + branch_mlp + outer_bias.astype(jnp.float32)).astype(jnp.bfloat16)
    again = (
        lax.all_gather(tok_hidden_w, "fsdp", axis=1, tiled=True),
        lax.all_gather(tok_hidden_b, "fsdp", axis=1, tiled=True),
        lax.all_gather(tok_out_w, "fsdp", axis=0, tiled=True),
        lax.all_gather(tok_res_w, "fsdp", axis=0, tiled=True),
        lax.all_gather(tok_out_b, "fsdp", axis=0, tiled=True),
        lax.all_gather(attn_gain, "fsdp", axis=0, tiled=True),
        lax.all_gather(qkv_w, "fsdp", axis=0, tiled=True),
        lax.all_gather(attn_out_w, "fsdp", axis=0, tiled=True),
        lax.all_gather(mlp_gain, "fsdp", axis=0, tiled=True),
        lax.all_gather(mlp_in_w, "fsdp", axis=0, tiled=True),
        lax.all_gather(mlp_in_b, "fsdp", axis=1, tiled=True),
        lax.all_gather(mlp_out_w, "fsdp", axis=0, tiled=True),
        lax.all_gather(mlp_out_b, "fsdp", axis=0, tiled=True),
    )
    (
        hidden_full,
        hidden_bias,
        token_full,
        residual_full,
        token_bias,
        first_gain,
        project_full,
        attend_full,
        second_gain,
        inner_full,
        inner_bias,
        outer_full,
        outer_bias,
    ) = again
    hidden_matrix = hidden_full.reshape(-1, 2 * PL)
    project_matrix = project_full.reshape(D, 3 * local_width)
    grad_outer_bias = jnp.sum(cotangent, axis=0, dtype=jnp.float32)
    grad_outer = dot_rows(cotangent, activation)
    d_pre = (dot_plain(cotangent, outer_full) * silu_slope(pre_mlp)).astype(jnp.bfloat16)
    grad_inner_bias = jnp.sum(d_pre, axis=0, dtype=jnp.float32).reshape(1, -1)
    grad_inner = dot_rows(normed_two, d_pre)
    d_normed_two = lax.psum(dot_last(d_pre, inner_full).astype(jnp.bfloat16), "tp").astype(
        jnp.float32
    )
    through_two, grad_second_gain = norm_back(
        d_normed_two, normal_two, factor_two, second_gain.astype(jnp.float32)
    )
    d_state_one = cotangent.astype(jnp.float32) + through_two
    d_branch = d_state_one.astype(jnp.bfloat16)
    grad_attend = dot_rows(d_branch, attended)
    d_attended = (
        dot_plain(d_branch, attend_full)
        .astype(jnp.bfloat16)
        .reshape(contexts, CTXLEN, local_heads, HEAD_DIM)
    )
    probs = jnp.exp(scores_of(queries, keys_rot) - log_total)
    probs_b = probs.astype(jnp.bfloat16)
    d_probs = jnp.einsum(
        "cihd,cjhd->chij", d_attended, values_b, preferred_element_type=jnp.float32
    )
    d_values = jnp.einsum(
        "chij,cihd->cjhd", probs_b, d_attended, preferred_element_type=jnp.float32
    ).astype(jnp.bfloat16)
    row_inner = jnp.sum(probs * d_probs, axis=-1, keepdims=True)
    d_scores = (probs * (d_probs - row_inner)).astype(jnp.bfloat16)
    d_queries = (
        jnp.einsum("chij,cjhd->cihd", d_scores, keys_rot, preferred_element_type=jnp.float32)
        * scale
    )
    d_keys = (
        jnp.einsum("chij,cihd->cjhd", d_scores, queries, preferred_element_type=jnp.float32) * scale
    )
    d_queries = rotate_back(d_queries, cosine, sine).astype(jnp.bfloat16)
    d_keys = rotate_back(d_keys, cosine, sine).astype(jnp.bfloat16)
    d_projected = jnp.stack([d_queries, d_keys, d_values], axis=2).reshape(rows, 3 * local_width)
    grad_project = dot_rows(normed_one, d_projected).reshape(D, 3, local_width)
    d_normed_one = lax.psum(
        dot_last(d_projected, project_matrix).astype(jnp.bfloat16), "tp"
    ).astype(jnp.float32)
    through_one, grad_first_gain = norm_back(
        d_normed_one, normal_one, factor_one, first_gain.astype(jnp.float32)
    )
    d_state_zero = d_state_one + through_one
    grad_token_bias = jnp.sum(d_state_zero, axis=0)
    d_embedded = d_state_zero.astype(jnp.bfloat16)
    grad_token = dot_rows(d_embedded, hidden_tok)
    grad_residual = dot_rows(d_embedded, half_features)
    d_pre_tok = (dot_plain(d_embedded, token_full) * silu_slope(pre_tok)).astype(jnp.bfloat16)
    grad_hidden_bias = jnp.sum(d_pre_tok, axis=0, dtype=jnp.float32).reshape(1, -1)
    grad_hidden = dot_rows(d_pre_tok, features).reshape(1, -1, 2 * PL)
    through_hidden = dot_plain(d_pre_tok, hidden_matrix)[:, :PL]
    through_residual = dot_plain(d_embedded, residual_full)
    point_terms = through_hidden + jnp.where(tensor_rank == 0, through_residual, 0.0)
    point_sums = lax.psum(point_terms, "tp")
    points_grad = (point_sums * kept_mask).reshape(contexts, CTXLEN * PL)
    owned = (
        lax.psum_scatter(grad_hidden, "fsdp", scatter_dimension=1, tiled=True),
        lax.psum_scatter(grad_hidden_bias, "fsdp", scatter_dimension=1, tiled=True),
        lax.psum_scatter(grad_token, "fsdp", scatter_dimension=0, tiled=True),
        lax.psum_scatter(grad_residual, "fsdp", scatter_dimension=0, tiled=True),
        lax.psum_scatter(grad_token_bias, "fsdp", scatter_dimension=0, tiled=True),
        lax.psum_scatter(grad_first_gain, "fsdp", scatter_dimension=0, tiled=True),
        lax.psum_scatter(grad_project, "fsdp", scatter_dimension=0, tiled=True),
        lax.psum_scatter(grad_attend, "fsdp", scatter_dimension=0, tiled=True),
        lax.psum_scatter(grad_second_gain, "fsdp", scatter_dimension=0, tiled=True),
        lax.psum_scatter(grad_inner, "fsdp", scatter_dimension=0, tiled=True),
        lax.psum_scatter(grad_inner_bias, "fsdp", scatter_dimension=1, tiled=True),
        lax.psum_scatter(grad_outer, "fsdp", scatter_dimension=0, tiled=True),
        lax.psum_scatter(grad_outer_bias, "fsdp", scatter_dimension=0, tiled=True),
    )
    return (
        output,
        points_grad,
        owned[0],
        owned[1],
        owned[2],
        owned[3],
        owned[4],
        owned[5],
        owned[6],
        owned[7],
        owned[8],
        owned[9],
        owned[10],
        owned[11],
        owned[12],
    )


MESH = pl.DeviceIdType.MESH
TOK = 384
OWN = 192
PART = 96
HALF = 80
C_QKV, C_IN, C_OUT, C_ALL, C_ONE = 512, 1792, 2432, 3072, 2176
C_MLP = 896
BOTH = 2 * TOK
MLP_TILES = ((0, 256), (256, 256), (512, 128))
SPLIT = 640
CHUNKS = (
    (0, 256, 128, 0),
    (128, 256, 128, 128),
    (512, 640, 256, 256),
    (768, 640, 256, 512),
    (1024, 640, 128, 768),
    (1792, 0, 256, 896),
    (2048, 0, 384, 1152),
    (2432, 0, 256, 1536),
    (2688, 0, 256, 1792),
    (2944, 0, 128, 2048),
)
GATHER_ORDER = ("zxy", "zyx", "zxy", "zyx", "zxy", "zy", "zy", "zy", "zy", "zy")
SUM_ORDER = ("yxz", "xyz", "yxz", "xyz", "yxz", "yz", "yz", "yz", "yz", "yz")
(
    FIRST, OWNED, SECOND, THIRD, HERE, SUM, FEATS, COT, COT_HERE, TOKENS, VECTORS, NORM_1, PROJECT, TURN, ATTEND,
    NORM_2, INNER, GRAD_OUT, OUTER, GRAD_IN, BACK_2, D_ATT, ATTEND_B, TURN_B, FINISH, GRAD_QKV, GRAD_BIAS, BACK_1,
    D_HID, GRAD_TOK, GRAD_HID, POINTS, SEND, PASS, COT_PASS, NORM_PASS, CROSS, HIDDEN,
) = range(38)
PLAN = (
    (FIRST, 0), (FIRST, 4), (FIRST, 2), (FIRST, 1), (OWNED, 0), (FIRST, 3), (OWNED, 1), (FIRST, 7), (OWNED, 3),
    (FIRST, 5), (OWNED, 4), (SECOND, 0), (FIRST, 8), (SECOND, 1), (OWNED, 2), (FEATS,), (COT,), (THIRD, 1),
    (THIRD, 0), (SECOND, 4), (SECOND, 3), (SECOND, 2), (HERE, 0), (OWNED, 5), (FIRST, 6), (HERE, 1), (HIDDEN,),
    (TOKENS, 1), (THIRD, 4), (OWNED, 7), (TOKENS, 0), (FIRST, 9), (SEND, 0, 1), (THIRD, 2), (SEND, 0, 0),
    (PASS, 0, 1), (THIRD, 3), (OWNED, 6), (SECOND, 5), (PASS, 0, 0), (OWNED, 8), (VECTORS,), (HERE, 3), (HERE, 4),
    (NORM_1, 1), (SECOND, 7), (HERE, 2), (PROJECT, 1), (TURN, 1), (ATTEND, 1), (SEND, 1, 1), (PASS, 1, 1),
    (NORM_1, 0), (SECOND, 6), (COT_PASS,), (OWNED, 9), (PROJECT, 0), (TURN, 0), (ATTEND, 0), (SEND, 1, 0), (HERE, 5),
    (PASS, 1, 0), (SECOND, 8), (NORM_2, 1), (SECOND, 9), (NORM_2, 0), (COT_HERE,), (HERE, 6), (NORM_PASS, 1),
    (INNER, 0, 1), (HERE, 7), (HERE, 8), (INNER, 1, 1), (HERE, 9), (OUTER, 1), (SEND, 2, 1), (SEND, 3, 1),
    (NORM_PASS, 0), (CROSS, 2, 1), (INNER, 0, 0), (INNER, 1, 0), (GRAD_OUT, 7), (OUTER, 0), (SEND, 2, 0),
    (PASS, 2, 1), (CROSS, 2, 0), (CROSS, 3, 1), (GRAD_IN, 5), (SUM, 7), (GRAD_IN, 6), (PASS, 2, 0), (BACK_2, 1),
    (SEND, 3, 0), (SUM, 5), (D_ATT, 1), (ATTEND_B, 1), (GRAD_OUT, 8), (PASS, 3, 1), (TURN_B, 1), (SEND, 4, 1),
    (BACK_2, 0), (GRAD_OUT, 9), (GRAD_BIAS,), (CROSS, 3, 0), (D_ATT, 0), (SUM, 6), (PASS, 4, 1), (ATTEND_B, 0),
    (TURN_B, 0), (SUM, 6), (SUM, 7), (SEND, 4, 0), (GRAD_QKV, 4), (SUM, 5), (PASS, 4, 0), (GRAD_QKV, 3),
    (GRAD_QKV, 2), (BACK_1, 1), (SUM, 4), (SUM, 8), (SUM, 9), (PASS, 3, 0), (D_HID, 1), (BACK_1, 0), (D_HID, 0),
    (SUM, 3), (POINTS, 0), (SUM, 2), (SUM, 4), (SUM, 5), (GRAD_TOK,), (SUM, 2), (SUM, 7), (GRAD_HID,), (SUM, 8),
    (SUM, 4), (POINTS, 1), (SUM, 2), (SUM, 3), (SUM, 4), (SUM, 9), (SUM, 6), (SUM, 3), (SUM, 0), (SUM, 1), (SUM, 0),
    (SUM, 8), (SUM, 1), (FINISH,), (SUM, 3), (SUM, 0), (SUM, 1), (POINTS, 2), (SUM, 2), (SUM, 0), (SUM, 1), (SUM, 9),
    (POINTS, 3),
)
L_RES, L_ONE, L_VEC, L_BIN, L_HID = 32, 40, 41, 45, 47
TILE = 256
TILES = D // TILE
SCALE = 1.0 / math.sqrt(HEAD_DIM)


def iota(shape, dim):
    return lax.broadcasted_iota(jnp.int32, shape, dim)


def one_hot(cond):
    return jnp.where(cond, 1.0, 0.0).astype(jnp.bfloat16)


def layer_kernel(
    points, missing, hid_w, hid_b, tok_in, res_t, tok_b, gain1, qkv_in, att_in, gain2, win_in, b_in, wout_in,
    out_b, cot_in, rot_c, rot_a, rot_b,
    out_o, pts_o, fb,
    w, g, rb, rbm, fe, cot, part, pre, act, dpre, n1, n2, db, de, x0, x1, x2,
    hc, dpe, pret, q_s, k_s, v_s, att, datt, dpj, ps, gbs, ghs, hidf, hid, vec, bin_s, sums, ptx, ptr,
    pk, pkf, srcf, tmp,
    part3, cs, cr, ys, yr, xs, xr,
    ag_s, ag_r, rs_s, rs_r, ar_s, ar_r, nx_s, nx_r, in_s, in_r, lo_s, tk_s, tk_r, fin_s, fin_r, pt_s, pt_r,
):
    f32, bf16 = jnp.float32, jnp.bfloat16
    f = lax.axis_index("fsdp")
    x = lax.axis_index("tp")
    z = lax.div(f, 4)
    zh = lax.div(z, 2)
    l = z - 2 * zh
    y = lax.div(f, 2) - 2 * z
    c = f - 4 * z - 2 * y
    m = 2 * l + c
    mate = {"fsdp": f + 1 - 2 * c}
    beside = {"fsdp": f + 4 - 8 * l}
    corner = {"fsdp": f + 4 - 8 * l + 1 - 2 * c}
    along = {"z": {"fsdp": f + 8 - 16 * zh}, "y": {"fsdp": f + 2 - 4 * y}, "x": {"tp": 1 - x}}
    own0 = pl.multiple_of(PART * c, PART)
    oth0 = pl.multiple_of(PART * (1 - c), PART)

    def m16(v):
        return pl.multiple_of(v, 16)

    def remote(src, dst, s_sem, r_sem, to):
        return pltpu.make_async_remote_copy(
            src_ref=src, dst_ref=dst, send_sem=s_sem, recv_sem=r_sem, device_id=to, device_id_type=MESH
        )

    sent = []

    def go(copy):
        copy.start()
        sent.append(copy)

    barrier = pltpu.get_barrier_semaphore()
    peers = (mate, beside, corner, along["z"], along["y"], along["x"])
    for to in peers:
        pl.semaphore_signal(barrier, inc=1, device_id=to, device_id_type=MESH)

    part[0:80, 0:640] = tok_in[...].astype(f32)
    part[80:160, 0:640] = att_in[...].astype(f32)
    part[160:240, 0:640] = qkv_in[0].astype(f32)
    part[240:320, 0:640] = qkv_in[1].astype(f32)
    part[0:80, 640:1280] = qkv_in[2].astype(f32)
    srcf[...] = jnp.zeros(srcf.shape, f32)
    srcf[0:32, 0:80] = res_t[...].astype(f32)
    for i, v in enumerate((gain1, gain2, out_b, tok_b)):
        srcf[32 + i : 33 + i, 0:80] = v[...].astype(f32)
    tmp[0:1, 0:160] = b_in[...].astype(f32)
    srcf[36:37, 0:80] = tmp[0:1, 0:80]
    srcf[37:38, 0:80] = tmp[0:1, 80:160]
    srcf[40:80, 0:64] = hid_w[...].astype(f32)
    src = srcf[...].astype(bf16)
    row = iota((80, 128), 0)
    lane = iota((80, 128), 1)
    for q in range(4):
        col = 160 * q
        pkf[:, 0:160] = part[0:80, col : col + 160]
        pkf[:, 160:256] = jnp.zeros((80, 96), f32)
        place = (row < 32) & (row >= 8 * q) & (row < 8 * q + 8) & (lane == L_RES + row - 8 * q)
        place = place | ((row >= 32) & (row < 38) & (lane == L_VEC + row - 32))
        place = place | ((row >= 40) & (lane == L_HID + row - 40))
        pkf[:, 128:256] = pkf[:, 128:256] + dot_rows(src, one_hot(place))[0:80]
        pkf[64:65, 128 + L_HID : 128 + L_HID + 40] = hid_b[...].astype(f32)
        pkf[:, 256:416] = part[160:240, col : col + 160]
        pkf[:, 416:576] = part[240:320, col : col + 160]
        pkf[:, 576:736] = part[0:80, 640 + col : 800 + col]
        pkf[:, 736:896] = part[80:160, col : col + 160]
        pk[q] = pkf[...].astype(bf16)

    pl.semaphore_wait(barrier, len(peers))

    def cols(k, h):
        first, apart, width, _ = CHUNKS[k]
        return pl.ds(pl.multiple_of(first + apart * h, 128), width)

    def piece(k, member):
        first, _, width, at = CHUNKS[k]
        if at < 896:
            return pk.at[member, :, at : at + width]
        src, base = (win_in, 896) if at < 1536 else (wout_in, 1536)
        return src.at[:, pl.ds(pl.multiple_of(640 * member + at - base, 128), width)]

    group = ((mate, 2 * l + 1 - c), (beside, 2 - 2 * l + c), (corner, 3 - 2 * l - c))
    home = w.at[pl.ds(m16(HALF * f), HALF)]
    locals_in = {}

    def rows_of(to):
        return pl.ds(m16(HALF * to["fsdp"]), HALF)

    def g_first(k):
        dst = w.at[pl.ds(m16(HALF * f), HALF), cols(k, x)]
        for i, (to, member) in enumerate(group):
            go(remote(piece(k, member), dst, in_s.at[k, i], in_r.at[k, i], to))
        locals_in[k] = pltpu.make_async_copy(piece(k, m), dst, lo_s.at[k])
        locals_in[k].start()

    w4 = w.reshape(4, 2, 160, C_ALL)
    g4 = g.reshape(4, 2, 160, C_ALL)

    def block(ref, k, flips):
        zz = 1 - zh if "z" in flips else zh
        yy = 1 - y if "y" in flips else y
        h = 1 - x if "x" in flips else x
        return ref.at[pl.ds(2 * zz, 2), yy, :, cols(k, h)]

    def g_send(k, i, flips, axis):
        ref = block(w4, k, flips)
        go(remote(ref, ref, ag_s.at[k, i], ag_r.at[k, i], along[axis]))

    def g_recv(k, i, flips):
        ref = block(w4, k, flips)
        remote(ref, ref, ag_s.at[k, i], ag_r.at[k, i], along[flips[-1]]).wait_recv()

    def g_own(k):
        order = GATHER_ORDER[k]
        locals_in[k].wait()
        for i, (to, member) in enumerate(group):
            ref = w.at[rows_of(to), cols(k, x)]
            remote(ref, ref, in_s.at[k, i], in_r.at[k, i], to).wait_recv()
        for axis, i in zip(order, (0, 1, 3)):
            g_send(k, i, "", axis)

    def g_second(k):
        a, *rest = GATHER_ORDER[k]
        g_recv(k, 0, a)
        for axis, i in zip(rest, (2, 4)):
            g_send(k, i, a, axis)

    def g_third(k):
        a, b, d = GATHER_ORDER[k]
        g_recv(k, 1, b)
        g_send(k, 5, b, d)
        g_recv(k, 2, a + b)
        g_send(k, 6, a + b, d)

    def g_done(k):
        order = GATHER_ORDER[k]
        if len(order) == 2:
            g_recv(k, 1, order[1])
            g_recv(k, 2, order)
            return
        a, b, d = order
        g_recv(k, 3, d)
        g_recv(k, 4, a + d)
        g_recv(k, 5, b + d)
        g_recv(k, 6, order)

    def s_buf(k, i):
        _, _, width, at = CHUNKS[k]
        return rb.at[i, :, :, at : at + width] if at < C_MLP else rbm.at[i, :, :, at - C_MLP : at - C_MLP + width]

    def s_send(k, i, flips, axis):
        go(remote(block(g4, k, flips), s_buf(k, i), rs_s.at[k, i], rs_r.at[k, i], along[axis]))

    def s_add(k, i, flips, axis):
        ref = s_buf(k, i)
        remote(ref, ref, rs_s.at[k, i], rs_r.at[k, i], along[axis]).wait_recv()
        _, _, width, at = CHUNKS[k]
        zz = 1 - zh if "z" in flips else zh
        yy = 1 - y if "y" in flips else y
        there = cols(k, 1 - x if "x" in flips else x)

        def step(j, carry):
            half = lax.div(j, 2)
            inside = 80 * (j - 2 * half)
            here = pl.ds(m16(640 * zz + 320 * half + 160 * yy + inside), 80)
            rows = pl.ds(m16(inside), 80)
            if at < C_MLP:
                came = rb[i, half, rows, at : at + width]
            else:
                came = rbm[i, half, rows, at - C_MLP : at - C_MLP + width]
            g[here, there] = g[here, there] + came
            return carry

        lax.fori_loop(0, 4, step, 0)

    def s_start(k):
        a, b, *last = SUM_ORDER[k]
        if last:
            d = last[0]
            s_send(k, 0, a + b + d, a)
            s_send(k, 1, a + b, a)
            s_send(k, 2, a + d, a)
            s_send(k, 3, a, a)
        else:
            s_send(k, 0, a + b, a)
            s_send(k, 1, a, a)
        s_at[k] = 0

    def s_step(k):
        a, b, *last = SUM_ORDER[k]
        stage = s_at[k]
        s_at[k] = stage + 1
        if not last:
            if stage == 0:
                s_add(k, 0, b, a)
                s_send(k, 2, b, b)
            elif stage == 1:
                s_add(k, 1, "", a)
            else:
                s_add(k, 2, "", b)
                s_out(k)
            return
        d = last[0]
        if stage == 0:
            s_add(k, 0, b + d, a)
            s_send(k, 4, b + d, b)
            s_add(k, 1, b, a)
            s_send(k, 5, b, b)
        elif stage == 1:
            s_add(k, 2, d, a)
            s_add(k, 4, d, b)
            s_send(k, 6, d, d)
        elif stage == 2:
            s_add(k, 3, "", a)
            s_add(k, 5, "", b)
        else:
            s_add(k, 6, "", d)
            s_out(k)

    def s_out(k):
        _, _, width, at = CHUNKS[k]
        for i, (to, member) in enumerate(group):
            src = g.at[rows_of(to), cols(k, x)]
            go(remote(src, fb.at[m, :, at : at + width], fin_s.at[k, i], fin_r.at[k, i], to))
        fb[m, :, at : at + width] = g[pl.ds(m16(HALF * f), HALF), cols(k, x)]

    s_at = {}

    def ar_tile(i):
        return slice(SPLIT * i, SPLIT * i + SPLIT)

    def cs_ref(a, p, i):
        rows = OWN if a in (2, 3) else PART
        return cs.at[a % 2, p, 0:rows, ar_tile(i)], cr.at[a % 2, p, 0:rows, ar_tile(i)]

    def total(a):
        return part3 if a == 3 else part

    def ar_begin(a, p):
        if a >= 2:
            for i in range(2):
                done, there = cs_ref(a - 2, p, i)
                remote(done, there, ar_s.at[a - 2, 0, p, i], ar_r.at[a - 2, 0, p, i], mate).wait_send()
        for i in range(2):
            for n, first in enumerate((0, TOK) if a in (2, 3) else (0,)):
                rows = slice(first + OWN * p, first + OWN * p + OWN)
                value = None
                for left, lo, col, width in operands[a]:
                    more = dot_last(left[rows, lo : lo + width], w[ar_tile(i), col : col + width])
                    value = more if value is None else value + more
                total(a)[rows, ar_tile(i)] = value
                away = pl.ds(m16(first + OWN * p + oth0), PART)
                cs[a % 2, p, PART * n : PART * n + PART, ar_tile(i)] = total(a)[away, ar_tile(i)].astype(bf16)
            src, there = cs_ref(a, p, i)
            copy = remote(src, there, ar_s.at[a, 0, p, i], ar_r.at[a, 0, p, i], mate)
            copy.start()
            if a >= 3:
                sent.append(copy)

    def ar_cross(a, p):
        b = a - 2
        near = pl.ds(m16(TOK * x + OWN * p + own0), PART)
        far = pl.ds(m16(TOK * (1 - x) + OWN * p + own0), PART)
        for i in range(2):
            _, here = cs_ref(a, p, i)
            remote(here, here, ar_s.at[a, 0, p, i], ar_r.at[a, 0, p, i], mate).wait_recv()
            came = cr[a % 2, p, pl.ds(m16(PART * (1 - x)), PART), ar_tile(i)].astype(f32)
            ys[b, p, :, ar_tile(i)] = (total(a)[far, ar_tile(i)] + came).astype(bf16)
            go(remote(
                ys.at[b, p, :, ar_tile(i)], yr.at[b, p, :, ar_tile(i)], ar_s.at[a, 2, p, i], ar_r.at[a, 2, p, i],
                along["x"],
            ))
            total(a)[near, ar_tile(i)] = total(a)[near, ar_tile(i)] + cr[
                a % 2, p, pl.ds(m16(PART * x), PART), ar_tile(i)
            ].astype(f32)

    def ar_mid(a, p):
        b = a % 2
        if a >= 2:
            for i in range(2):
                done = xs.at[b, p, :, ar_tile(i)]
                remote(done, done, ar_s.at[a - 2, 1, p, i], ar_r.at[a - 2, 1, p, i], beside).wait_send()
        for i in range(2):
            if a in (2, 3):
                here = yr.at[a - 2, p, :, ar_tile(i)]
                remote(here, here, ar_s.at[a, 2, p, i], ar_r.at[a, 2, p, i], along["x"]).wait_recv()
                mine = total(a)[pl.ds(m16(TOK * x + OWN * p + own0), PART), ar_tile(i)]
                came = yr[a - 2, p, :, ar_tile(i)]
            else:
                _, here = cs_ref(a, p, i)
                remote(here, here, ar_s.at[a, 0, p, i], ar_r.at[a, 0, p, i], mate).wait_recv()
                mine = part[pl.ds(m16(OWN * p + own0), PART), ar_tile(i)]
                came = cr[b, p, 0:PART, ar_tile(i)]
            xs[b, p, :, ar_tile(i)] = (mine + came.astype(f32)).astype(bf16)
            copy = remote(
                xs.at[b, p, :, ar_tile(i)], xr.at[a % 3, p, :, ar_tile(i)], ar_s.at[a, 1, p, i], ar_r.at[a, 1, p, i],
                beside,
            )
            copy.start()
            if a >= 3:
                sent.append(copy)

    def ar_end(a, p):
        for i in range(2):
            here = xr.at[a % 3, p, :, ar_tile(i)]
            remote(here, here, ar_s.at[a, 1, p, i], ar_r.at[a, 1, p, i], beside).wait_recv()

    def summed(a, p, rows):
        return xs[a % 2, p, rows, :].astype(f32) + xr[a % 3, p, rows, :].astype(f32)

    def own_rows(body):
        def step(j, carry):
            body(pl.multiple_of(32 * j, 32))
            return carry

        lax.fori_loop(0, PART // 32, step, 0)

    def at32(start):
        return pl.ds(m16(start), 32)

    def share(j, p, ref, first=0, to=None):
        rows = ref.at[pl.ds(m16(first + OWN * p + own0), PART)]
        go(remote(rows, rows, nx_s.at[j, p], nx_r.at[j, p], mate if to is None else to))

    def shared(j, p, ref, first=0, start=None, to=None):
        rows = ref.at[pl.ds(m16(first + OWN * p + (oth0 if start is None else start)), PART)]
        remote(rows, rows, nx_s.at[j, p], nx_r.at[j, p], mate if to is None else to).wait_recv()

    def rms(v):
        return lax.rsqrt(jnp.mean(v * v, axis=-1, keepdims=True) + 1e-06)

    def fold(v):
        return jnp.sum(v.reshape(v.shape[0] // 8, 8, v.shape[1]), axis=0)

    def tiles_loop(count, body):
        def step(i, carry):
            body(pl.ds(pl.multiple_of(TILE * i, TILE), TILE), i)
            return carry

        lax.fori_loop(0, count, step, 0)

    def slab(h):
        return slice(128 + 256 * h, 256 + 256 * h)

    spread = one_hot(lax.div(iota((OWN, 12), 0), CTXLEN) == iota((OWN, 12), 1))
    right_patch = lax.div(iota((OWN, 512), 1), PL) == (iota((OWN, 512), 0) & (CTXLEN - 1))
    lane_of = iota((512, 128), 1)
    place_of = iota((512, 128), 0) & (PL - 1)
    mine0 = m16(OWN * l + own0)
    cot_part = cot_in.reshape(2, PART, D)
    cot_rows = cot.reshape(2, TOK, D)
    cot_copy = pltpu.make_async_copy(cot_part, cot_rows.at[:, pl.ds(mine0, PART)], lo_s.at[len(CHUNKS)])
    lane512 = iota((OWN, 512), 1) & 255
    units = lane512 < 160
    resids = (lane512 >= 128 + L_RES) & (lane512 < 128 + L_RES + 8)

    def part_rows(p, first=0):
        return slice(first + OWN * p, first + OWN * p + OWN)

    def features():
        keep = 1.0 - missing[...].astype(f32)
        seen = dot_plain(spread, (points[...].astype(f32) * keep).astype(bf16))
        gone = dot_plain(spread, missing[...].astype(f32).astype(bf16))
        feats = dot_plain(jnp.where(right_patch, seen, 0.0).astype(bf16), one_hot(lane_of == place_of))
        feats = feats + dot_plain(jnp.where(right_patch, gone, 0.0).astype(bf16), one_hot(lane_of == place_of + PL))
        ptx[0:OWN, :] = jnp.where(iota((OWN, 128), 1) == 2 * PL, 1.0, feats)
        fe[pl.ds(mine0, PART), :] = ptx[pl.ds(m16(PART * x), PART), :].astype(bf16)
        for i, (to, member) in enumerate(group):
            rows = fe.at[pl.ds(mine0, PART)]
            go(remote(rows, rows, tk_s.at[0, i], tk_r.at[0, i], to))
        sums[...] = jnp.zeros(sums.shape, f32)
        hidf[...] = jnp.zeros(hidf.shape, f32)

    def cot_out():
        cot_copy.start()
        for i, to in enumerate((mate, beside)):
            go(remote(cot_part, cot_rows.at[:, pl.ds(mine0, PART)], tk_s.at[1, i], tk_r.at[1, i], to))

    def cot_pass():
        rows = cot_rows.at[:, pl.ds(m16(OWN * (1 - l) + own0), PART)]
        remote(rows, rows, tk_s.at[1, 1], tk_r.at[1, 1], beside).wait_recv()
        go(remote(rows, rows, tk_s.at[1, 2], tk_r.at[1, 2], mate))

    def cot_here():
        cot_copy.wait()
        for i, ll in ((0, l), (2, 1 - l)):
            rows = cot_rows.at[:, pl.ds(m16(OWN * ll + oth0), PART)]
            remote(rows, rows, tk_s.at[1, i], tk_r.at[1, i], mate).wait_recv()

    def hidden():
        for h in (0, 1):
            for j in range(4):
                rows = pl.ds(m16(320 * m + 80 * j), 80)
                tmp[:, 0:128] = w[rows, slab(h)].astype(f32)
                hidf[0:72, 256 * h + 40 * j : 256 * h + 40 * j + 40] = tmp[0:72, L_HID : L_HID + 40]
            row = iota((128, 128), 0)
            lane = iota((128, 128), 1)
            chosen = (lane >= L_RES) & (lane < L_RES + 8) & (row == PL * h + 8 * m + lane - L_RES)
            hidf[:, slab(h)] = jnp.where(chosen, 1.0, hidf[:, slab(h)])
        hid[...] = hidf[...].astype(bf16)
        for i, (to, member) in enumerate(group):
            cc = 1 - c if i != 1 else c
            ll = l if i == 0 else 1 - l
            rows = fe.at[pl.ds(m16(OWN * ll + PART * cc), PART)]
            remote(rows, rows, tk_s.at[0, i], tk_r.at[0, i], to).wait_recv()

    def tokenize(p):
        v = dot_plain(fe[part_rows(p), :], hid[...])
        pret[part_rows(p), :] = v
        hc[part_rows(p), :] = jnp.where(
            units, v * jax.nn.sigmoid(v), jnp.where(resids, v, jnp.where(lane512 == 128 + L_ONE, 1.0, 0.0))
        ).astype(bf16)

    def vectors():
        row16 = iota((16, 128), 0)
        lane16 = iota((16, 128), 1)
        vec[...] = dot_last(one_hot((row16 < 4) & (lane16 == L_VEC + row16)), w[:, slab(0)])
        own_slab = pl.ds(pl.multiple_of(128 + 256 * x, 128), 128)
        pair = dot_last(one_hot((row16 < 2) & (lane16 == L_BIN + row16)), w[pl.ds(m16(320 * m), 320), own_slab])
        tmp[0:16, 0:320] = pair
        for j in range(4):
            at = 160 * j
            bin_s[0:1, at : at + 80] = tmp[0:1, 80 * j : 80 * j + 80]
            bin_s[0:1, at + 80 : at + 160] = tmp[1:2, 80 * j : 80 * j + 80]

    def first_norm(p):
        ar_end(0, p)

        def body(start):
            v = summed(0, p, pl.ds(start, 32)) + vec[3:4, :]
            x0[at32(PART * p + start), :] = v
            n1[at32(OWN * p + own0 + start), :] = (v * rms(v) * vec[0:1, :]).astype(bf16)

        own_rows(body)
        share(0, p, n1)

    def project(p):
        shared(0, p, n1)
        rows = part_rows(p)
        for h in (0, 1):
            for lo in (0, 256):
                col = C_QKV + 640 * h + lo
                part[rows, 512 * h + lo : 512 * h + lo + 256] = dot_plain(n1[rows, :], w[:, col : col + 256])

    def turn(p):
        def body(j, carry):
            rows = pl.ds(m16(OWN * p + 48 * j), 48)
            for h in (0, 1):
                v = part[rows, 512 * h : 512 * h + 512]
                v = v * rot_c[...] + pltpu.roll(v, 472, 1) * rot_a[...] + pltpu.roll(v, 40, 1) * rot_b[...]
                q_s[h, rows, :] = v[:, 0:256].astype(bf16)
                k_s[h, rows, :] = pltpu.roll(v, 352, 1)[:, 0:256].astype(bf16)
                v_s[h, rows, :] = pltpu.roll(v, 288, 1)[:, 0:256].astype(bf16)
            return carry

        lax.fori_loop(0, OWN // 48, body, 0)

    def one_head(v, first, i):
        lane = iota(v.shape, 1)
        inside = (lane >= first + HEAD_DIM * i) & (lane < first + HEAD_DIM * i + HEAD_DIM)
        return jnp.where(inside, v, jnp.zeros_like(v))

    def stacked(v, first):
        return jnp.concatenate([one_head(v, first, 0), one_head(v, first, 1)], axis=0)

    def by_head(probs, v, first):
        return dot_plain(probs[0:OWN], one_head(v, first, 0)) + dot_plain(probs[OWN:TOK], one_head(v, first, 1))

    def attend(p):
        rows = part_rows(p)
        qi = iota((TOK, OWN), 0)
        qi = jnp.where(qi >= OWN, qi - OWN, qi)
        kj = iota((TOK, OWN), 1)
        allowed = ((qi >> 4) == (kj >> 4)) & (kj <= qi)
        for h in (0, 1):
            scores = dot_last(stacked(q_s[h, rows, :], 0), k_s[h, rows, :]) * SCALE
            scores = jnp.where(allowed, scores, -1e30)
            e = jnp.exp(scores - jnp.max(scores, axis=-1, keepdims=True))
            probs = e * (1.0 / jnp.sum(e, axis=-1, keepdims=True))
            ps[p, h] = probs
            att[rows, 256 * h : 256 * h + 256] = by_head(probs.astype(bf16), v_s[h, rows, :], 96).astype(bf16)

    def second_norm(p):
        ar_end(1, p)

        def body(start):
            own = at32(PART * p + start)
            v = x0[own, :] + summed(1, p, pl.ds(start, 32))
            x1[own, :] = v
            n2[at32(TOK * x + OWN * p + own0 + start), :] = (v * rms(v) * vec[1:2, :]).astype(bf16)

        own_rows(body)
        share(1, p, n2, TOK * x, along["x"])
        share(4, p, n2, TOK * x)

    def norm_pass(p):
        far = TOK * (1 - x)
        shared(1, p, n2, far, own0, along["x"])
        rows = n2.at[pl.ds(m16(far + OWN * p + own0), PART)]
        go(remote(rows, rows, nx_s.at[5, p], nx_r.at[5, p], mate))

    def inner(which, p):
        first = TOK * (x if which == 0 else 1 - x)
        shared(4 if which == 0 else 5, p, n2, first)
        rows = pl.ds(m16(first + OWN * p), OWN)
        for lo, width in MLP_TILES:
            at = slice(lo, lo + width)
            v = dot_plain(n2[rows, :], w[:, C_IN + lo : C_IN + lo + width]) + bin_s[0:1, at]
            pre[rows, at] = v
            act[rows, at] = (v * jax.nn.sigmoid(v)).astype(bf16)

    def outer_back(p):
        for first in (0, TOK):
            rows = part_rows(p, first)
            for lo, width in MLP_TILES:
                at = slice(lo, lo + width)
                v = pre[rows, at]
                s = jax.nn.sigmoid(v)
                d = dot_plain(cot[rows, :], w[:, C_OUT + lo : C_OUT + lo + width])
                dpre[rows, at] = (d * (s * (1.0 + v * (1.0 - s)))).astype(bf16)

    def norm_back(dn, v, gain):
        r = rms(v)
        xh = v * r
        scaled = dn * gain
        inside = jnp.mean(scaled * xh, axis=-1, keepdims=True)
        return r * (scaled - xh * inside), fold(dn * xh)

    def second_back(p):
        ar_end(2, p)

        def body(start):
            own = at32(PART * p + start)
            d, by_gain = norm_back(summed(2, p, pl.ds(start, 32)), x1[own, :], vec[1:2, :])
            ct = cot[at32(TOK * x + OWN * p + own0 + start), :].astype(f32)
            d = ct + d
            x2[own, :] = d
            db[at32(OWN * p + own0 + start), :] = d.astype(bf16)
            sums[8:16, :] += by_gain
            sums[16:24, :] += fold(ct)

        own_rows(body)
        share(2, p, db)

    def attended_back(p):
        shared(2, p, db)
        rows = part_rows(p)
        for h in (0, 1):
            col = C_QKV + 640 * h + 384
            datt[rows, 256 * h : 256 * h + 256] = dot_plain(db[rows, :], w[:, col : col + 256]).astype(bf16)

    def attend_back(p):
        rows = part_rows(p)
        for h in (0, 1):
            probs = ps[p, h]
            heads_d = stacked(datt[rows, 256 * h : 256 * h + 256], 96)
            dp = dot_last(heads_d, v_s[h, rows, :])
            ds = (probs * (dp - jnp.sum(probs * dp, axis=-1, keepdims=True))).astype(bf16)
            part[rows, 512 * h : 512 * h + 256] = by_head(ds, k_s[h, rows, :], 0) * SCALE
            part[rows, 512 * h + 160 : 512 * h + 416] = dot_rows(ds, stacked(q_s[h, rows, :], 0)) * SCALE
            dv = dot_rows(probs.astype(bf16), heads_d)
            dv = jnp.concatenate([dv, jnp.zeros((OWN, 128), f32)], axis=1)
            part[rows, 512 * h + 320 : 512 * h + 512] = dv[:, 96:288]

    def turn_back(p):
        def body(j, carry):
            rows = pl.ds(m16(OWN * p + 48 * j), 48)
            for h in (0, 1):
                v = part[rows, 512 * h : 512 * h + 512]
                v = v * rot_c[...] - pltpu.roll(v, 472, 1) * rot_a[...] - pltpu.roll(v, 40, 1) * rot_b[...]
                dpj[rows, 512 * h : 512 * h + 512] = v.astype(bf16)
            return carry

        lax.fori_loop(0, OWN // 48, body, 0)

    def finish():
        ar_end(3, 0)
        ar_end(3, 1)

        def body(start):
            rows = pl.ds(start, 32)
            v = xs[1, l, rows, :].astype(f32) + xr[0, l, rows, :].astype(f32)
            out_o[at32(PART * x + start), :] = (x1[at32(PART * l + start), :] + v + vec[2:3, :]).astype(bf16)

        own_rows(body)
        ref = out_o.at[pl.ds(m16(PART * x), PART)]
        go(remote(ref, ref, pt_s.at[3], pt_r.at[3], along["x"]))

    def grad_mlp(k, left, right, base):
        first, _, width, _ = CHUNKS[k]

        def body(rows, i):
            lo = first - base
            g[rows, first : first + width] = dot_rows(left[:, rows], right[:, lo : lo + width]).astype(bf16)

        tiles_loop(TILES, body)
        s_start(k)

    def grad_out(k):
        grad_mlp(k, cot, act, C_OUT)

    def grad_in(k):
        grad_mlp(k, n2, dpre, C_IN)

    def grad_qkv(k):
        first, apart, width, _ = CHUNKS[k]

        def body(rows, i):
            for h in (0, 1):
                for lo in range(first - C_QKV, first - C_QKV + width, 128):
                    value = None
                    if lo < 512:
                        value = dot_rows(n1[:, rows], dpj[:, 512 * h + lo : 512 * h + lo + 128])
                    if lo >= 384:
                        more = dot_rows(db[:, rows], att[:, 256 * h + lo - 384 : 256 * h + lo - 256])
                        value = more if value is None else value + more
                    col = C_QKV + apart * h + lo
                    g[rows, col : col + 128] = value.astype(bf16)

        tiles_loop(TILES, body)
        s_start(k)

    def grad_bias():
        ones = one_hot((iota((BOTH, 128), 1) >= L_BIN) & (iota((BOTH, 128), 1) < L_BIN + 2))
        for lo, width in MLP_TILES:
            gbs[lo : lo + width, :] = dot_rows(dpre[:, lo : lo + width], ones)

    def first_back(p):
        ar_end(4, p)

        def body(start):
            own = at32(PART * p + start)
            d, by_gain = norm_back(summed(4, p, pl.ds(start, 32)), x0[own, :], vec[0:1, :])
            de[at32(OWN * p + own0 + start), :] = (x2[own, :] + d).astype(bf16)
            sums[0:8, :] += by_gain

        own_rows(body)
        share(3, p, de)

    def hidden_back(p):
        shared(3, p, de)
        rows = part_rows(p)
        v = pret[rows, :]
        s = jax.nn.sigmoid(v)
        d = dot_plain(de[rows, :], w[:, 0:512])
        dpe[rows, :] = jnp.where(units, d * (s * (1.0 + v * (1.0 - s))), jnp.where(resids, d, 0.0)).astype(bf16)

    def grad_tok():
        row32 = iota((32, 128), 0)
        pick = one_hot((row32 < 24) & (iota((32, 128), 1) == L_VEC + (row32 >> 3)))

        def body(rows, i):
            both = dot_rows(de[:, rows], hc[...])
            columns = dot_rows(sums[:, rows].astype(bf16), pick)
            for h in (0, 1):
                g[rows, 256 * h : 256 * h + 128] = both[:, 256 * h : 256 * h + 128].astype(bf16)
                g[rows, slab(h)] = (both[:, slab(h)] + columns).astype(bf16)

        tiles_loop(TILES, body)
        s_start(0)

    def grad_hidden():
        ghs[...] = dot_rows(fe[...], dpe[...])
        lane = iota((80, 128), 1)
        for h in (0, 1):
            for j in range(4):
                at = 160 * j
                tmp[:, 0:128] = jnp.where((lane == L_BIN) & (x == h), gbs[at : at + 80, :], 0.0) + jnp.where(
                    (lane == L_BIN + 1) & (x == h), gbs[at + 80 : at + 160, :], 0.0
                )
                tmp[:, L_HID : L_HID + 40] = ghs[0:80, 256 * h + 40 * j : 256 * h + 40 * j + 40]
                rows = pl.ds(m16(320 * m + 80 * j), 80)
                g[rows, slab(h)] = (g[rows, slab(h)].astype(f32) + tmp[:, 0:128]).astype(bf16)
        s_start(1)

    def points_back(stage):
        if stage == 0:
            ptx[...] = dot_last(dpe[...], hid[...])
            away = ptx.reshape(2, OWN, 128).at[:, pl.ds(oth0, PART)]
            go(remote(away, ptr.at[0], pt_s.at[0], pt_r.at[0], mate))
        elif stage == 1:
            remote(ptr.at[0], ptr.at[0], pt_s.at[0], pt_r.at[0], mate).wait_recv()
            for p in (0, 1):
                ptr[1, p] = ptx[pl.ds(m16(OWN * p + own0), PART), :] + ptr[0, p]
            go(remote(ptr.at[1, 1 - l], ptr.at[2, 1 - l], pt_s.at[1], pt_r.at[1], beside))
        elif stage == 2:
            there = ptr.at[2, l]
            remote(there, there, pt_s.at[1], pt_r.at[1], beside).wait_recv()
            ptr[3, x] = ptr[1, l] + ptr[2, l]
            go(remote(ptr.at[3, x], ptr.at[3, x], pt_s.at[2], pt_r.at[2], along["x"]))
        else:
            there = ptr.at[3, 1 - x]
            remote(there, there, pt_s.at[2], pt_r.at[2], along["x"]).wait_recv()
            every = ptr[3].reshape(OWN, 128).astype(bf16)
            wide = dot_last(every, one_hot(lane_of == place_of))
            wide = jnp.where(right_patch, wide, 0.0).astype(bf16)
            pts_o[...] = dot_rows(spread, wide) * (1.0 - missing[...].astype(f32))

    operands = (
        ((hc, 0, 0, 512),),
        ((att, 0, 896, 256), (att, 256, 1536, 256)),
        ((dpre, 0, C_IN, 640),),
        ((act, 0, C_OUT, 640),),
        ((dpj, 0, 512, 512), (dpj, 512, 1152, 512)),
    )
    steps = (
        g_first, g_own, g_second, g_third, g_done, s_step, features, cot_out, cot_here, tokenize, vectors,
        first_norm, project, turn, attend, second_norm, inner, grad_out, outer_back, grad_in, second_back,
        attended_back, attend_back, turn_back, finish, grad_qkv, grad_bias, first_back, hidden_back, grad_tok,
        grad_hidden, points_back, ar_begin, ar_mid, cot_pass, norm_pass, ar_cross, hidden,
    )
    for name, *which in PLAN:
        steps[name](*which)

    there = out_o.at[pl.ds(m16(PART * (1 - x)), PART)]
    remote(there, there, pt_s.at[3], pt_r.at[3], along["x"]).wait_recv()
    for k, (_, _, width, at) in enumerate(CHUNKS):
        for i, (to, member) in enumerate(group):
            there = fb.at[member, :, at : at + width]
            remote(there, there, fin_s.at[k, i], fin_r.at[k, i], to).wait_recv()
    for copy in sent:
        copy.wait_send()


def unpack_kernel(
    out_i, pts_i, fb,
    out_o, pts_o, hw_o, hb_o, tok_o, res_o, tokb_o, gain1_o, qkv_o, att_o, gain2_o, in_o, inb_o, outw_o, outb_o,
):
    f32 = jnp.float32
    out_o[...] = out_i[...]
    pts_o[...] = pts_i[...]
    turned = []
    hidden = jnp.zeros((8, 128), f32)
    for q in range(4):
        at = slice(160 * q, 160 * q + 160)
        lead = fb[q, :, 0:256].astype(f32)
        tok_o[:, at] = lead[:, 0:160]
        tile = lead[:, 128:256]
        hidden = hidden + tile[64:72]
        t = jnp.transpose(jnp.concatenate([tile, jnp.zeros((48, 128), f32)], axis=0))
        turned.append(t)
        res_o[8 * q : 8 * q + 8, :] = t[L_RES : L_RES + 8, 0:80]
        qkv = fb[q, :, 256:896].astype(f32)
        for j in range(3):
            qkv_o[j, :, at] = qkv[:, 160 * j : 160 * j + 160]
        att_o[:, at] = qkv[:, 480:640]
        in_o[:, 640 * q : 640 * q + 640] = fb[q, :, 896:1536].astype(f32)
        outw_o[:, 640 * q : 640 * q + 640] = fb[q, :, 1536:2176].astype(f32)
    both = turned[0] + turned[1]
    every = both + turned[2] + turned[3]
    tokb_o[...] = turned[0][L_ONE : L_ONE + 1, 0:80]
    gain1_o[...] = both[L_VEC : L_VEC + 1, 0:80]
    gain2_o[...] = both[L_VEC + 1 : L_VEC + 2, 0:80]
    outb_o[...] = both[L_VEC + 2 : L_VEC + 3, 0:80]
    inb_o[:, 0:80] = every[L_BIN : L_BIN + 1, 0:80]
    inb_o[:, 80:160] = every[L_BIN + 1 : L_BIN + 2, 0:80]
    hw_o[...] = every[L_HID : L_HID + 40, 0:64]
    hb_o[...] = hidden[0:1, L_HID : L_HID + 40]


def rotary_lanes():
    lanes = np.arange(512)
    inside = lanes % HEAD_DIM
    turned = lanes < 320
    freqs = 10000.0 ** (-2.0 * (inside % 40) / HEAD_DIM)
    angles = (np.arange(48) % CTXLEN)[:, None] * freqs[None, :]
    cosine = np.where(turned, np.cos(angles), 1.0)
    sine = np.where(turned, np.sin(angles), 0.0)
    lower = np.where(inside < 40, -sine, 0.0)
    upper = np.where(inside >= 40, sine, 0.0)
    return [np.asarray(t, np.float32) for t in (cosine, lower, upper)]


def fast_body(
    points, missing, tok_hidden_w, tok_hidden_b, tok_out_w, tok_res_w, tok_out_b, attn_gain, qkv_w, attn_out_w,
    mlp_gain, mlp_in_w, mlp_in_b, mlp_out_w, mlp_out_b, cotangent,
):
    f32, bf16 = jnp.float32, jnp.bfloat16
    any_space = pl.BlockSpec(memory_space=pl.ANY)
    vmem = pl.BlockSpec(memory_space=pltpu.VMEM)

    def sems(*shape):
        return pltpu.SemaphoreType.DMA(shape)

    def like(*shape):
        return jax.ShapeDtypeStruct(shape, f32)

    chunks = len(CHUNKS)
    specs = [vmem] * 19
    specs[11] = specs[13] = specs[15] = any_space
    out, pts, packed = pl.pallas_call(
        layer_kernel,
        out_shape=(
            jax.ShapeDtypeStruct((OWN, D), bf16),
            like(12, 512),
            jax.ShapeDtypeStruct((4, HALF, C_ONE), bf16),
        ),
        in_specs=specs,
        out_specs=[vmem] * 3,
        scratch_shapes=[
            pltpu.VMEM((D, C_ALL), bf16),
            pltpu.VMEM((D, C_ALL), bf16),
            pltpu.VMEM((7, 2, 160, C_MLP), bf16),
            pltpu.VMEM((3, 2, 160, C_ONE - C_MLP), bf16),
            pltpu.VMEM((TOK, 128), bf16),
            pltpu.VMEM((BOTH, D), bf16),
            pltpu.VMEM((BOTH, D), f32),
            pltpu.VMEM((BOTH, 640), f32),
            pltpu.VMEM((BOTH, 640), bf16),
            pltpu.VMEM((BOTH, 640), bf16),
            pltpu.VMEM((TOK, D), bf16),
            pltpu.VMEM((BOTH, D), bf16),
            pltpu.VMEM((TOK, D), bf16),
            pltpu.VMEM((TOK, D), bf16),
            pltpu.VMEM((OWN, D), f32),
            pltpu.VMEM((OWN, D), f32),
            pltpu.VMEM((OWN, D), f32),
            pltpu.VMEM((TOK, 512), bf16),
            pltpu.VMEM((TOK, 512), bf16),
            pltpu.VMEM((TOK, 512), f32),
            pltpu.VMEM((2, TOK, 256), bf16),
            pltpu.VMEM((2, TOK, 256), bf16),
            pltpu.VMEM((2, TOK, 256), bf16),
            pltpu.VMEM((TOK, 512), bf16),
            pltpu.VMEM((TOK, 512), bf16),
            pltpu.VMEM((TOK, 1024), bf16),
            pltpu.VMEM((2, 2, TOK, OWN), f32),
            pltpu.VMEM((640, 128), f32),
            pltpu.VMEM((128, 512), f32),
            pltpu.VMEM((128, 512), f32),
            pltpu.VMEM((128, 512), bf16),
            pltpu.VMEM((16, D), f32),
            pltpu.VMEM((8, 640), f32),
            pltpu.VMEM((32, D), f32),
            pltpu.VMEM((TOK, 128), f32),
            pltpu.VMEM((4, 2, PART, 128), f32),
            pltpu.VMEM((4, HALF, 896), bf16),
            pltpu.VMEM((HALF, 896), f32),
            pltpu.VMEM((HALF, 128), f32),
            pltpu.VMEM((HALF, 384), f32),
            pltpu.VMEM((BOTH, D), f32),
            pltpu.VMEM((2, 2, OWN, D), bf16),
            pltpu.VMEM((2, 2, OWN, D), bf16),
            pltpu.VMEM((2, 2, PART, D), bf16),
            pltpu.VMEM((2, 2, PART, D), bf16),
            pltpu.VMEM((2, 2, PART, D), bf16),
            pltpu.VMEM((3, 2, PART, D), bf16),
            sems(chunks, 7), sems(chunks, 7), sems(chunks, 7), sems(chunks, 7),
            sems(5, 3, 2, 2), sems(5, 3, 2, 2),
            sems(6, 2), sems(6, 2), sems(chunks, 3), sems(chunks, 3), sems(chunks + 1), sems(2, 3), sems(2, 3),
            sems(chunks, 3), sems(chunks, 3), sems(4), sems(4),
        ],
        compiler_params=pltpu.CompilerParams(
            collective_id=0, has_side_effects=True, vmem_limit_bytes=64 * 1024 * 1024 - 512 * 1024
        ),
        cost_estimate=pl.CostEstimate(flops=13 * 10**9, bytes_accessed=10**7, transcendentals=10**6),
    )(
        points, missing, tok_hidden_w[0], tok_hidden_b, tok_out_w, tok_res_w.T, tok_out_b[None], attn_gain[None],
        qkv_w.transpose(1, 0, 2), attn_out_w, mlp_gain[None], mlp_in_w, mlp_in_b, mlp_out_w, mlp_out_b[None],
        cotangent, *[jnp.asarray(t) for t in rotary_lanes()],
    )
    (
        output, points_grad, hidden_w, hidden_b, tok, res_t, tok_b, gain1, qkv, att, gain2, inner, inner_b, outer,
        outer_b,
    ) = pl.pallas_call(
        unpack_kernel,
        out_shape=(
            jax.ShapeDtypeStruct((OWN, D), bf16),
            like(12, 512), like(40, 64), like(1, 40), like(HALF, 640), like(32, HALF), like(1, HALF), like(1, HALF),
            like(3, HALF, 640), like(HALF, 640), like(1, HALF), like(HALF, 2560), like(1, 160), like(HALF, 2560),
            like(1, HALF),
        ),
        in_specs=[vmem] * 3,
        out_specs=[vmem] * 15,
        compiler_params=pltpu.CompilerParams(vmem_limit_bytes=32 * 1024 * 1024),
    )(out, pts, packed)
    return (
        output, points_grad, hidden_w[None], hidden_b, tok, res_t.T, tok_b[0], gain1[0], qkv.transpose(1, 0, 2), att,
        gain2[0], inner, inner_b, outer, outer_b[0],
    )


def solution(mesh):
    placed = (
        P("fsdp", None),
        P("fsdp", None),
        P("tp", "fsdp", None),
        P("tp", "fsdp"),
        P("fsdp", "tp"),
        P("fsdp", "tp"),
        P("fsdp"),
        P("fsdp"),
        P("fsdp", None, "tp"),
        P("fsdp", "tp"),
        P("fsdp"),
        P("fsdp", "tp"),
        P("tp", "fsdp"),
        P("fsdp", "tp"),
        P("fsdp"),
        P("fsdp", None),
    )
    small_slice = mesh.shape["fsdp"] == 16 and mesh.shape["tp"] == 2
    return jax.shard_map(
        fast_body if small_slice else body,
        mesh=mesh,
        in_specs=placed,
        out_specs=(
            P("fsdp", None),
            P("fsdp", None),
            P("tp", "fsdp", None),
            P("tp", "fsdp"),
            P("fsdp", "tp"),
            P("fsdp", "tp"),
            P("fsdp"),
            P("fsdp"),
            P("fsdp", None, "tp"),
            P("fsdp", "tp"),
            P("fsdp"),
            P("fsdp", "tp"),
            P("tp", "fsdp"),
            P("fsdp", "tp"),
            P("fsdp"),
        ),
        check_vma=False,
    )
```

```python
import math

import jax
import jax.numpy as jnp
import numpy as np
from jax import lax
from jax.experimental import pallas as pl
from jax.experimental.pallas import tpu as pltpu
from jax.sharding import PartitionSpec as P

D = 1280
HEAD_DIM = 80
PL = 32
CTXLEN = 16


def dot_plain(left, right):
    return jnp.dot(left, right, preferred_element_type=jnp.float32)


def dot_last(left, right):
    return lax.dot_general(
        left, right, (((1,), (1,)), ((), ())), preferred_element_type=jnp.float32
    )


def dot_rows(left, right):
    return lax.dot_general(
        left, right, (((0,), (0,)), ((), ())), preferred_element_type=jnp.float32
    )


def silu_slope(values):
    sigma = jax.nn.sigmoid(values)
    return sigma * (1.0 + values * (1.0 - sigma))


def rotary_tables():
    positions = jnp.arange(CTXLEN, dtype=jnp.float32)
    freqs = 10000.0 ** (-2.0 * jnp.arange(HEAD_DIM // 2, dtype=jnp.float32) / HEAD_DIM)
    angles = positions[:, None] * freqs[None, :]
    return (jnp.cos(angles)[None, :, None, :], jnp.sin(angles)[None, :, None, :])


def rotate(vector, cosine, sine):
    half = vector.shape[-1] // 2
    first = vector[..., :half]
    second = vector[..., half:]
    return jnp.concatenate(
        [first * cosine - second * sine, second * cosine + first * sine], axis=-1
    )


def rotate_back(vector, cosine, sine):
    half = vector.shape[-1] // 2
    first = vector[..., :half]
    second = vector[..., half:]
    return jnp.concatenate(
        [first * cosine + second * sine, second * cosine - first * sine], axis=-1
    )


def norm_stats(values):
    factor = lax.rsqrt(jnp.mean(values * values, axis=-1, keepdims=True) + 1e-06)
    return (factor, values * factor)


def norm_back(grad, normal, factor, gain):
    scaled = grad * gain
    inner = jnp.mean(scaled * normal, axis=-1, keepdims=True)
    return (factor * (scaled - normal * inner), jnp.sum(grad * normal, axis=0))


def body(
    points,
    missing,
    tok_hidden_w,
    tok_hidden_b,
    tok_out_w,
    tok_res_w,
    tok_out_b,
    attn_gain,
    qkv_w,
    attn_out_w,
    mlp_gain,
    mlp_in_w,
    mlp_in_b,
    mlp_out_w,
    mlp_out_b,
    cotangent,
):
    gathered = (
        lax.all_gather(tok_hidden_w, "fsdp", axis=1, tiled=True),
        lax.all_gather(tok_hidden_b, "fsdp", axis=1, tiled=True),
        lax.all_gather(tok_out_w, "fsdp", axis=0, tiled=True),
        lax.all_gather(tok_res_w, "fsdp", axis=0, tiled=True),
        lax.all_gather(tok_out_b, "fsdp", axis=0, tiled=True),
        lax.all_gather(attn_gain, "fsdp", axis=0, tiled=True),
        lax.all_gather(qkv_w, "fsdp", axis=0, tiled=True),
        lax.all_gather(attn_out_w, "fsdp", axis=0, tiled=True),
        lax.all_gather(mlp_gain, "fsdp", axis=0, tiled=True),
        lax.all_gather(mlp_in_w, "fsdp", axis=0, tiled=True),
        lax.all_gather(mlp_in_b, "fsdp", axis=1, tiled=True),
        lax.all_gather(mlp_out_w, "fsdp", axis=0, tiled=True),
        lax.all_gather(mlp_out_b, "fsdp", axis=0, tiled=True),
    )
    (
        hidden_full,
        hidden_bias,
        token_full,
        residual_full,
        token_bias,
        first_gain,
        project_full,
        attend_full,
        second_gain,
        inner_full,
        inner_bias,
        outer_full,
        outer_bias,
    ) = gathered
    contexts = points.shape[0]
    rows = contexts * CTXLEN
    tensor_rank = lax.axis_index("tp")
    kept_mask = (1 - missing).astype(jnp.float32).reshape(rows, PL)
    absent = missing.astype(jnp.float32).reshape(rows, PL)
    observed = points.astype(jnp.float32).reshape(rows, PL) * kept_mask
    features = jnp.concatenate([observed, absent], axis=1).astype(jnp.bfloat16)
    half_features = jnp.where(tensor_rank == 0, observed, absent).astype(jnp.bfloat16)
    hidden_matrix = hidden_full.reshape(-1, 2 * PL)
    pre_tok = dot_last(features, hidden_matrix) + hidden_bias.reshape(-1).astype(jnp.float32)
    hidden_tok = jax.nn.silu(pre_tok).astype(jnp.bfloat16)
    partial_tok = dot_last(hidden_tok, token_full) + dot_last(half_features, residual_full)
    embedded = lax.psum(partial_tok.astype(jnp.bfloat16), "tp").astype(jnp.float32)
    state_zero = embedded + token_bias.astype(jnp.float32)
    factor_one, normal_one = norm_stats(state_zero)
    normed_one = (normal_one * first_gain.astype(jnp.float32)).astype(jnp.bfloat16)
    local_width = project_full.shape[2]
    local_heads = local_width // HEAD_DIM
    project_matrix = project_full.reshape(D, 3 * local_width)
    projected = dot_plain(normed_one, project_matrix).reshape(
        contexts, CTXLEN, 3, local_heads, HEAD_DIM
    )
    cosine, sine = rotary_tables()
    queries = rotate(projected[:, :, 0], cosine, sine).astype(jnp.bfloat16)
    keys_rot = rotate(projected[:, :, 1], cosine, sine).astype(jnp.bfloat16)
    values_b = projected[:, :, 2].astype(jnp.bfloat16)
    scale = 1.0 / math.sqrt(HEAD_DIM)
    causal = jnp.arange(CTXLEN)[:, None] >= jnp.arange(CTXLEN)[None, :]

    def scores_of(left, right):
        raw = jnp.einsum("cihd,cjhd->chij", left, right, preferred_element_type=jnp.float32) * scale
        return jnp.where(causal, raw, -1e30)

    scores = scores_of(queries, keys_rot)
    row_top = jnp.max(scores, axis=-1, keepdims=True)
    log_total = row_top + jnp.log(jnp.sum(jnp.exp(scores - row_top), axis=-1, keepdims=True))
    probs_b = jnp.exp(scores - log_total).astype(jnp.bfloat16)
    attended = jnp.einsum("chij,cjhd->cihd", probs_b, values_b, preferred_element_type=jnp.float32)
    attended = attended.astype(jnp.bfloat16).reshape(rows, local_width)
    branch_attn = lax.psum(dot_last(attended, attend_full).astype(jnp.bfloat16), "tp").astype(
        jnp.float32
    )
    state_one = state_zero + branch_attn
    factor_two, normal_two = norm_stats(state_one)
    normed_two = (normal_two * second_gain.astype(jnp.float32)).astype(jnp.bfloat16)
    pre_mlp = dot_plain(normed_two, inner_full) + inner_bias.reshape(-1).astype(jnp.float32)
    activation = jax.nn.silu(pre_mlp).astype(jnp.bfloat16)
    branch_mlp = lax.psum(dot_last(activation, outer_full).astype(jnp.bfloat16), "tp").astype(
        jnp.float32
    )
    output = (state_one + branch_mlp + outer_bias.astype(jnp.float32)).astype(jnp.bfloat16)
    again = (
        lax.all_gather(tok_hidden_w, "fsdp", axis=1, tiled=True),
        lax.all_gather(tok_hidden_b, "fsdp", axis=1, tiled=True),
        lax.all_gather(tok_out_w, "fsdp", axis=0, tiled=True),
        lax.all_gather(tok_res_w, "fsdp", axis=0, tiled=True),
        lax.all_gather(tok_out_b, "fsdp", axis=0, tiled=True),
        lax.all_gather(attn_gain, "fsdp", axis=0, tiled=True),
        lax.all_gather(qkv_w, "fsdp", axis=0, tiled=True),
        lax.all_gather(attn_out_w, "fsdp", axis=0, tiled=True),
        lax.all_gather(mlp_gain, "fsdp", axis=0, tiled=True),
        lax.all_gather(mlp_in_w, "fsdp", axis=0, tiled=True),
        lax.all_gather(mlp_in_b, "fsdp", axis=1, tiled=True),
        lax.all_gather(mlp_out_w, "fsdp", axis=0, tiled=True),
        lax.all_gather(mlp_out_b, "fsdp", axis=0, tiled=True),
    )
    (
        hidden_full,
        hidden_bias,
        token_full,
        residual_full,
        token_bias,
        first_gain,
        project_full,
        attend_full,
        second_gain,
        inner_full,
        inner_bias,
        outer_full,
        outer_bias,
    ) = again
    hidden_matrix = hidden_full.reshape(-1, 2 * PL)
    project_matrix = project_full.reshape(D, 3 * local_width)
    grad_outer_bias = jnp.sum(cotangent, axis=0, dtype=jnp.float32)
    grad_outer = dot_rows(cotangent, activation)
    d_pre = (dot_plain(cotangent, outer_full) * silu_slope(pre_mlp)).astype(jnp.bfloat16)
    grad_inner_bias = jnp.sum(d_pre, axis=0, dtype=jnp.float32).reshape(1, -1)
    grad_inner = dot_rows(normed_two, d_pre)
    d_normed_two = lax.psum(dot_last(d_pre, inner_full).astype(jnp.bfloat16), "tp").astype(
        jnp.float32
    )
    through_two, grad_second_gain = norm_back(
        d_normed_two, normal_two, factor_two, second_gain.astype(jnp.float32)
    )
    d_state_one = cotangent.astype(jnp.float32) + through_two
    d_branch = d_state_one.astype(jnp.bfloat16)
    grad_attend = dot_rows(d_branch, attended)
    d_attended = (
        dot_plain(d_branch, attend_full)
        .astype(jnp.bfloat16)
        .reshape(contexts, CTXLEN, local_heads, HEAD_DIM)
    )
    probs = jnp.exp(scores_of(queries, keys_rot) - log_total)
    probs_b = probs.astype(jnp.bfloat16)
    d_probs = jnp.einsum(
        "cihd,cjhd->chij", d_attended, values_b, preferred_element_type=jnp.float32
    )
    d_values = jnp.einsum(
        "chij,cihd->cjhd", probs_b, d_attended, preferred_element_type=jnp.float32
    ).astype(jnp.bfloat16)
    row_inner = jnp.sum(probs * d_probs, axis=-1, keepdims=True)
    d_scores = (probs * (d_probs - row_inner)).astype(jnp.bfloat16)
    d_queries = (
        jnp.einsum("chij,cjhd->cihd", d_scores, keys_rot, preferred_element_type=jnp.float32)
        * scale
    )
    d_keys = (
        jnp.einsum("chij,cihd->cjhd", d_scores, queries, preferred_element_type=jnp.float32) * scale
    )
    d_queries = rotate_back(d_queries, cosine, sine).astype(jnp.bfloat16)
    d_keys = rotate_back(d_keys, cosine, sine).astype(jnp.bfloat16)
    d_projected = jnp.stack([d_queries, d_keys, d_values], axis=2).reshape(rows, 3 * local_width)
    grad_project = dot_rows(normed_one, d_projected).reshape(D, 3, local_width)
    d_normed_one = lax.psum(
        dot_last(d_projected, project_matrix).astype(jnp.bfloat16), "tp"
    ).astype(jnp.float32)
    through_one, grad_first_gain = norm_back(
        d_normed_one, normal_one, factor_one, first_gain.astype(jnp.float32)
    )
    d_state_zero = d_state_one + through_one
    grad_token_bias = jnp.sum(d_state_zero, axis=0)
    d_embedded = d_state_zero.astype(jnp.bfloat16)
    grad_token = dot_rows(d_embedded, hidden_tok)
    grad_residual = dot_rows(d_embedded, half_features)
    d_pre_tok = (dot_plain(d_embedded, token_full) * silu_slope(pre_tok)).astype(jnp.bfloat16)
    grad_hidden_bias = jnp.sum(d_pre_tok, axis=0, dtype=jnp.float32).reshape(1, -1)
    grad_hidden = dot_rows(d_pre_tok, features).reshape(1, -1, 2 * PL)
    through_hidden = dot_plain(d_pre_tok, hidden_matrix)[:, :PL]
    through_residual = dot_plain(d_embedded, residual_full)
    point_terms = through_hidden + jnp.where(tensor_rank == 0, through_residual, 0.0)
    point_sums = lax.psum(point_terms, "tp")
    points_grad = (point_sums * kept_mask).reshape(contexts, CTXLEN * PL)
    owned = (
        lax.psum_scatter(grad_hidden, "fsdp", scatter_dimension=1, tiled=True),
        lax.psum_scatter(grad_hidden_bias, "fsdp", scatter_dimension=1, tiled=True),
        lax.psum_scatter(grad_token, "fsdp", scatter_dimension=0, tiled=True),
        lax.psum_scatter(grad_residual, "fsdp", scatter_dimension=0, tiled=True),
        lax.psum_scatter(grad_token_bias, "fsdp", scatter_dimension=0, tiled=True),
        lax.psum_scatter(grad_first_gain, "fsdp", scatter_dimension=0, tiled=True),
        lax.psum_scatter(grad_project, "fsdp", scatter_dimension=0, tiled=True),
        lax.psum_scatter(grad_attend, "fsdp", scatter_dimension=0, tiled=True),
        lax.psum_scatter(grad_second_gain, "fsdp", scatter_dimension=0, tiled=True),
        lax.psum_scatter(grad_inner, "fsdp", scatter_dimension=0, tiled=True),
        lax.psum_scatter(grad_inner_bias, "fsdp", scatter_dimension=1, tiled=True),
        lax.psum_scatter(grad_outer, "fsdp", scatter_dimension=0, tiled=True),
        lax.psum_scatter(grad_outer_bias, "fsdp", scatter_dimension=0, tiled=True),
    )
    return (
        output,
        points_grad,
        owned[0],
        owned[1],
        owned[2],
        owned[3],
        owned[4],
        owned[5],
        owned[6],
        owned[7],
        owned[8],
        owned[9],
        owned[10],
        owned[11],
        owned[12],
    )


MESH = pl.DeviceIdType.MESH
TOK = 384
OWN = 192
PART = 96
HALF = 80
C_QKV, C_IN, C_OUT, C_ALL, C_ONE = 512, 1792, 2432, 3072, 2176
C_MLP = 896
BOTH = 2 * TOK
MLP_TILES = ((0, 256), (256, 256), (512, 128))
SPLIT = 640
CHUNKS = (
    (0, 256, 128, 0),
    (128, 256, 128, 128),
    (512, 640, 256, 256),
    (768, 640, 256, 512),
    (1024, 640, 128, 768),
    (1792, 0, 256, 896),
    (2048, 0, 384, 1152),
    (2432, 0, 256, 1536),
    (2688, 0, 256, 1792),
    (2944, 0, 128, 2048),
)
GATHER_ORDER = ("zxy", "zyx", "zyx", "zyx", "zxy", "zy", "zy", "zy", "zy", "zy")
SUM_ORDER = ("xyz", "xyz", "yxz", "xyz", "xyz", "yz", "yz", "yz", "yz", "yz")
(
    FIRST, OWNED, SECOND, THIRD, HERE, SUM, FEATS, COT, COT_HERE, TOKENS, VECTORS, NORM_1, PROJECT, TURN, ATTEND,
    NORM_2, INNER, GRAD_OUT, OUTER, GRAD_IN, BACK_2, D_ATT, ATTEND_B, TURN_B, FINISH, GRAD_QKV, GRAD_BIAS, BACK_1,
    D_HID, GRAD_TOK, GRAD_HID, POINTS, SEND, PASS, COT_PASS, NORM_PASS, CROSS, HIDDEN,
) = range(38)
PLAN = (
    (FIRST, 1), (FIRST, 0), (FIRST, 3), (OWNED, 1), (FIRST, 2), (OWNED, 0), (OWNED, 3), (FIRST, 5), (OWNED, 2),
    (FEATS,), (FIRST, 4), (SECOND, 1), (COT,), (THIRD, 1), (SECOND, 0), (OWNED, 5), (FIRST, 8), (THIRD, 0), (HERE, 1),
    (FIRST, 6), (SECOND, 3), (OWNED, 4), (HERE, 0), (HIDDEN,), (TOKENS, 1), (SECOND, 2), (FIRST, 7), (OWNED, 8),
    (TOKENS, 0), (SEND, 0, 1), (THIRD, 3), (OWNED, 6), (PASS, 0, 1), (SEND, 0, 0), (SECOND, 4), (THIRD, 2),
    (VECTORS,), (THIRD, 4), (PASS, 0, 0), (HERE, 3), (NORM_1, 1), (SECOND, 5), (OWNED, 7), (HERE, 2), (PROJECT, 1),
    (TURN, 1), (HERE, 4), (ATTEND, 1), (FIRST, 9), (SEND, 1, 1), (PASS, 1, 1), (SECOND, 8), (NORM_1, 0), (SECOND, 6),
    (COT_PASS, 0), (PROJECT, 0), (OWNED, 9), (TURN, 0), (ATTEND, 0), (SEND, 1, 0), (PASS, 1, 0), (COT_PASS, 1),
    (NORM_2, 1), (SECOND, 7), (SECOND, 9), (HERE, 6), (COT_HERE,), (NORM_2, 0), (HERE, 5), (INNER, 0, 1),
    (NORM_PASS, 1), (HERE, 9), (HERE, 7), (HERE, 8), (INNER, 1, 1), (OUTER, 1), (SEND, 2, 1), (INNER, 0, 0),
    (NORM_PASS, 0), (CROSS, 2, 1), (INNER, 1, 0), (GRAD_OUT, 7), (OUTER, 0), (SEND, 2, 0), (PASS, 2, 1),
    (CROSS, 2, 0), (SEND, 3, 1), (GRAD_IN, 5), (SUM, 7), (GRAD_IN, 6), (CROSS, 3, 1), (PASS, 2, 0), (BACK_2, 1),
    (SEND, 3, 0), (D_ATT, 1), (ATTEND_B, 1), (TURN_B, 1), (SEND, 4, 1), (SUM, 5), (CROSS, 3, 0), (PASS, 4, 1),
    (BACK_2, 0), (GRAD_OUT, 8), (D_ATT, 0), (GRAD_QKV, 4), (ATTEND_B, 0), (SUM, 6), (TURN_B, 0), (SEND, 4, 0),
    (GRAD_OUT, 9), (PASS, 4, 0), (GRAD_QKV, 3), (SUM, 4), (SUM, 8), (SUM, 8), (BACK_1, 1), (SUM, 7), (GRAD_QKV, 2),
    (SUM, 9), (SUM, 7), (D_HID, 1), (SUM, 4), (PASS, 3, 0), (BACK_1, 0), (SUM, 5), (GRAD_BIAS,), (SUM, 2), (SUM, 6),
    (D_HID, 0), (SUM, 3), (POINTS, 0), (GRAD_TOK,), (SUM, 2), (POINTS, 1), (GRAD_HID,), (SUM, 5), (SUM, 2), (FINISH,),
    (SUM, 3), (SUM, 4), (SUM, 4), (SUM, 0), (SUM, 6), (SUM, 0), (SUM, 0), (SUM, 1), (SUM, 8), (SUM, 1), (SUM, 2),
    (SUM, 3), (SUM, 9), (SUM, 3), (SUM, 1), (SUM, 0), (POINTS, 2), (SUM, 9), (SUM, 1), (POINTS, 3),
)
L_RES, L_ONE, L_VEC, L_BIN, L_HID = 32, 40, 41, 45, 47
TILE = 256
TILES = D // TILE
SCALE = 1.0 / math.sqrt(HEAD_DIM)


def iota(shape, dim):
    return lax.broadcasted_iota(jnp.int32, shape, dim)


def one_hot(cond):
    return jnp.where(cond, 1.0, 0.0).astype(jnp.bfloat16)


def layer_kernel(
    points, missing, hid_w, hid_b, tok_in, res_t, tok_b, gain1, qkv_in, att_in, gain2, win_in, b_in, wout_in,
    out_b, cot_in, rot_c, rot_a, rot_b,
    out_o, pts_o, fb,
    w, g, rb, rbm, fe, cot, part, pre, act, dpre, n1, n2, db, de, x0, x1, x2,
    hc, dpe, pret, q_s, k_s, v_s, att, datt, dpj, ps, gbs, ghs, hidf, hid, vec, bin_s, sums, ptx, ptr,
    pk, pkf, srcf, tmp,
    part3, ob, cs, cr, ys, yr, xs, xr,
    ag_s, ag_r, rs_s, rs_r, cs_s, cs_r, xs_s, xs_r, ys_s, ys_r, nx_s, nx_r, in_s, in_r, lo_s, tk_s, tk_r,
    fin_s, fin_r, pt_s, pt_r, keep_s,
):
    f32, bf16 = jnp.float32, jnp.bfloat16
    f = lax.axis_index("fsdp")
    x = lax.axis_index("tp")
    z = lax.div(f, 4)
    zh = lax.div(z, 2)
    l = z - 2 * zh
    y = lax.div(f, 2) - 2 * z
    c = f - 4 * z - 2 * y
    m = 2 * l + c
    mate = {"fsdp": f + 1 - 2 * c}
    beside = {"fsdp": f + 4 - 8 * l}
    corner = {"fsdp": f + 4 - 8 * l + 1 - 2 * c}
    along = {"z": {"fsdp": f + 8 - 16 * zh}, "y": {"fsdp": f + 2 - 4 * y}, "x": {"tp": 1 - x}}
    own0 = pl.multiple_of(PART * c, PART)
    oth0 = pl.multiple_of(PART * (1 - c), PART)

    def m16(v):
        return pl.multiple_of(v, 16)

    def remote(src, dst, s_sem, r_sem, to):
        return pltpu.make_async_remote_copy(
            src_ref=src, dst_ref=dst, send_sem=s_sem, recv_sem=r_sem, device_id=to, device_id_type=MESH
        )

    sent = []

    def go(copy):
        copy.start()
        sent.append(copy)

    def came(ref, sem):
        remote(ref, ref, sem, sem, mate).wait_recv()

    def left(ref, sem):
        remote(ref, ref, sem, sem, mate).wait_send()

    barrier = pltpu.get_barrier_semaphore()
    peers = (mate, beside, corner, along["z"], along["y"], along["x"])
    for to in peers:
        pl.semaphore_signal(barrier, inc=1, device_id=to, device_id_type=MESH)

    part[0:80, 0:640] = tok_in[...].astype(f32)
    part[80:160, 0:640] = att_in[...].astype(f32)
    part[160:240, 0:640] = qkv_in[0].astype(f32)
    part[240:320, 0:640] = qkv_in[1].astype(f32)
    part[0:80, 640:1280] = qkv_in[2].astype(f32)
    srcf[...] = jnp.zeros(srcf.shape, f32)
    srcf[0:32, 0:80] = res_t[...].astype(f32)
    for i, v in enumerate((gain1, gain2, out_b, tok_b)):
        srcf[32 + i : 33 + i, 0:80] = v[...].astype(f32)
    tmp[0:1, 0:160] = b_in[...].astype(f32)
    srcf[36:37, 0:80] = tmp[0:1, 0:80]
    srcf[37:38, 0:80] = tmp[0:1, 80:160]
    srcf[40:80, 0:64] = hid_w[...].astype(f32)
    src = srcf[...].astype(bf16)
    row = iota((80, 128), 0)
    lane = iota((80, 128), 1)
    for q in range(4):
        col = 160 * q
        pkf[:, 0:160] = part[0:80, col : col + 160]
        pkf[:, 160:256] = jnp.zeros((80, 96), f32)
        place = (row < 32) & (row >= 8 * q) & (row < 8 * q + 8) & (lane == L_RES + row - 8 * q)
        place = place | ((row >= 32) & (row < 38) & (lane == L_VEC + row - 32))
        place = place | ((row >= 40) & (lane == L_HID + row - 40))
        pkf[:, 128:256] = pkf[:, 128:256] + dot_rows(src, one_hot(place))[0:80]
        pkf[64:65, 128 + L_HID : 128 + L_HID + 40] = hid_b[...].astype(f32)
        pkf[:, 256:416] = part[160:240, col : col + 160]
        pkf[:, 416:576] = part[240:320, col : col + 160]
        pkf[:, 576:736] = part[0:80, 640 + col : 800 + col]
        pkf[:, 736:896] = part[80:160, col : col + 160]
        pk[q] = pkf[...].astype(bf16)

    pl.semaphore_wait(barrier, len(peers))

    def cols(k, h):
        first, apart, width, _ = CHUNKS[k]
        return pl.ds(pl.multiple_of(first + apart * h, 128), width)

    def piece(k, member):
        first, _, width, at = CHUNKS[k]
        if at < 896:
            return pk.at[member, :, at : at + width]
        src, base = (win_in, 896) if at < 1536 else (wout_in, 1536)
        return src.at[:, pl.ds(pl.multiple_of(640 * member + at - base, 128), width)]

    group = ((mate, 2 * l + 1 - c), (beside, 2 - 2 * l + c), (corner, 3 - 2 * l - c))
    home = w.at[pl.ds(m16(HALF * f), HALF)]
    locals_in = {}

    def rows_of(to):
        return pl.ds(m16(HALF * to["fsdp"]), HALF)

    def g_first(k):
        dst = w.at[pl.ds(m16(HALF * f), HALF), cols(k, x)]
        for to, member in group:
            remote(piece(k, member), dst, in_s.at[0], in_r.at[k], to).start()
        locals_in[k] = pltpu.make_async_copy(piece(k, m), dst, lo_s.at[k])
        locals_in[k].start()

    w4 = w.reshape(4, 2, 160, C_ALL)
    g4 = g.reshape(4, 2, 160, C_ALL)

    def block(ref, k, flips):
        zz = 1 - zh if "z" in flips else zh
        yy = 1 - y if "y" in flips else y
        h = 1 - x if "x" in flips else x
        return ref.at[pl.ds(2 * zz, 2), yy, :, cols(k, h)]

    wide = sum(1 for chunk in CHUNKS if chunk[3] < C_MLP)

    def g_sem(k, i):
        return ag_r.at[4 * k + min(i, 3) if k < wide else 4 * wide + 2 * (k - wide) + min(i, 1)]

    def g_send(k, i, flips, axis):
        ref = block(w4, k, flips)
        remote(ref, ref, ag_s.at[0 if k < wide else 1], g_sem(k, i), along[axis]).start()

    def g_recv(k, i, flips):
        came(block(w4, k, flips), g_sem(k, i))

    def g_own(k):
        order = GATHER_ORDER[k]
        locals_in[k].wait()
        came(w.at[0 : 3 * HALF, 0 : CHUNKS[k][2]], in_r.at[k])
        for axis, i in zip(order, (0, 1, 3)):
            g_send(k, i, "", axis)

    def g_second(k):
        a, *rest = GATHER_ORDER[k]
        g_recv(k, 0, a)
        for axis, i in zip(rest, (2, 4)):
            g_send(k, i, a, axis)

    def g_third(k):
        a, b, d = GATHER_ORDER[k]
        g_recv(k, 1, b)
        g_send(k, 5, b, d)
        g_recv(k, 2, a + b)
        g_send(k, 6, a + b, d)

    def g_done(k):
        _, _, width, at = CHUNKS[k]
        if k < wide:
            came(rb.at[0:4, :, :, at : at + width], g_sem(k, 3))
        else:
            came(rbm.at[0:2, :, :, at - C_MLP : at - C_MLP + width], g_sem(k, 1))

    def s_buf(k, i):
        _, _, width, at = CHUNKS[k]
        return rb.at[i, :, :, at : at + width] if at < C_MLP else rbm.at[i, :, :, at - C_MLP : at - C_MLP + width]

    def s_sem(k, i):
        return rs_r.at[7 * k + i if k < wide else 7 * wide + 3 * (k - wide) + i]

    def s_send(k, i, flips, axis):
        remote(block(g4, k, flips), s_buf(k, i), rs_s.at[0 if k < wide else 1], s_sem(k, i), along[axis]).start()

    def s_add(k, i, flips, axis):
        came(s_buf(k, i), s_sem(k, i))
        _, _, width, at = CHUNKS[k]
        zz = 1 - zh if "z" in flips else zh
        yy = 1 - y if "y" in flips else y
        there = cols(k, 1 - x if "x" in flips else x)

        def step(j, carry):
            half = lax.div(j, 2)
            inside = 80 * (j - 2 * half)
            here = pl.ds(m16(640 * zz + 320 * half + 160 * yy + inside), 80)
            rows = pl.ds(m16(inside), 80)
            if at < C_MLP:
                more = rb[i, half, rows, at : at + width]
            else:
                more = rbm[i, half, rows, at - C_MLP : at - C_MLP + width]
            g[here, there] = g[here, there] + more
            return carry

        lax.fori_loop(0, 4, step, 0)

    def s_start(k):
        a, b, *last = SUM_ORDER[k]
        if last:
            d = last[0]
            s_send(k, 0, a + b + d, a)
            s_send(k, 1, a + b, a)
            s_send(k, 2, a + d, a)
            s_send(k, 3, a, a)
        else:
            s_send(k, 0, a + b, a)
            s_send(k, 1, a, a)
        s_at[k] = 0

    def s_step(k):
        a, b, *last = SUM_ORDER[k]
        stage = s_at[k]
        s_at[k] = stage + 1
        if not last:
            if stage == 0:
                s_add(k, 0, b, a)
                s_send(k, 2, b, b)
            elif stage == 1:
                s_add(k, 1, "", a)
            else:
                s_add(k, 2, "", b)
                s_out(k)
            return
        d = last[0]
        if stage == 0:
            s_add(k, 0, b + d, a)
            s_send(k, 4, b + d, b)
            s_add(k, 1, b, a)
            s_send(k, 5, b, b)
        elif stage == 1:
            s_add(k, 2, d, a)
            s_add(k, 4, d, b)
            s_send(k, 6, d, d)
        elif stage == 2:
            s_add(k, 3, "", a)
            s_add(k, 5, "", b)
        else:
            s_add(k, 6, "", d)
            s_out(k)

    def s_out(k):
        _, _, width, at = CHUNKS[k]
        dst = fb.at[m, :, at : at + width]
        for to, member in group:
            remote(g.at[rows_of(to), cols(k, x)], dst, fin_s.at[0], fin_r.at[0], to).start()
        pltpu.make_async_copy(g.at[pl.ds(m16(HALF * f), HALF), cols(k, x)], dst, keep_s.at[0]).start()

    s_at = {}

    def ar_tile(i):
        return slice(SPLIT * i, SPLIT * i + SPLIT)

    def cs_ref(a, p, i):
        rows = OWN if a in (2, 3) else PART
        return cs.at[a % 2, p, 0:rows, ar_tile(i)], cr.at[a % 2, p, 0:rows, ar_tile(i)]

    def total(a):
        return part3 if a == 3 else part

    def ar_begin(a, p):
        if a >= 2:
            left(cs.at[a % 2, p, 0 : OWN if a == 4 else PART, :], cs_s.at[a - 2, p])
        for i in range(2):
            for n, first in enumerate((0, TOK) if a in (2, 3) else (0,)):
                rows = slice(first + OWN * p, first + OWN * p + OWN)
                value = None
                for ref, lo, col, width in operands[a]:
                    more = dot_last(ref[rows, lo : lo + width], w[ar_tile(i), col : col + width])
                    value = more if value is None else value + more
                total(a)[rows, ar_tile(i)] = value
                away = pl.ds(m16(first + OWN * p + oth0), PART)
                cs[a % 2, p, PART * n : PART * n + PART, ar_tile(i)] = total(a)[away, ar_tile(i)].astype(bf16)
            src, there = cs_ref(a, p, i)
            remote(src, there, cs_s.at[a, p], cs_r.at[a, p, i], mate).start()

    def ar_cross(a, p):
        b = a - 2
        near = pl.ds(m16(TOK * x + OWN * p + own0), PART)
        far = pl.ds(m16(TOK * (1 - x) + OWN * p + own0), PART)
        for i in range(2):
            _, here = cs_ref(a, p, i)
            came(here, cs_r.at[a, p, i])
            more = cr[a % 2, p, pl.ds(m16(PART * (1 - x)), PART), ar_tile(i)].astype(f32)
            ys[b, p, :, ar_tile(i)] = (total(a)[far, ar_tile(i)] + more).astype(bf16)
            remote(
                ys.at[b, p, :, ar_tile(i)], yr.at[b, p, :, ar_tile(i)], ys_s.at[0], ys_r.at[b, p, i], along["x"]
            ).start()
            total(a)[near, ar_tile(i)] = total(a)[near, ar_tile(i)] + cr[
                a % 2, p, pl.ds(m16(PART * x), PART), ar_tile(i)
            ].astype(f32)

    def fold_out():
        for p in (0, 1):
            left(xs.at[1, p], xs_s.at[1, p])
        for i in range(2):
            for p in (0, 1):
                came(yr.at[1, p, :, ar_tile(i)], ys_r.at[1, p, i])
            mine = part3[pl.ds(m16(TOK * x + OWN * (1 - l) + own0), PART), ar_tile(i)]
            xs[1, 0, :, ar_tile(i)] = (mine + yr[1, 1 - l, :, ar_tile(i)].astype(f32)).astype(bf16)
            remote(
                xs.at[1, 0, :, ar_tile(i)], xr.at[0, 0, :, ar_tile(i)], xs_s.at[3, 0], xs_r.at[3, 0], beside
            ).start()

    def ar_mid(a, p):
        if a == 3:
            return fold_out()
        b = a % 2
        if a >= 2:
            left(xs.at[b, p], xs_s.at[a - 2, p])
        for i in range(2):
            if a == 2:
                came(yr.at[0, p, :, ar_tile(i)], ys_r.at[0, p, i])
                mine = part[pl.ds(m16(TOK * x + OWN * p + own0), PART), ar_tile(i)]
                more = yr[0, p, :, ar_tile(i)]
            else:
                came(cs_ref(a, p, i)[1], cs_r.at[a, p, i])
                mine = part[pl.ds(m16(OWN * p + own0), PART), ar_tile(i)]
                more = cr[b, p, 0:PART, ar_tile(i)]
            xs[b, p, :, ar_tile(i)] = (mine + more.astype(f32)).astype(bf16)
            remote(
                xs.at[b, p, :, ar_tile(i)], xr.at[a % 3, p, :, ar_tile(i)], xs_s.at[a, p], xs_r.at[a, p], beside
            ).start()

    def ar_end(a, p):
        came(xr.at[a % 3, p], xs_r.at[a, p])

    def summed(a, p, rows):
        return xs[a % 2, p, rows, :].astype(f32) + xr[a % 3, p, rows, :].astype(f32)

    def own_rows(body):
        def step(j, carry):
            body(pl.multiple_of(32 * j, 32))
            return carry

        lax.fori_loop(0, PART // 32, step, 0)

    def at32(start):
        return pl.ds(m16(start), 32)

    def share(j, p, ref, first=0, to=None):
        rows = ref.at[pl.ds(m16(first + OWN * p + own0), PART)]
        remote(rows, rows, nx_s.at[0], nx_r.at[j, p], mate if to is None else to).start()

    def shared(j, p, ref, first=0, start=None):
        came(ref.at[pl.ds(m16(first + OWN * p + (oth0 if start is None else start)), PART)], nx_r.at[j, p])

    def rms(v):
        return lax.rsqrt(jnp.mean(v * v, axis=-1, keepdims=True) + 1e-06)

    def fold(v):
        return jnp.sum(v.reshape(v.shape[0] // 8, 8, v.shape[1]), axis=0)

    def tiles_loop(count, body):
        def step(i, carry):
            body(pl.ds(pl.multiple_of(TILE * i, TILE), TILE), i)
            return carry

        lax.fori_loop(0, count, step, 0)

    def slab(h):
        return slice(128 + 256 * h, 256 + 256 * h)

    spread = one_hot(lax.div(iota((OWN, 12), 0), CTXLEN) == iota((OWN, 12), 1))
    right_patch = lax.div(iota((OWN, 512), 1), PL) == (iota((OWN, 512), 0) & (CTXLEN - 1))
    lane_of = iota((512, 128), 1)
    place_of = iota((512, 128), 0) & (PL - 1)
    mine0 = m16(OWN * l + own0)
    cot_part = cot_in.reshape(2, PART, D)
    cot_rows = cot.reshape(2, TOK, D)
    cot_copy = pltpu.make_async_copy(cot_part, cot_rows.at[:, pl.ds(mine0, PART)], lo_s.at[len(CHUNKS)])
    lane512 = iota((OWN, 512), 1) & 255
    units = lane512 < 160
    resids = (lane512 >= 128 + L_RES) & (lane512 < 128 + L_RES + 8)

    def part_rows(p, first=0):
        return slice(first + OWN * p, first + OWN * p + OWN)

    def features():
        keep = 1.0 - missing[...].astype(f32)
        seen = dot_plain(spread, (points[...].astype(f32) * keep).astype(bf16))
        gone = dot_plain(spread, missing[...].astype(f32).astype(bf16))
        feats = dot_plain(jnp.where(right_patch, seen, 0.0).astype(bf16), one_hot(lane_of == place_of))
        feats = feats + dot_plain(jnp.where(right_patch, gone, 0.0).astype(bf16), one_hot(lane_of == place_of + PL))
        ptx[0:OWN, :] = jnp.where(iota((OWN, 128), 1) == 2 * PL, 1.0, feats)
        fe[pl.ds(mine0, PART), :] = ptx[pl.ds(m16(PART * x), PART), :].astype(bf16)
        for to, member in group:
            rows = fe.at[pl.ds(mine0, PART)]
            remote(rows, rows, tk_s.at[0], tk_r.at[0], to).start()
        sums[...] = jnp.zeros(sums.shape, f32)
        hidf[...] = jnp.zeros(hidf.shape, f32)

    def cot_out():
        cot_copy.start()
        dst = cot_rows.at[:, pl.ds(mine0, PART)]
        remote(cot_part, dst, tk_s.at[1], tk_r.at[1], mate).start()
        remote(cot_part.at[x], cot_rows.at[x, pl.ds(mine0, PART)], tk_s.at[1], tk_r.at[2], beside).start()

    def cot_pass(stage):
        here = pl.ds(m16(OWN * (1 - l) + own0), PART)
        near, far = cot_rows.at[x, here], cot_rows.at[1 - x, here]
        if stage == 0:
            came(near, tk_r.at[2])
            remote(near, near, tk_s.at[1], tk_r.at[3], along["x"]).start()
            remote(near, near, tk_s.at[1], tk_r.at[4], mate).start()
        else:
            came(far, tk_r.at[3])
            remote(far, far, tk_s.at[1], tk_r.at[5], mate).start()

    def cot_here():
        cot_copy.wait()
        came(cot_rows.at[:, pl.ds(m16(OWN * l + oth0), PART)], tk_r.at[1])
        for i, xx in ((4, x), (5, 1 - x)):
            came(cot_rows.at[xx, pl.ds(m16(OWN * (1 - l) + oth0), PART)], tk_r.at[i])

    def hidden():
        for h in (0, 1):
            for j in range(4):
                rows = pl.ds(m16(320 * m + 80 * j), 80)
                tmp[:, 0:128] = w[rows, slab(h)].astype(f32)
                hidf[0:72, 256 * h + 40 * j : 256 * h + 40 * j + 40] = tmp[0:72, L_HID : L_HID + 40]
            row = iota((128, 128), 0)
            lane = iota((128, 128), 1)
            chosen = (lane >= L_RES) & (lane < L_RES + 8) & (row == PL * h + 8 * m + lane - L_RES)
            hidf[:, slab(h)] = jnp.where(chosen, 1.0, hidf[:, slab(h)])
        hid[...] = hidf[...].astype(bf16)
        came(fe.at[0 : 3 * PART], tk_r.at[0])

    def tokenize(p):
        v = dot_plain(fe[part_rows(p), :], hid[...])
        pret[part_rows(p), :] = v
        hc[part_rows(p), :] = jnp.where(
            units, v * jax.nn.sigmoid(v), jnp.where(resids, v, jnp.where(lane512 == 128 + L_ONE, 1.0, 0.0))
        ).astype(bf16)

    def vectors():
        row16 = iota((16, 128), 0)
        lane16 = iota((16, 128), 1)
        vec[...] = dot_last(one_hot((row16 < 4) & (lane16 == L_VEC + row16)), w[:, slab(0)])
        own_slab = pl.ds(pl.multiple_of(128 + 256 * x, 128), 128)
        pair = dot_last(one_hot((row16 < 2) & (lane16 == L_BIN + row16)), w[pl.ds(m16(320 * m), 320), own_slab])
        tmp[0:16, 0:320] = pair
        for j in range(4):
            at = 160 * j
            bin_s[0:1, at : at + 80] = tmp[0:1, 80 * j : 80 * j + 80]
            bin_s[0:1, at + 80 : at + 160] = tmp[1:2, 80 * j : 80 * j + 80]

    def first_norm(p):
        ar_end(0, p)

        def body(start):
            v = summed(0, p, pl.ds(start, 32)) + vec[3:4, :]
            x0[at32(PART * p + start), :] = v
            n1[at32(OWN * p + own0 + start), :] = (v * rms(v) * vec[0:1, :]).astype(bf16)

        own_rows(body)
        share(0, p, n1)

    def project(p):
        shared(0, p, n1)
        rows = part_rows(p)
        for h in (0, 1):
            for lo in (0, 256):
                col = C_QKV + 640 * h + lo
                part[rows, 512 * h + lo : 512 * h + lo + 256] = dot_plain(n1[rows, :], w[:, col : col + 256])

    def turn(p):
        def body(j, carry):
            rows = pl.ds(m16(OWN * p + 48 * j), 48)
            for h in (0, 1):
                v = part[rows, 512 * h : 512 * h + 512]
                v = v * rot_c[...] + pltpu.roll(v, 472, 1) * rot_a[...] + pltpu.roll(v, 40, 1) * rot_b[...]
                q_s[h, rows, :] = v[:, 0:256].astype(bf16)
                k_s[h, rows, :] = pltpu.roll(v, 352, 1)[:, 0:256].astype(bf16)
                v_s[h, rows, :] = pltpu.roll(v, 288, 1)[:, 0:256].astype(bf16)
            return carry

        lax.fori_loop(0, OWN // 48, body, 0)

    def one_head(v, first, i):
        lane = iota(v.shape, 1)
        inside = (lane >= first + HEAD_DIM * i) & (lane < first + HEAD_DIM * i + HEAD_DIM)
        return jnp.where(inside, v, jnp.zeros_like(v))

    def stacked(v, first):
        return jnp.concatenate([one_head(v, first, 0), one_head(v, first, 1)], axis=0)

    def by_head(probs, v, first):
        return dot_plain(probs[0:OWN], one_head(v, first, 0)) + dot_plain(probs[OWN:TOK], one_head(v, first, 1))

    def attend(p):
        rows = part_rows(p)
        qi = iota((TOK, OWN), 0)
        qi = jnp.where(qi >= OWN, qi - OWN, qi)
        kj = iota((TOK, OWN), 1)
        allowed = ((qi >> 4) == (kj >> 4)) & (kj <= qi)
        for h in (0, 1):
            scores = dot_last(stacked(q_s[h, rows, :], 0), k_s[h, rows, :]) * SCALE
            scores = jnp.where(allowed, scores, -1e30)
            e = jnp.exp(scores - jnp.max(scores, axis=-1, keepdims=True))
            probs = e * (1.0 / jnp.sum(e, axis=-1, keepdims=True))
            ps[p, h] = probs
            att[rows, 256 * h : 256 * h + 256] = by_head(probs.astype(bf16), v_s[h, rows, :], 96).astype(bf16)

    def second_norm(p):
        ar_end(1, p)

        def body(start):
            own = at32(PART * p + start)
            v = x0[own, :] + summed(1, p, pl.ds(start, 32))
            x1[own, :] = v
            n2[at32(TOK * x + OWN * p + own0 + start), :] = (v * rms(v) * vec[1:2, :]).astype(bf16)

        own_rows(body)
        share(1, p, n2, TOK * x, along["x"])
        share(4, p, n2, TOK * x)

    def norm_pass(p):
        far = TOK * (1 - x)
        shared(1, p, n2, far, own0)
        rows = n2.at[pl.ds(m16(far + OWN * p + own0), PART)]
        remote(rows, rows, nx_s.at[0], nx_r.at[5, p], mate).start()

    def inner(which, p):
        first = TOK * (x if which == 0 else 1 - x)
        shared(4 if which == 0 else 5, p, n2, first)
        rows = pl.ds(m16(first + OWN * p), OWN)
        for lo, width in MLP_TILES:
            at = slice(lo, lo + width)
            v = dot_plain(n2[rows, :], w[:, C_IN + lo : C_IN + lo + width]) + bin_s[0:1, at]
            pre[rows, at] = v
            act[rows, at] = (v * jax.nn.sigmoid(v)).astype(bf16)

    def outer_back(p):
        for first in (0, TOK):
            rows = part_rows(p, first)
            for lo, width in MLP_TILES:
                at = slice(lo, lo + width)
                v = pre[rows, at]
                s = jax.nn.sigmoid(v)
                d = dot_plain(cot[rows, :], w[:, C_OUT + lo : C_OUT + lo + width])
                dpre[rows, at] = (d * (s * (1.0 + v * (1.0 - s)))).astype(bf16)

    def norm_back(dn, v, gain):
        r = rms(v)
        xh = v * r
        scaled = dn * gain
        inside = jnp.mean(scaled * xh, axis=-1, keepdims=True)
        return r * (scaled - xh * inside), fold(dn * xh)

    def second_back(p):
        ar_end(2, p)

        def body(start):
            own = at32(PART * p + start)
            d, by_gain = norm_back(summed(2, p, pl.ds(start, 32)), x1[own, :], vec[1:2, :])
            ct = cot[at32(TOK * x + OWN * p + own0 + start), :].astype(f32)
            d = ct + d
            x2[own, :] = d
            db[at32(OWN * p + own0 + start), :] = d.astype(bf16)
            sums[8:16, :] += by_gain
            sums[16:24, :] += fold(ct)

        own_rows(body)
        share(2, p, db)

    def attended_back(p):
        shared(2, p, db)
        rows = part_rows(p)
        for h in (0, 1):
            col = C_QKV + 640 * h + 384
            datt[rows, 256 * h : 256 * h + 256] = dot_plain(db[rows, :], w[:, col : col + 256]).astype(bf16)

    def attend_back(p):
        rows = part_rows(p)
        for h in (0, 1):
            probs = ps[p, h]
            heads_d = stacked(datt[rows, 256 * h : 256 * h + 256], 96)
            dp = dot_last(heads_d, v_s[h, rows, :])
            ds = (probs * (dp - jnp.sum(probs * dp, axis=-1, keepdims=True))).astype(bf16)
            part[rows, 512 * h : 512 * h + 256] = by_head(ds, k_s[h, rows, :], 0) * SCALE
            part[rows, 512 * h + 160 : 512 * h + 416] = dot_rows(ds, stacked(q_s[h, rows, :], 0)) * SCALE
            dv = dot_rows(probs.astype(bf16), heads_d)
            dv = jnp.concatenate([dv, jnp.zeros((OWN, 128), f32)], axis=1)
            part[rows, 512 * h + 320 : 512 * h + 512] = dv[:, 96:288]

    def turn_back(p):
        def body(j, carry):
            rows = pl.ds(m16(OWN * p + 48 * j), 48)
            for h in (0, 1):
                v = part[rows, 512 * h : 512 * h + 512]
                v = v * rot_c[...] - pltpu.roll(v, 472, 1) * rot_a[...] - pltpu.roll(v, 40, 1) * rot_b[...]
                dpj[rows, 512 * h : 512 * h + 512] = v.astype(bf16)
            return carry

        lax.fori_loop(0, OWN // 48, body, 0)

    def finish():
        ar_end(3, 0)

        def body(start):
            rows = pl.ds(start, 32)
            v = part3[at32(TOK * x + OWN * l + own0 + start), :] + yr[1, l, rows, :].astype(f32)
            v = v + xr[0, 0, rows, :].astype(f32)
            ob[rows, :] = (x1[at32(PART * l + start), :] + v + vec[2:3, :]).astype(bf16)

        own_rows(body)
        ref = out_o.at[pl.ds(m16(PART * x), PART)]
        go(remote(ob, ref, pt_s.at[3], pt_r.at[3], along["x"]))
        pltpu.make_async_copy(ob, ref, keep_s.at[1]).start()

    def grad_mlp(k, left, right, base):
        first, _, width, _ = CHUNKS[k]

        def body(rows, i):
            lo = first - base
            g[rows, first : first + width] = dot_rows(left[:, rows], right[:, lo : lo + width]).astype(bf16)

        tiles_loop(TILES, body)
        s_start(k)

    def grad_out(k):
        grad_mlp(k, cot, act, C_OUT)

    def grad_in(k):
        grad_mlp(k, n2, dpre, C_IN)

    def grad_qkv(k):
        first, apart, width, _ = CHUNKS[k]

        def body(rows, i):
            for h in (0, 1):
                for lo in range(first - C_QKV, first - C_QKV + width, 128):
                    value = None
                    if lo < 512:
                        value = dot_rows(n1[:, rows], dpj[:, 512 * h + lo : 512 * h + lo + 128])
                    if lo >= 384:
                        more = dot_rows(db[:, rows], att[:, 256 * h + lo - 384 : 256 * h + lo - 256])
                        value = more if value is None else value + more
                    col = C_QKV + apart * h + lo
                    g[rows, col : col + 128] = value.astype(bf16)

        tiles_loop(TILES, body)
        s_start(k)

    def grad_bias():
        ones = one_hot((iota((BOTH, 128), 1) >= L_BIN) & (iota((BOTH, 128), 1) < L_BIN + 2))
        for lo, width in MLP_TILES:
            gbs[lo : lo + width, :] = dot_rows(dpre[:, lo : lo + width], ones)

    def first_back(p):
        ar_end(4, p)

        def body(start):
            own = at32(PART * p + start)
            d, by_gain = norm_back(summed(4, p, pl.ds(start, 32)), x0[own, :], vec[0:1, :])
            de[at32(OWN * p + own0 + start), :] = (x2[own, :] + d).astype(bf16)
            sums[0:8, :] += by_gain

        own_rows(body)
        share(3, p, de)

    def hidden_back(p):
        shared(3, p, de)
        rows = part_rows(p)
        v = pret[rows, :]
        s = jax.nn.sigmoid(v)
        d = dot_plain(de[rows, :], w[:, 0:512])
        dpe[rows, :] = jnp.where(units, d * (s * (1.0 + v * (1.0 - s))), jnp.where(resids, d, 0.0)).astype(bf16)

    def grad_tok():
        row32 = iota((32, 128), 0)
        pick = one_hot((row32 < 24) & (iota((32, 128), 1) == L_VEC + (row32 >> 3)))

        def body(rows, i):
            both = dot_rows(de[:, rows], hc[...])
            columns = dot_rows(sums[:, rows].astype(bf16), pick)
            for h in (0, 1):
                g[rows, 256 * h : 256 * h + 128] = both[:, 256 * h : 256 * h + 128].astype(bf16)
                g[rows, slab(h)] = (both[:, slab(h)] + columns).astype(bf16)

        tiles_loop(TILES, body)
        s_start(0)

    def grad_hidden():
        ghs[...] = dot_rows(fe[...], dpe[...])
        lane = iota((80, 128), 1)
        for h in (0, 1):
            for j in range(4):
                at = 160 * j
                tmp[:, 0:128] = jnp.where((lane == L_BIN) & (x == h), gbs[at : at + 80, :], 0.0) + jnp.where(
                    (lane == L_BIN + 1) & (x == h), gbs[at + 80 : at + 160, :], 0.0
                )
                tmp[:, L_HID : L_HID + 40] = ghs[0:80, 256 * h + 40 * j : 256 * h + 40 * j + 40]
                rows = pl.ds(m16(320 * m + 80 * j), 80)
                g[rows, slab(h)] = (g[rows, slab(h)].astype(f32) + tmp[:, 0:128]).astype(bf16)
        s_start(1)

    def points_back(stage):
        if stage == 0:
            ptx[...] = dot_last(dpe[...], hid[...])
            away = ptx.reshape(2, OWN, 128).at[:, pl.ds(oth0, PART)]
            go(remote(away, ptr.at[0], pt_s.at[0], pt_r.at[0], mate))
        elif stage == 1:
            remote(ptr.at[0], ptr.at[0], pt_s.at[0], pt_r.at[0], mate).wait_recv()
            for p in (0, 1):
                ptr[1, p] = ptx[pl.ds(m16(OWN * p + own0), PART), :] + ptr[0, p]
            go(remote(ptr.at[1, 1 - l], ptr.at[2, 1 - l], pt_s.at[1], pt_r.at[1], beside))
        elif stage == 2:
            there = ptr.at[2, l]
            remote(there, there, pt_s.at[1], pt_r.at[1], beside).wait_recv()
            ptr[3, x] = ptr[1, l] + ptr[2, l]
            go(remote(ptr.at[3, x], ptr.at[3, x], pt_s.at[2], pt_r.at[2], along["x"]))
        else:
            there = ptr.at[3, 1 - x]
            remote(there, there, pt_s.at[2], pt_r.at[2], along["x"]).wait_recv()
            every = ptr[3].reshape(OWN, 128).astype(bf16)
            wide = dot_last(every, one_hot(lane_of == place_of))
            wide = jnp.where(right_patch, wide, 0.0).astype(bf16)
            pts_o[...] = dot_rows(spread, wide) * (1.0 - missing[...].astype(f32))

    operands = (
        ((hc, 0, 0, 512),),
        ((att, 0, 896, 256), (att, 256, 1536, 256)),
        ((dpre, 0, C_IN, 640),),
        ((act, 0, C_OUT, 640),),
        ((dpj, 0, 512, 512), (dpj, 512, 1152, 512)),
    )
    steps = (
        g_first, g_own, g_second, g_third, g_done, s_step, features, cot_out, cot_here, tokenize, vectors,
        first_norm, project, turn, attend, second_norm, inner, grad_out, outer_back, grad_in, second_back,
        attended_back, attend_back, turn_back, finish, grad_qkv, grad_bias, first_back, hidden_back, grad_tok,
        grad_hidden, points_back, ar_begin, ar_mid, cot_pass, norm_pass, ar_cross, hidden,
    )
    for name, *which in PLAN:
        steps[name](*which)

    came(out_o.at[pl.ds(m16(PART * (1 - x)), PART)], pt_r.at[3])
    came(fb.at[0:3], fin_r.at[0])
    pltpu.make_async_copy(g.at[0:HALF, 0:C_ONE], fb.at[m], keep_s.at[0]).wait()
    pltpu.make_async_copy(ob, out_o.at[pl.ds(m16(PART * x), PART)], keep_s.at[1]).wait()
    for ref, sem in (
        (rb, ag_s.at[0]), (rbm, ag_s.at[1]), (rb, rs_s.at[0]), (rbm, rs_s.at[1]),
        (w.at[0 : 3 * HALF, 0:C_ONE], in_s.at[0]), (g.at[0 : 3 * HALF, 0:C_ONE], fin_s.at[0]),
        (cs.at[1, 0], cs_s.at[3, 0]), (cs.at[1, 1], cs_s.at[3, 1]),
        (cs.at[0, 0, 0:PART], cs_s.at[4, 0]), (cs.at[0, 1, 0:PART], cs_s.at[4, 1]),
        (xs.at[1, 0], xs_s.at[3, 0]), (xs.at[0, 0], xs_s.at[4, 0]), (xs.at[0, 1], xs_s.at[4, 1]),
        (ys, ys_s.at[0]), (w.at[0 : 12 * PART, 0:D], nx_s.at[0]),
        (fe.at[0 : 3 * PART], tk_s.at[0]), (cot.at[0 : 6 * PART], tk_s.at[1]),
    ):
        left(ref, sem)
    for copy in sent:
        copy.wait_send()


def unpack_kernel(
    out_i, pts_i, fb_i,
    out_o, pts_o, hw_o, hb_o, tok_o, res_o, tokb_o, gain1_o, qkv_o, att_o, gain2_o, in_o, inb_o, outw_o, outb_o,
    fb, sem,
):
    f32 = jnp.float32
    copies = [pltpu.make_async_copy(fb_i.at[q], fb.at[q], sem.at[q]) for q in range(4)]
    copies.append(pltpu.make_async_copy(out_i, out_o, sem.at[4]))
    for copy in copies:
        copy.start()
    pts_o[...] = pts_i[...]
    turned = []
    hidden = jnp.zeros((8, 128), f32)
    for q in range(4):
        copies[q].wait()
        at = slice(160 * q, 160 * q + 160)
        lead = fb[q, :, 0:256].astype(f32)
        tok_o[:, at] = lead[:, 0:160]
        tile = lead[:, 128:256]
        hidden = hidden + tile[64:72]
        t = jnp.transpose(jnp.concatenate([tile, jnp.zeros((48, 128), f32)], axis=0))
        turned.append(t)
        res_o[8 * q : 8 * q + 8, :] = t[L_RES : L_RES + 8, 0:80]
        qkv = fb[q, :, 256:896].astype(f32)
        for j in range(3):
            qkv_o[j, :, at] = qkv[:, 160 * j : 160 * j + 160]
        att_o[:, at] = qkv[:, 480:640]
        in_o[:, 640 * q : 640 * q + 640] = fb[q, :, 896:1536].astype(f32)
        outw_o[:, 640 * q : 640 * q + 640] = fb[q, :, 1536:2176].astype(f32)
    both = turned[0] + turned[1]
    every = both + turned[2] + turned[3]
    tokb_o[...] = turned[0][L_ONE : L_ONE + 1, 0:80]
    gain1_o[...] = both[L_VEC : L_VEC + 1, 0:80]
    gain2_o[...] = both[L_VEC + 1 : L_VEC + 2, 0:80]
    outb_o[...] = both[L_VEC + 2 : L_VEC + 3, 0:80]
    inb_o[:, 0:80] = every[L_BIN : L_BIN + 1, 0:80]
    inb_o[:, 80:160] = every[L_BIN + 1 : L_BIN + 2, 0:80]
    hw_o[...] = every[L_HID : L_HID + 40, 0:64]
    hb_o[...] = hidden[0:1, L_HID : L_HID + 40]
    copies[4].wait()


def rotary_lanes():
    lanes = np.arange(512)
    inside = lanes % HEAD_DIM
    turned = lanes < 320
    freqs = 10000.0 ** (-2.0 * (inside % 40) / HEAD_DIM)
    angles = (np.arange(48) % CTXLEN)[:, None] * freqs[None, :]
    cosine = np.where(turned, np.cos(angles), 1.0)
    sine = np.where(turned, np.sin(angles), 0.0)
    lower = np.where(inside < 40, -sine, 0.0)
    upper = np.where(inside >= 40, sine, 0.0)
    return [np.asarray(t, np.float32) for t in (cosine, lower, upper)]


def fast_body(
    points, missing, tok_hidden_w, tok_hidden_b, tok_out_w, tok_res_w, tok_out_b, attn_gain, qkv_w, attn_out_w,
    mlp_gain, mlp_in_w, mlp_in_b, mlp_out_w, mlp_out_b, cotangent,
):
    f32, bf16 = jnp.float32, jnp.bfloat16
    any_space = pl.BlockSpec(memory_space=pl.ANY)
    vmem = pl.BlockSpec(memory_space=pltpu.VMEM)

    def sems(*shape):
        return pltpu.SemaphoreType.DMA(shape)

    def like(*shape):
        return jax.ShapeDtypeStruct(shape, f32)

    chunks = len(CHUNKS)
    wide = sum(1 for chunk in CHUNKS if chunk[3] < C_MLP)
    specs = [vmem] * 19
    specs[11] = specs[13] = specs[15] = any_space
    out, pts, packed = pl.pallas_call(
        layer_kernel,
        out_shape=(
            jax.ShapeDtypeStruct((OWN, D), bf16),
            like(12, 512),
            jax.ShapeDtypeStruct((4, HALF, C_ONE), bf16),
        ),
        in_specs=specs,
        out_specs=[any_space, vmem, any_space],
        scratch_shapes=[
            pltpu.VMEM((D, C_ALL), bf16),
            pltpu.VMEM((D, C_ALL), bf16),
            pltpu.VMEM((7, 2, 160, C_MLP), bf16),
            pltpu.VMEM((3, 2, 160, C_ONE - C_MLP), bf16),
            pltpu.VMEM((TOK, 128), bf16),
            pltpu.VMEM((BOTH, D), bf16),
            pltpu.VMEM((BOTH, D), f32),
            pltpu.VMEM((BOTH, 640), f32),
            pltpu.VMEM((BOTH, 640), bf16),
            pltpu.VMEM((BOTH, 640), bf16),
            pltpu.VMEM((TOK, D), bf16),
            pltpu.VMEM((BOTH, D), bf16),
            pltpu.VMEM((TOK, D), bf16),
            pltpu.VMEM((TOK, D), bf16),
            pltpu.VMEM((OWN, D), f32),
            pltpu.VMEM((OWN, D), f32),
            pltpu.VMEM((OWN, D), f32),
            pltpu.VMEM((TOK, 512), bf16),
            pltpu.VMEM((TOK, 512), bf16),
            pltpu.VMEM((TOK, 512), f32),
            pltpu.VMEM((2, TOK, 256), bf16),
            pltpu.VMEM((2, TOK, 256), bf16),
            pltpu.VMEM((2, TOK, 256), bf16),
            pltpu.VMEM((TOK, 512), bf16),
            pltpu.VMEM((TOK, 512), bf16),
            pltpu.VMEM((TOK, 1024), bf16),
            pltpu.VMEM((2, 2, TOK, OWN), f32),
            pltpu.VMEM((640, 128), f32),
            pltpu.VMEM((128, 512), f32),
            pltpu.VMEM((128, 512), f32),
            pltpu.VMEM((128, 512), bf16),
            pltpu.VMEM((16, D), f32),
            pltpu.VMEM((8, 640), f32),
            pltpu.VMEM((32, D), f32),
            pltpu.VMEM((TOK, 128), f32),
            pltpu.VMEM((4, 2, PART, 128), f32),
            pltpu.VMEM((4, HALF, 896), bf16),
            pltpu.VMEM((HALF, 896), f32),
            pltpu.VMEM((HALF, 128), f32),
            pltpu.VMEM((HALF, 384), f32),
            pltpu.VMEM((BOTH, D), f32),
            pltpu.VMEM((PART, D), bf16),
            pltpu.VMEM((2, 2, OWN, D), bf16),
            pltpu.VMEM((2, 2, OWN, D), bf16),
            pltpu.VMEM((2, 2, PART, D), bf16),
            pltpu.VMEM((2, 2, PART, D), bf16),
            pltpu.VMEM((2, 2, PART, D), bf16),
            pltpu.VMEM((3, 2, PART, D), bf16),
            sems(2), sems(4 * wide + 2 * (chunks - wide)), sems(2), sems(7 * wide + 3 * (chunks - wide)),
            sems(5, 2), sems(5, 2, 2), sems(5, 2), sems(5, 2), sems(1), sems(2, 2, 2),
            sems(1), sems(6, 2), sems(1), sems(chunks), sems(chunks + 1), sems(2), sems(6),
            sems(1), sems(1), sems(4), sems(4), sems(2),
        ],
        compiler_params=pltpu.CompilerParams(
            collective_id=0, has_side_effects=True, vmem_limit_bytes=64 * 1024 * 1024 - 512 * 1024
        ),
        cost_estimate=pl.CostEstimate(flops=13 * 10**9, bytes_accessed=10**7, transcendentals=10**6),
    )(
        points, missing, tok_hidden_w[0], tok_hidden_b, tok_out_w, tok_res_w.T, tok_out_b[None], attn_gain[None],
        qkv_w.transpose(1, 0, 2), attn_out_w, mlp_gain[None], mlp_in_w, mlp_in_b, mlp_out_w, mlp_out_b[None],
        cotangent, *[jnp.asarray(t) for t in rotary_lanes()],
    )
    (
        output, points_grad, hidden_w, hidden_b, tok, res_t, tok_b, gain1, qkv, att, gain2, inner, inner_b, outer,
        outer_b,
    ) = pl.pallas_call(
        unpack_kernel,
        out_shape=(
            jax.ShapeDtypeStruct((OWN, D), bf16),
            like(12, 512), like(40, 64), like(1, 40), like(HALF, 640), like(32, HALF), like(1, HALF), like(1, HALF),
            like(3, HALF, 640), like(HALF, 640), like(1, HALF), like(HALF, 2560), like(1, 160), like(HALF, 2560),
            like(1, HALF),
        ),
        in_specs=[any_space, vmem, any_space],
        out_specs=[any_space] + [vmem] * 14,
        scratch_shapes=[pltpu.VMEM((4, HALF, C_ONE), bf16), sems(5)],
        compiler_params=pltpu.CompilerParams(vmem_limit_bytes=32 * 1024 * 1024),
    )(out, pts, packed)
    return (
        output, points_grad, hidden_w[None], hidden_b, tok, res_t.T, tok_b[0], gain1[0], qkv.transpose(1, 0, 2), att,
        gain2[0], inner, inner_b, outer, outer_b[0],
    )


def solution(mesh):
    placed = (
        P("fsdp", None),
        P("fsdp", None),
        P("tp", "fsdp", None),
        P("tp", "fsdp"),
        P("fsdp", "tp"),
        P("fsdp", "tp"),
        P("fsdp"),
        P("fsdp"),
        P("fsdp", None, "tp"),
        P("fsdp", "tp"),
        P("fsdp"),
        P("fsdp", "tp"),
        P("tp", "fsdp"),
        P("fsdp", "tp"),
        P("fsdp"),
        P("fsdp", None),
    )
    small_slice = mesh.shape["fsdp"] == 16 and mesh.shape["tp"] == 2
    return jax.shard_map(
        fast_body if small_slice else body,
        mesh=mesh,
        in_specs=placed,
        out_specs=(
            P("fsdp", None),
            P("fsdp", None),
            P("tp", "fsdp", None),
            P("tp", "fsdp"),
            P("fsdp", "tp"),
            P("fsdp", "tp"),
            P("fsdp"),
            P("fsdp"),
            P("fsdp", None, "tp"),
            P("fsdp", "tp"),
            P("fsdp"),
            P("fsdp", "tp"),
            P("tp", "fsdp"),
            P("fsdp", "tp"),
            P("fsdp"),
        ),
        check_vma=False,
    )
```

```python
import math

import jax
import jax.numpy as jnp
import numpy as np
from jax import lax
from jax.experimental import pallas as pl
from jax.experimental.pallas import tpu as pltpu
from jax.sharding import PartitionSpec as P

D = 1280
HEAD_DIM = 80
PL = 32
CTXLEN = 16


def dot_plain(left, right):
    return jnp.dot(left, right, preferred_element_type=jnp.float32)


def dot_last(left, right):
    return lax.dot_general(
        left, right, (((1,), (1,)), ((), ())), preferred_element_type=jnp.float32
    )


def dot_rows(left, right):
    return lax.dot_general(
        left, right, (((0,), (0,)), ((), ())), preferred_element_type=jnp.float32
    )


def silu_slope(values):
    sigma = jax.nn.sigmoid(values)
    return sigma * (1.0 + values * (1.0 - sigma))


def rotary_tables():
    positions = jnp.arange(CTXLEN, dtype=jnp.float32)
    freqs = 10000.0 ** (-2.0 * jnp.arange(HEAD_DIM // 2, dtype=jnp.float32) / HEAD_DIM)
    angles = positions[:, None] * freqs[None, :]
    return (jnp.cos(angles)[None, :, None, :], jnp.sin(angles)[None, :, None, :])


def rotate(vector, cosine, sine):
    half = vector.shape[-1] // 2
    first = vector[..., :half]
    second = vector[..., half:]
    return jnp.concatenate(
        [first * cosine - second * sine, second * cosine + first * sine], axis=-1
    )


def rotate_back(vector, cosine, sine):
    half = vector.shape[-1] // 2
    first = vector[..., :half]
    second = vector[..., half:]
    return jnp.concatenate(
        [first * cosine + second * sine, second * cosine - first * sine], axis=-1
    )


def norm_stats(values):
    factor = lax.rsqrt(jnp.mean(values * values, axis=-1, keepdims=True) + 1e-06)
    return (factor, values * factor)


def norm_back(grad, normal, factor, gain):
    scaled = grad * gain
    inner = jnp.mean(scaled * normal, axis=-1, keepdims=True)
    return (factor * (scaled - normal * inner), jnp.sum(grad * normal, axis=0))


def body(
    points,
    missing,
    tok_hidden_w,
    tok_hidden_b,
    tok_out_w,
    tok_res_w,
    tok_out_b,
    attn_gain,
    qkv_w,
    attn_out_w,
    mlp_gain,
    mlp_in_w,
    mlp_in_b,
    mlp_out_w,
    mlp_out_b,
    cotangent,
):
    gathered = (
        lax.all_gather(tok_hidden_w, "fsdp", axis=1, tiled=True),
        lax.all_gather(tok_hidden_b, "fsdp", axis=1, tiled=True),
        lax.all_gather(tok_out_w, "fsdp", axis=0, tiled=True),
        lax.all_gather(tok_res_w, "fsdp", axis=0, tiled=True),
        lax.all_gather(tok_out_b, "fsdp", axis=0, tiled=True),
        lax.all_gather(attn_gain, "fsdp", axis=0, tiled=True),
        lax.all_gather(qkv_w, "fsdp", axis=0, tiled=True),
        lax.all_gather(attn_out_w, "fsdp", axis=0, tiled=True),
        lax.all_gather(mlp_gain, "fsdp", axis=0, tiled=True),
        lax.all_gather(mlp_in_w, "fsdp", axis=0, tiled=True),
        lax.all_gather(mlp_in_b, "fsdp", axis=1, tiled=True),
        lax.all_gather(mlp_out_w, "fsdp", axis=0, tiled=True),
        lax.all_gather(mlp_out_b, "fsdp", axis=0, tiled=True),
    )
    (
        hidden_full,
        hidden_bias,
        token_full,
        residual_full,
        token_bias,
        first_gain,
        project_full,
        attend_full,
        second_gain,
        inner_full,
        inner_bias,
        outer_full,
        outer_bias,
    ) = gathered
    contexts = points.shape[0]
    rows = contexts * CTXLEN
    tensor_rank = lax.axis_index("tp")
    kept_mask = (1 - missing).astype(jnp.float32).reshape(rows, PL)
    absent = missing.astype(jnp.float32).reshape(rows, PL)
    observed = points.astype(jnp.float32).reshape(rows, PL) * kept_mask
    features = jnp.concatenate([observed, absent], axis=1).astype(jnp.bfloat16)
    half_features = jnp.where(tensor_rank == 0, observed, absent).astype(jnp.bfloat16)
    hidden_matrix = hidden_full.reshape(-1, 2 * PL)
    pre_tok = dot_last(features, hidden_matrix) + hidden_bias.reshape(-1).astype(jnp.float32)
    hidden_tok = jax.nn.silu(pre_tok).astype(jnp.bfloat16)
    partial_tok = dot_last(hidden_tok, token_full) + dot_last(half_features, residual_full)
    embedded = lax.psum(partial_tok.astype(jnp.bfloat16), "tp").astype(jnp.float32)
    state_zero = embedded + token_bias.astype(jnp.float32)
    factor_one, normal_one = norm_stats(state_zero)
    normed_one = (normal_one * first_gain.astype(jnp.float32)).astype(jnp.bfloat16)
    local_width = project_full.shape[2]
    local_heads = local_width // HEAD_DIM
    project_matrix = project_full.reshape(D, 3 * local_width)
    projected = dot_plain(normed_one, project_matrix).reshape(
        contexts, CTXLEN, 3, local_heads, HEAD_DIM
    )
    cosine, sine = rotary_tables()
    queries = rotate(projected[:, :, 0], cosine, sine).astype(jnp.bfloat16)
    keys_rot = rotate(projected[:, :, 1], cosine, sine).astype(jnp.bfloat16)
    values_b = projected[:, :, 2].astype(jnp.bfloat16)
    scale = 1.0 / math.sqrt(HEAD_DIM)
    causal = jnp.arange(CTXLEN)[:, None] >= jnp.arange(CTXLEN)[None, :]

    def scores_of(left, right):
        raw = jnp.einsum("cihd,cjhd->chij", left, right, preferred_element_type=jnp.float32) * scale
        return jnp.where(causal, raw, -1e30)

    scores = scores_of(queries, keys_rot)
    row_top = jnp.max(scores, axis=-1, keepdims=True)
    log_total = row_top + jnp.log(jnp.sum(jnp.exp(scores - row_top), axis=-1, keepdims=True))
    probs_b = jnp.exp(scores - log_total).astype(jnp.bfloat16)
    attended = jnp.einsum("chij,cjhd->cihd", probs_b, values_b, preferred_element_type=jnp.float32)
    attended = attended.astype(jnp.bfloat16).reshape(rows, local_width)
    branch_attn = lax.psum(dot_last(attended, attend_full).astype(jnp.bfloat16), "tp").astype(
        jnp.float32
    )
    state_one = state_zero + branch_attn
    factor_two, normal_two = norm_stats(state_one)
    normed_two = (normal_two * second_gain.astype(jnp.float32)).astype(jnp.bfloat16)
    pre_mlp = dot_plain(normed_two, inner_full) + inner_bias.reshape(-1).astype(jnp.float32)
    activation = jax.nn.silu(pre_mlp).astype(jnp.bfloat16)
    branch_mlp = lax.psum(dot_last(activation, outer_full).astype(jnp.bfloat16), "tp").astype(
        jnp.float32
    )
    output = (state_one + branch_mlp + outer_bias.astype(jnp.float32)).astype(jnp.bfloat16)
    again = (
        lax.all_gather(tok_hidden_w, "fsdp", axis=1, tiled=True),
        lax.all_gather(tok_hidden_b, "fsdp", axis=1, tiled=True),
        lax.all_gather(tok_out_w, "fsdp", axis=0, tiled=True),
        lax.all_gather(tok_res_w, "fsdp", axis=0, tiled=True),
        lax.all_gather(tok_out_b, "fsdp", axis=0, tiled=True),
        lax.all_gather(attn_gain, "fsdp", axis=0, tiled=True),
        lax.all_gather(qkv_w, "fsdp", axis=0, tiled=True),
        lax.all_gather(attn_out_w, "fsdp", axis=0, tiled=True),
        lax.all_gather(mlp_gain, "fsdp", axis=0, tiled=True),
        lax.all_gather(mlp_in_w, "fsdp", axis=0, tiled=True),
        lax.all_gather(mlp_in_b, "fsdp", axis=1, tiled=True),
        lax.all_gather(mlp_out_w, "fsdp", axis=0, tiled=True),
        lax.all_gather(mlp_out_b, "fsdp", axis=0, tiled=True),
    )
    (
        hidden_full,
        hidden_bias,
        token_full,
        residual_full,
        token_bias,
        first_gain,
        project_full,
        attend_full,
        second_gain,
        inner_full,
        inner_bias,
        outer_full,
        outer_bias,
    ) = again
    hidden_matrix = hidden_full.reshape(-1, 2 * PL)
    project_matrix = project_full.reshape(D, 3 * local_width)
    grad_outer_bias = jnp.sum(cotangent, axis=0, dtype=jnp.float32)
    grad_outer = dot_rows(cotangent, activation)
    d_pre = (dot_plain(cotangent, outer_full) * silu_slope(pre_mlp)).astype(jnp.bfloat16)
    grad_inner_bias = jnp.sum(d_pre, axis=0, dtype=jnp.float32).reshape(1, -1)
    grad_inner = dot_rows(normed_two, d_pre)
    d_normed_two = lax.psum(dot_last(d_pre, inner_full).astype(jnp.bfloat16), "tp").astype(
        jnp.float32
    )
    through_two, grad_second_gain = norm_back(
        d_normed_two, normal_two, factor_two, second_gain.astype(jnp.float32)
    )
    d_state_one = cotangent.astype(jnp.float32) + through_two
    d_branch = d_state_one.astype(jnp.bfloat16)
    grad_attend = dot_rows(d_branch, attended)
    d_attended = (
        dot_plain(d_branch, attend_full)
        .astype(jnp.bfloat16)
        .reshape(contexts, CTXLEN, local_heads, HEAD_DIM)
    )
    probs = jnp.exp(scores_of(queries, keys_rot) - log_total)
    probs_b = probs.astype(jnp.bfloat16)
    d_probs = jnp.einsum(
        "cihd,cjhd->chij", d_attended, values_b, preferred_element_type=jnp.float32
    )
    d_values = jnp.einsum(
        "chij,cihd->cjhd", probs_b, d_attended, preferred_element_type=jnp.float32
    ).astype(jnp.bfloat16)
    row_inner = jnp.sum(probs * d_probs, axis=-1, keepdims=True)
    d_scores = (probs * (d_probs - row_inner)).astype(jnp.bfloat16)
    d_queries = (
        jnp.einsum("chij,cjhd->cihd", d_scores, keys_rot, preferred_element_type=jnp.float32)
        * scale
    )
    d_keys = (
        jnp.einsum("chij,cihd->cjhd", d_scores, queries, preferred_element_type=jnp.float32) * scale
    )
    d_queries = rotate_back(d_queries, cosine, sine).astype(jnp.bfloat16)
    d_keys = rotate_back(d_keys, cosine, sine).astype(jnp.bfloat16)
    d_projected = jnp.stack([d_queries, d_keys, d_values], axis=2).reshape(rows, 3 * local_width)
    grad_project = dot_rows(normed_one, d_projected).reshape(D, 3, local_width)
    d_normed_one = lax.psum(
        dot_last(d_projected, project_matrix).astype(jnp.bfloat16), "tp"
    ).astype(jnp.float32)
    through_one, grad_first_gain = norm_back(
        d_normed_one, normal_one, factor_one, first_gain.astype(jnp.float32)
    )
    d_state_zero = d_state_one + through_one
    grad_token_bias = jnp.sum(d_state_zero, axis=0)
    d_embedded = d_state_zero.astype(jnp.bfloat16)
    grad_token = dot_rows(d_embedded, hidden_tok)
    grad_residual = dot_rows(d_embedded, half_features)
    d_pre_tok = (dot_plain(d_embedded, token_full) * silu_slope(pre_tok)).astype(jnp.bfloat16)
    grad_hidden_bias = jnp.sum(d_pre_tok, axis=0, dtype=jnp.float32).reshape(1, -1)
    grad_hidden = dot_rows(d_pre_tok, features).reshape(1, -1, 2 * PL)
    through_hidden = dot_plain(d_pre_tok, hidden_matrix)[:, :PL]
    through_residual = dot_plain(d_embedded, residual_full)
    point_terms = through_hidden + jnp.where(tensor_rank == 0, through_residual, 0.0)
    point_sums = lax.psum(point_terms, "tp")
    points_grad = (point_sums * kept_mask).reshape(contexts, CTXLEN * PL)
    owned = (
        lax.psum_scatter(grad_hidden, "fsdp", scatter_dimension=1, tiled=True),
        lax.psum_scatter(grad_hidden_bias, "fsdp", scatter_dimension=1, tiled=True),
        lax.psum_scatter(grad_token, "fsdp", scatter_dimension=0, tiled=True),
        lax.psum_scatter(grad_residual, "fsdp", scatter_dimension=0, tiled=True),
        lax.psum_scatter(grad_token_bias, "fsdp", scatter_dimension=0, tiled=True),
        lax.psum_scatter(grad_first_gain, "fsdp", scatter_dimension=0, tiled=True),
        lax.psum_scatter(grad_project, "fsdp", scatter_dimension=0, tiled=True),
        lax.psum_scatter(grad_attend, "fsdp", scatter_dimension=0, tiled=True),
        lax.psum_scatter(grad_second_gain, "fsdp", scatter_dimension=0, tiled=True),
        lax.psum_scatter(grad_inner, "fsdp", scatter_dimension=0, tiled=True),
        lax.psum_scatter(grad_inner_bias, "fsdp", scatter_dimension=1, tiled=True),
        lax.psum_scatter(grad_outer, "fsdp", scatter_dimension=0, tiled=True),
        lax.psum_scatter(grad_outer_bias, "fsdp", scatter_dimension=0, tiled=True),
    )
    return (
        output,
        points_grad,
        owned[0],
        owned[1],
        owned[2],
        owned[3],
        owned[4],
        owned[5],
        owned[6],
        owned[7],
        owned[8],
        owned[9],
        owned[10],
        owned[11],
        owned[12],
    )


MESH = pl.DeviceIdType.MESH
TOK = 384
OWN = 192
PART = 96
HALF = 80
C_QKV, C_IN, C_OUT, C_ALL, C_ONE = 512, 1792, 2432, 3072, 2176
C_MLP = 896
BOTH = 2 * TOK
MLP_TILES = ((0, 256), (256, 256), (512, 128))
SPLIT = 640
CHUNKS = (
    (0, 256, 128, 0),
    (128, 256, 128, 128),
    (512, 640, 256, 256),
    (768, 640, 256, 512),
    (1024, 640, 128, 768),
    (1792, 0, 256, 896),
    (2048, 0, 384, 1152),
    (2432, 0, 256, 1536),
    (2688, 0, 256, 1792),
    (2944, 0, 128, 2048),
)
GATHER_ORDER = ("zxy", "zyx", "zyx", "zyx", "zxy", "zy", "zy", "zy", "zy", "zy")
SUM_ORDER = ("xyz", "xyz", "yxz", "xyz", "xyz", "yz", "yz", "yz", "yz", "yz")
(
    FIRST, OWNED, SECOND, THIRD, HERE, SUM, FEATS, COT, COT_HERE, TOKENS, VECTORS, NORM_1, PROJECT, TURN, ATTEND,
    NORM_2, INNER, GRAD_OUT, OUTER, GRAD_IN, BACK_2, D_ATT, ATTEND_B, TURN_B, FINISH, GRAD_QKV, GRAD_BIAS, BACK_1,
    D_HID, GRAD_TOK, GRAD_HID, POINTS, SEND, PASS, COT_PASS, NORM_PASS, CROSS, HIDDEN,
) = range(38)
PLAN = (
    (FIRST, 0), (FIRST, 1), (FIRST, 4), (FIRST, 9), (FIRST, 3), (OWNED, 0), (OWNED, 1), (FIRST, 8), (OWNED, 4),
    (FIRST, 2), (FEATS,), (FIRST, 7), (FIRST, 5), (OWNED, 9), (OWNED, 3), (SECOND, 0), (FIRST, 6), (SECOND, 1),
    (THIRD, 0), (THIRD, 1), (OWNED, 2), (OWNED, 7), (HERE, 1), (HERE, 0), (HIDDEN,), (TOKENS, 1), (SEND, 0, 1),
    (SECOND, 4), (TOKENS, 0), (PASS, 0, 1), (SECOND, 3), (SEND, 0, 0), (OWNED, 5), (THIRD, 3), (PASS, 0, 0),
    (SECOND, 2), (OWNED, 6), (COT,), (THIRD, 2), (VECTORS,), (HERE, 3), (NORM_1, 1), (THIRD, 4), (NORM_1, 0),
    (HERE, 4), (HERE, 2), (PROJECT, 1), (SECOND, 5), (OWNED, 8), (PROJECT, 0), (TURN, 1), (SECOND, 7), (ATTEND, 1),
    (SEND, 1, 1), (PASS, 1, 1), (TURN, 0), (ATTEND, 0), (SEND, 1, 0), (COT_PASS, 0), (PASS, 1, 0), (SECOND, 6),
    (SECOND, 8), (NORM_2, 1), (SECOND, 9), (COT_PASS, 1), (NORM_2, 0), (HERE, 6), (COT_HERE,), (HERE, 7),
    (NORM_PASS, 1), (HERE, 5), (INNER, 0, 0), (HERE, 9), (HERE, 8), (INNER, 0, 1), (INNER, 1, 1), (OUTER, 1),
    (SEND, 2, 1), (NORM_PASS, 0), (CROSS, 2, 1), (INNER, 1, 0), (GRAD_OUT, 9), (OUTER, 0), (GRAD_IN, 6), (SEND, 2, 0),
    (PASS, 2, 1), (SUM, 9), (CROSS, 2, 0), (SEND, 3, 1), (SEND, 3, 0), (GRAD_OUT, 7), (GRAD_OUT, 8), (PASS, 2, 0),
    (BACK_2, 1), (SUM, 6), (CROSS, 3, 0), (CROSS, 3, 1), (D_ATT, 1), (ATTEND_B, 1), (TURN_B, 1), (SEND, 4, 1),
    (SUM, 7), (PASS, 4, 1), (BACK_2, 0), (GRAD_IN, 5), (D_ATT, 0), (GRAD_QKV, 4), (ATTEND_B, 0), (TURN_B, 0),
    (SEND, 4, 0), (GRAD_BIAS,), (PASS, 4, 0), (GRAD_QKV, 3), (SUM, 4), (SUM, 5), (GRAD_QKV, 2), (BACK_1, 1), (SUM, 5),
    (SUM, 8), (PASS, 3, 0), (BACK_1, 0), (SUM, 6), (SUM, 4), (D_HID, 0), (D_HID, 1), (SUM, 6), (SUM, 3), (SUM, 2),
    (SUM, 4), (SUM, 8), (GRAD_TOK,), (SUM, 2), (SUM, 9), (SUM, 8), (GRAD_HID,), (SUM, 7), (SUM, 7), (SUM, 2),
    (SUM, 3), (SUM, 4), (SUM, 0), (POINTS, 0), (FINISH,), (SUM, 3), (POINTS, 1), (SUM, 0), (SUM, 2), (SUM, 1),
    (SUM, 1), (SUM, 3), (SUM, 0), (SUM, 0), (SUM, 5), (SUM, 1), (POINTS, 2), (SUM, 1), (SUM, 9), (POINTS, 3),
)
L_RES, L_ONE, L_VEC, L_BIN, L_HID = 32, 40, 41, 45, 47
TILE = 256
TILES = D // TILE
SCALE = 1.0 / math.sqrt(HEAD_DIM)


def iota(shape, dim):
    return lax.broadcasted_iota(jnp.int32, shape, dim)


def one_hot(cond):
    return jnp.where(cond, 1.0, 0.0).astype(jnp.bfloat16)


def layer_kernel(
    points, missing, hid_w, hid_b, tok_in, res_t, tok_b, gain1, qkv_in, att_in, gain2, win_in, b_in, wout_in,
    out_b, cot_in, rot_c, rot_a, rot_b,
    out_o, pts_o, fb,
    w, g, rb, rbm, fe, cot, part, pre, act, dpre, n1, n2, db, de, x0, x1, x2,
    hc, dpe, pret, q_s, k_s, v_s, att, datt, dpj, ps, gbs, ghs, hidf, hid, vec, bin_s, sums, ptx, ptr,
    pk, pkf, srcf, tmp,
    part3, ob, pts_v, cs, cr, ys, yr, xs, xr,
    ag_s, ag_r, rs_s, rs_r, cs_s, cs_r, xs_s, xs_r, ys_s, ys_r, nx_s, nx_r, in_s, in_r, lo_s, tk_s, tk_r,
    fin_s, fin_r, pt_s, pt_r, keep_s,
):
    f32, bf16 = jnp.float32, jnp.bfloat16
    f = lax.axis_index("fsdp")
    x = lax.axis_index("tp")
    z = lax.div(f, 4)
    zh = lax.div(z, 2)
    l = z - 2 * zh
    y = lax.div(f, 2) - 2 * z
    c = f - 4 * z - 2 * y
    m = 2 * l + c
    mate = {"fsdp": f + 1 - 2 * c}
    beside = {"fsdp": f + 4 - 8 * l}
    corner = {"fsdp": f + 4 - 8 * l + 1 - 2 * c}
    along = {"z": {"fsdp": f + 8 - 16 * zh}, "y": {"fsdp": f + 2 - 4 * y}, "x": {"tp": 1 - x}}
    own0 = pl.multiple_of(PART * c, PART)
    oth0 = pl.multiple_of(PART * (1 - c), PART)

    def m16(v):
        return pl.multiple_of(v, 16)

    def remote(src, dst, s_sem, r_sem, to):
        return pltpu.make_async_remote_copy(
            src_ref=src, dst_ref=dst, send_sem=s_sem, recv_sem=r_sem, device_id=to, device_id_type=MESH
        )

    sent = []

    def go(copy):
        copy.start()
        sent.append(copy)

    def came(ref, sem):
        remote(ref, ref, sem, sem, mate).wait_recv()

    def left(ref, sem):
        remote(ref, ref, sem, sem, mate).wait_send()

    barrier = pltpu.get_barrier_semaphore()
    peers = (mate, beside, corner, along["z"], along["y"], along["x"])
    for to in peers:
        pl.semaphore_signal(barrier, inc=1, device_id=to, device_id_type=MESH)

    part[0:80, 0:640] = tok_in[...].astype(f32)
    part[80:160, 0:640] = att_in[...].astype(f32)
    part[160:240, 0:640] = qkv_in[0].astype(f32)
    part[240:320, 0:640] = qkv_in[1].astype(f32)
    part[0:80, 640:1280] = qkv_in[2].astype(f32)
    srcf[...] = jnp.zeros(srcf.shape, f32)
    srcf[0:32, 0:80] = res_t[...].astype(f32)
    for i, v in enumerate((gain1, gain2, out_b, tok_b)):
        srcf[32 + i : 33 + i, 0:80] = v[...].astype(f32)
    tmp[0:1, 0:160] = b_in[...].astype(f32)
    srcf[36:37, 0:80] = tmp[0:1, 0:80]
    srcf[37:38, 0:80] = tmp[0:1, 80:160]
    srcf[40:80, 0:64] = hid_w[...].astype(f32)
    src = srcf[...].astype(bf16)
    row = iota((80, 128), 0)
    lane = iota((80, 128), 1)
    for q in range(4):
        col = 160 * q
        pkf[:, 0:160] = part[0:80, col : col + 160]
        pkf[:, 160:256] = jnp.zeros((80, 96), f32)
        place = (row < 32) & (row >= 8 * q) & (row < 8 * q + 8) & (lane == L_RES + row - 8 * q)
        place = place | ((row >= 32) & (row < 38) & (lane == L_VEC + row - 32))
        place = place | ((row >= 40) & (lane == L_HID + row - 40))
        pkf[:, 128:256] = pkf[:, 128:256] + dot_rows(src, one_hot(place))[0:80]
        pkf[64:65, 128 + L_HID : 128 + L_HID + 40] = hid_b[...].astype(f32)
        pkf[:, 256:416] = part[160:240, col : col + 160]
        pkf[:, 416:576] = part[240:320, col : col + 160]
        pkf[:, 576:736] = part[0:80, 640 + col : 800 + col]
        pkf[:, 736:896] = part[80:160, col : col + 160]
        pk[q] = pkf[...].astype(bf16)

    pl.semaphore_wait(barrier, len(peers))

    def cols(k, h):
        first, apart, width, _ = CHUNKS[k]
        return pl.ds(pl.multiple_of(first + apart * h, 128), width)

    def piece(k, member):
        first, _, width, at = CHUNKS[k]
        if at < 896:
            return pk.at[member, :, at : at + width]
        src, base = (win_in, 896) if at < 1536 else (wout_in, 1536)
        return src.at[:, pl.ds(pl.multiple_of(640 * member + at - base, 128), width)]

    group = ((mate, 2 * l + 1 - c), (beside, 2 - 2 * l + c), (corner, 3 - 2 * l - c))
    home = w.at[pl.ds(m16(HALF * f), HALF)]
    locals_in = {}

    def rows_of(to):
        return pl.ds(m16(HALF * to["fsdp"]), HALF)

    def g_first(k):
        dst = w.at[pl.ds(m16(HALF * f), HALF), cols(k, x)]
        for to, member in group:
            remote(piece(k, member), dst, in_s.at[0], in_r.at[k], to).start()
        locals_in[k] = pltpu.make_async_copy(piece(k, m), dst, lo_s.at[k])
        locals_in[k].start()

    w4 = w.reshape(4, 2, 160, C_ALL)
    g4 = g.reshape(4, 2, 160, C_ALL)

    def block(ref, k, flips):
        zz = 1 - zh if "z" in flips else zh
        yy = 1 - y if "y" in flips else y
        h = 1 - x if "x" in flips else x
        return ref.at[pl.ds(2 * zz, 2), yy, :, cols(k, h)]

    wide = sum(1 for chunk in CHUNKS if chunk[3] < C_MLP)

    def g_sem(k, i):
        return ag_r.at[4 * k + min(i, 3) if k < wide else 4 * wide + 2 * (k - wide) + min(i, 1)]

    def g_send(k, i, flips, axis):
        ref = block(w4, k, flips)
        remote(ref, ref, ag_s.at[0 if k < wide else 1], g_sem(k, i), along[axis]).start()

    def g_recv(k, i, flips):
        came(block(w4, k, flips), g_sem(k, i))

    def g_own(k):
        order = GATHER_ORDER[k]
        locals_in[k].wait()
        came(w.at[0 : 3 * HALF, 0 : CHUNKS[k][2]], in_r.at[k])
        for axis, i in zip(order, (0, 1, 3)):
            g_send(k, i, "", axis)

    def g_second(k):
        a, *rest = GATHER_ORDER[k]
        g_recv(k, 0, a)
        for axis, i in zip(rest, (2, 4)):
            g_send(k, i, a, axis)

    def g_third(k):
        a, b, d = GATHER_ORDER[k]
        g_recv(k, 1, b)
        g_send(k, 5, b, d)
        g_recv(k, 2, a + b)
        g_send(k, 6, a + b, d)

    def g_done(k):
        _, _, width, at = CHUNKS[k]
        if k < wide:
            came(rb.at[0:4, :, :, at : at + width], g_sem(k, 3))
        else:
            came(rbm.at[0:2, :, :, at - C_MLP : at - C_MLP + width], g_sem(k, 1))

    def s_buf(k, i):
        _, _, width, at = CHUNKS[k]
        return rb.at[i, :, :, at : at + width] if at < C_MLP else rbm.at[i, :, :, at - C_MLP : at - C_MLP + width]

    def s_sem(k, i):
        return rs_r.at[7 * k + i if k < wide else 7 * wide + 3 * (k - wide) + i]

    def s_send(k, i, flips, axis):
        remote(block(g4, k, flips), s_buf(k, i), rs_s.at[0 if k < wide else 1], s_sem(k, i), along[axis]).start()

    def s_add(k, i, flips, axis):
        came(s_buf(k, i), s_sem(k, i))
        _, _, width, at = CHUNKS[k]
        zz = 1 - zh if "z" in flips else zh
        yy = 1 - y if "y" in flips else y
        there = cols(k, 1 - x if "x" in flips else x)

        def step(j, carry):
            half = lax.div(j, 2)
            inside = 80 * (j - 2 * half)
            here = pl.ds(m16(640 * zz + 320 * half + 160 * yy + inside), 80)
            rows = pl.ds(m16(inside), 80)
            if at < C_MLP:
                more = rb[i, half, rows, at : at + width]
            else:
                more = rbm[i, half, rows, at - C_MLP : at - C_MLP + width]
            g[here, there] = g[here, there] + more
            return carry

        lax.fori_loop(0, 4, step, 0)

    def s_start(k):
        a, b, *last = SUM_ORDER[k]
        if last:
            d = last[0]
            s_send(k, 0, a + b + d, a)
            s_send(k, 1, a + b, a)
            s_send(k, 2, a + d, a)
            s_send(k, 3, a, a)
        else:
            s_send(k, 0, a + b, a)
            s_send(k, 1, a, a)
        s_at[k] = 0

    def s_step(k):
        a, b, *last = SUM_ORDER[k]
        stage = s_at[k]
        s_at[k] = stage + 1
        if not last:
            if stage == 0:
                s_add(k, 0, b, a)
                s_send(k, 2, b, b)
            elif stage == 1:
                s_add(k, 1, "", a)
            else:
                s_add(k, 2, "", b)
                s_out(k)
            return
        d = last[0]
        if stage == 0:
            s_add(k, 0, b + d, a)
            s_send(k, 4, b + d, b)
            s_add(k, 1, b, a)
            s_send(k, 5, b, b)
        elif stage == 1:
            s_add(k, 2, d, a)
            s_add(k, 4, d, b)
            s_send(k, 6, d, d)
        elif stage == 2:
            s_add(k, 3, "", a)
            s_add(k, 5, "", b)
        else:
            s_add(k, 6, "", d)
            s_out(k)

    def s_out(k):
        _, _, width, at = CHUNKS[k]
        dst = fb.at[m, :, at : at + width]
        for to, member in group:
            remote(g.at[rows_of(to), cols(k, x)], dst, fin_s.at[0], fin_r.at[0], to).start()
        pltpu.make_async_copy(g.at[pl.ds(m16(HALF * f), HALF), cols(k, x)], dst, keep_s.at[0]).start()

    s_at = {}

    def ar_tile(i):
        return slice(SPLIT * i, SPLIT * i + SPLIT)

    def cs_ref(a, p, i):
        rows = OWN if a in (2, 3) else PART
        return cs.at[a % 2, p, 0:rows, ar_tile(i)], cr.at[a % 2, p, 0:rows, ar_tile(i)]

    def total(a):
        return part3 if a == 3 else part

    def ar_begin(a, p):
        if a >= 2:
            left(cs.at[a % 2, p, 0 : OWN if a == 4 else PART, :], cs_s.at[a - 2, p])
        for i in range(2):
            for n, first in enumerate((0, TOK) if a in (2, 3) else (0,)):
                rows = slice(first + OWN * p, first + OWN * p + OWN)
                value = None
                for ref, lo, col, width in operands[a]:
                    more = dot_last(ref[rows, lo : lo + width], w[ar_tile(i), col : col + width])
                    value = more if value is None else value + more
                total(a)[rows, ar_tile(i)] = value
                away = pl.ds(m16(first + OWN * p + oth0), PART)
                cs[a % 2, p, PART * n : PART * n + PART, ar_tile(i)] = total(a)[away, ar_tile(i)].astype(bf16)
            src, there = cs_ref(a, p, i)
            remote(src, there, cs_s.at[a, p], cs_r.at[a, p, i], mate).start()

    def ar_cross(a, p):
        b = a - 2
        near = pl.ds(m16(TOK * x + OWN * p + own0), PART)
        far = pl.ds(m16(TOK * (1 - x) + OWN * p + own0), PART)
        for i in range(2):
            _, here = cs_ref(a, p, i)
            came(here, cs_r.at[a, p, i])
            more = cr[a % 2, p, pl.ds(m16(PART * (1 - x)), PART), ar_tile(i)].astype(f32)
            ys[b, p, :, ar_tile(i)] = (total(a)[far, ar_tile(i)] + more).astype(bf16)
            remote(
                ys.at[b, p, :, ar_tile(i)], yr.at[b, p, :, ar_tile(i)], ys_s.at[0], ys_r.at[b, p, i], along["x"]
            ).start()
            total(a)[near, ar_tile(i)] = total(a)[near, ar_tile(i)] + cr[
                a % 2, p, pl.ds(m16(PART * x), PART), ar_tile(i)
            ].astype(f32)

    def fold_out():
        for p in (0, 1):
            left(xs.at[1, p], xs_s.at[1, p])
        for i in range(2):
            for p in (0, 1):
                came(yr.at[1, p, :, ar_tile(i)], ys_r.at[1, p, i])
            mine = part3[pl.ds(m16(TOK * x + OWN * (1 - l) + own0), PART), ar_tile(i)]
            xs[1, 0, :, ar_tile(i)] = (mine + yr[1, 1 - l, :, ar_tile(i)].astype(f32)).astype(bf16)
            remote(
                xs.at[1, 0, :, ar_tile(i)], xr.at[0, 0, :, ar_tile(i)], xs_s.at[3, 0], xs_r.at[3, 0], beside
            ).start()

    def ar_mid(a, p):
        if a == 3:
            return fold_out()
        b = a % 2
        if a >= 2:
            left(xs.at[b, p], xs_s.at[a - 2, p])
        for i in range(2):
            if a == 2:
                came(yr.at[0, p, :, ar_tile(i)], ys_r.at[0, p, i])
                mine = part[pl.ds(m16(TOK * x + OWN * p + own0), PART), ar_tile(i)]
                more = yr[0, p, :, ar_tile(i)]
            else:
                came(cs_ref(a, p, i)[1], cs_r.at[a, p, i])
                mine = part[pl.ds(m16(OWN * p + own0), PART), ar_tile(i)]
                more = cr[b, p, 0:PART, ar_tile(i)]
            xs[b, p, :, ar_tile(i)] = (mine + more.astype(f32)).astype(bf16)
            remote(
                xs.at[b, p, :, ar_tile(i)], xr.at[a % 3, p, :, ar_tile(i)], xs_s.at[a, p], xs_r.at[a, p], beside
            ).start()

    def ar_end(a, p):
        came(xr.at[a % 3, p], xs_r.at[a, p])

    def summed(a, p, rows):
        return xs[a % 2, p, rows, :].astype(f32) + xr[a % 3, p, rows, :].astype(f32)

    def own_rows(body):
        def step(j, carry):
            body(pl.multiple_of(32 * j, 32))
            return carry

        lax.fori_loop(0, PART // 32, step, 0)

    def at32(start):
        return pl.ds(m16(start), 32)

    def share(j, p, ref, first=0, to=None):
        rows = ref.at[pl.ds(m16(first + OWN * p + own0), PART)]
        remote(rows, rows, nx_s.at[0], nx_r.at[j, p], mate if to is None else to).start()

    def shared(j, p, ref, first=0, start=None):
        came(ref.at[pl.ds(m16(first + OWN * p + (oth0 if start is None else start)), PART)], nx_r.at[j, p])

    def rms(v):
        return lax.rsqrt(jnp.mean(v * v, axis=-1, keepdims=True) + 1e-06)

    def fold(v):
        return jnp.sum(v.reshape(v.shape[0] // 8, 8, v.shape[1]), axis=0)

    def tiles_loop(count, body):
        def step(i, carry):
            body(pl.ds(pl.multiple_of(TILE * i, TILE), TILE), i)
            return carry

        lax.fori_loop(0, count, step, 0)

    def slab(h):
        return slice(128 + 256 * h, 256 + 256 * h)

    spread = one_hot(lax.div(iota((OWN, 12), 0), CTXLEN) == iota((OWN, 12), 1))
    right_patch = lax.div(iota((OWN, 512), 1), PL) == (iota((OWN, 512), 0) & (CTXLEN - 1))
    lane_of = iota((512, 128), 1)
    place_of = iota((512, 128), 0) & (PL - 1)
    mine0 = m16(OWN * l + own0)
    cot_part = cot_in.reshape(2, PART, D)
    cot_rows = cot.reshape(2, TOK, D)
    cot_copy = pltpu.make_async_copy(cot_part, cot_rows.at[:, pl.ds(mine0, PART)], lo_s.at[len(CHUNKS)])
    lane512 = iota((OWN, 512), 1) & 255
    units = lane512 < 160
    resids = (lane512 >= 128 + L_RES) & (lane512 < 128 + L_RES + 8)

    def part_rows(p, first=0):
        return slice(first + OWN * p, first + OWN * p + OWN)

    def features():
        keep = 1.0 - missing[...].astype(f32)
        seen = dot_plain(spread, (points[...].astype(f32) * keep).astype(bf16))
        gone = dot_plain(spread, missing[...].astype(f32).astype(bf16))
        feats = dot_plain(jnp.where(right_patch, seen, 0.0).astype(bf16), one_hot(lane_of == place_of))
        feats = feats + dot_plain(jnp.where(right_patch, gone, 0.0).astype(bf16), one_hot(lane_of == place_of + PL))
        ptx[0:OWN, :] = jnp.where(iota((OWN, 128), 1) == 2 * PL, 1.0, feats)
        fe[pl.ds(mine0, PART), :] = ptx[pl.ds(m16(PART * x), PART), :].astype(bf16)
        for to, member in group:
            rows = fe.at[pl.ds(mine0, PART)]
            remote(rows, rows, tk_s.at[0], tk_r.at[0], to).start()
        sums[...] = jnp.zeros(sums.shape, f32)
        hidf[...] = jnp.zeros(hidf.shape, f32)

    def cot_out():
        cot_copy.start()
        dst = cot_rows.at[:, pl.ds(mine0, PART)]
        remote(cot_part, dst, tk_s.at[1], tk_r.at[1], mate).start()
        remote(cot_part.at[x], cot_rows.at[x, pl.ds(mine0, PART)], tk_s.at[1], tk_r.at[2], beside).start()

    def cot_pass(stage):
        here = pl.ds(m16(OWN * (1 - l) + own0), PART)
        near, far = cot_rows.at[x, here], cot_rows.at[1 - x, here]
        if stage == 0:
            came(near, tk_r.at[2])
            remote(near, near, tk_s.at[1], tk_r.at[3], along["x"]).start()
            remote(near, near, tk_s.at[1], tk_r.at[4], mate).start()
        else:
            came(far, tk_r.at[3])
            remote(far, far, tk_s.at[1], tk_r.at[5], mate).start()

    def cot_here():
        cot_copy.wait()
        came(cot_rows.at[:, pl.ds(m16(OWN * l + oth0), PART)], tk_r.at[1])
        for i, xx in ((4, x), (5, 1 - x)):
            came(cot_rows.at[xx, pl.ds(m16(OWN * (1 - l) + oth0), PART)], tk_r.at[i])

    def hidden():
        for h in (0, 1):
            for j in range(4):
                rows = pl.ds(m16(320 * m + 80 * j), 80)
                tmp[:, 0:128] = w[rows, slab(h)].astype(f32)
                hidf[0:72, 256 * h + 40 * j : 256 * h + 40 * j + 40] = tmp[0:72, L_HID : L_HID + 40]
            row = iota((128, 128), 0)
            lane = iota((128, 128), 1)
            chosen = (lane >= L_RES) & (lane < L_RES + 8) & (row == PL * h + 8 * m + lane - L_RES)
            hidf[:, slab(h)] = jnp.where(chosen, 1.0, hidf[:, slab(h)])
        hid[...] = hidf[...].astype(bf16)
        came(fe.at[0 : 3 * PART], tk_r.at[0])

    def tokenize(p):
        v = dot_plain(fe[part_rows(p), :], hid[...])
        pret[part_rows(p), :] = v
        hc[part_rows(p), :] = jnp.where(
            units, v * jax.nn.sigmoid(v), jnp.where(resids, v, jnp.where(lane512 == 128 + L_ONE, 1.0, 0.0))
        ).astype(bf16)

    def vectors():
        row16 = iota((16, 128), 0)
        lane16 = iota((16, 128), 1)
        vec[...] = dot_last(one_hot((row16 < 4) & (lane16 == L_VEC + row16)), w[:, slab(0)])
        own_slab = pl.ds(pl.multiple_of(128 + 256 * x, 128), 128)
        pair = dot_last(one_hot((row16 < 2) & (lane16 == L_BIN + row16)), w[pl.ds(m16(320 * m), 320), own_slab])
        tmp[0:16, 0:320] = pair
        for j in range(4):
            at = 160 * j
            bin_s[0:1, at : at + 80] = tmp[0:1, 80 * j : 80 * j + 80]
            bin_s[0:1, at + 80 : at + 160] = tmp[1:2, 80 * j : 80 * j + 80]

    def first_norm(p):
        ar_end(0, p)

        def body(start):
            v = summed(0, p, pl.ds(start, 32)) + vec[3:4, :]
            x0[at32(PART * p + start), :] = v
            n1[at32(OWN * p + own0 + start), :] = (v * rms(v) * vec[0:1, :]).astype(bf16)

        own_rows(body)
        share(0, p, n1)

    def project(p):
        shared(0, p, n1)
        rows = part_rows(p)
        for h in (0, 1):
            for lo in (0, 256):
                col = C_QKV + 640 * h + lo
                part[rows, 512 * h + lo : 512 * h + lo + 256] = dot_plain(n1[rows, :], w[:, col : col + 256])

    def turn(p):
        def body(j, carry):
            rows = pl.ds(m16(OWN * p + 48 * j), 48)
            for h in (0, 1):
                v = part[rows, 512 * h : 512 * h + 512]
                v = v * rot_c[...] + pltpu.roll(v, 472, 1) * rot_a[...] + pltpu.roll(v, 40, 1) * rot_b[...]
                q_s[h, rows, :] = v[:, 0:256].astype(bf16)
                k_s[h, rows, :] = pltpu.roll(v, 352, 1)[:, 0:256].astype(bf16)
                v_s[h, rows, :] = pltpu.roll(v, 288, 1)[:, 0:256].astype(bf16)
            return carry

        lax.fori_loop(0, OWN // 48, body, 0)

    def one_head(v, first, i):
        lane = iota(v.shape, 1)
        inside = (lane >= first + HEAD_DIM * i) & (lane < first + HEAD_DIM * i + HEAD_DIM)
        return jnp.where(inside, v, jnp.zeros_like(v))

    def stacked(v, first):
        return jnp.concatenate([one_head(v, first, 0), one_head(v, first, 1)], axis=0)

    def by_head(probs, v, first):
        return dot_plain(probs[0:OWN], one_head(v, first, 0)) + dot_plain(probs[OWN:TOK], one_head(v, first, 1))

    def attend(p):
        rows = part_rows(p)
        qi = iota((TOK, OWN), 0)
        qi = jnp.where(qi >= OWN, qi - OWN, qi)
        kj = iota((TOK, OWN), 1)
        allowed = ((qi >> 4) == (kj >> 4)) & (kj <= qi)
        for h in (0, 1):
            scores = dot_last(stacked(q_s[h, rows, :], 0), k_s[h, rows, :]) * SCALE
            scores = jnp.where(allowed, scores, -1e30)
            e = jnp.exp(scores - jnp.max(scores, axis=-1, keepdims=True))
            probs = e * (1.0 / jnp.sum(e, axis=-1, keepdims=True))
            ps[p, h] = probs
            att[rows, 256 * h : 256 * h + 256] = by_head(probs.astype(bf16), v_s[h, rows, :], 96).astype(bf16)

    def second_norm(p):
        ar_end(1, p)

        def body(start):
            own = at32(PART * p + start)
            v = x0[own, :] + summed(1, p, pl.ds(start, 32))
            x1[own, :] = v
            n2[at32(TOK * x + OWN * p + own0 + start), :] = (v * rms(v) * vec[1:2, :]).astype(bf16)

        own_rows(body)
        share(1, p, n2, TOK * x, along["x"])
        share(4, p, n2, TOK * x)

    def norm_pass(p):
        far = TOK * (1 - x)
        shared(1, p, n2, far, own0)
        rows = n2.at[pl.ds(m16(far + OWN * p + own0), PART)]
        remote(rows, rows, nx_s.at[0], nx_r.at[5, p], mate).start()

    def inner(which, p):
        first = TOK * (x if which == 0 else 1 - x)
        shared(4 if which == 0 else 5, p, n2, first)
        rows = pl.ds(m16(first + OWN * p), OWN)
        for lo, width in MLP_TILES:
            at = slice(lo, lo + width)
            v = dot_plain(n2[rows, :], w[:, C_IN + lo : C_IN + lo + width]) + bin_s[0:1, at]
            pre[rows, at] = v
            act[rows, at] = (v * jax.nn.sigmoid(v)).astype(bf16)

    def outer_back(p):
        for first in (0, TOK):
            rows = part_rows(p, first)
            for lo, width in MLP_TILES:
                at = slice(lo, lo + width)
                v = pre[rows, at]
                s = jax.nn.sigmoid(v)
                d = dot_plain(cot[rows, :], w[:, C_OUT + lo : C_OUT + lo + width])
                dpre[rows, at] = (d * (s * (1.0 + v * (1.0 - s)))).astype(bf16)

    def norm_back(dn, v, gain):
        r = rms(v)
        xh = v * r
        scaled = dn * gain
        inside = jnp.mean(scaled * xh, axis=-1, keepdims=True)
        return r * (scaled - xh * inside), fold(dn * xh)

    def second_back(p):
        ar_end(2, p)

        def body(start):
            own = at32(PART * p + start)
            d, by_gain = norm_back(summed(2, p, pl.ds(start, 32)), x1[own, :], vec[1:2, :])
            ct = cot[at32(TOK * x + OWN * p + own0 + start), :].astype(f32)
            d = ct + d
            x2[own, :] = d
            db[at32(OWN * p + own0 + start), :] = d.astype(bf16)
            sums[8:16, :] += by_gain
            sums[16:24, :] += fold(ct)

        own_rows(body)
        share(2, p, db)

    def attended_back(p):
        shared(2, p, db)
        rows = part_rows(p)
        for h in (0, 1):
            col = C_QKV + 640 * h + 384
            datt[rows, 256 * h : 256 * h + 256] = dot_plain(db[rows, :], w[:, col : col + 256]).astype(bf16)

    def attend_back(p):
        rows = part_rows(p)
        for h in (0, 1):
            probs = ps[p, h]
            heads_d = stacked(datt[rows, 256 * h : 256 * h + 256], 96)
            dp = dot_last(heads_d, v_s[h, rows, :])
            ds = (probs * (dp - jnp.sum(probs * dp, axis=-1, keepdims=True))).astype(bf16)
            part[rows, 512 * h : 512 * h + 256] = by_head(ds, k_s[h, rows, :], 0) * SCALE
            part[rows, 512 * h + 160 : 512 * h + 416] = dot_rows(ds, stacked(q_s[h, rows, :], 0)) * SCALE
            dv = dot_rows(probs.astype(bf16), heads_d)
            dv = jnp.concatenate([dv, jnp.zeros((OWN, 128), f32)], axis=1)
            part[rows, 512 * h + 320 : 512 * h + 512] = dv[:, 96:288]

    def turn_back(p):
        def body(j, carry):
            rows = pl.ds(m16(OWN * p + 48 * j), 48)
            for h in (0, 1):
                v = part[rows, 512 * h : 512 * h + 512]
                v = v * rot_c[...] - pltpu.roll(v, 472, 1) * rot_a[...] - pltpu.roll(v, 40, 1) * rot_b[...]
                dpj[rows, 512 * h : 512 * h + 512] = v.astype(bf16)
            return carry

        lax.fori_loop(0, OWN // 48, body, 0)

    def finish():
        ar_end(3, 0)

        def body(start):
            rows = pl.ds(start, 32)
            v = part3[at32(TOK * x + OWN * l + own0 + start), :] + yr[1, l, rows, :].astype(f32)
            v = v + xr[0, 0, rows, :].astype(f32)
            ob[rows, :] = (x1[at32(PART * l + start), :] + v + vec[2:3, :]).astype(bf16)

        own_rows(body)
        ref = out_o.at[pl.ds(m16(PART * x), PART)]
        go(remote(ob, ref, pt_s.at[3], pt_r.at[3], along["x"]))
        pltpu.make_async_copy(ob, ref, keep_s.at[1]).start()

    def grad_mlp(k, left, right, base):
        first, _, width, _ = CHUNKS[k]

        def body(rows, i):
            lo = first - base
            g[rows, first : first + width] = dot_rows(left[:, rows], right[:, lo : lo + width]).astype(bf16)

        tiles_loop(TILES, body)
        s_start(k)

    def grad_out(k):
        grad_mlp(k, cot, act, C_OUT)

    def grad_in(k):
        grad_mlp(k, n2, dpre, C_IN)

    def grad_qkv(k):
        first, apart, width, _ = CHUNKS[k]
        lo, hi = first - C_QKV, first - C_QKV + width
        mid, cut = min(hi, 512), max(lo, 384)

        def body(rows, i):
            for h in (0, 1):
                col = C_QKV + apart * h
                if lo < mid:
                    value = dot_rows(n1[:, rows], dpj[:, 512 * h + lo : 512 * h + mid])
                    if cut >= mid:
                        g[rows, col + lo : col + mid] = value.astype(bf16)
                    else:
                        more = dot_rows(db[:, rows], att[:, 256 * h + cut - 384 : 256 * h + mid - 384])
                        if cut > lo:
                            g[rows, col + lo : col + cut] = value[:, 0 : cut - lo].astype(bf16)
                        g[rows, col + cut : col + mid] = (value[:, cut - lo :] + more).astype(bf16)
                if hi > 512:
                    start = max(lo, 512)
                    value = dot_rows(db[:, rows], att[:, 256 * h + start - 384 : 256 * h + hi - 384])
                    g[rows, col + start : col + hi] = value.astype(bf16)

        tiles_loop(TILES, body)
        s_start(k)

    def grad_bias():
        ones = one_hot((iota((BOTH, 128), 1) >= L_BIN) & (iota((BOTH, 128), 1) < L_BIN + 2))
        for lo, width in MLP_TILES:
            gbs[lo : lo + width, :] = dot_rows(dpre[:, lo : lo + width], ones)

    def first_back(p):
        ar_end(4, p)

        def body(start):
            own = at32(PART * p + start)
            d, by_gain = norm_back(summed(4, p, pl.ds(start, 32)), x0[own, :], vec[0:1, :])
            de[at32(OWN * p + own0 + start), :] = (x2[own, :] + d).astype(bf16)
            sums[0:8, :] += by_gain

        own_rows(body)
        share(3, p, de)

    def hidden_back(p):
        shared(3, p, de)
        rows = part_rows(p)
        v = pret[rows, :]
        s = jax.nn.sigmoid(v)
        d = dot_plain(de[rows, :], w[:, 0:512])
        dpe[rows, :] = jnp.where(units, d * (s * (1.0 + v * (1.0 - s))), jnp.where(resids, d, 0.0)).astype(bf16)

    def grad_tok():
        row32 = iota((32, 128), 0)
        pick = one_hot((row32 < 24) & (iota((32, 128), 1) == L_VEC + (row32 >> 3)))

        def body(rows, i):
            both = dot_rows(de[:, rows], hc[...])
            columns = dot_rows(sums[:, rows].astype(bf16), pick)
            for h in (0, 1):
                g[rows, 256 * h : 256 * h + 128] = both[:, 256 * h : 256 * h + 128].astype(bf16)
                g[rows, slab(h)] = (both[:, slab(h)] + columns).astype(bf16)

        tiles_loop(TILES, body)
        s_start(0)

    def grad_hidden():
        ghs[...] = dot_rows(fe[...], dpe[...])
        lane = iota((80, 128), 1)
        for h in (0, 1):
            for j in range(4):
                at = 160 * j
                tmp[:, 0:128] = jnp.where((lane == L_BIN) & (x == h), gbs[at : at + 80, :], 0.0) + jnp.where(
                    (lane == L_BIN + 1) & (x == h), gbs[at + 80 : at + 160, :], 0.0
                )
                tmp[:, L_HID : L_HID + 40] = ghs[0:80, 256 * h + 40 * j : 256 * h + 40 * j + 40]
                rows = pl.ds(m16(320 * m + 80 * j), 80)
                g[rows, slab(h)] = (g[rows, slab(h)].astype(f32) + tmp[:, 0:128]).astype(bf16)
        s_start(1)

    def points_back(stage):
        if stage == 0:
            ptx[...] = dot_last(dpe[...], hid[...])
            away = ptx.reshape(2, OWN, 128).at[:, pl.ds(oth0, PART)]
            go(remote(away, ptr.at[0], pt_s.at[0], pt_r.at[0], mate))
        elif stage == 1:
            remote(ptr.at[0], ptr.at[0], pt_s.at[0], pt_r.at[0], mate).wait_recv()
            for p in (0, 1):
                ptr[1, p] = ptx[pl.ds(m16(OWN * p + own0), PART), :] + ptr[0, p]
            go(remote(ptr.at[1, 1 - l], ptr.at[2, 1 - l], pt_s.at[1], pt_r.at[1], beside))
        elif stage == 2:
            there = ptr.at[2, l]
            remote(there, there, pt_s.at[1], pt_r.at[1], beside).wait_recv()
            ptr[3, x] = ptr[1, l] + ptr[2, l]
            go(remote(ptr.at[3, x], ptr.at[3, x], pt_s.at[2], pt_r.at[2], along["x"]))
        else:
            there = ptr.at[3, 1 - x]
            remote(there, there, pt_s.at[2], pt_r.at[2], along["x"]).wait_recv()
            every = ptr[3].reshape(OWN, 128).astype(bf16)
            wide = dot_last(every, one_hot(lane_of == place_of))
            wide = jnp.where(right_patch, wide, 0.0).astype(bf16)
            pts_v[...] = dot_rows(spread, wide) * (1.0 - missing[...].astype(f32))
            pltpu.make_async_copy(pts_v, pts_o, keep_s.at[2]).start()

    operands = (
        ((hc, 0, 0, 512),),
        ((att, 0, 896, 256), (att, 256, 1536, 256)),
        ((dpre, 0, C_IN, 640),),
        ((act, 0, C_OUT, 640),),
        ((dpj, 0, 512, 512), (dpj, 512, 1152, 512)),
    )
    steps = (
        g_first, g_own, g_second, g_third, g_done, s_step, features, cot_out, cot_here, tokenize, vectors,
        first_norm, project, turn, attend, second_norm, inner, grad_out, outer_back, grad_in, second_back,
        attended_back, attend_back, turn_back, finish, grad_qkv, grad_bias, first_back, hidden_back, grad_tok,
        grad_hidden, points_back, ar_begin, ar_mid, cot_pass, norm_pass, ar_cross, hidden,
    )
    for name, *which in PLAN:
        steps[name](*which)

    came(out_o.at[pl.ds(m16(PART * (1 - x)), PART)], pt_r.at[3])
    came(fb.at[0:3], fin_r.at[0])
    pltpu.make_async_copy(g.at[0:HALF, 0:C_ONE], fb.at[m], keep_s.at[0]).wait()
    pltpu.make_async_copy(ob, out_o.at[pl.ds(m16(PART * x), PART)], keep_s.at[1]).wait()
    pltpu.make_async_copy(pts_v, pts_o, keep_s.at[2]).wait()
    for ref, sem in (
        (rb, ag_s.at[0]), (rbm, ag_s.at[1]), (rb, rs_s.at[0]), (rbm, rs_s.at[1]),
        (w.at[0 : 3 * HALF, 0:C_ONE], in_s.at[0]), (g.at[0 : 3 * HALF, 0:C_ONE], fin_s.at[0]),
        (cs.at[1, 0], cs_s.at[3, 0]), (cs.at[1, 1], cs_s.at[3, 1]),
        (cs.at[0, 0, 0:PART], cs_s.at[4, 0]), (cs.at[0, 1, 0:PART], cs_s.at[4, 1]),
        (xs.at[1, 0], xs_s.at[3, 0]), (xs.at[0, 0], xs_s.at[4, 0]), (xs.at[0, 1], xs_s.at[4, 1]),
        (ys, ys_s.at[0]), (w.at[0 : 12 * PART, 0:D], nx_s.at[0]),
        (fe.at[0 : 3 * PART], tk_s.at[0]), (cot.at[0 : 6 * PART], tk_s.at[1]),
    ):
        left(ref, sem)
    for copy in sent:
        copy.wait_send()


def unpack_kernel(
    out_i, pts_i, fb_i,
    out_o, pts_o, hw_o, hb_o, tok_o, res_o, tokb_o, gain1_o, qkv_o, att_o, gain2_o, in_o, inb_o, outw_o, outb_o,
    fb, sem,
):
    f32 = jnp.float32
    copies = [pltpu.make_async_copy(fb_i.at[q], fb.at[q], sem.at[q]) for q in range(4)]
    copies.append(pltpu.make_async_copy(out_i, out_o, sem.at[4]))
    for copy in copies:
        copy.start()
    pts_o[...] = pts_i[...]
    turned = []
    hidden = jnp.zeros((8, 128), f32)
    for q in range(4):
        copies[q].wait()
        at = slice(160 * q, 160 * q + 160)
        lead = fb[q, :, 0:256].astype(f32)
        tok_o[:, at] = lead[:, 0:160]
        tile = lead[:, 128:256]
        hidden = hidden + tile[64:72]
        t = jnp.transpose(jnp.concatenate([tile, jnp.zeros((48, 128), f32)], axis=0))
        turned.append(t)
        res_o[8 * q : 8 * q + 8, :] = t[L_RES : L_RES + 8, 0:80]
        qkv = fb[q, :, 256:896].astype(f32)
        for j in range(3):
            qkv_o[j, :, at] = qkv[:, 160 * j : 160 * j + 160]
        att_o[:, at] = qkv[:, 480:640]
        in_o[:, 640 * q : 640 * q + 640] = fb[q, :, 896:1536].astype(f32)
        outw_o[:, 640 * q : 640 * q + 640] = fb[q, :, 1536:2176].astype(f32)
    both = turned[0] + turned[1]
    every = both + turned[2] + turned[3]
    tokb_o[...] = turned[0][L_ONE : L_ONE + 1, 0:80]
    gain1_o[...] = both[L_VEC : L_VEC + 1, 0:80]
    gain2_o[...] = both[L_VEC + 1 : L_VEC + 2, 0:80]
    outb_o[...] = both[L_VEC + 2 : L_VEC + 3, 0:80]
    inb_o[:, 0:80] = every[L_BIN : L_BIN + 1, 0:80]
    inb_o[:, 80:160] = every[L_BIN + 1 : L_BIN + 2, 0:80]
    hw_o[...] = every[L_HID : L_HID + 40, 0:64]
    hb_o[...] = hidden[0:1, L_HID : L_HID + 40]
    copies[4].wait()


def rotary_lanes():
    lanes = np.arange(512)
    inside = lanes % HEAD_DIM
    turned = lanes < 320
    freqs = 10000.0 ** (-2.0 * (inside % 40) / HEAD_DIM)
    angles = (np.arange(48) % CTXLEN)[:, None] * freqs[None, :]
    cosine = np.where(turned, np.cos(angles), 1.0)
    sine = np.where(turned, np.sin(angles), 0.0)
    lower = np.where(inside < 40, -sine, 0.0)
    upper = np.where(inside >= 40, sine, 0.0)
    return [np.asarray(t, np.float32) for t in (cosine, lower, upper)]


def fast_body(
    points, missing, tok_hidden_w, tok_hidden_b, tok_out_w, tok_res_w, tok_out_b, attn_gain, qkv_w, attn_out_w,
    mlp_gain, mlp_in_w, mlp_in_b, mlp_out_w, mlp_out_b, cotangent,
):
    f32, bf16 = jnp.float32, jnp.bfloat16
    any_space = pl.BlockSpec(memory_space=pl.ANY)
    vmem = pl.BlockSpec(memory_space=pltpu.VMEM)

    def sems(*shape):
        return pltpu.SemaphoreType.DMA(shape)

    def like(*shape):
        return jax.ShapeDtypeStruct(shape, f32)

    chunks = len(CHUNKS)
    wide = sum(1 for chunk in CHUNKS if chunk[3] < C_MLP)
    specs = [vmem] * 19
    specs[11] = specs[13] = specs[15] = any_space
    out, pts, packed = pl.pallas_call(
        layer_kernel,
        out_shape=(
            jax.ShapeDtypeStruct((OWN, D), bf16),
            like(12, 512),
            jax.ShapeDtypeStruct((4, HALF, C_ONE), bf16),
        ),
        in_specs=specs,
        out_specs=[any_space] * 3,
        scratch_shapes=[
            pltpu.VMEM((D, C_ALL), bf16),
            pltpu.VMEM((D, C_ALL), bf16),
            pltpu.VMEM((7, 2, 160, C_MLP), bf16),
            pltpu.VMEM((3, 2, 160, C_ONE - C_MLP), bf16),
            pltpu.VMEM((TOK, 128), bf16),
            pltpu.VMEM((BOTH, D), bf16),
            pltpu.VMEM((BOTH, D), f32),
            pltpu.VMEM((BOTH, 640), f32),
            pltpu.VMEM((BOTH, 640), bf16),
            pltpu.VMEM((BOTH, 640), bf16),
            pltpu.VMEM((TOK, D), bf16),
            pltpu.VMEM((BOTH, D), bf16),
            pltpu.VMEM((TOK, D), bf16),
            pltpu.VMEM((TOK, D), bf16),
            pltpu.VMEM((OWN, D), f32),
            pltpu.VMEM((OWN, D), f32),
            pltpu.VMEM((OWN, D), f32),
            pltpu.VMEM((TOK, 512), bf16),
            pltpu.VMEM((TOK, 512), bf16),
            pltpu.VMEM((TOK, 512), f32),
            pltpu.VMEM((2, TOK, 256), bf16),
            pltpu.VMEM((2, TOK, 256), bf16),
            pltpu.VMEM((2, TOK, 256), bf16),
            pltpu.VMEM((TOK, 512), bf16),
            pltpu.VMEM((TOK, 512), bf16),
            pltpu.VMEM((TOK, 1024), bf16),
            pltpu.VMEM((2, 2, TOK, OWN), f32),
            pltpu.VMEM((640, 128), f32),
            pltpu.VMEM((128, 512), f32),
            pltpu.VMEM((128, 512), f32),
            pltpu.VMEM((128, 512), bf16),
            pltpu.VMEM((16, D), f32),
            pltpu.VMEM((8, 640), f32),
            pltpu.VMEM((32, D), f32),
            pltpu.VMEM((TOK, 128), f32),
            pltpu.VMEM((4, 2, PART, 128), f32),
            pltpu.VMEM((4, HALF, 896), bf16),
            pltpu.VMEM((HALF, 896), f32),
            pltpu.VMEM((HALF, 128), f32),
            pltpu.VMEM((HALF, 384), f32),
            pltpu.VMEM((BOTH, D), f32),
            pltpu.VMEM((PART, D), bf16),
            pltpu.VMEM((12, 512), f32),
            pltpu.VMEM((2, 2, OWN, D), bf16),
            pltpu.VMEM((2, 2, OWN, D), bf16),
            pltpu.VMEM((2, 2, PART, D), bf16),
            pltpu.VMEM((2, 2, PART, D), bf16),
            pltpu.VMEM((2, 2, PART, D), bf16),
            pltpu.VMEM((3, 2, PART, D), bf16),
            sems(2), sems(4 * wide + 2 * (chunks - wide)), sems(2), sems(7 * wide + 3 * (chunks - wide)),
            sems(5, 2), sems(5, 2, 2), sems(5, 2), sems(5, 2), sems(1), sems(2, 2, 2),
            sems(1), sems(6, 2), sems(1), sems(chunks), sems(chunks + 1), sems(2), sems(6),
            sems(1), sems(1), sems(4), sems(4), sems(3),
        ],
        compiler_params=pltpu.CompilerParams(
            collective_id=0, has_side_effects=True, vmem_limit_bytes=64 * 1024 * 1024 - 512 * 1024
        ),
        cost_estimate=pl.CostEstimate(flops=13 * 10**9, bytes_accessed=10**7, transcendentals=10**6),
    )(
        points, missing, tok_hidden_w[0], tok_hidden_b, tok_out_w, tok_res_w.T, tok_out_b[None], attn_gain[None],
        qkv_w.transpose(1, 0, 2), attn_out_w, mlp_gain[None], mlp_in_w, mlp_in_b, mlp_out_w, mlp_out_b[None],
        cotangent, *[jnp.asarray(t) for t in rotary_lanes()],
    )
    (
        output, points_grad, hidden_w, hidden_b, tok, res_t, tok_b, gain1, qkv, att, gain2, inner, inner_b, outer,
        outer_b,
    ) = pl.pallas_call(
        unpack_kernel,
        out_shape=(
            jax.ShapeDtypeStruct((OWN, D), bf16),
            like(12, 512), like(40, 64), like(1, 40), like(HALF, 640), like(32, HALF), like(1, HALF), like(1, HALF),
            like(3, HALF, 640), like(HALF, 640), like(1, HALF), like(HALF, 2560), like(1, 160), like(HALF, 2560),
            like(1, HALF),
        ),
        in_specs=[any_space, vmem, any_space],
        out_specs=[vmem] * 15,
        scratch_shapes=[pltpu.VMEM((4, HALF, C_ONE), bf16), sems(5)],
        compiler_params=pltpu.CompilerParams(vmem_limit_bytes=63 * 1024 * 1024),
    )(out, pts, packed)
    return (
        output, points_grad, hidden_w[None], hidden_b, tok, res_t.T, tok_b[0], gain1[0], qkv.transpose(1, 0, 2), att,
        gain2[0], inner, inner_b, outer, outer_b[0],
    )


def solution(mesh):
    placed = (
        P("fsdp", None),
        P("fsdp", None),
        P("tp", "fsdp", None),
        P("tp", "fsdp"),
        P("fsdp", "tp"),
        P("fsdp", "tp"),
        P("fsdp"),
        P("fsdp"),
        P("fsdp", None, "tp"),
        P("fsdp", "tp"),
        P("fsdp"),
        P("fsdp", "tp"),
        P("tp", "fsdp"),
        P("fsdp", "tp"),
        P("fsdp"),
        P("fsdp", None),
    )
    small_slice = mesh.shape["fsdp"] == 16 and mesh.shape["tp"] == 2
    return jax.shard_map(
        fast_body if small_slice else body,
        mesh=mesh,
        in_specs=placed,
        out_specs=(
            P("fsdp", None),
            P("fsdp", None),
            P("tp", "fsdp", None),
            P("tp", "fsdp"),
            P("fsdp", "tp"),
            P("fsdp", "tp"),
            P("fsdp"),
            P("fsdp"),
            P("fsdp", None, "tp"),
            P("fsdp", "tp"),
            P("fsdp"),
            P("fsdp", "tp"),
            P("tp", "fsdp"),
            P("fsdp", "tp"),
            P("fsdp"),
        ),
        check_vma=False,
    )
```

```python
import math

import jax
import jax.numpy as jnp
import numpy as np
from jax import lax
from jax.experimental import pallas as pl
from jax.experimental.pallas import tpu as pltpu
from jax.sharding import PartitionSpec as P

D = 1280
HEAD_DIM = 80
PL = 32
CTXLEN = 16


def dot_plain(left, right):
    return jnp.dot(left, right, preferred_element_type=jnp.float32)


def dot_last(left, right):
    return lax.dot_general(
        left, right, (((1,), (1,)), ((), ())), preferred_element_type=jnp.float32
    )


def dot_rows(left, right):
    return lax.dot_general(
        left, right, (((0,), (0,)), ((), ())), preferred_element_type=jnp.float32
    )


def silu_slope(values):
    sigma = jax.nn.sigmoid(values)
    return sigma * (1.0 + values * (1.0 - sigma))


def rotary_tables():
    positions = jnp.arange(CTXLEN, dtype=jnp.float32)
    freqs = 10000.0 ** (-2.0 * jnp.arange(HEAD_DIM // 2, dtype=jnp.float32) / HEAD_DIM)
    angles = positions[:, None] * freqs[None, :]
    return (jnp.cos(angles)[None, :, None, :], jnp.sin(angles)[None, :, None, :])


def rotate(vector, cosine, sine):
    half = vector.shape[-1] // 2
    first = vector[..., :half]
    second = vector[..., half:]
    return jnp.concatenate(
        [first * cosine - second * sine, second * cosine + first * sine], axis=-1
    )


def rotate_back(vector, cosine, sine):
    half = vector.shape[-1] // 2
    first = vector[..., :half]
    second = vector[..., half:]
    return jnp.concatenate(
        [first * cosine + second * sine, second * cosine - first * sine], axis=-1
    )


def norm_stats(values):
    factor = lax.rsqrt(jnp.mean(values * values, axis=-1, keepdims=True) + 1e-06)
    return (factor, values * factor)


def norm_back(grad, normal, factor, gain):
    scaled = grad * gain
    inner = jnp.mean(scaled * normal, axis=-1, keepdims=True)
    return (factor * (scaled - normal * inner), jnp.sum(grad * normal, axis=0))


def body(
    points,
    missing,
    tok_hidden_w,
    tok_hidden_b,
    tok_out_w,
    tok_res_w,
    tok_out_b,
    attn_gain,
    qkv_w,
    attn_out_w,
    mlp_gain,
    mlp_in_w,
    mlp_in_b,
    mlp_out_w,
    mlp_out_b,
    cotangent,
):
    gathered = (
        lax.all_gather(tok_hidden_w, "fsdp", axis=1, tiled=True),
        lax.all_gather(tok_hidden_b, "fsdp", axis=1, tiled=True),
        lax.all_gather(tok_out_w, "fsdp", axis=0, tiled=True),
        lax.all_gather(tok_res_w, "fsdp", axis=0, tiled=True),
        lax.all_gather(tok_out_b, "fsdp", axis=0, tiled=True),
        lax.all_gather(attn_gain, "fsdp", axis=0, tiled=True),
        lax.all_gather(qkv_w, "fsdp", axis=0, tiled=True),
        lax.all_gather(attn_out_w, "fsdp", axis=0, tiled=True),
        lax.all_gather(mlp_gain, "fsdp", axis=0, tiled=True),
        lax.all_gather(mlp_in_w, "fsdp", axis=0, tiled=True),
        lax.all_gather(mlp_in_b, "fsdp", axis=1, tiled=True),
        lax.all_gather(mlp_out_w, "fsdp", axis=0, tiled=True),
        lax.all_gather(mlp_out_b, "fsdp", axis=0, tiled=True),
    )
    (
        hidden_full,
        hidden_bias,
        token_full,
        residual_full,
        token_bias,
        first_gain,
        project_full,
        attend_full,
        second_gain,
        inner_full,
        inner_bias,
        outer_full,
        outer_bias,
    ) = gathered
    contexts = points.shape[0]
    rows = contexts * CTXLEN
    tensor_rank = lax.axis_index("tp")
    kept_mask = (1 - missing).astype(jnp.float32).reshape(rows, PL)
    absent = missing.astype(jnp.float32).reshape(rows, PL)
    observed = points.astype(jnp.float32).reshape(rows, PL) * kept_mask
    features = jnp.concatenate([observed, absent], axis=1).astype(jnp.bfloat16)
    half_features = jnp.where(tensor_rank == 0, observed, absent).astype(jnp.bfloat16)
    hidden_matrix = hidden_full.reshape(-1, 2 * PL)
    pre_tok = dot_last(features, hidden_matrix) + hidden_bias.reshape(-1).astype(jnp.float32)
    hidden_tok = jax.nn.silu(pre_tok).astype(jnp.bfloat16)
    partial_tok = dot_last(hidden_tok, token_full) + dot_last(half_features, residual_full)
    embedded = lax.psum(partial_tok.astype(jnp.bfloat16), "tp").astype(jnp.float32)
    state_zero = embedded + token_bias.astype(jnp.float32)
    factor_one, normal_one = norm_stats(state_zero)
    normed_one = (normal_one * first_gain.astype(jnp.float32)).astype(jnp.bfloat16)
    local_width = project_full.shape[2]
    local_heads = local_width // HEAD_DIM
    project_matrix = project_full.reshape(D, 3 * local_width)
    projected = dot_plain(normed_one, project_matrix).reshape(
        contexts, CTXLEN, 3, local_heads, HEAD_DIM
    )
    cosine, sine = rotary_tables()
    queries = rotate(projected[:, :, 0], cosine, sine).astype(jnp.bfloat16)
    keys_rot = rotate(projected[:, :, 1], cosine, sine).astype(jnp.bfloat16)
    values_b = projected[:, :, 2].astype(jnp.bfloat16)
    scale = 1.0 / math.sqrt(HEAD_DIM)
    causal = jnp.arange(CTXLEN)[:, None] >= jnp.arange(CTXLEN)[None, :]

    def scores_of(left, right):
        raw = jnp.einsum("cihd,cjhd->chij", left, right, preferred_element_type=jnp.float32) * scale
        return jnp.where(causal, raw, -1e30)

    scores = scores_of(queries, keys_rot)
    row_top = jnp.max(scores, axis=-1, keepdims=True)
    log_total = row_top + jnp.log(jnp.sum(jnp.exp(scores - row_top), axis=-1, keepdims=True))
    probs_b = jnp.exp(scores - log_total).astype(jnp.bfloat16)
    attended = jnp.einsum("chij,cjhd->cihd", probs_b, values_b, preferred_element_type=jnp.float32)
    attended = attended.astype(jnp.bfloat16).reshape(rows, local_width)
    branch_attn = lax.psum(dot_last(attended, attend_full).astype(jnp.bfloat16), "tp").astype(
        jnp.float32
    )
    state_one = state_zero + branch_attn
    factor_two, normal_two = norm_stats(state_one)
    normed_two = (normal_two * second_gain.astype(jnp.float32)).astype(jnp.bfloat16)
    pre_mlp = dot_plain(normed_two, inner_full) + inner_bias.reshape(-1).astype(jnp.float32)
    activation = jax.nn.silu(pre_mlp).astype(jnp.bfloat16)
    branch_mlp = lax.psum(dot_last(activation, outer_full).astype(jnp.bfloat16), "tp").astype(
        jnp.float32
    )
    output = (state_one + branch_mlp + outer_bias.astype(jnp.float32)).astype(jnp.bfloat16)
    again = (
        lax.all_gather(tok_hidden_w, "fsdp", axis=1, tiled=True),
        lax.all_gather(tok_hidden_b, "fsdp", axis=1, tiled=True),
        lax.all_gather(tok_out_w, "fsdp", axis=0, tiled=True),
        lax.all_gather(tok_res_w, "fsdp", axis=0, tiled=True),
        lax.all_gather(tok_out_b, "fsdp", axis=0, tiled=True),
        lax.all_gather(attn_gain, "fsdp", axis=0, tiled=True),
        lax.all_gather(qkv_w, "fsdp", axis=0, tiled=True),
        lax.all_gather(attn_out_w, "fsdp", axis=0, tiled=True),
        lax.all_gather(mlp_gain, "fsdp", axis=0, tiled=True),
        lax.all_gather(mlp_in_w, "fsdp", axis=0, tiled=True),
        lax.all_gather(mlp_in_b, "fsdp", axis=1, tiled=True),
        lax.all_gather(mlp_out_w, "fsdp", axis=0, tiled=True),
        lax.all_gather(mlp_out_b, "fsdp", axis=0, tiled=True),
    )
    (
        hidden_full,
        hidden_bias,
        token_full,
        residual_full,
        token_bias,
        first_gain,
        project_full,
        attend_full,
        second_gain,
        inner_full,
        inner_bias,
        outer_full,
        outer_bias,
    ) = again
    hidden_matrix = hidden_full.reshape(-1, 2 * PL)
    project_matrix = project_full.reshape(D, 3 * local_width)
    grad_outer_bias = jnp.sum(cotangent, axis=0, dtype=jnp.float32)
    grad_outer = dot_rows(cotangent, activation)
    d_pre = (dot_plain(cotangent, outer_full) * silu_slope(pre_mlp)).astype(jnp.bfloat16)
    grad_inner_bias = jnp.sum(d_pre, axis=0, dtype=jnp.float32).reshape(1, -1)
    grad_inner = dot_rows(normed_two, d_pre)
    d_normed_two = lax.psum(dot_last(d_pre, inner_full).astype(jnp.bfloat16), "tp").astype(
        jnp.float32
    )
    through_two, grad_second_gain = norm_back(
        d_normed_two, normal_two, factor_two, second_gain.astype(jnp.float32)
    )
    d_state_one = cotangent.astype(jnp.float32) + through_two
    d_branch = d_state_one.astype(jnp.bfloat16)
    grad_attend = dot_rows(d_branch, attended)
    d_attended = (
        dot_plain(d_branch, attend_full)
        .astype(jnp.bfloat16)
        .reshape(contexts, CTXLEN, local_heads, HEAD_DIM)
    )
    probs = jnp.exp(scores_of(queries, keys_rot) - log_total)
    probs_b = probs.astype(jnp.bfloat16)
    d_probs = jnp.einsum(
        "cihd,cjhd->chij", d_attended, values_b, preferred_element_type=jnp.float32
    )
    d_values = jnp.einsum(
        "chij,cihd->cjhd", probs_b, d_attended, preferred_element_type=jnp.float32
    ).astype(jnp.bfloat16)
    row_inner = jnp.sum(probs * d_probs, axis=-1, keepdims=True)
    d_scores = (probs * (d_probs - row_inner)).astype(jnp.bfloat16)
    d_queries = (
        jnp.einsum("chij,cjhd->cihd", d_scores, keys_rot, preferred_element_type=jnp.float32)
        * scale
    )
    d_keys = (
        jnp.einsum("chij,cihd->cjhd", d_scores, queries, preferred_element_type=jnp.float32) * scale
    )
    d_queries = rotate_back(d_queries, cosine, sine).astype(jnp.bfloat16)
    d_keys = rotate_back(d_keys, cosine, sine).astype(jnp.bfloat16)
    d_projected = jnp.stack([d_queries, d_keys, d_values], axis=2).reshape(rows, 3 * local_width)
    grad_project = dot_rows(normed_one, d_projected).reshape(D, 3, local_width)
    d_normed_one = lax.psum(
        dot_last(d_projected, project_matrix).astype(jnp.bfloat16), "tp"
    ).astype(jnp.float32)
    through_one, grad_first_gain = norm_back(
        d_normed_one, normal_one, factor_one, first_gain.astype(jnp.float32)
    )
    d_state_zero = d_state_one + through_one
    grad_token_bias = jnp.sum(d_state_zero, axis=0)
    d_embedded = d_state_zero.astype(jnp.bfloat16)
    grad_token = dot_rows(d_embedded, hidden_tok)
    grad_residual = dot_rows(d_embedded, half_features)
    d_pre_tok = (dot_plain(d_embedded, token_full) * silu_slope(pre_tok)).astype(jnp.bfloat16)
    grad_hidden_bias = jnp.sum(d_pre_tok, axis=0, dtype=jnp.float32).reshape(1, -1)
    grad_hidden = dot_rows(d_pre_tok, features).reshape(1, -1, 2 * PL)
    through_hidden = dot_plain(d_pre_tok, hidden_matrix)[:, :PL]
    through_residual = dot_plain(d_embedded, residual_full)
    point_terms = through_hidden + jnp.where(tensor_rank == 0, through_residual, 0.0)
    point_sums = lax.psum(point_terms, "tp")
    points_grad = (point_sums * kept_mask).reshape(contexts, CTXLEN * PL)
    owned = (
        lax.psum_scatter(grad_hidden, "fsdp", scatter_dimension=1, tiled=True),
        lax.psum_scatter(grad_hidden_bias, "fsdp", scatter_dimension=1, tiled=True),
        lax.psum_scatter(grad_token, "fsdp", scatter_dimension=0, tiled=True),
        lax.psum_scatter(grad_residual, "fsdp", scatter_dimension=0, tiled=True),
        lax.psum_scatter(grad_token_bias, "fsdp", scatter_dimension=0, tiled=True),
        lax.psum_scatter(grad_first_gain, "fsdp", scatter_dimension=0, tiled=True),
        lax.psum_scatter(grad_project, "fsdp", scatter_dimension=0, tiled=True),
        lax.psum_scatter(grad_attend, "fsdp", scatter_dimension=0, tiled=True),
        lax.psum_scatter(grad_second_gain, "fsdp", scatter_dimension=0, tiled=True),
        lax.psum_scatter(grad_inner, "fsdp", scatter_dimension=0, tiled=True),
        lax.psum_scatter(grad_inner_bias, "fsdp", scatter_dimension=1, tiled=True),
        lax.psum_scatter(grad_outer, "fsdp", scatter_dimension=0, tiled=True),
        lax.psum_scatter(grad_outer_bias, "fsdp", scatter_dimension=0, tiled=True),
    )
    return (
        output,
        points_grad,
        owned[0],
        owned[1],
        owned[2],
        owned[3],
        owned[4],
        owned[5],
        owned[6],
        owned[7],
        owned[8],
        owned[9],
        owned[10],
        owned[11],
        owned[12],
    )


MESH = pl.DeviceIdType.MESH
TOK = 384
OWN = 192
PART = 96
HALF = 80
C_QKV, C_IN, C_OUT, C_ALL, C_ONE = 512, 1792, 2432, 3072, 2176
C_MLP = 896
BOTH = 2 * TOK
MLP_TILES = ((0, 256), (256, 256), (512, 128))
SPLIT = 640
CHUNKS = (
    (0, 256, 128, 0),
    (128, 256, 128, 128),
    (512, 640, 256, 256),
    (768, 640, 256, 512),
    (1024, 640, 128, 768),
    (1792, 0, 256, 896),
    (2048, 0, 384, 1152),
    (2432, 0, 256, 1536),
    (2688, 0, 256, 1792),
    (2944, 0, 128, 2048),
)
GATHER_ORDER = ("zyx", "zxy", "zyx", "zyx", "zxy", "zy", "zy", "zy", "zy", "zy")
SUM_ORDER = ("xyz", "xyz", "yxz", "xyz", "xyz", "yz", "yz", "yz", "yz", "yz")
(
    FIRST, OWNED, SECOND, THIRD, HERE, SUM, FEATS, COT, COT_HERE, TOKENS, VECTORS, NORM_1, PROJECT, TURN, ATTEND,
    NORM_2, INNER, GRAD_OUT, OUTER, GRAD_IN, BACK_2, D_ATT, ATTEND_B, TURN_B, FINISH, GRAD_QKV, GRAD_BIAS, BACK_1,
    D_HID, GRAD_TOK, GRAD_HID, POINTS, SEND, PASS, COT_PASS, NORM_PASS, CROSS, HIDDEN,
) = range(38)
PLAN = (
    (FIRST, 1), (FIRST, 0), (FIRST, 3), (FIRST, 4), (OWNED, 1), (FIRST, 2), (OWNED, 0), (FIRST, 5), (FIRST, 9),
    (OWNED, 3), (FEATS,), (FIRST, 6), (SECOND, 1), (OWNED, 4), (SECOND, 0), (THIRD, 1), (THIRD, 0), (OWNED, 2),
    (FIRST, 8), (HERE, 1), (FIRST, 7), (SECOND, 3), (HERE, 0), (OWNED, 5), (HIDDEN,), (VECTORS,), (TOKENS, 1),
    (SEND, 0, 1), (TOKENS, 0), (SECOND, 4), (PASS, 0, 1), (SEND, 0, 0), (THIRD, 3), (OWNED, 6), (OWNED, 7),
    (PASS, 0, 0), (SECOND, 2), (NORM_1, 1), (THIRD, 4), (COT,), (SECOND, 5), (THIRD, 2), (OWNED, 8), (HERE, 3),
    (HERE, 2), (PROJECT, 1), (TURN, 1), (NORM_1, 0), (HERE, 4), (ATTEND, 1), (SEND, 1, 1), (SECOND, 6), (PASS, 1, 1),
    (PROJECT, 0), (TURN, 0), (ATTEND, 0), (SEND, 1, 0), (COT_PASS, 0), (SECOND, 8), (PASS, 1, 0), (NORM_2, 1),
    (OWNED, 9), (HERE, 5), (COT_PASS, 1), (SECOND, 7), (NORM_2, 0), (SECOND, 9), (NORM_PASS, 1), (HERE, 6),
    (INNER, 0, 1), (HERE, 7), (HERE, 8), (COT_HERE,), (INNER, 1, 1), (INNER, 0, 0), (HERE, 9), (OUTER, 1),
    (NORM_PASS, 0), (SEND, 2, 1), (INNER, 1, 0), (CROSS, 2, 1), (GRAD_OUT, 7), (OUTER, 0), (SEND, 2, 0), (SEND, 3, 0),
    (PASS, 2, 1), (CROSS, 2, 0), (GRAD_OUT, 8), (SUM, 7), (GRAD_IN, 6), (GRAD_IN, 5), (PASS, 2, 0), (BACK_2, 1),
    (CROSS, 3, 0), (SEND, 3, 1), (D_ATT, 1), (SUM, 8), (ATTEND_B, 1), (TURN_B, 1), (SEND, 4, 1), (CROSS, 3, 1),
    (SUM, 8), (PASS, 4, 1), (BACK_2, 0), (GRAD_OUT, 9), (SUM, 6), (D_ATT, 0), (GRAD_QKV, 4), (ATTEND_B, 0),
    (TURN_B, 0), (SEND, 4, 0), (GRAD_QKV, 3), (PASS, 4, 0), (SUM, 5), (SUM, 4), (GRAD_QKV, 2), (GRAD_BIAS,), (SUM, 9),
    (BACK_1, 1), (SUM, 9), (SUM, 7), (SUM, 6), (D_HID, 1), (SUM, 4), (SUM, 3), (BACK_1, 0), (PASS, 3, 0), (SUM, 6),
    (D_HID, 0), (POINTS, 0), (SUM, 2), (SUM, 8), (GRAD_TOK,), (SUM, 2), (SUM, 9), (SUM, 7), (GRAD_HID,), (SUM, 5),
    (SUM, 4), (FINISH,), (POINTS, 1), (SUM, 2), (SUM, 3), (SUM, 0), (SUM, 4), (SUM, 0), (SUM, 1), (SUM, 2), (SUM, 1),
    (SUM, 5), (SUM, 0), (SUM, 1), (POINTS, 2), (SUM, 3), (SUM, 0), (SUM, 3), (SUM, 1), (POINTS, 3),
)
L_RES, L_ONE, L_VEC, L_BIN, L_HID = 32, 40, 41, 45, 47
TILE = 256
TILES = D // TILE
SCALE = 1.0 / math.sqrt(HEAD_DIM)


def iota(shape, dim):
    return lax.broadcasted_iota(jnp.int32, shape, dim)


def one_hot(cond):
    return jnp.where(cond, 1.0, 0.0).astype(jnp.bfloat16)


def layer_kernel(
    points, missing, hid_w, hid_b, tok_in, res_t, tok_b, gain1, qkv_in, att_in, gain2, win_in, b_in, wout_in,
    out_b, cot_in, rot_c, rot_a, rot_b,
    out_o, pts_o, fb,
    w, g, rb, rbm, fe, cot, part, pre, act, dpre, n1, n2, db, de, x0, x1, x2,
    hc, dpe, pret, q_s, k_s, v_s, att, datt, dpj, ps, gbs, ghs, hidf, hid, vec, bin_s, sums, ptx, ptr,
    pk, pkf, srcf, tmp,
    part3, ob, pts_v, cs, cr, ys, yr, xs, xr,
    ag_s, ag_r, rs_s, rs_r, cs_s, cs_r, xs_s, xs_r, ys_s, ys_r, nx_s, nx_r, in_s, in_r, lo_s, tk_s, tk_r,
    fin_s, fin_r, pt_s, pt_r, keep_s,
):
    f32, bf16 = jnp.float32, jnp.bfloat16
    f = lax.axis_index("fsdp")
    x = lax.axis_index("tp")
    z = lax.div(f, 4)
    zh = lax.div(z, 2)
    l = z - 2 * zh
    y = lax.div(f, 2) - 2 * z
    c = f - 4 * z - 2 * y
    m = 2 * l + c
    mate = {"fsdp": f + 1 - 2 * c}
    beside = {"fsdp": f + 4 - 8 * l}
    corner = {"fsdp": f + 4 - 8 * l + 1 - 2 * c}
    along = {"z": {"fsdp": f + 8 - 16 * zh}, "y": {"fsdp": f + 2 - 4 * y}, "x": {"tp": 1 - x}}
    own0 = pl.multiple_of(PART * c, PART)
    oth0 = pl.multiple_of(PART * (1 - c), PART)

    def m16(v):
        return pl.multiple_of(v, 16)

    def remote(src, dst, s_sem, r_sem, to):
        return pltpu.make_async_remote_copy(
            src_ref=src, dst_ref=dst, send_sem=s_sem, recv_sem=r_sem, device_id=to, device_id_type=MESH
        )

    sent = []

    def go(copy):
        copy.start()
        sent.append(copy)

    def came(ref, sem):
        remote(ref, ref, sem, sem, mate).wait_recv()

    def left(ref, sem):
        remote(ref, ref, sem, sem, mate).wait_send()

    barrier = pltpu.get_barrier_semaphore()
    peers = (mate, beside, corner, along["z"], along["y"], along["x"])
    for to in peers:
        pl.semaphore_signal(barrier, inc=1, device_id=to, device_id_type=MESH)

    part[0:80, 0:640] = tok_in[...].astype(f32)
    part[80:160, 0:640] = att_in[...].astype(f32)
    part[160:240, 0:640] = qkv_in[0].astype(f32)
    part[240:320, 0:640] = qkv_in[1].astype(f32)
    part[0:80, 640:1280] = qkv_in[2].astype(f32)
    srcf[...] = jnp.zeros(srcf.shape, f32)
    srcf[0:32, 0:80] = res_t[...].astype(f32)
    for i, v in enumerate((gain1, gain2, out_b, tok_b)):
        srcf[32 + i : 33 + i, 0:80] = v[...].astype(f32)
    tmp[0:1, 0:160] = b_in[...].astype(f32)
    srcf[36:37, 0:80] = tmp[0:1, 0:80]
    srcf[37:38, 0:80] = tmp[0:1, 80:160]
    srcf[40:80, 0:64] = hid_w[...].astype(f32)
    src = srcf[...].astype(bf16)
    row = iota((80, 128), 0)
    lane = iota((80, 128), 1)
    for q in range(4):
        col = 160 * q
        pkf[:, 0:160] = part[0:80, col : col + 160]
        pkf[:, 160:256] = jnp.zeros((80, 96), f32)
        place = (row < 32) & (row >= 8 * q) & (row < 8 * q + 8) & (lane == L_RES + row - 8 * q)
        place = place | ((row >= 32) & (row < 38) & (lane == L_VEC + row - 32))
        place = place | ((row >= 40) & (lane == L_HID + row - 40))
        pkf[:, 128:256] = pkf[:, 128:256] + dot_rows(src, one_hot(place))[0:80]
        pkf[64:65, 128 + L_HID : 128 + L_HID + 40] = hid_b[...].astype(f32)
        pkf[:, 256:416] = part[160:240, col : col + 160]
        pkf[:, 416:576] = part[240:320, col : col + 160]
        pkf[:, 576:736] = part[0:80, 640 + col : 800 + col]
        pkf[:, 736:896] = part[80:160, col : col + 160]
        pk[q] = pkf[...].astype(bf16)

    pl.semaphore_wait(barrier, len(peers))

    def cols(k, h):
        first, apart, width, _ = CHUNKS[k]
        return pl.ds(pl.multiple_of(first + apart * h, 128), width)

    def piece(k, member):
        first, _, width, at = CHUNKS[k]
        if at < 896:
            return pk.at[member, :, at : at + width]
        src, base = (win_in, 896) if at < 1536 else (wout_in, 1536)
        return src.at[:, pl.ds(pl.multiple_of(640 * member + at - base, 128), width)]

    group = ((mate, 2 * l + 1 - c), (beside, 2 - 2 * l + c), (corner, 3 - 2 * l - c))
    home = w.at[pl.ds(m16(HALF * f), HALF)]
    locals_in = {}

    def rows_of(to):
        return pl.ds(m16(HALF * to["fsdp"]), HALF)

    def g_first(k):
        dst = w.at[pl.ds(m16(HALF * f), HALF), cols(k, x)]
        for to, member in group:
            remote(piece(k, member), dst, in_s.at[0], in_r.at[k], to).start()
        locals_in[k] = pltpu.make_async_copy(piece(k, m), dst, lo_s.at[k])
        locals_in[k].start()

    w4 = w.reshape(4, 2, 160, C_ALL)
    g4 = g.reshape(4, 2, 160, C_ALL)

    def block(ref, k, flips):
        zz = 1 - zh if "z" in flips else zh
        yy = 1 - y if "y" in flips else y
        h = 1 - x if "x" in flips else x
        return ref.at[pl.ds(2 * zz, 2), yy, :, cols(k, h)]

    wide = sum(1 for chunk in CHUNKS if chunk[3] < C_MLP)

    def g_sem(k, i):
        return ag_r.at[4 * k + min(i, 3) if k < wide else 4 * wide + 2 * (k - wide) + min(i, 1)]

    def g_send(k, i, flips, axis):
        ref = block(w4, k, flips)
        remote(ref, ref, ag_s.at[0 if k < wide else 1], g_sem(k, i), along[axis]).start()

    def g_recv(k, i, flips):
        came(block(w4, k, flips), g_sem(k, i))

    def g_own(k):
        order = GATHER_ORDER[k]
        locals_in[k].wait()
        came(w.at[0 : 3 * HALF, 0 : CHUNKS[k][2]], in_r.at[k])
        for axis, i in zip(order, (0, 1, 3)):
            g_send(k, i, "", axis)

    def g_second(k):
        a, *rest = GATHER_ORDER[k]
        g_recv(k, 0, a)
        for axis, i in zip(rest, (2, 4)):
            g_send(k, i, a, axis)

    def g_third(k):
        a, b, d = GATHER_ORDER[k]
        g_recv(k, 1, b)
        g_send(k, 5, b, d)
        g_recv(k, 2, a + b)
        g_send(k, 6, a + b, d)

    def g_done(k):
        _, _, width, at = CHUNKS[k]
        if k < wide:
            came(rb.at[0:4, :, :, at : at + width], g_sem(k, 3))
        else:
            came(rbm.at[0:2, :, :, at - C_MLP : at - C_MLP + width], g_sem(k, 1))

    def s_buf(k, i):
        _, _, width, at = CHUNKS[k]
        return rb.at[i, :, :, at : at + width] if at < C_MLP else rbm.at[i, :, :, at - C_MLP : at - C_MLP + width]

    def s_sem(k, i):
        return rs_r.at[7 * k + i if k < wide else 7 * wide + 3 * (k - wide) + i]

    def s_send(k, i, flips, axis):
        remote(block(g4, k, flips), s_buf(k, i), rs_s.at[0 if k < wide else 1], s_sem(k, i), along[axis]).start()

    def s_add(k, i, flips, axis):
        came(s_buf(k, i), s_sem(k, i))
        _, _, width, at = CHUNKS[k]
        zz = 1 - zh if "z" in flips else zh
        yy = 1 - y if "y" in flips else y
        there = cols(k, 1 - x if "x" in flips else x)

        def step(j, carry):
            half = lax.div(j, 2)
            inside = 80 * (j - 2 * half)
            here = pl.ds(m16(640 * zz + 320 * half + 160 * yy + inside), 80)
            rows = pl.ds(m16(inside), 80)
            if at < C_MLP:
                more = rb[i, half, rows, at : at + width]
            else:
                more = rbm[i, half, rows, at - C_MLP : at - C_MLP + width]
            g[here, there] = g[here, there] + more
            return carry

        lax.fori_loop(0, 4, step, 0)

    def s_start(k):
        a, b, *last = SUM_ORDER[k]
        if last:
            d = last[0]
            s_send(k, 0, a + b + d, a)
            s_send(k, 1, a + b, a)
            s_send(k, 2, a + d, a)
            s_send(k, 3, a, a)
        else:
            s_send(k, 0, a + b, a)
            s_send(k, 1, a, a)
        s_at[k] = 0

    def s_step(k):
        a, b, *last = SUM_ORDER[k]
        stage = s_at[k]
        s_at[k] = stage + 1
        if not last:
            if stage == 0:
                s_add(k, 0, b, a)
                s_send(k, 2, b, b)
            elif stage == 1:
                s_add(k, 1, "", a)
            else:
                s_add(k, 2, "", b)
                s_out(k)
            return
        d = last[0]
        if stage == 0:
            s_add(k, 0, b + d, a)
            s_send(k, 4, b + d, b)
            s_add(k, 1, b, a)
            s_send(k, 5, b, b)
        elif stage == 1:
            s_add(k, 2, d, a)
            s_add(k, 4, d, b)
            s_send(k, 6, d, d)
        elif stage == 2:
            s_add(k, 3, "", a)
            s_add(k, 5, "", b)
        else:
            s_add(k, 6, "", d)
            s_out(k)

    def s_out(k):
        _, _, width, at = CHUNKS[k]
        dst = fb.at[m, :, at : at + width]
        for to, member in group:
            remote(g.at[rows_of(to), cols(k, x)], dst, fin_s.at[0], fin_r.at[0], to).start()
        pltpu.make_async_copy(g.at[pl.ds(m16(HALF * f), HALF), cols(k, x)], dst, keep_s.at[0]).start()

    s_at = {}

    def ar_tile(i):
        return slice(SPLIT * i, SPLIT * i + SPLIT)

    def cs_ref(a, p, i):
        rows = OWN if a in (2, 3) else PART
        return cs.at[a % 2, p, 0:rows, ar_tile(i)], cr.at[a % 2, p, 0:rows, ar_tile(i)]

    def total(a):
        return part3 if a == 3 else part

    def ar_begin(a, p):
        if a >= 2:
            left(cs.at[a % 2, p, 0 : OWN if a == 4 else PART, :], cs_s.at[a - 2, p])
        for i in range(2):
            for n, first in enumerate((0, TOK) if a in (2, 3) else (0,)):
                rows = slice(first + OWN * p, first + OWN * p + OWN)
                value = None
                for ref, lo, col, width in operands[a]:
                    more = dot_last(ref[rows, lo : lo + width], w[ar_tile(i), col : col + width])
                    value = more if value is None else value + more
                total(a)[rows, ar_tile(i)] = value
                away = pl.ds(m16(first + OWN * p + oth0), PART)
                cs[a % 2, p, PART * n : PART * n + PART, ar_tile(i)] = total(a)[away, ar_tile(i)].astype(bf16)
            src, there = cs_ref(a, p, i)
            remote(src, there, cs_s.at[a, p], cs_r.at[a, p, i], mate).start()

    def ar_cross(a, p):
        b = a - 2
        near = pl.ds(m16(TOK * x + OWN * p + own0), PART)
        far = pl.ds(m16(TOK * (1 - x) + OWN * p + own0), PART)
        for i in range(2):
            _, here = cs_ref(a, p, i)
            came(here, cs_r.at[a, p, i])
            more = cr[a % 2, p, pl.ds(m16(PART * (1 - x)), PART), ar_tile(i)].astype(f32)
            ys[b, p, :, ar_tile(i)] = (total(a)[far, ar_tile(i)] + more).astype(bf16)
            remote(
                ys.at[b, p, :, ar_tile(i)], yr.at[b, p, :, ar_tile(i)], ys_s.at[0], ys_r.at[b, p, i], along["x"]
            ).start()
            total(a)[near, ar_tile(i)] = total(a)[near, ar_tile(i)] + cr[
                a % 2, p, pl.ds(m16(PART * x), PART), ar_tile(i)
            ].astype(f32)

    def fold_out():
        for p in (0, 1):
            left(xs.at[1, p], xs_s.at[1, p])
        for i in range(2):
            for p in (0, 1):
                came(yr.at[1, p, :, ar_tile(i)], ys_r.at[1, p, i])
            mine = part3[pl.ds(m16(TOK * x + OWN * (1 - l) + own0), PART), ar_tile(i)]
            xs[1, 0, :, ar_tile(i)] = (mine + yr[1, 1 - l, :, ar_tile(i)].astype(f32)).astype(bf16)
            remote(
                xs.at[1, 0, :, ar_tile(i)], xr.at[0, 0, :, ar_tile(i)], xs_s.at[3, 0], xs_r.at[3, 0], beside
            ).start()

    def ar_mid(a, p):
        if a == 3:
            return fold_out()
        b = a % 2
        if a >= 2:
            left(xs.at[b, p], xs_s.at[a - 2, p])
        for i in range(2):
            if a == 2:
                came(yr.at[0, p, :, ar_tile(i)], ys_r.at[0, p, i])
                mine = part[pl.ds(m16(TOK * x + OWN * p + own0), PART), ar_tile(i)]
                more = yr[0, p, :, ar_tile(i)]
            else:
                came(cs_ref(a, p, i)[1], cs_r.at[a, p, i])
                mine = part[pl.ds(m16(OWN * p + own0), PART), ar_tile(i)]
                more = cr[b, p, 0:PART, ar_tile(i)]
            xs[b, p, :, ar_tile(i)] = (mine + more.astype(f32)).astype(bf16)
            remote(
                xs.at[b, p, :, ar_tile(i)], xr.at[a % 3, p, :, ar_tile(i)], xs_s.at[a, p], xs_r.at[a, p], beside
            ).start()

    def ar_end(a, p):
        came(xr.at[a % 3, p], xs_r.at[a, p])

    def summed(a, p, rows):
        return xs[a % 2, p, rows, :].astype(f32) + xr[a % 3, p, rows, :].astype(f32)

    def own_rows(body):
        def step(j, carry):
            body(pl.multiple_of(32 * j, 32))
            return carry

        lax.fori_loop(0, PART // 32, step, 0)

    def at32(start):
        return pl.ds(m16(start), 32)

    def share(j, p, ref, first=0, to=None):
        rows = ref.at[pl.ds(m16(first + OWN * p + own0), PART)]
        remote(rows, rows, nx_s.at[0], nx_r.at[j, p], mate if to is None else to).start()

    def shared(j, p, ref, first=0, start=None):
        came(ref.at[pl.ds(m16(first + OWN * p + (oth0 if start is None else start)), PART)], nx_r.at[j, p])

    def rms(v):
        return lax.rsqrt(jnp.mean(v * v, axis=-1, keepdims=True) + 1e-06)

    def fold(v):
        return jnp.sum(v.reshape(v.shape[0] // 8, 8, v.shape[1]), axis=0)

    def tiles_loop(count, body):
        def step(i, carry):
            body(pl.ds(pl.multiple_of(TILE * i, TILE), TILE), i)
            return carry

        lax.fori_loop(0, count, step, 0)

    def slab(h):
        return slice(128 + 256 * h, 256 + 256 * h)

    spread = one_hot(lax.div(iota((OWN, 12), 0), CTXLEN) == iota((OWN, 12), 1))
    right_patch = lax.div(iota((OWN, 512), 1), PL) == (iota((OWN, 512), 0) & (CTXLEN - 1))
    lane_of = iota((512, 128), 1)
    place_of = iota((512, 128), 0) & (PL - 1)
    mine0 = m16(OWN * l + own0)
    cot_part = cot_in.reshape(2, PART, D)
    cot_rows = cot.reshape(2, TOK, D)
    cot_copy = pltpu.make_async_copy(cot_part, cot_rows.at[:, pl.ds(mine0, PART)], lo_s.at[len(CHUNKS)])
    lane512 = iota((OWN, 512), 1) & 255
    units = lane512 < 160
    resids = (lane512 >= 128 + L_RES) & (lane512 < 128 + L_RES + 8)

    def part_rows(p, first=0):
        return slice(first + OWN * p, first + OWN * p + OWN)

    def features():
        keep = 1.0 - missing[...].astype(f32)
        seen = dot_plain(spread, (points[...].astype(f32) * keep).astype(bf16))
        gone = dot_plain(spread, missing[...].astype(f32).astype(bf16))
        feats = dot_plain(jnp.where(right_patch, seen, 0.0).astype(bf16), one_hot(lane_of == place_of))
        feats = feats + dot_plain(jnp.where(right_patch, gone, 0.0).astype(bf16), one_hot(lane_of == place_of + PL))
        ptx[0:OWN, :] = jnp.where(iota((OWN, 128), 1) == 2 * PL, 1.0, feats)
        fe[pl.ds(mine0, PART), :] = ptx[pl.ds(m16(PART * x), PART), :].astype(bf16)
        for to, member in group:
            rows = fe.at[pl.ds(mine0, PART)]
            remote(rows, rows, tk_s.at[0], tk_r.at[0], to).start()
        sums[...] = jnp.zeros(sums.shape, f32)
        hidf[...] = jnp.zeros(hidf.shape, f32)

    def cot_out():
        cot_copy.start()
        dst = cot_rows.at[:, pl.ds(mine0, PART)]
        remote(cot_part, dst, tk_s.at[1], tk_r.at[1], mate).start()
        remote(cot_part.at[x], cot_rows.at[x, pl.ds(mine0, PART)], tk_s.at[1], tk_r.at[2], beside).start()

    def cot_pass(stage):
        here = pl.ds(m16(OWN * (1 - l) + own0), PART)
        near, far = cot_rows.at[x, here], cot_rows.at[1 - x, here]
        if stage == 0:
            came(near, tk_r.at[2])
            remote(near, near, tk_s.at[1], tk_r.at[3], along["x"]).start()
            remote(near, near, tk_s.at[1], tk_r.at[4], mate).start()
        else:
            came(far, tk_r.at[3])
            remote(far, far, tk_s.at[1], tk_r.at[5], mate).start()

    def cot_here():
        cot_copy.wait()
        came(cot_rows.at[:, pl.ds(m16(OWN * l + oth0), PART)], tk_r.at[1])
        for i, xx in ((4, x), (5, 1 - x)):
            came(cot_rows.at[xx, pl.ds(m16(OWN * (1 - l) + oth0), PART)], tk_r.at[i])

    def hidden():
        for h in (0, 1):
            for j in range(4):
                rows = pl.ds(m16(320 * m + 80 * j), 80)
                tmp[:, 0:128] = w[rows, slab(h)].astype(f32)
                hidf[0:72, 256 * h + 40 * j : 256 * h + 40 * j + 40] = tmp[0:72, L_HID : L_HID + 40]
            row = iota((128, 128), 0)
            lane = iota((128, 128), 1)
            chosen = (lane >= L_RES) & (lane < L_RES + 8) & (row == PL * h + 8 * m + lane - L_RES)
            hidf[:, slab(h)] = jnp.where(chosen, 1.0, hidf[:, slab(h)])
        hid[...] = hidf[...].astype(bf16)
        came(fe.at[0 : 3 * PART], tk_r.at[0])

    def tokenize(p):
        v = dot_plain(fe[part_rows(p), :], hid[...])
        pret[part_rows(p), :] = v
        hc[part_rows(p), :] = jnp.where(
            units, v * jax.nn.sigmoid(v), jnp.where(resids, v, jnp.where(lane512 == 128 + L_ONE, 1.0, 0.0))
        ).astype(bf16)

    def vectors():
        row16 = iota((16, 128), 0)
        lane16 = iota((16, 128), 1)
        vec[...] = dot_last(one_hot((row16 < 4) & (lane16 == L_VEC + row16)), w[:, slab(0)])
        own_slab = pl.ds(pl.multiple_of(128 + 256 * x, 128), 128)
        pair = dot_last(one_hot((row16 < 2) & (lane16 == L_BIN + row16)), w[pl.ds(m16(320 * m), 320), own_slab])
        tmp[0:16, 0:320] = pair
        for j in range(4):
            at = 160 * j
            bin_s[0:1, at : at + 80] = tmp[0:1, 80 * j : 80 * j + 80]
            bin_s[0:1, at + 80 : at + 160] = tmp[1:2, 80 * j : 80 * j + 80]

    def first_norm(p):
        ar_end(0, p)

        def body(start):
            v = summed(0, p, pl.ds(start, 32)) + vec[3:4, :]
            x0[at32(PART * p + start), :] = v
            n1[at32(OWN * p + own0 + start), :] = (v * rms(v) * vec[0:1, :]).astype(bf16)

        own_rows(body)
        share(0, p, n1)

    def project(p):
        shared(0, p, n1)
        rows = part_rows(p)
        for h in (0, 1):
            for lo in (0, 256):
                col = C_QKV + 640 * h + lo
                part[rows, 512 * h + lo : 512 * h + lo + 256] = dot_plain(n1[rows, :], w[:, col : col + 256])

    def turn(p):
        def body(j, carry):
            rows = pl.ds(m16(OWN * p + 48 * j), 48)
            for h in (0, 1):
                v = part[rows, 512 * h : 512 * h + 512]
                v = v * rot_c[...] + pltpu.roll(v, 472, 1) * rot_a[...] + pltpu.roll(v, 40, 1) * rot_b[...]
                q_s[h, rows, :] = v[:, 0:256].astype(bf16)
                k_s[h, rows, :] = pltpu.roll(v, 352, 1)[:, 0:256].astype(bf16)
                v_s[h, rows, :] = pltpu.roll(v, 288, 1)[:, 0:256].astype(bf16)
            return carry

        lax.fori_loop(0, OWN // 48, body, 0)

    def one_head(v, first, i):
        lane = iota(v.shape, 1)
        inside = (lane >= first + HEAD_DIM * i) & (lane < first + HEAD_DIM * i + HEAD_DIM)
        return jnp.where(inside, v, jnp.zeros_like(v))

    def stacked(v, first):
        return jnp.concatenate([one_head(v, first, 0), one_head(v, first, 1)], axis=0)

    def by_head(probs, v, first):
        return dot_plain(probs[0:OWN], one_head(v, first, 0)) + dot_plain(probs[OWN:TOK], one_head(v, first, 1))

    def attend(p):
        rows = part_rows(p)
        qi = iota((TOK, OWN), 0)
        qi = jnp.where(qi >= OWN, qi - OWN, qi)
        kj = iota((TOK, OWN), 1)
        allowed = ((qi >> 4) == (kj >> 4)) & (kj <= qi)
        for h in (0, 1):
            scores = dot_last(stacked(q_s[h, rows, :], 0), k_s[h, rows, :]) * SCALE
            scores = jnp.where(allowed, scores, -1e30)
            e = jnp.exp(scores - jnp.max(scores, axis=-1, keepdims=True))
            probs = e * (1.0 / jnp.sum(e, axis=-1, keepdims=True))
            ps[p, h] = probs
            att[rows, 256 * h : 256 * h + 256] = by_head(probs.astype(bf16), v_s[h, rows, :], 96).astype(bf16)

    def second_norm(p):
        ar_end(1, p)

        def body(start):
            own = at32(PART * p + start)
            v = x0[own, :] + summed(1, p, pl.ds(start, 32))
            x1[own, :] = v
            n2[at32(TOK * x + OWN * p + own0 + start), :] = (v * rms(v) * vec[1:2, :]).astype(bf16)

        own_rows(body)
        share(1, p, n2, TOK * x, along["x"])
        share(4, p, n2, TOK * x)

    def norm_pass(p):
        far = TOK * (1 - x)
        shared(1, p, n2, far, own0)
        rows = n2.at[pl.ds(m16(far + OWN * p + own0), PART)]
        remote(rows, rows, nx_s.at[0], nx_r.at[5, p], mate).start()

    def inner(which, p):
        first = TOK * (x if which == 0 else 1 - x)
        shared(4 if which == 0 else 5, p, n2, first)
        rows = pl.ds(m16(first + OWN * p), OWN)
        for lo, width in MLP_TILES:
            at = slice(lo, lo + width)
            v = dot_plain(n2[rows, :], w[:, C_IN + lo : C_IN + lo + width]) + bin_s[0:1, at]
            pre[rows, at] = v
            act[rows, at] = (v * jax.nn.sigmoid(v)).astype(bf16)

    def outer_back(p):
        for first in (0, TOK):
            rows = part_rows(p, first)
            for lo, width in MLP_TILES:
                at = slice(lo, lo + width)
                v = pre[rows, at]
                s = jax.nn.sigmoid(v)
                d = dot_plain(cot[rows, :], w[:, C_OUT + lo : C_OUT + lo + width])
                dpre[rows, at] = (d * (s * (1.0 + v * (1.0 - s)))).astype(bf16)

    def norm_back(dn, v, gain):
        r = rms(v)
        xh = v * r
        scaled = dn * gain
        inside = jnp.mean(scaled * xh, axis=-1, keepdims=True)
        return r * (scaled - xh * inside), fold(dn * xh)

    def second_back(p):
        ar_end(2, p)

        def body(start):
            own = at32(PART * p + start)
            d, by_gain = norm_back(summed(2, p, pl.ds(start, 32)), x1[own, :], vec[1:2, :])
            ct = cot[at32(TOK * x + OWN * p + own0 + start), :].astype(f32)
            d = ct + d
            x2[own, :] = d
            db[at32(OWN * p + own0 + start), :] = d.astype(bf16)
            sums[8:16, :] += by_gain
            sums[16:24, :] += fold(ct)

        own_rows(body)
        share(2, p, db)

    def attended_back(p):
        shared(2, p, db)
        rows = part_rows(p)
        for h in (0, 1):
            col = C_QKV + 640 * h + 384
            datt[rows, 256 * h : 256 * h + 256] = dot_plain(db[rows, :], w[:, col : col + 256]).astype(bf16)

    def attend_back(p):
        rows = part_rows(p)
        for h in (0, 1):
            probs = ps[p, h]
            heads_d = stacked(datt[rows, 256 * h : 256 * h + 256], 96)
            dp = dot_last(heads_d, v_s[h, rows, :])
            ds = (probs * (dp - jnp.sum(probs * dp, axis=-1, keepdims=True))).astype(bf16)
            part[rows, 512 * h : 512 * h + 256] = by_head(ds, k_s[h, rows, :], 0) * SCALE
            part[rows, 512 * h + 160 : 512 * h + 416] = dot_rows(ds, stacked(q_s[h, rows, :], 0)) * SCALE
            dv = dot_rows(probs.astype(bf16), heads_d)
            dv = jnp.concatenate([dv, jnp.zeros((OWN, 128), f32)], axis=1)
            part[rows, 512 * h + 320 : 512 * h + 512] = dv[:, 96:288]

    def turn_back(p):
        def body(j, carry):
            rows = pl.ds(m16(OWN * p + 48 * j), 48)
            for h in (0, 1):
                v = part[rows, 512 * h : 512 * h + 512]
                v = v * rot_c[...] - pltpu.roll(v, 472, 1) * rot_a[...] - pltpu.roll(v, 40, 1) * rot_b[...]
                dpj[rows, 512 * h : 512 * h + 512] = v.astype(bf16)
            return carry

        lax.fori_loop(0, OWN // 48, body, 0)

    def finish():
        ar_end(3, 0)

        def body(start):
            rows = pl.ds(start, 32)
            v = part3[at32(TOK * x + OWN * l + own0 + start), :] + yr[1, l, rows, :].astype(f32)
            v = v + xr[0, 0, rows, :].astype(f32)
            ob[rows, :] = (x1[at32(PART * l + start), :] + v + vec[2:3, :]).astype(bf16)

        own_rows(body)
        ref = out_o.at[pl.ds(m16(PART * x), PART)]
        go(remote(ob, ref, pt_s.at[3], pt_r.at[3], along["x"]))
        pltpu.make_async_copy(ob, ref, keep_s.at[1]).start()

    def grad_mlp(k, left, right, base):
        first, _, width, _ = CHUNKS[k]

        def body(rows, i):
            lo = first - base
            g[rows, first : first + width] = dot_rows(left[:, rows], right[:, lo : lo + width]).astype(bf16)

        tiles_loop(TILES, body)
        s_start(k)

    def grad_out(k):
        grad_mlp(k, cot, act, C_OUT)

    def grad_in(k):
        grad_mlp(k, n2, dpre, C_IN)

    def grad_qkv(k):
        first, apart, width, _ = CHUNKS[k]
        lo, hi = first - C_QKV, first - C_QKV + width
        mid, cut = min(hi, 512), max(lo, 384)

        def body(rows, i):
            for h in (0, 1):
                col = C_QKV + apart * h
                if lo < mid:
                    value = dot_rows(n1[:, rows], dpj[:, 512 * h + lo : 512 * h + mid])
                    if cut >= mid:
                        g[rows, col + lo : col + mid] = value.astype(bf16)
                    else:
                        more = dot_rows(db[:, rows], att[:, 256 * h + cut - 384 : 256 * h + mid - 384])
                        if cut > lo:
                            g[rows, col + lo : col + cut] = value[:, 0 : cut - lo].astype(bf16)
                        g[rows, col + cut : col + mid] = (value[:, cut - lo :] + more).astype(bf16)
                if hi > 512:
                    start = max(lo, 512)
                    value = dot_rows(db[:, rows], att[:, 256 * h + start - 384 : 256 * h + hi - 384])
                    g[rows, col + start : col + hi] = value.astype(bf16)

        tiles_loop(TILES, body)
        s_start(k)

    def grad_bias():
        ones = one_hot((iota((BOTH, 128), 1) >= L_BIN) & (iota((BOTH, 128), 1) < L_BIN + 2))
        for lo, width in MLP_TILES:
            gbs[lo : lo + width, :] = dot_rows(dpre[:, lo : lo + width], ones)

    def first_back(p):
        ar_end(4, p)

        def body(start):
            own = at32(PART * p + start)
            d, by_gain = norm_back(summed(4, p, pl.ds(start, 32)), x0[own, :], vec[0:1, :])
            de[at32(OWN * p + own0 + start), :] = (x2[own, :] + d).astype(bf16)
            sums[0:8, :] += by_gain

        own_rows(body)
        share(3, p, de)

    def hidden_back(p):
        shared(3, p, de)
        rows = part_rows(p)
        v = pret[rows, :]
        s = jax.nn.sigmoid(v)
        d = dot_plain(de[rows, :], w[:, 0:512])
        dpe[rows, :] = jnp.where(units, d * (s * (1.0 + v * (1.0 - s))), jnp.where(resids, d, 0.0)).astype(bf16)

    def grad_tok():
        row32 = iota((32, 128), 0)
        pick = one_hot((row32 < 24) & (iota((32, 128), 1) == L_VEC + (row32 >> 3)))

        def body(rows, i):
            both = dot_rows(de[:, rows], hc[...])
            columns = dot_rows(sums[:, rows].astype(bf16), pick)
            for h in (0, 1):
                g[rows, 256 * h : 256 * h + 128] = both[:, 256 * h : 256 * h + 128].astype(bf16)
                g[rows, slab(h)] = (both[:, slab(h)] + columns).astype(bf16)

        tiles_loop(TILES, body)
        s_start(0)

    def grad_hidden():
        ghs[...] = dot_rows(fe[...], dpe[...])
        lane = iota((80, 128), 1)
        for h in (0, 1):
            for j in range(4):
                at = 160 * j
                tmp[:, 0:128] = jnp.where((lane == L_BIN) & (x == h), gbs[at : at + 80, :], 0.0) + jnp.where(
                    (lane == L_BIN + 1) & (x == h), gbs[at + 80 : at + 160, :], 0.0
                )
                tmp[:, L_HID : L_HID + 40] = ghs[0:80, 256 * h + 40 * j : 256 * h + 40 * j + 40]
                rows = pl.ds(m16(320 * m + 80 * j), 80)
                g[rows, slab(h)] = (g[rows, slab(h)].astype(f32) + tmp[:, 0:128]).astype(bf16)
        s_start(1)

    def points_back(stage):
        if stage == 0:
            ptx[...] = dot_last(dpe[...], hid[...])
            away = ptx.reshape(2, OWN, 128).at[:, pl.ds(oth0, PART)]
            go(remote(away, ptr.at[0], pt_s.at[0], pt_r.at[0], mate))
        elif stage == 1:
            remote(ptr.at[0], ptr.at[0], pt_s.at[0], pt_r.at[0], mate).wait_recv()
            for p in (0, 1):
                ptr[1, p] = ptx[pl.ds(m16(OWN * p + own0), PART), :] + ptr[0, p]
            go(remote(ptr.at[1, 1 - l], ptr.at[2, 1 - l], pt_s.at[1], pt_r.at[1], beside))
        elif stage == 2:
            there = ptr.at[2, l]
            remote(there, there, pt_s.at[1], pt_r.at[1], beside).wait_recv()
            ptr[3, x] = ptr[1, l] + ptr[2, l]
            go(remote(ptr.at[3, x], ptr.at[3, x], pt_s.at[2], pt_r.at[2], along["x"]))
        else:
            there = ptr.at[3, 1 - x]
            remote(there, there, pt_s.at[2], pt_r.at[2], along["x"]).wait_recv()
            every = ptr[3].reshape(OWN, 128).astype(bf16)
            wide = dot_last(every, one_hot(lane_of == place_of))
            wide = jnp.where(right_patch, wide, 0.0).astype(bf16)
            pts_v[...] = dot_rows(spread, wide) * (1.0 - missing[...].astype(f32))
            pltpu.make_async_copy(pts_v, pts_o, keep_s.at[2]).start()

    operands = (
        ((hc, 0, 0, 512),),
        ((att, 0, 896, 256), (att, 256, 1536, 256)),
        ((dpre, 0, C_IN, 640),),
        ((act, 0, C_OUT, 640),),
        ((dpj, 0, 512, 512), (dpj, 512, 1152, 512)),
    )
    steps = (
        g_first, g_own, g_second, g_third, g_done, s_step, features, cot_out, cot_here, tokenize, vectors,
        first_norm, project, turn, attend, second_norm, inner, grad_out, outer_back, grad_in, second_back,
        attended_back, attend_back, turn_back, finish, grad_qkv, grad_bias, first_back, hidden_back, grad_tok,
        grad_hidden, points_back, ar_begin, ar_mid, cot_pass, norm_pass, ar_cross, hidden,
    )
    for name, *which in PLAN:
        steps[name](*which)

    came(out_o.at[pl.ds(m16(PART * (1 - x)), PART)], pt_r.at[3])
    came(fb.at[0:3], fin_r.at[0])
    pltpu.make_async_copy(g.at[0:HALF, 0:C_ONE], fb.at[m], keep_s.at[0]).wait()
    pltpu.make_async_copy(ob, out_o.at[pl.ds(m16(PART * x), PART)], keep_s.at[1]).wait()
    pltpu.make_async_copy(pts_v, pts_o, keep_s.at[2]).wait()
    for ref, sem in (
        (rb, ag_s.at[0]), (rbm, ag_s.at[1]), (rb, rs_s.at[0]), (rbm, rs_s.at[1]),
        (w.at[0 : 3 * HALF, 0:C_ONE], in_s.at[0]), (g.at[0 : 3 * HALF, 0:C_ONE], fin_s.at[0]),
        (cs.at[1, 0], cs_s.at[3, 0]), (cs.at[1, 1], cs_s.at[3, 1]),
        (cs.at[0, 0, 0:PART], cs_s.at[4, 0]), (cs.at[0, 1, 0:PART], cs_s.at[4, 1]),
        (xs.at[1, 0], xs_s.at[3, 0]), (xs.at[0, 0], xs_s.at[4, 0]), (xs.at[0, 1], xs_s.at[4, 1]),
        (ys, ys_s.at[0]), (w.at[0 : 12 * PART, 0:D], nx_s.at[0]),
        (fe.at[0 : 3 * PART], tk_s.at[0]), (cot.at[0 : 6 * PART], tk_s.at[1]),
    ):
        left(ref, sem)
    for copy in sent:
        copy.wait_send()


def unpack_kernel(
    out_i, pts_i, fb_i,
    out_o, pts_o, hw_o, hb_o, tok_o, res_o, tokb_o, gain1_o, qkv_o, att_o, gain2_o, in_o, inb_o, outw_o, outb_o,
    fb, sem,
):
    f32 = jnp.float32
    copies = [pltpu.make_async_copy(fb_i.at[q], fb.at[q], sem.at[q]) for q in range(4)]
    copies.append(pltpu.make_async_copy(out_i, out_o, sem.at[4]))
    for copy in copies:
        copy.start()
    pts_o[...] = pts_i[...]
    turned = []
    hidden = jnp.zeros((8, 128), f32)
    for q in range(4):
        copies[q].wait()
        at = slice(160 * q, 160 * q + 160)
        lead = fb[q, :, 0:256].astype(f32)
        tok_o[:, at] = lead[:, 0:160]
        tile = lead[:, 128:256]
        hidden = hidden + tile[64:72]
        t = jnp.transpose(jnp.concatenate([tile, jnp.zeros((48, 128), f32)], axis=0))
        turned.append(t)
        res_o[8 * q : 8 * q + 8, :] = t[L_RES : L_RES + 8, 0:80]
        qkv = fb[q, :, 256:896].astype(f32)
        for j in range(3):
            qkv_o[j, :, at] = qkv[:, 160 * j : 160 * j + 160]
        att_o[:, at] = qkv[:, 480:640]
        in_o[:, 640 * q : 640 * q + 640] = fb[q, :, 896:1536].astype(f32)
        outw_o[:, 640 * q : 640 * q + 640] = fb[q, :, 1536:2176].astype(f32)
    both = turned[0] + turned[1]
    every = both + turned[2] + turned[3]
    tokb_o[...] = turned[0][L_ONE : L_ONE + 1, 0:80]
    gain1_o[...] = both[L_VEC : L_VEC + 1, 0:80]
    gain2_o[...] = both[L_VEC + 1 : L_VEC + 2, 0:80]
    outb_o[...] = both[L_VEC + 2 : L_VEC + 3, 0:80]
    inb_o[:, 0:80] = every[L_BIN : L_BIN + 1, 0:80]
    inb_o[:, 80:160] = every[L_BIN + 1 : L_BIN + 2, 0:80]
    hw_o[...] = every[L_HID : L_HID + 40, 0:64]
    hb_o[...] = hidden[0:1, L_HID : L_HID + 40]
    copies[4].wait()


def rotary_lanes():
    lanes = np.arange(512)
    inside = lanes % HEAD_DIM
    turned = lanes < 320
    freqs = 10000.0 ** (-2.0 * (inside % 40) / HEAD_DIM)
    angles = (np.arange(48) % CTXLEN)[:, None] * freqs[None, :]
    cosine = np.where(turned, np.cos(angles), 1.0)
    sine = np.where(turned, np.sin(angles), 0.0)
    lower = np.where(inside < 40, -sine, 0.0)
    upper = np.where(inside >= 40, sine, 0.0)
    return [np.asarray(t, np.float32) for t in (cosine, lower, upper)]


def fast_body(
    points, missing, tok_hidden_w, tok_hidden_b, tok_out_w, tok_res_w, tok_out_b, attn_gain, qkv_w, attn_out_w,
    mlp_gain, mlp_in_w, mlp_in_b, mlp_out_w, mlp_out_b, cotangent,
):
    f32, bf16 = jnp.float32, jnp.bfloat16
    any_space = pl.BlockSpec(memory_space=pl.ANY)
    vmem = pl.BlockSpec(memory_space=pltpu.VMEM)

    def sems(*shape):
        return pltpu.SemaphoreType.DMA(shape)

    def like(*shape):
        return jax.ShapeDtypeStruct(shape, f32)

    chunks = len(CHUNKS)
    wide = sum(1 for chunk in CHUNKS if chunk[3] < C_MLP)
    specs = [vmem] * 19
    specs[11] = specs[13] = specs[15] = any_space
    out, pts, packed = pl.pallas_call(
        layer_kernel,
        out_shape=(
            jax.ShapeDtypeStruct((OWN, D), bf16),
            like(12, 512),
            jax.ShapeDtypeStruct((4, HALF, C_ONE), bf16),
        ),
        in_specs=specs,
        out_specs=[any_space] * 3,
        scratch_shapes=[
            pltpu.VMEM((D, C_ALL), bf16),
            pltpu.VMEM((D, C_ALL), bf16),
            pltpu.VMEM((7, 2, 160, C_MLP), bf16),
            pltpu.VMEM((3, 2, 160, C_ONE - C_MLP), bf16),
            pltpu.VMEM((TOK, 128), bf16),
            pltpu.VMEM((BOTH, D), bf16),
            pltpu.VMEM((BOTH, D), f32),
            pltpu.VMEM((BOTH, 640), f32),
            pltpu.VMEM((BOTH, 640), bf16),
            pltpu.VMEM((BOTH, 640), bf16),
            pltpu.VMEM((TOK, D), bf16),
            pltpu.VMEM((BOTH, D), bf16),
            pltpu.VMEM((TOK, D), bf16),
            pltpu.VMEM((TOK, D), bf16),
            pltpu.VMEM((OWN, D), f32),
            pltpu.VMEM((OWN, D), f32),
            pltpu.VMEM((OWN, D), f32),
            pltpu.VMEM((TOK, 512), bf16),
            pltpu.VMEM((TOK, 512), bf16),
            pltpu.VMEM((TOK, 512), f32),
            pltpu.VMEM((2, TOK, 256), bf16),
            pltpu.VMEM((2, TOK, 256), bf16),
            pltpu.VMEM((2, TOK, 256), bf16),
            pltpu.VMEM((TOK, 512), bf16),
            pltpu.VMEM((TOK, 512), bf16),
            pltpu.VMEM((TOK, 1024), bf16),
            pltpu.VMEM((2, 2, TOK, OWN), f32),
            pltpu.VMEM((640, 128), f32),
            pltpu.VMEM((128, 512), f32),
            pltpu.VMEM((128, 512), f32),
            pltpu.VMEM((128, 512), bf16),
            pltpu.VMEM((16, D), f32),
            pltpu.VMEM((8, 640), f32),
            pltpu.VMEM((32, D), f32),
            pltpu.VMEM((TOK, 128), f32),
            pltpu.VMEM((4, 2, PART, 128), f32),
            pltpu.VMEM((4, HALF, 896), bf16),
            pltpu.VMEM((HALF, 896), f32),
            pltpu.VMEM((HALF, 128), f32),
            pltpu.VMEM((HALF, 384), f32),
            pltpu.VMEM((BOTH, D), f32),
            pltpu.VMEM((PART, D), bf16),
            pltpu.VMEM((12, 512), f32),
            pltpu.VMEM((2, 2, OWN, D), bf16),
            pltpu.VMEM((2, 2, OWN, D), bf16),
            pltpu.VMEM((2, 2, PART, D), bf16),
            pltpu.VMEM((2, 2, PART, D), bf16),
            pltpu.VMEM((2, 2, PART, D), bf16),
            pltpu.VMEM((3, 2, PART, D), bf16),
            sems(2), sems(4 * wide + 2 * (chunks - wide)), sems(2), sems(7 * wide + 3 * (chunks - wide)),
            sems(5, 2), sems(5, 2, 2), sems(5, 2), sems(5, 2), sems(1), sems(2, 2, 2),
            sems(1), sems(6, 2), sems(1), sems(chunks), sems(chunks + 1), sems(2), sems(6),
            sems(1), sems(1), sems(4), sems(4), sems(3),
        ],
        compiler_params=pltpu.CompilerParams(
            collective_id=0, has_side_effects=True, vmem_limit_bytes=64 * 1024 * 1024 - 512 * 1024
        ),
        cost_estimate=pl.CostEstimate(flops=13 * 10**9, bytes_accessed=10**7, transcendentals=10**6),
    )(
        points, missing, tok_hidden_w[0], tok_hidden_b, tok_out_w, tok_res_w.T, tok_out_b[None], attn_gain[None],
        qkv_w.transpose(1, 0, 2), attn_out_w, mlp_gain[None], mlp_in_w, mlp_in_b, mlp_out_w, mlp_out_b[None],
        cotangent, *[jnp.asarray(t) for t in rotary_lanes()],
    )
    (
        output, points_grad, hidden_w, hidden_b, tok, res_t, tok_b, gain1, qkv, att, gain2, inner, inner_b, outer,
        outer_b,
    ) = pl.pallas_call(
        unpack_kernel,
        out_shape=(
            jax.ShapeDtypeStruct((OWN, D), bf16),
            like(12, 512), like(40, 64), like(1, 40), like(HALF, 640), like(32, HALF), like(1, HALF), like(1, HALF),
            like(3, HALF, 640), like(HALF, 640), like(1, HALF), like(HALF, 2560), like(1, 160), like(HALF, 2560),
            like(1, HALF),
        ),
        in_specs=[any_space, vmem, any_space],
        out_specs=[vmem] * 15,
        scratch_shapes=[pltpu.VMEM((4, HALF, C_ONE), bf16), sems(5)],
        compiler_params=pltpu.CompilerParams(vmem_limit_bytes=63 * 1024 * 1024),
    )(out, pts, packed)
    return (
        output, points_grad, hidden_w[None], hidden_b, tok, res_t.T, tok_b[0], gain1[0], qkv.transpose(1, 0, 2), att,
        gain2[0], inner, inner_b, outer, outer_b[0],
    )


def solution(mesh):
    placed = (
        P("fsdp", None),
        P("fsdp", None),
        P("tp", "fsdp", None),
        P("tp", "fsdp"),
        P("fsdp", "tp"),
        P("fsdp", "tp"),
        P("fsdp"),
        P("fsdp"),
        P("fsdp", None, "tp"),
        P("fsdp", "tp"),
        P("fsdp"),
        P("fsdp", "tp"),
        P("tp", "fsdp"),
        P("fsdp", "tp"),
        P("fsdp"),
        P("fsdp", None),
    )
    small_slice = mesh.shape["fsdp"] == 16 and mesh.shape["tp"] == 2
    return jax.shard_map(
        fast_body if small_slice else body,
        mesh=mesh,
        in_specs=placed,
        out_specs=(
            P("fsdp", None),
            P("fsdp", None),
            P("tp", "fsdp", None),
            P("tp", "fsdp"),
            P("fsdp", "tp"),
            P("fsdp", "tp"),
            P("fsdp"),
            P("fsdp"),
            P("fsdp", None, "tp"),
            P("fsdp", "tp"),
            P("fsdp"),
            P("fsdp", "tp"),
            P("tp", "fsdp"),
            P("fsdp", "tp"),
            P("fsdp"),
        ),
        check_vma=False,
    )
```

```python
import math

import jax
import jax.numpy as jnp
import numpy as np
from jax import lax
from jax.experimental import pallas as pl
from jax.experimental.pallas import tpu as pltpu
from jax.sharding import PartitionSpec as P

D = 1280
HEAD_DIM = 80
PL = 32
CTXLEN = 16


def dot_plain(left, right):
    return jnp.dot(left, right, preferred_element_type=jnp.float32)


def dot_last(left, right):
    return lax.dot_general(
        left, right, (((1,), (1,)), ((), ())), preferred_element_type=jnp.float32
    )


def dot_rows(left, right):
    return lax.dot_general(
        left, right, (((0,), (0,)), ((), ())), preferred_element_type=jnp.float32
    )


def silu_slope(values):
    sigma = jax.nn.sigmoid(values)
    return sigma * (1.0 + values * (1.0 - sigma))


def rotary_tables():
    positions = jnp.arange(CTXLEN, dtype=jnp.float32)
    freqs = 10000.0 ** (-2.0 * jnp.arange(HEAD_DIM // 2, dtype=jnp.float32) / HEAD_DIM)
    angles = positions[:, None] * freqs[None, :]
    return (jnp.cos(angles)[None, :, None, :], jnp.sin(angles)[None, :, None, :])


def rotate(vector, cosine, sine):
    half = vector.shape[-1] // 2
    first = vector[..., :half]
    second = vector[..., half:]
    return jnp.concatenate(
        [first * cosine - second * sine, second * cosine + first * sine], axis=-1
    )


def rotate_back(vector, cosine, sine):
    half = vector.shape[-1] // 2
    first = vector[..., :half]
    second = vector[..., half:]
    return jnp.concatenate(
        [first * cosine + second * sine, second * cosine - first * sine], axis=-1
    )


def norm_stats(values):
    factor = lax.rsqrt(jnp.mean(values * values, axis=-1, keepdims=True) + 1e-06)
    return (factor, values * factor)


def norm_back(grad, normal, factor, gain):
    scaled = grad * gain
    inner = jnp.mean(scaled * normal, axis=-1, keepdims=True)
    return (factor * (scaled - normal * inner), jnp.sum(grad * normal, axis=0))


def body(
    points,
    missing,
    tok_hidden_w,
    tok_hidden_b,
    tok_out_w,
    tok_res_w,
    tok_out_b,
    attn_gain,
    qkv_w,
    attn_out_w,
    mlp_gain,
    mlp_in_w,
    mlp_in_b,
    mlp_out_w,
    mlp_out_b,
    cotangent,
):
    gathered = (
        lax.all_gather(tok_hidden_w, "fsdp", axis=1, tiled=True),
        lax.all_gather(tok_hidden_b, "fsdp", axis=1, tiled=True),
        lax.all_gather(tok_out_w, "fsdp", axis=0, tiled=True),
        lax.all_gather(tok_res_w, "fsdp", axis=0, tiled=True),
        lax.all_gather(tok_out_b, "fsdp", axis=0, tiled=True),
        lax.all_gather(attn_gain, "fsdp", axis=0, tiled=True),
        lax.all_gather(qkv_w, "fsdp", axis=0, tiled=True),
        lax.all_gather(attn_out_w, "fsdp", axis=0, tiled=True),
        lax.all_gather(mlp_gain, "fsdp", axis=0, tiled=True),
        lax.all_gather(mlp_in_w, "fsdp", axis=0, tiled=True),
        lax.all_gather(mlp_in_b, "fsdp", axis=1, tiled=True),
        lax.all_gather(mlp_out_w, "fsdp", axis=0, tiled=True),
        lax.all_gather(mlp_out_b, "fsdp", axis=0, tiled=True),
    )
    (
        hidden_full,
        hidden_bias,
        token_full,
        residual_full,
        token_bias,
        first_gain,
        project_full,
        attend_full,
        second_gain,
        inner_full,
        inner_bias,
        outer_full,
        outer_bias,
    ) = gathered
    contexts = points.shape[0]
    rows = contexts * CTXLEN
    tensor_rank = lax.axis_index("tp")
    kept_mask = (1 - missing).astype(jnp.float32).reshape(rows, PL)
    absent = missing.astype(jnp.float32).reshape(rows, PL)
    observed = points.astype(jnp.float32).reshape(rows, PL) * kept_mask
    features = jnp.concatenate([observed, absent], axis=1).astype(jnp.bfloat16)
    half_features = jnp.where(tensor_rank == 0, observed, absent).astype(jnp.bfloat16)
    hidden_matrix = hidden_full.reshape(-1, 2 * PL)
    pre_tok = dot_last(features, hidden_matrix) + hidden_bias.reshape(-1).astype(jnp.float32)
    hidden_tok = jax.nn.silu(pre_tok).astype(jnp.bfloat16)
    partial_tok = dot_last(hidden_tok, token_full) + dot_last(half_features, residual_full)
    embedded = lax.psum(partial_tok.astype(jnp.bfloat16), "tp").astype(jnp.float32)
    state_zero = embedded + token_bias.astype(jnp.float32)
    factor_one, normal_one = norm_stats(state_zero)
    normed_one = (normal_one * first_gain.astype(jnp.float32)).astype(jnp.bfloat16)
    local_width = project_full.shape[2]
    local_heads = local_width // HEAD_DIM
    project_matrix = project_full.reshape(D, 3 * local_width)
    projected = dot_plain(normed_one, project_matrix).reshape(
        contexts, CTXLEN, 3, local_heads, HEAD_DIM
    )
    cosine, sine = rotary_tables()
    queries = rotate(projected[:, :, 0], cosine, sine).astype(jnp.bfloat16)
    keys_rot = rotate(projected[:, :, 1], cosine, sine).astype(jnp.bfloat16)
    values_b = projected[:, :, 2].astype(jnp.bfloat16)
    scale = 1.0 / math.sqrt(HEAD_DIM)
    causal = jnp.arange(CTXLEN)[:, None] >= jnp.arange(CTXLEN)[None, :]

    def scores_of(left, right):
        raw = jnp.einsum("cihd,cjhd->chij", left, right, preferred_element_type=jnp.float32) * scale
        return jnp.where(causal, raw, -1e30)

    scores = scores_of(queries, keys_rot)
    row_top = jnp.max(scores, axis=-1, keepdims=True)
    log_total = row_top + jnp.log(jnp.sum(jnp.exp(scores - row_top), axis=-1, keepdims=True))
    probs_b = jnp.exp(scores - log_total).astype(jnp.bfloat16)
    attended = jnp.einsum("chij,cjhd->cihd", probs_b, values_b, preferred_element_type=jnp.float32)
    attended = attended.astype(jnp.bfloat16).reshape(rows, local_width)
    branch_attn = lax.psum(dot_last(attended, attend_full).astype(jnp.bfloat16), "tp").astype(
        jnp.float32
    )
    state_one = state_zero + branch_attn
    factor_two, normal_two = norm_stats(state_one)
    normed_two = (normal_two * second_gain.astype(jnp.float32)).astype(jnp.bfloat16)
    pre_mlp = dot_plain(normed_two, inner_full) + inner_bias.reshape(-1).astype(jnp.float32)
    activation = jax.nn.silu(pre_mlp).astype(jnp.bfloat16)
    branch_mlp = lax.psum(dot_last(activation, outer_full).astype(jnp.bfloat16), "tp").astype(
        jnp.float32
    )
    output = (state_one + branch_mlp + outer_bias.astype(jnp.float32)).astype(jnp.bfloat16)
    again = (
        lax.all_gather(tok_hidden_w, "fsdp", axis=1, tiled=True),
        lax.all_gather(tok_hidden_b, "fsdp", axis=1, tiled=True),
        lax.all_gather(tok_out_w, "fsdp", axis=0, tiled=True),
        lax.all_gather(tok_res_w, "fsdp", axis=0, tiled=True),
        lax.all_gather(tok_out_b, "fsdp", axis=0, tiled=True),
        lax.all_gather(attn_gain, "fsdp", axis=0, tiled=True),
        lax.all_gather(qkv_w, "fsdp", axis=0, tiled=True),
        lax.all_gather(attn_out_w, "fsdp", axis=0, tiled=True),
        lax.all_gather(mlp_gain, "fsdp", axis=0, tiled=True),
        lax.all_gather(mlp_in_w, "fsdp", axis=0, tiled=True),
        lax.all_gather(mlp_in_b, "fsdp", axis=1, tiled=True),
        lax.all_gather(mlp_out_w, "fsdp", axis=0, tiled=True),
        lax.all_gather(mlp_out_b, "fsdp", axis=0, tiled=True),
    )
    (
        hidden_full,
        hidden_bias,
        token_full,
        residual_full,
        token_bias,
        first_gain,
        project_full,
        attend_full,
        second_gain,
        inner_full,
        inner_bias,
        outer_full,
        outer_bias,
    ) = again
    hidden_matrix = hidden_full.reshape(-1, 2 * PL)
    project_matrix = project_full.reshape(D, 3 * local_width)
    grad_outer_bias = jnp.sum(cotangent, axis=0, dtype=jnp.float32)
    grad_outer = dot_rows(cotangent, activation)
    d_pre = (dot_plain(cotangent, outer_full) * silu_slope(pre_mlp)).astype(jnp.bfloat16)
    grad_inner_bias = jnp.sum(d_pre, axis=0, dtype=jnp.float32).reshape(1, -1)
    grad_inner = dot_rows(normed_two, d_pre)
    d_normed_two = lax.psum(dot_last(d_pre, inner_full).astype(jnp.bfloat16), "tp").astype(
        jnp.float32
    )
    through_two, grad_second_gain = norm_back(
        d_normed_two, normal_two, factor_two, second_gain.astype(jnp.float32)
    )
    d_state_one = cotangent.astype(jnp.float32) + through_two
    d_branch = d_state_one.astype(jnp.bfloat16)
    grad_attend = dot_rows(d_branch, attended)
    d_attended = (
        dot_plain(d_branch, attend_full)
        .astype(jnp.bfloat16)
        .reshape(contexts, CTXLEN, local_heads, HEAD_DIM)
    )
    probs = jnp.exp(scores_of(queries, keys_rot) - log_total)
    probs_b = probs.astype(jnp.bfloat16)
    d_probs = jnp.einsum(
        "cihd,cjhd->chij", d_attended, values_b, preferred_element_type=jnp.float32
    )
    d_values = jnp.einsum(
        "chij,cihd->cjhd", probs_b, d_attended, preferred_element_type=jnp.float32
    ).astype(jnp.bfloat16)
    row_inner = jnp.sum(probs * d_probs, axis=-1, keepdims=True)
    d_scores = (probs * (d_probs - row_inner)).astype(jnp.bfloat16)
    d_queries = (
        jnp.einsum("chij,cjhd->cihd", d_scores, keys_rot, preferred_element_type=jnp.float32)
        * scale
    )
    d_keys = (
        jnp.einsum("chij,cihd->cjhd", d_scores, queries, preferred_element_type=jnp.float32) * scale
    )
    d_queries = rotate_back(d_queries, cosine, sine).astype(jnp.bfloat16)
    d_keys = rotate_back(d_keys, cosine, sine).astype(jnp.bfloat16)
    d_projected = jnp.stack([d_queries, d_keys, d_values], axis=2).reshape(rows, 3 * local_width)
    grad_project = dot_rows(normed_one, d_projected).reshape(D, 3, local_width)
    d_normed_one = lax.psum(
        dot_last(d_projected, project_matrix).astype(jnp.bfloat16), "tp"
    ).astype(jnp.float32)
    through_one, grad_first_gain = norm_back(
        d_normed_one, normal_one, factor_one, first_gain.astype(jnp.float32)
    )
    d_state_zero = d_state_one + through_one
    grad_token_bias = jnp.sum(d_state_zero, axis=0)
    d_embedded = d_state_zero.astype(jnp.bfloat16)
    grad_token = dot_rows(d_embedded, hidden_tok)
    grad_residual = dot_rows(d_embedded, half_features)
    d_pre_tok = (dot_plain(d_embedded, token_full) * silu_slope(pre_tok)).astype(jnp.bfloat16)
    grad_hidden_bias = jnp.sum(d_pre_tok, axis=0, dtype=jnp.float32).reshape(1, -1)
    grad_hidden = dot_rows(d_pre_tok, features).reshape(1, -1, 2 * PL)
    through_hidden = dot_plain(d_pre_tok, hidden_matrix)[:, :PL]
    through_residual = dot_plain(d_embedded, residual_full)
    point_terms = through_hidden + jnp.where(tensor_rank == 0, through_residual, 0.0)
    point_sums = lax.psum(point_terms, "tp")
    points_grad = (point_sums * kept_mask).reshape(contexts, CTXLEN * PL)
    owned = (
        lax.psum_scatter(grad_hidden, "fsdp", scatter_dimension=1, tiled=True),
        lax.psum_scatter(grad_hidden_bias, "fsdp", scatter_dimension=1, tiled=True),
        lax.psum_scatter(grad_token, "fsdp", scatter_dimension=0, tiled=True),
        lax.psum_scatter(grad_residual, "fsdp", scatter_dimension=0, tiled=True),
        lax.psum_scatter(grad_token_bias, "fsdp", scatter_dimension=0, tiled=True),
        lax.psum_scatter(grad_first_gain, "fsdp", scatter_dimension=0, tiled=True),
        lax.psum_scatter(grad_project, "fsdp", scatter_dimension=0, tiled=True),
        lax.psum_scatter(grad_attend, "fsdp", scatter_dimension=0, tiled=True),
        lax.psum_scatter(grad_second_gain, "fsdp", scatter_dimension=0, tiled=True),
        lax.psum_scatter(grad_inner, "fsdp", scatter_dimension=0, tiled=True),
        lax.psum_scatter(grad_inner_bias, "fsdp", scatter_dimension=1, tiled=True),
        lax.psum_scatter(grad_outer, "fsdp", scatter_dimension=0, tiled=True),
        lax.psum_scatter(grad_outer_bias, "fsdp", scatter_dimension=0, tiled=True),
    )
    return (
        output,
        points_grad,
        owned[0],
        owned[1],
        owned[2],
        owned[3],
        owned[4],
        owned[5],
        owned[6],
        owned[7],
        owned[8],
        owned[9],
        owned[10],
        owned[11],
        owned[12],
    )


MESH = pl.DeviceIdType.MESH
TOK = 384
OWN = 192
PART = 96
HALF = 80
C_QKV, C_IN, C_OUT, C_ALL, C_ONE = 512, 1792, 2432, 3072, 2176
C_MLP = 896
BOTH = 2 * TOK
MLP_TILES = ((0, 256), (256, 256), (512, 128))
SPLIT = 640
CHUNKS = (
    (0, 256, 128, 0),
    (128, 256, 128, 128),
    (512, 640, 256, 256),
    (768, 640, 256, 512),
    (1024, 640, 128, 768),
    (1792, 0, 256, 896),
    (2048, 0, 384, 1152),
    (2432, 0, 256, 1536),
    (2688, 0, 256, 1792),
    (2944, 0, 128, 2048),
)
GATHER_ORDER = ("zyx", "zxy", "zyx", "zyx", "zxy", "zy", "zy", "zy", "zy", "zy")
SUM_ORDER = ("xyz", "xyz", "yxz", "xyz", "xyz", "yz", "yz", "yz", "yz", "yz")
(
    FIRST, OWNED, SECOND, THIRD, HERE, SUM, FEATS, COT, COT_HERE, TOKENS, VECTORS, NORM_1, PROJECT, TURN, ATTEND,
    NORM_2, INNER, GRAD_OUT, OUTER, GRAD_IN, BACK_2, D_ATT, ATTEND_B, TURN_B, FINISH, GRAD_QKV, GRAD_BIAS, BACK_1,
    D_HID, GRAD_TOK, GRAD_HID, POINTS, SEND, PASS, COT_PASS, NORM_PASS, CROSS, HIDDEN,
) = range(38)
PLAN = (
    (FIRST, 1), (FIRST, 0), (FIRST, 3), (FIRST, 4), (OWNED, 1), (FIRST, 2), (OWNED, 0), (FIRST, 5), (FIRST, 9),
    (OWNED, 3), (FEATS,), (FIRST, 6), (SECOND, 1), (OWNED, 4), (SECOND, 0), (THIRD, 1), (THIRD, 0), (OWNED, 2),
    (FIRST, 8), (HERE, 1), (FIRST, 7), (SECOND, 3), (HERE, 0), (OWNED, 5), (HIDDEN,), (VECTORS,), (TOKENS, 1),
    (SEND, 0, 1), (TOKENS, 0), (SECOND, 4), (PASS, 0, 1), (SEND, 0, 0), (THIRD, 3), (OWNED, 6), (OWNED, 7),
    (PASS, 0, 0), (SECOND, 2), (NORM_1, 1), (THIRD, 4), (COT,), (SECOND, 5), (THIRD, 2), (OWNED, 8), (HERE, 3),
    (HERE, 2), (PROJECT, 1), (TURN, 1), (NORM_1, 0), (HERE, 4), (ATTEND, 1), (SEND, 1, 1), (SECOND, 6), (PASS, 1, 1),
    (PROJECT, 0), (TURN, 0), (ATTEND, 0), (SEND, 1, 0), (COT_PASS, 0), (SECOND, 8), (PASS, 1, 0), (NORM_2, 1),
    (OWNED, 9), (HERE, 5), (COT_PASS, 1), (SECOND, 7), (NORM_2, 0), (SECOND, 9), (NORM_PASS, 1), (HERE, 6),
    (INNER, 0, 1), (HERE, 7), (HERE, 8), (COT_HERE,), (INNER, 1, 1), (INNER, 0, 0), (HERE, 9), (OUTER, 1),
    (NORM_PASS, 0), (SEND, 2, 1), (INNER, 1, 0), (CROSS, 2, 1), (GRAD_OUT, 7), (OUTER, 0), (SEND, 2, 0), (SEND, 3, 0),
    (PASS, 2, 1), (CROSS, 2, 0), (GRAD_OUT, 8), (SUM, 7), (GRAD_IN, 6), (GRAD_IN, 5), (PASS, 2, 0), (BACK_2, 1),
    (CROSS, 3, 0), (SEND, 3, 1), (D_ATT, 1), (SUM, 8), (ATTEND_B, 1), (TURN_B, 1), (SEND, 4, 1), (CROSS, 3, 1),
    (SUM, 8), (PASS, 4, 1), (BACK_2, 0), (GRAD_OUT, 9), (SUM, 6), (D_ATT, 0), (GRAD_QKV, 4), (ATTEND_B, 0),
    (TURN_B, 0), (SEND, 4, 0), (GRAD_QKV, 3), (PASS, 4, 0), (SUM, 5), (SUM, 4), (GRAD_QKV, 2), (GRAD_BIAS,), (SUM, 9),
    (BACK_1, 1), (SUM, 9), (SUM, 7), (SUM, 6), (D_HID, 1), (SUM, 4), (SUM, 3), (BACK_1, 0), (PASS, 3, 0), (SUM, 6),
    (D_HID, 0), (POINTS, 0), (SUM, 2), (SUM, 8), (GRAD_TOK,), (SUM, 2), (SUM, 9), (SUM, 7), (GRAD_HID,), (SUM, 5),
    (SUM, 4), (FINISH,), (POINTS, 1), (SUM, 2), (SUM, 3), (SUM, 0), (SUM, 4), (SUM, 0), (SUM, 1), (SUM, 2), (SUM, 1),
    (SUM, 5), (SUM, 0), (SUM, 1), (POINTS, 2), (SUM, 3), (SUM, 0), (SUM, 3), (SUM, 1), (POINTS, 3),
)
L_RES, L_ONE, L_VEC, L_BIN, L_HID = 32, 40, 41, 45, 47
TILE = 256
TILES = D // TILE
SCALE = 1.0 / math.sqrt(HEAD_DIM)


def iota(shape, dim):
    return lax.broadcasted_iota(jnp.int32, shape, dim)


def one_hot(cond):
    return jnp.where(cond, 1.0, 0.0).astype(jnp.bfloat16)


def layer_kernel(
    points, missing, hid_w, hid_b, tok_in, res_t, tok_b, gain1, qkv_in, att_in, gain2, win_in, b_in, wout_in,
    out_b, cot_in, rot_c, rot_a, rot_b,
    out_o, pts_o, fb,
    w, g, rb, rbm, fe, cot, part, pre, act, dpre, n1, n2, db, de, x0, x1, x2,
    hc, dpe, pret, q_s, k_s, v_s, att, datt, dpj, ps, gbs, ghs, hidf, hid, vec, bin_s, sums, ptx, ptr,
    pk, pkf, srcf, tmp,
    part3, ob, pts_v, cs, cr, ys, yr, xs, xr,
    ag_s, ag_r, rs_s, rs_r, cs_s, cs_r, xs_s, xs_r, ys_s, ys_r, nx_s, nx_r, in_s, in_r, lo_s, tk_s, tk_r,
    fin_s, fin_r, pt_s, pt_r, keep_s,
):
    f32, bf16 = jnp.float32, jnp.bfloat16
    f = lax.axis_index("fsdp")
    x = lax.axis_index("tp")
    z = lax.div(f, 4)
    zh = lax.div(z, 2)
    l = z - 2 * zh
    y = lax.div(f, 2) - 2 * z
    c = f - 4 * z - 2 * y
    m = 2 * l + c
    mate = {"fsdp": f + 1 - 2 * c}
    beside = {"fsdp": f + 4 - 8 * l}
    corner = {"fsdp": f + 4 - 8 * l + 1 - 2 * c}
    along = {"z": {"fsdp": f + 8 - 16 * zh}, "y": {"fsdp": f + 2 - 4 * y}, "x": {"tp": 1 - x}}
    own0 = pl.multiple_of(PART * c, PART)
    oth0 = pl.multiple_of(PART * (1 - c), PART)

    def m16(v):
        return pl.multiple_of(v, 16)

    def remote(src, dst, s_sem, r_sem, to):
        return pltpu.make_async_remote_copy(
            src_ref=src, dst_ref=dst, send_sem=s_sem, recv_sem=r_sem, device_id=to, device_id_type=MESH
        )

    sent = []

    def go(copy):
        copy.start()
        sent.append(copy)

    def came(ref, sem):
        remote(ref, ref, sem, sem, mate).wait_recv()

    def left(ref, sem):
        remote(ref, ref, sem, sem, mate).wait_send()

    barrier = pltpu.get_barrier_semaphore()
    peers = (along["z"], corner, beside, along["y"], along["x"], mate)
    for to in peers:
        pl.semaphore_signal(barrier, inc=1, device_id=to, device_id_type=MESH)

    part[0:80, 0:640] = tok_in[...].astype(f32)
    part[80:160, 0:640] = att_in[...].astype(f32)
    part[160:240, 0:640] = qkv_in[0].astype(f32)
    part[240:320, 0:640] = qkv_in[1].astype(f32)
    part[0:80, 640:1280] = qkv_in[2].astype(f32)
    srcf[...] = jnp.zeros(srcf.shape, f32)
    srcf[0:32, 0:80] = res_t[...].astype(f32)
    for i, v in enumerate((gain1, gain2, out_b, tok_b)):
        srcf[32 + i : 33 + i, 0:80] = v[...].astype(f32)
    tmp[0:1, 0:160] = b_in[...].astype(f32)
    srcf[36:37, 0:80] = tmp[0:1, 0:80]
    srcf[37:38, 0:80] = tmp[0:1, 80:160]
    srcf[40:80, 0:64] = hid_w[...].astype(f32)
    src = srcf[...].astype(bf16)
    row = iota((80, 128), 0)
    lane = iota((80, 128), 1)
    for q in range(4):
        col = 160 * q
        pkf[:, 0:160] = part[0:80, col : col + 160]
        pkf[:, 160:256] = jnp.zeros((80, 96), f32)
        place = (row < 32) & (row >= 8 * q) & (row < 8 * q + 8) & (lane == L_RES + row - 8 * q)
        place = place | ((row >= 32) & (row < 38) & (lane == L_VEC + row - 32))
        place = place | ((row >= 40) & (lane == L_HID + row - 40))
        pkf[:, 128:256] = pkf[:, 128:256] + dot_rows(src, one_hot(place))[0:80]
        pkf[64:65, 128 + L_HID : 128 + L_HID + 40] = hid_b[...].astype(f32)
        pkf[:, 256:416] = part[160:240, col : col + 160]
        pkf[:, 416:576] = part[240:320, col : col + 160]
        pkf[:, 576:736] = part[0:80, 640 + col : 800 + col]
        pkf[:, 736:896] = part[80:160, col : col + 160]
        pk[q] = pkf[...].astype(bf16)

    pl.semaphore_wait(barrier, len(peers))

    def cols(k, h):
        first, apart, width, _ = CHUNKS[k]
        return pl.ds(pl.multiple_of(first + apart * h, 128), width)

    def piece(k, member):
        first, _, width, at = CHUNKS[k]
        if at < 896:
            return pk.at[member, :, at : at + width]
        src, base = (win_in, 896) if at < 1536 else (wout_in, 1536)
        return src.at[:, pl.ds(pl.multiple_of(640 * member + at - base, 128), width)]

    group = ((mate, 2 * l + 1 - c), (beside, 2 - 2 * l + c), (corner, 3 - 2 * l - c))
    home = w.at[pl.ds(m16(HALF * f), HALF)]
    locals_in = {}

    def rows_of(to):
        return pl.ds(m16(HALF * to["fsdp"]), HALF)

    def g_first(k):
        dst = w.at[pl.ds(m16(HALF * f), HALF), cols(k, x)]
        for to, member in group:
            remote(piece(k, member), dst, in_s.at[0], in_r.at[k], to).start()
        locals_in[k] = pltpu.make_async_copy(piece(k, m), dst, lo_s.at[k])
        locals_in[k].start()

    w4 = w.reshape(4, 2, 160, C_ALL)
    g4 = g.reshape(4, 2, 160, C_ALL)

    def block(ref, k, flips):
        zz = 1 - zh if "z" in flips else zh
        yy = 1 - y if "y" in flips else y
        h = 1 - x if "x" in flips else x
        return ref.at[pl.ds(2 * zz, 2), yy, :, cols(k, h)]

    wide = sum(1 for chunk in CHUNKS if chunk[3] < C_MLP)

    def g_sem(k, i):
        return ag_r.at[4 * k + min(i, 3) if k < wide else 4 * wide + 2 * (k - wide) + min(i, 1)]

    def g_send(k, i, flips, axis):
        ref = block(w4, k, flips)
        remote(ref, ref, ag_s.at[0 if k < wide else 1], g_sem(k, i), along[axis]).start()

    def g_recv(k, i, flips):
        came(block(w4, k, flips), g_sem(k, i))

    def g_own(k):
        order = GATHER_ORDER[k]
        locals_in[k].wait()
        came(w.at[0 : 3 * HALF, 0 : CHUNKS[k][2]], in_r.at[k])
        for axis, i in zip(order, (0, 1, 3)):
            g_send(k, i, "", axis)

    def g_second(k):
        a, *rest = GATHER_ORDER[k]
        g_recv(k, 0, a)
        for axis, i in zip(rest, (2, 4)):
            g_send(k, i, a, axis)

    def g_third(k):
        a, b, d = GATHER_ORDER[k]
        g_recv(k, 1, b)
        g_send(k, 5, b, d)
        g_recv(k, 2, a + b)
        g_send(k, 6, a + b, d)

    def g_done(k):
        _, _, width, at = CHUNKS[k]
        if k < wide:
            came(rb.at[0:4, :, :, at : at + width], g_sem(k, 3))
        else:
            came(rbm.at[0:2, :, :, at - C_MLP : at - C_MLP + width], g_sem(k, 1))

    def s_buf(k, i):
        _, _, width, at = CHUNKS[k]
        return rb.at[i, :, :, at : at + width] if at < C_MLP else rbm.at[i, :, :, at - C_MLP : at - C_MLP + width]

    def s_sem(k, i):
        return rs_r.at[7 * k + i if k < wide else 7 * wide + 3 * (k - wide) + i]

    def s_send(k, i, flips, axis):
        remote(block(g4, k, flips), s_buf(k, i), rs_s.at[0 if k < wide else 1], s_sem(k, i), along[axis]).start()

    def s_add(k, i, flips, axis):
        came(s_buf(k, i), s_sem(k, i))
        _, _, width, at = CHUNKS[k]
        zz = 1 - zh if "z" in flips else zh
        yy = 1 - y if "y" in flips else y
        there = cols(k, 1 - x if "x" in flips else x)

        def step(j, carry):
            half = lax.div(j, 2)
            inside = 80 * (j - 2 * half)
            here = pl.ds(m16(640 * zz + 320 * half + 160 * yy + inside), 80)
            rows = pl.ds(m16(inside), 80)
            if at < C_MLP:
                more = rb[i, half, rows, at : at + width]
            else:
                more = rbm[i, half, rows, at - C_MLP : at - C_MLP + width]
            g[here, there] = g[here, there] + more
            return carry

        lax.fori_loop(0, 4, step, 0)

    def s_start(k):
        a, b, *last = SUM_ORDER[k]
        if last:
            d = last[0]
            s_send(k, 0, a + b + d, a)
            s_send(k, 1, a + b, a)
            s_send(k, 2, a + d, a)
            s_send(k, 3, a, a)
        else:
            s_send(k, 0, a + b, a)
            s_send(k, 1, a, a)
        s_at[k] = 0

    def s_step(k):
        a, b, *last = SUM_ORDER[k]
        stage = s_at[k]
        s_at[k] = stage + 1
        if not last:
            if stage == 0:
                s_add(k, 0, b, a)
                s_send(k, 2, b, b)
            elif stage == 1:
                s_add(k, 1, "", a)
            else:
                s_add(k, 2, "", b)
                s_out(k)
            return
        d = last[0]
        if stage == 0:
            s_add(k, 0, b + d, a)
            s_send(k, 4, b + d, b)
            s_add(k, 1, b, a)
            s_send(k, 5, b, b)
        elif stage == 1:
            s_add(k, 2, d, a)
            s_add(k, 4, d, b)
            s_send(k, 6, d, d)
        elif stage == 2:
            s_add(k, 3, "", a)
            s_add(k, 5, "", b)
        else:
            s_add(k, 6, "", d)
            s_out(k)

    def s_out(k):
        _, _, width, at = CHUNKS[k]
        dst = fb.at[m, :, at : at + width]
        for to, member in group:
            remote(g.at[rows_of(to), cols(k, x)], dst, fin_s.at[0], fin_r.at[0], to).start()
        pltpu.make_async_copy(g.at[pl.ds(m16(HALF * f), HALF), cols(k, x)], dst, keep_s.at[0]).start()

    s_at = {}

    def ar_tile(i):
        return slice(SPLIT * i, SPLIT * i + SPLIT)

    def cs_ref(a, p, i):
        rows = OWN if a in (2, 3) else PART
        return cs.at[a % 2, p, 0:rows, ar_tile(i)], cr.at[a % 2, p, 0:rows, ar_tile(i)]

    def total(a):
        return part3 if a == 3 else part

    def ar_begin(a, p):
        if a >= 2:
            left(cs.at[a % 2, p, 0 : OWN if a == 4 else PART, :], cs_s.at[a - 2, p])
        for i in range(2):
            for n, first in enumerate((0, TOK) if a in (2, 3) else (0,)):
                rows = slice(first + OWN * p, first + OWN * p + OWN)
                value = None
                for ref, lo, col, width in operands[a]:
                    more = dot_last(ref[rows, lo : lo + width], w[ar_tile(i), col : col + width])
                    value = more if value is None else value + more
                total(a)[rows, ar_tile(i)] = value
                away = pl.ds(m16(first + OWN * p + oth0), PART)
                cs[a % 2, p, PART * n : PART * n + PART, ar_tile(i)] = total(a)[away, ar_tile(i)].astype(bf16)
            src, there = cs_ref(a, p, i)
            remote(src, there, cs_s.at[a, p], cs_r.at[a, p, i], mate).start()

    def ar_cross(a, p):
        b = a - 2
        near = pl.ds(m16(TOK * x + OWN * p + own0), PART)
        far = pl.ds(m16(TOK * (1 - x) + OWN * p + own0), PART)
        for i in range(2):
            _, here = cs_ref(a, p, i)
            came(here, cs_r.at[a, p, i])
            more = cr[a % 2, p, pl.ds(m16(PART * (1 - x)), PART), ar_tile(i)].astype(f32)
            ys[b, p, :, ar_tile(i)] = (total(a)[far, ar_tile(i)] + more).astype(bf16)
            remote(
                ys.at[b, p, :, ar_tile(i)], yr.at[b, p, :, ar_tile(i)], ys_s.at[0], ys_r.at[b, p, i], along["x"]
            ).start()
            total(a)[near, ar_tile(i)] = total(a)[near, ar_tile(i)] + cr[
                a % 2, p, pl.ds(m16(PART * x), PART), ar_tile(i)
            ].astype(f32)

    def fold_out():
        for p in (0, 1):
            left(xs.at[1, p], xs_s.at[1, p])
        for i in range(2):
            for p in (0, 1):
                came(yr.at[1, p, :, ar_tile(i)], ys_r.at[1, p, i])
            mine = part3[pl.ds(m16(TOK * x + OWN * (1 - l) + own0), PART), ar_tile(i)]
            xs[1, 0, :, ar_tile(i)] = (mine + yr[1, 1 - l, :, ar_tile(i)].astype(f32)).astype(bf16)
            remote(
                xs.at[1, 0, :, ar_tile(i)], xr.at[0, 0, :, ar_tile(i)], xs_s.at[3, 0], xs_r.at[3, 0], beside
            ).start()

    def ar_mid(a, p):
        if a == 3:
            return fold_out()
        b = a % 2
        if a >= 2:
            left(xs.at[b, p], xs_s.at[a - 2, p])
        for i in range(2):
            if a == 2:
                came(yr.at[0, p, :, ar_tile(i)], ys_r.at[0, p, i])
                mine = part[pl.ds(m16(TOK * x + OWN * p + own0), PART), ar_tile(i)]
                more = yr[0, p, :, ar_tile(i)]
            else:
                came(cs_ref(a, p, i)[1], cs_r.at[a, p, i])
                mine = part[pl.ds(m16(OWN * p + own0), PART), ar_tile(i)]
                more = cr[b, p, 0:PART, ar_tile(i)]
            xs[b, p, :, ar_tile(i)] = (mine + more.astype(f32)).astype(bf16)
            remote(
                xs.at[b, p, :, ar_tile(i)], xr.at[a % 3, p, :, ar_tile(i)], xs_s.at[a, p], xs_r.at[a, p], beside
            ).start()

    def ar_end(a, p):
        came(xr.at[a % 3, p], xs_r.at[a, p])

    def summed(a, p, rows):
        return xs[a % 2, p, rows, :].astype(f32) + xr[a % 3, p, rows, :].astype(f32)

    def own_rows(body):
        def step(j, carry):
            body(pl.multiple_of(32 * j, 32))
            return carry

        lax.fori_loop(0, PART // 32, step, 0)

    def at32(start):
        return pl.ds(m16(start), 32)

    def share(j, p, ref, first=0, to=None):
        rows = ref.at[pl.ds(m16(first + OWN * p + own0), PART)]
        remote(rows, rows, nx_s.at[0], nx_r.at[j, p], mate if to is None else to).start()

    def shared(j, p, ref, first=0, start=None):
        came(ref.at[pl.ds(m16(first + OWN * p + (oth0 if start is None else start)), PART)], nx_r.at[j, p])

    def rms(v):
        return lax.rsqrt(jnp.mean(v * v, axis=-1, keepdims=True) + 1e-06)

    def fold(v):
        return jnp.sum(v.reshape(v.shape[0] // 8, 8, v.shape[1]), axis=0)

    def tiles_loop(count, body):
        def step(i, carry):
            body(pl.ds(pl.multiple_of(TILE * i, TILE), TILE), i)
            return carry

        lax.fori_loop(0, count, step, 0)

    def slab(h):
        return slice(128 + 256 * h, 256 + 256 * h)

    spread = one_hot(lax.div(iota((OWN, 12), 0), CTXLEN) == iota((OWN, 12), 1))
    right_patch = lax.div(iota((OWN, 512), 1), PL) == (iota((OWN, 512), 0) & (CTXLEN - 1))
    lane_of = iota((512, 128), 1)
    place_of = iota((512, 128), 0) & (PL - 1)
    mine0 = m16(OWN * l + own0)
    cot_part = cot_in.reshape(2, PART, D)
    cot_rows = cot.reshape(2, TOK, D)
    cot_copy = pltpu.make_async_copy(cot_part, cot_rows.at[:, pl.ds(mine0, PART)], lo_s.at[len(CHUNKS)])
    lane512 = iota((OWN, 512), 1) & 255
    units = lane512 < 160
    resids = (lane512 >= 128 + L_RES) & (lane512 < 128 + L_RES + 8)

    def part_rows(p, first=0):
        return slice(first + OWN * p, first + OWN * p + OWN)

    def features():
        keep = 1.0 - missing[...].astype(f32)
        seen = dot_plain(spread, (points[...].astype(f32) * keep).astype(bf16))
        gone = dot_plain(spread, missing[...].astype(f32).astype(bf16))
        feats = dot_plain(jnp.where(right_patch, seen, 0.0).astype(bf16), one_hot(lane_of == place_of))
        feats = feats + dot_plain(jnp.where(right_patch, gone, 0.0).astype(bf16), one_hot(lane_of == place_of + PL))
        ptx[0:OWN, :] = jnp.where(iota((OWN, 128), 1) == 2 * PL, 1.0, feats)
        fe[pl.ds(mine0, PART), :] = ptx[pl.ds(m16(PART * x), PART), :].astype(bf16)
        for to, member in group:
            rows = fe.at[pl.ds(mine0, PART)]
            remote(rows, rows, tk_s.at[0], tk_r.at[0], to).start()
        sums[...] = jnp.zeros(sums.shape, f32)
        hidf[...] = jnp.zeros(hidf.shape, f32)

    def cot_out():
        cot_copy.start()
        dst = cot_rows.at[:, pl.ds(mine0, PART)]
        remote(cot_part, dst, tk_s.at[1], tk_r.at[1], mate).start()
        remote(cot_part.at[x], cot_rows.at[x, pl.ds(mine0, PART)], tk_s.at[1], tk_r.at[2], beside).start()

    def cot_pass(stage):
        here = pl.ds(m16(OWN * (1 - l) + own0), PART)
        near, far = cot_rows.at[x, here], cot_rows.at[1 - x, here]
        if stage == 0:
            came(near, tk_r.at[2])
            remote(near, near, tk_s.at[1], tk_r.at[3], along["x"]).start()
            remote(near, near, tk_s.at[1], tk_r.at[4], mate).start()
        else:
            came(far, tk_r.at[3])
            remote(far, far, tk_s.at[1], tk_r.at[5], mate).start()

    def cot_here():
        cot_copy.wait()
        came(cot_rows.at[:, pl.ds(m16(OWN * l + oth0), PART)], tk_r.at[1])
        for i, xx in ((4, x), (5, 1 - x)):
            came(cot_rows.at[xx, pl.ds(m16(OWN * (1 - l) + oth0), PART)], tk_r.at[i])

    def hidden():
        for h in (0, 1):
            for j in range(4):
                rows = pl.ds(m16(320 * m + 80 * j), 80)
                tmp[:, 0:128] = w[rows, slab(h)].astype(f32)
                hidf[0:72, 256 * h + 40 * j : 256 * h + 40 * j + 40] = tmp[0:72, L_HID : L_HID + 40]
            row = iota((128, 128), 0)
            lane = iota((128, 128), 1)
            chosen = (lane >= L_RES) & (lane < L_RES + 8) & (row == PL * h + 8 * m + lane - L_RES)
            hidf[:, slab(h)] = jnp.where(chosen, 1.0, hidf[:, slab(h)])
        hid[...] = hidf[...].astype(bf16)
        came(fe.at[0 : 3 * PART], tk_r.at[0])

    def tokenize(p):
        v = dot_plain(fe[part_rows(p), :], hid[...])
        pret[part_rows(p), :] = v
        hc[part_rows(p), :] = jnp.where(
            units, v * jax.nn.sigmoid(v), jnp.where(resids, v, jnp.where(lane512 == 128 + L_ONE, 1.0, 0.0))
        ).astype(bf16)

    def vectors():
        row16 = iota((16, 128), 0)
        lane16 = iota((16, 128), 1)
        vec[...] = dot_last(one_hot((row16 < 4) & (lane16 == L_VEC + row16)), w[:, slab(0)])
        own_slab = pl.ds(pl.multiple_of(128 + 256 * x, 128), 128)
        pair = dot_last(one_hot((row16 < 2) & (lane16 == L_BIN + row16)), w[pl.ds(m16(320 * m), 320), own_slab])
        tmp[0:16, 0:320] = pair
        for j in range(4):
            at = 160 * j
            bin_s[0:1, at : at + 80] = tmp[0:1, 80 * j : 80 * j + 80]
            bin_s[0:1, at + 80 : at + 160] = tmp[1:2, 80 * j : 80 * j + 80]

    def first_norm(p):
        ar_end(0, p)

        def body(start):
            v = summed(0, p, pl.ds(start, 32)) + vec[3:4, :]
            x0[at32(PART * p + start), :] = v
            n1[at32(OWN * p + own0 + start), :] = (v * rms(v) * vec[0:1, :]).astype(bf16)

        own_rows(body)
        share(0, p, n1)

    def project(p):
        shared(0, p, n1)
        rows = part_rows(p)
        for h in (0, 1):
            for lo in (0, 256):
                col = C_QKV + 640 * h + lo
                part[rows, 512 * h + lo : 512 * h + lo + 256] = dot_plain(n1[rows, :], w[:, col : col + 256])

    def turn(p):
        def body(j, carry):
            rows = pl.ds(m16(OWN * p + 48 * j), 48)
            for h in (0, 1):
                v = part[rows, 512 * h : 512 * h + 512]
                v = v * rot_c[...] + pltpu.roll(v, 472, 1) * rot_a[...] + pltpu.roll(v, 40, 1) * rot_b[...]
                q_s[h, rows, :] = v[:, 0:256].astype(bf16)
                k_s[h, rows, :] = pltpu.roll(v, 352, 1)[:, 0:256].astype(bf16)
                v_s[h, rows, :] = pltpu.roll(v, 288, 1)[:, 0:256].astype(bf16)
            return carry

        lax.fori_loop(0, OWN // 48, body, 0)

    def one_head(v, first, i):
        lane = iota(v.shape, 1)
        inside = (lane >= first + HEAD_DIM * i) & (lane < first + HEAD_DIM * i + HEAD_DIM)
        return jnp.where(inside, v, jnp.zeros_like(v))

    def stacked(v, first):
        return jnp.concatenate([one_head(v, first, 0), one_head(v, first, 1)], axis=0)

    def by_head(probs, v, first):
        return dot_plain(probs[0:OWN], one_head(v, first, 0)) + dot_plain(probs[OWN:TOK], one_head(v, first, 1))

    def attend(p):
        rows = part_rows(p)
        qi = iota((TOK, OWN), 0)
        qi = jnp.where(qi >= OWN, qi - OWN, qi)
        kj = iota((TOK, OWN), 1)
        allowed = ((qi >> 4) == (kj >> 4)) & (kj <= qi)
        for h in (0, 1):
            scores = dot_last(stacked(q_s[h, rows, :], 0), k_s[h, rows, :]) * SCALE
            scores = jnp.where(allowed, scores, -1e30)
            e = jnp.exp(scores - jnp.max(scores, axis=-1, keepdims=True))
            probs = e * (1.0 / jnp.sum(e, axis=-1, keepdims=True))
            ps[p, h] = probs
            att[rows, 256 * h : 256 * h + 256] = by_head(probs.astype(bf16), v_s[h, rows, :], 96).astype(bf16)

    def second_norm(p):
        ar_end(1, p)

        def body(start):
            own = at32(PART * p + start)
            v = x0[own, :] + summed(1, p, pl.ds(start, 32))
            x1[own, :] = v
            n2[at32(TOK * x + OWN * p + own0 + start), :] = (v * rms(v) * vec[1:2, :]).astype(bf16)

        own_rows(body)
        share(1, p, n2, TOK * x, along["x"])
        share(4, p, n2, TOK * x)

    def norm_pass(p):
        far = TOK * (1 - x)
        shared(1, p, n2, far, own0)
        rows = n2.at[pl.ds(m16(far + OWN * p + own0), PART)]
        remote(rows, rows, nx_s.at[0], nx_r.at[5, p], mate).start()

    def inner(which, p):
        first = TOK * (x if which == 0 else 1 - x)
        shared(4 if which == 0 else 5, p, n2, first)
        rows = pl.ds(m16(first + OWN * p), OWN)
        for lo, width in MLP_TILES:
            at = slice(lo, lo + width)
            v = dot_plain(n2[rows, :], w[:, C_IN + lo : C_IN + lo + width]) + bin_s[0:1, at]
            pre[rows, at] = v
            act[rows, at] = (v * jax.nn.sigmoid(v)).astype(bf16)

    def outer_back(p):
        for first in (0, TOK):
            rows = part_rows(p, first)
            for lo, width in MLP_TILES:
                at = slice(lo, lo + width)
                v = pre[rows, at]
                s = jax.nn.sigmoid(v)
                d = dot_plain(cot[rows, :], w[:, C_OUT + lo : C_OUT + lo + width])
                dpre[rows, at] = (d * (s * (1.0 + v * (1.0 - s)))).astype(bf16)

    def norm_back(dn, v, gain):
        r = rms(v)
        xh = v * r
        scaled = dn * gain
        inside = jnp.mean(scaled * xh, axis=-1, keepdims=True)
        return r * (scaled - xh * inside), fold(dn * xh)

    def second_back(p):
        ar_end(2, p)

        def body(start):
            own = at32(PART * p + start)
            d, by_gain = norm_back(summed(2, p, pl.ds(start, 32)), x1[own, :], vec[1:2, :])
            ct = cot[at32(TOK * x + OWN * p + own0 + start), :].astype(f32)
            d = ct + d
            x2[own, :] = d
            db[at32(OWN * p + own0 + start), :] = d.astype(bf16)
            sums[8:16, :] += by_gain
            sums[16:24, :] += fold(ct)

        own_rows(body)
        share(2, p, db)

    def attended_back(p):
        shared(2, p, db)
        rows = part_rows(p)
        for h in (0, 1):
            col = C_QKV + 640 * h + 384
            datt[rows, 256 * h : 256 * h + 256] = dot_plain(db[rows, :], w[:, col : col + 256]).astype(bf16)

    def attend_back(p):
        rows = part_rows(p)
        for h in (0, 1):
            probs = ps[p, h]
            heads_d = stacked(datt[rows, 256 * h : 256 * h + 256], 96)
            dp = dot_last(heads_d, v_s[h, rows, :])
            ds = (probs * (dp - jnp.sum(probs * dp, axis=-1, keepdims=True))).astype(bf16)
            part[rows, 512 * h : 512 * h + 256] = by_head(ds, k_s[h, rows, :], 0) * SCALE
            part[rows, 512 * h + 160 : 512 * h + 416] = dot_rows(ds, stacked(q_s[h, rows, :], 0)) * SCALE
            dv = dot_rows(probs.astype(bf16), heads_d)
            dv = jnp.concatenate([dv, jnp.zeros((OWN, 128), f32)], axis=1)
            part[rows, 512 * h + 320 : 512 * h + 512] = dv[:, 96:288]

    def turn_back(p):
        def body(j, carry):
            rows = pl.ds(m16(OWN * p + 48 * j), 48)
            for h in (0, 1):
                v = part[rows, 512 * h : 512 * h + 512]
                v = v * rot_c[...] - pltpu.roll(v, 472, 1) * rot_a[...] - pltpu.roll(v, 40, 1) * rot_b[...]
                dpj[rows, 512 * h : 512 * h + 512] = v.astype(bf16)
            return carry

        lax.fori_loop(0, OWN // 48, body, 0)

    def finish():
        ar_end(3, 0)

        def body(start):
            rows = pl.ds(start, 32)
            v = part3[at32(TOK * x + OWN * l + own0 + start), :] + yr[1, l, rows, :].astype(f32)
            v = v + xr[0, 0, rows, :].astype(f32)
            ob[rows, :] = (x1[at32(PART * l + start), :] + v + vec[2:3, :]).astype(bf16)

        own_rows(body)
        ref = out_o.at[pl.ds(m16(PART * x), PART)]
        go(remote(ob, ref, pt_s.at[3], pt_r.at[3], along["x"]))
        pltpu.make_async_copy(ob, ref, keep_s.at[1]).start()

    def grad_mlp(k, left, right, base):
        first, _, width, _ = CHUNKS[k]

        def body(rows, i):
            lo = first - base
            g[rows, first : first + width] = dot_rows(left[:, rows], right[:, lo : lo + width]).astype(bf16)

        tiles_loop(TILES, body)
        s_start(k)

    def grad_out(k):
        grad_mlp(k, cot, act, C_OUT)

    def grad_in(k):
        grad_mlp(k, n2, dpre, C_IN)

    def grad_qkv(k):
        first, apart, width, _ = CHUNKS[k]
        lo, hi = first - C_QKV, first - C_QKV + width
        mid, cut = min(hi, 512), max(lo, 384)

        def body(rows, i):
            for h in (0, 1):
                col = C_QKV + apart * h
                if lo < mid:
                    value = dot_rows(n1[:, rows], dpj[:, 512 * h + lo : 512 * h + mid])
                    if cut >= mid:
                        g[rows, col + lo : col + mid] = value.astype(bf16)
                    else:
                        more = dot_rows(db[:, rows], att[:, 256 * h + cut - 384 : 256 * h + mid - 384])
                        if cut > lo:
                            g[rows, col + lo : col + cut] = value[:, 0 : cut - lo].astype(bf16)
                        g[rows, col + cut : col + mid] = (value[:, cut - lo :] + more).astype(bf16)
                if hi > 512:
                    start = max(lo, 512)
                    value = dot_rows(db[:, rows], att[:, 256 * h + start - 384 : 256 * h + hi - 384])
                    g[rows, col + start : col + hi] = value.astype(bf16)

        tiles_loop(TILES, body)
        s_start(k)

    def grad_bias():
        ones = one_hot((iota((BOTH, 128), 1) >= L_BIN) & (iota((BOTH, 128), 1) < L_BIN + 2))
        for lo, width in MLP_TILES:
            gbs[lo : lo + width, :] = dot_rows(dpre[:, lo : lo + width], ones)

    def first_back(p):
        ar_end(4, p)

        def body(start):
            own = at32(PART * p + start)
            d, by_gain = norm_back(summed(4, p, pl.ds(start, 32)), x0[own, :], vec[0:1, :])
            de[at32(OWN * p + own0 + start), :] = (x2[own, :] + d).astype(bf16)
            sums[0:8, :] += by_gain

        own_rows(body)
        share(3, p, de)

    def hidden_back(p):
        shared(3, p, de)
        rows = part_rows(p)
        v = pret[rows, :]
        s = jax.nn.sigmoid(v)
        d = dot_plain(de[rows, :], w[:, 0:512])
        dpe[rows, :] = jnp.where(units, d * (s * (1.0 + v * (1.0 - s))), jnp.where(resids, d, 0.0)).astype(bf16)

    def grad_tok():
        row32 = iota((32, 128), 0)
        pick = one_hot((row32 < 24) & (iota((32, 128), 1) == L_VEC + (row32 >> 3)))

        def body(rows, i):
            both = dot_rows(de[:, rows], hc[...])
            columns = dot_rows(sums[:, rows].astype(bf16), pick)
            for h in (0, 1):
                g[rows, 256 * h : 256 * h + 128] = both[:, 256 * h : 256 * h + 128].astype(bf16)
                g[rows, slab(h)] = (both[:, slab(h)] + columns).astype(bf16)

        tiles_loop(TILES, body)
        s_start(0)

    def grad_hidden():
        ghs[...] = dot_rows(fe[...], dpe[...])
        lane = iota((80, 128), 1)
        for h in (0, 1):
            for j in range(4):
                at = 160 * j
                tmp[:, 0:128] = jnp.where((lane == L_BIN) & (x == h), gbs[at : at + 80, :], 0.0) + jnp.where(
                    (lane == L_BIN + 1) & (x == h), gbs[at + 80 : at + 160, :], 0.0
                )
                tmp[:, L_HID : L_HID + 40] = ghs[0:80, 256 * h + 40 * j : 256 * h + 40 * j + 40]
                rows = pl.ds(m16(320 * m + 80 * j), 80)
                g[rows, slab(h)] = (g[rows, slab(h)].astype(f32) + tmp[:, 0:128]).astype(bf16)
        s_start(1)

    def points_back(stage):
        if stage == 0:
            ptx[...] = dot_last(dpe[...], hid[...])
            away = ptx.reshape(2, OWN, 128).at[:, pl.ds(oth0, PART)]
            go(remote(away, ptr.at[0], pt_s.at[0], pt_r.at[0], mate))
        elif stage == 1:
            remote(ptr.at[0], ptr.at[0], pt_s.at[0], pt_r.at[0], mate).wait_recv()
            for p in (0, 1):
                ptr[1, p] = ptx[pl.ds(m16(OWN * p + own0), PART), :] + ptr[0, p]
            go(remote(ptr.at[1, 1 - l], ptr.at[2, 1 - l], pt_s.at[1], pt_r.at[1], beside))
        elif stage == 2:
            there = ptr.at[2, l]
            remote(there, there, pt_s.at[1], pt_r.at[1], beside).wait_recv()
            ptr[3, x] = ptr[1, l] + ptr[2, l]
            go(remote(ptr.at[3, x], ptr.at[3, x], pt_s.at[2], pt_r.at[2], along["x"]))
        else:
            there = ptr.at[3, 1 - x]
            remote(there, there, pt_s.at[2], pt_r.at[2], along["x"]).wait_recv()
            every = ptr[3].reshape(OWN, 128).astype(bf16)
            wide = dot_last(every, one_hot(lane_of == place_of))
            wide = jnp.where(right_patch, wide, 0.0).astype(bf16)
            pts_v[...] = dot_rows(spread, wide) * (1.0 - missing[...].astype(f32))
            pltpu.make_async_copy(pts_v, pts_o, keep_s.at[2]).start()

    operands = (
        ((hc, 0, 0, 512),),
        ((att, 0, 896, 256), (att, 256, 1536, 256)),
        ((dpre, 0, C_IN, 640),),
        ((act, 0, C_OUT, 640),),
        ((dpj, 0, 512, 512), (dpj, 512, 1152, 512)),
    )
    steps = (
        g_first, g_own, g_second, g_third, g_done, s_step, features, cot_out, cot_here, tokenize, vectors,
        first_norm, project, turn, attend, second_norm, inner, grad_out, outer_back, grad_in, second_back,
        attended_back, attend_back, turn_back, finish, grad_qkv, grad_bias, first_back, hidden_back, grad_tok,
        grad_hidden, points_back, ar_begin, ar_mid, cot_pass, norm_pass, ar_cross, hidden,
    )
    for name, *which in PLAN:
        steps[name](*which)

    came(out_o.at[pl.ds(m16(PART * (1 - x)), PART)], pt_r.at[3])
    came(fb.at[0:3], fin_r.at[0])
    pltpu.make_async_copy(g.at[0:HALF, 0:C_ONE], fb.at[m], keep_s.at[0]).wait()
    pltpu.make_async_copy(ob, out_o.at[pl.ds(m16(PART * x), PART)], keep_s.at[1]).wait()
    pltpu.make_async_copy(pts_v, pts_o, keep_s.at[2]).wait()
    for ref, sem in (
        (rb, ag_s.at[0]), (rbm, ag_s.at[1]), (rb, rs_s.at[0]), (rbm, rs_s.at[1]),
        (w.at[0 : 3 * HALF, 0:C_ONE], in_s.at[0]), (g.at[0 : 3 * HALF, 0:C_ONE], fin_s.at[0]),
        (cs.at[1, 0], cs_s.at[3, 0]), (cs.at[1, 1], cs_s.at[3, 1]),
        (cs.at[0, 0, 0:PART], cs_s.at[4, 0]), (cs.at[0, 1, 0:PART], cs_s.at[4, 1]),
        (xs.at[1, 0], xs_s.at[3, 0]), (xs.at[0, 0], xs_s.at[4, 0]), (xs.at[0, 1], xs_s.at[4, 1]),
        (ys, ys_s.at[0]), (w.at[0 : 12 * PART, 0:D], nx_s.at[0]),
        (fe.at[0 : 3 * PART], tk_s.at[0]), (cot.at[0 : 6 * PART], tk_s.at[1]),
    ):
        left(ref, sem)
    for copy in sent:
        copy.wait_send()


def unpack_kernel(
    out_i, pts_i, fb_i,
    out_o, pts_o, hw_o, hb_o, tok_o, res_o, tokb_o, gain1_o, qkv_o, att_o, gain2_o, in_o, inb_o, outw_o, outb_o,
    fb, sem,
):
    f32 = jnp.float32
    copies = [pltpu.make_async_copy(fb_i.at[q], fb.at[q], sem.at[q]) for q in range(4)]
    copies.append(pltpu.make_async_copy(out_i, out_o, sem.at[4]))
    for copy in copies:
        copy.start()
    pts_o[...] = pts_i[...]
    turned = []
    hidden = jnp.zeros((8, 128), f32)
    for q in range(4):
        copies[q].wait()
        at = slice(160 * q, 160 * q + 160)
        lead = fb[q, :, 0:256].astype(f32)
        tok_o[:, at] = lead[:, 0:160]
        tile = lead[:, 128:256]
        hidden = hidden + tile[64:72]
        t = jnp.transpose(jnp.concatenate([tile, jnp.zeros((48, 128), f32)], axis=0))
        turned.append(t)
        res_o[8 * q : 8 * q + 8, :] = t[L_RES : L_RES + 8, 0:80]
        qkv = fb[q, :, 256:896].astype(f32)
        for j in range(3):
            qkv_o[j, :, at] = qkv[:, 160 * j : 160 * j + 160]
        att_o[:, at] = qkv[:, 480:640]
        in_o[:, 640 * q : 640 * q + 640] = fb[q, :, 896:1536].astype(f32)
        outw_o[:, 640 * q : 640 * q + 640] = fb[q, :, 1536:2176].astype(f32)
    both = turned[0] + turned[1]
    every = both + turned[2] + turned[3]
    tokb_o[...] = turned[0][L_ONE : L_ONE + 1, 0:80]
    gain1_o[...] = both[L_VEC : L_VEC + 1, 0:80]
    gain2_o[...] = both[L_VEC + 1 : L_VEC + 2, 0:80]
    outb_o[...] = both[L_VEC + 2 : L_VEC + 3, 0:80]
    inb_o[:, 0:80] = every[L_BIN : L_BIN + 1, 0:80]
    inb_o[:, 80:160] = every[L_BIN + 1 : L_BIN + 2, 0:80]
    hw_o[...] = every[L_HID : L_HID + 40, 0:64]
    hb_o[...] = hidden[0:1, L_HID : L_HID + 40]
    copies[4].wait()


def rotary_lanes():
    lanes = np.arange(512)
    inside = lanes % HEAD_DIM
    turned = lanes < 320
    freqs = 10000.0 ** (-2.0 * (inside % 40) / HEAD_DIM)
    angles = (np.arange(48) % CTXLEN)[:, None] * freqs[None, :]
    cosine = np.where(turned, np.cos(angles), 1.0)
    sine = np.where(turned, np.sin(angles), 0.0)
    lower = np.where(inside < 40, -sine, 0.0)
    upper = np.where(inside >= 40, sine, 0.0)
    return [np.asarray(t, np.float32) for t in (cosine, lower, upper)]


def fast_body(
    points, missing, tok_hidden_w, tok_hidden_b, tok_out_w, tok_res_w, tok_out_b, attn_gain, qkv_w, attn_out_w,
    mlp_gain, mlp_in_w, mlp_in_b, mlp_out_w, mlp_out_b, cotangent,
):
    f32, bf16 = jnp.float32, jnp.bfloat16
    any_space = pl.BlockSpec(memory_space=pl.ANY)
    vmem = pl.BlockSpec(memory_space=pltpu.VMEM)

    def sems(*shape):
        return pltpu.SemaphoreType.DMA(shape)

    def like(*shape):
        return jax.ShapeDtypeStruct(shape, f32)

    chunks = len(CHUNKS)
    wide = sum(1 for chunk in CHUNKS if chunk[3] < C_MLP)
    specs = [vmem] * 19
    specs[11] = specs[13] = specs[15] = any_space
    out, pts, packed = pl.pallas_call(
        layer_kernel,
        out_shape=(
            jax.ShapeDtypeStruct((OWN, D), bf16),
            like(12, 512),
            jax.ShapeDtypeStruct((4, HALF, C_ONE), bf16),
        ),
        in_specs=specs,
        out_specs=[any_space] * 3,
        scratch_shapes=[
            pltpu.VMEM((D, C_ALL), bf16),
            pltpu.VMEM((D, C_ALL), bf16),
            pltpu.VMEM((7, 2, 160, C_MLP), bf16),
            pltpu.VMEM((3, 2, 160, C_ONE - C_MLP), bf16),
            pltpu.VMEM((TOK, 128), bf16),
            pltpu.VMEM((BOTH, D), bf16),
            pltpu.VMEM((BOTH, D), f32),
            pltpu.VMEM((BOTH, 640), f32),
            pltpu.VMEM((BOTH, 640), bf16),
            pltpu.VMEM((BOTH, 640), bf16),
            pltpu.VMEM((TOK, D), bf16),
            pltpu.VMEM((BOTH, D), bf16),
            pltpu.VMEM((TOK, D), bf16),
            pltpu.VMEM((TOK, D), bf16),
            pltpu.VMEM((OWN, D), f32),
            pltpu.VMEM((OWN, D), f32),
            pltpu.VMEM((OWN, D), f32),
            pltpu.VMEM((TOK, 512), bf16),
            pltpu.VMEM((TOK, 512), bf16),
            pltpu.VMEM((TOK, 512), f32),
            pltpu.VMEM((2, TOK, 256), bf16),
            pltpu.VMEM((2, TOK, 256), bf16),
            pltpu.VMEM((2, TOK, 256), bf16),
            pltpu.VMEM((TOK, 512), bf16),
            pltpu.VMEM((TOK, 512), bf16),
            pltpu.VMEM((TOK, 1024), bf16),
            pltpu.VMEM((2, 2, TOK, OWN), f32),
            pltpu.VMEM((640, 128), f32),
            pltpu.VMEM((128, 512), f32),
            pltpu.VMEM((128, 512), f32),
            pltpu.VMEM((128, 512), bf16),
            pltpu.VMEM((16, D), f32),
            pltpu.VMEM((8, 640), f32),
            pltpu.VMEM((32, D), f32),
            pltpu.VMEM((TOK, 128), f32),
            pltpu.VMEM((4, 2, PART, 128), f32),
            pltpu.VMEM((4, HALF, 896), bf16),
            pltpu.VMEM((HALF, 896), f32),
            pltpu.VMEM((HALF, 128), f32),
            pltpu.VMEM((HALF, 384), f32),
            pltpu.VMEM((BOTH, D), f32),
            pltpu.VMEM((PART, D), bf16),
            pltpu.VMEM((12, 512), f32),
            pltpu.VMEM((2, 2, OWN, D), bf16),
            pltpu.VMEM((2, 2, OWN, D), bf16),
            pltpu.VMEM((2, 2, PART, D), bf16),
            pltpu.VMEM((2, 2, PART, D), bf16),
            pltpu.VMEM((2, 2, PART, D), bf16),
            pltpu.VMEM((3, 2, PART, D), bf16),
            sems(2), sems(4 * wide + 2 * (chunks - wide)), sems(2), sems(7 * wide + 3 * (chunks - wide)),
            sems(5, 2), sems(5, 2, 2), sems(5, 2), sems(5, 2), sems(1), sems(2, 2, 2),
            sems(1), sems(6, 2), sems(1), sems(chunks), sems(chunks + 1), sems(2), sems(6),
            sems(1), sems(1), sems(4), sems(4), sems(3),
        ],
        compiler_params=pltpu.CompilerParams(
            collective_id=0, has_side_effects=True, vmem_limit_bytes=64 * 1024 * 1024 - 512 * 1024
        ),
        cost_estimate=pl.CostEstimate(flops=13 * 10**9, bytes_accessed=10**7, transcendentals=10**6),
    )(
        points, missing, tok_hidden_w[0], tok_hidden_b, tok_out_w, tok_res_w.T, tok_out_b[None], attn_gain[None],
        qkv_w.transpose(1, 0, 2), attn_out_w, mlp_gain[None], mlp_in_w, mlp_in_b, mlp_out_w, mlp_out_b[None],
        cotangent, *[jnp.asarray(t) for t in rotary_lanes()],
    )
    (
        output, points_grad, hidden_w, hidden_b, tok, res_t, tok_b, gain1, qkv, att, gain2, inner, inner_b, outer,
        outer_b,
    ) = pl.pallas_call(
        unpack_kernel,
        out_shape=(
            jax.ShapeDtypeStruct((OWN, D), bf16),
            like(12, 512), like(40, 64), like(1, 40), like(HALF, 640), like(32, HALF), like(1, HALF), like(1, HALF),
            like(3, HALF, 640), like(HALF, 640), like(1, HALF), like(HALF, 2560), like(1, 160), like(HALF, 2560),
            like(1, HALF),
        ),
        in_specs=[any_space, vmem, any_space],
        out_specs=[vmem] * 15,
        scratch_shapes=[pltpu.VMEM((4, HALF, C_ONE), bf16), sems(5)],
        compiler_params=pltpu.CompilerParams(vmem_limit_bytes=63 * 1024 * 1024),
    )(out, pts, packed)
    return (
        output, points_grad, hidden_w[None], hidden_b, tok, res_t.T, tok_b[0], gain1[0], qkv.transpose(1, 0, 2), att,
        gain2[0], inner, inner_b, outer, outer_b[0],
    )


def solution(mesh):
    placed = (
        P("fsdp", None),
        P("fsdp", None),
        P("tp", "fsdp", None),
        P("tp", "fsdp"),
        P("fsdp", "tp"),
        P("fsdp", "tp"),
        P("fsdp"),
        P("fsdp"),
        P("fsdp", None, "tp"),
        P("fsdp", "tp"),
        P("fsdp"),
        P("fsdp", "tp"),
        P("tp", "fsdp"),
        P("fsdp", "tp"),
        P("fsdp"),
        P("fsdp", None),
    )
    small_slice = mesh.shape["fsdp"] == 16 and mesh.shape["tp"] == 2
    return jax.shard_map(
        fast_body if small_slice else body,
        mesh=mesh,
        in_specs=placed,
        out_specs=(
            P("fsdp", None),
            P("fsdp", None),
            P("tp", "fsdp", None),
            P("tp", "fsdp"),
            P("fsdp", "tp"),
            P("fsdp", "tp"),
            P("fsdp"),
            P("fsdp"),
            P("fsdp", None, "tp"),
            P("fsdp", "tp"),
            P("fsdp"),
            P("fsdp", "tp"),
            P("tp", "fsdp"),
            P("fsdp", "tp"),
            P("fsdp"),
        ),
        check_vma=False,
    )
```
